32 devices in a mesh: expert: 4 (over z), dp: 8 (over y, x, core).
Axes of the slice: x: 2, y: 2, z: 4, core: 2. Of those that a mesh axis runs over, the one named last changes fastest.
Arguments:
- tokens: bfloat16 [8, 2560, 768], P('dp', 'expert'), may hold values from -6 to 6
- prior_logits: float32 [8, 2560, 12], P('dp', 'expert'), may hold values from -6 to 6
- routes: int32 [8, 2560, 2], P('dp', 'expert'), may hold values from 0 to 11, all different within a row; in each aligned block of 640 rows (0 to 639, 640 to 1279, ..., all dimensions but the last counted through in order) at most 160 rows name the same one
- parents: int32 [8, 12], P('dp'), may hold values from 0 to 4, as said below
- cotangent: bfloat16 [8, 2560, 768], P('dp', 'expert'), may hold values from -6 to 6
- query_weight: bfloat16 [768, 768], replicated, may hold values from -0.3125 to 0.3125
- key_weight: bfloat16 [768, 768], replicated, may hold values from -0.21875 to 0.21875
- value_weight: bfloat16 [768, 768], replicated, may hold values from -0.21875 to 0.21875
- out_weight: bfloat16 [768, 768], replicated, may hold values from -0.875 to 0.875
- attention_gain: float32 [768], replicated, may hold values from 0.5 to 1.5
- expert_gain: float32 [768], replicated, may hold values from 0.5 to 1.5
- router_weight: bfloat16 [768, 12], replicated, may hold values from -0.15625 to 0.15625
- prior_weight: float32 [12, 12], replicated, may hold values from -0.875 to 0.875
- constant_weight: bfloat16 [768, 4], replicated, may hold values from -0.21875 to 0.21875
- constant_vector: float32 [2, 768], replicated, may hold values from -6 to 6
- gate_weight: bfloat16 [8, 768, 2048], P('expert', 'dp'), may hold values from -0.21875 to 0.21875
- up_weight: bfloat16 [8, 768, 2048], P('expert', 'dp'), may hold values from -0.21875 to 0.21875
- down_weight: bfloat16 [8, 2048, 768], P('expert', 'dp'), may hold values from -0.25 to 0.25
Outputs:
- output: bfloat16 [8, 2560, 768], P('dp', 'expert')
- tokens_grad: float32 [8, 2560, 768], P('dp', 'expert')
- prior_grad: float32 [8, 2560, 12], P('dp', 'expert')
- query_grad: float32 [768, 768], P('expert')
- key_grad: float32 [768, 768], P('expert')
- value_grad: float32 [768, 768], P('expert')
- out_grad: float32 [768, 768], P('expert')
- attention_gain_grad: float32 [768], P('expert')
- expert_gain_grad: float32 [768], P('expert')
- router_grad: float32 [768, 12], P('expert')
- prior_weight_grad: float32 [12, 12], P('expert')
- constant_weight_grad: float32 [768, 4], P('expert')
- constant_vector_grad: float32 [2, 768], P(None, 'expert')
- gate_grad: float32 [8, 768, 2048], P('expert', 'dp')
- up_grad: float32 [8, 768, 2048], P('expert', 'dp')
- down_grad: float32 [8, 2048, 768], P('expert', 'dp')
The draws below stay inside these ranges and needn't reach their ends.
Inputs may be any that keep to these rules, and one draw needn't show every extreme that they name: `routes`: each row names two different experts: 0 to 7 feed-forward, 8 zero, 9 copy, 10 and 11 constant. The rows of one device name no expert more than 160 times, a bound that some block reaches. `parents`: entry i names the parent of segment i + 1: for the branches (i < 4) a segment before it, for the leaves one of the branches 1 to 4.
All inputs are finite; a program needn't handle non-finite values.
Results may differ from the reference program's by a relative error of at most 0.03.
Values may be sent and summed in bfloat16 or wider, within the bound.
A program may use at most 192 MiB of HBM per device.

```python
import math
import jax
import jax.numpy as jnp
import numpy as np
from jax import lax

D = 768
FF = 2048
NFFN = 8
SEG = 128
HEAD_DIM = 64
NEXP_ALL = 12
TRUNK = 1024
TREE_LEN = 2560
TOK_DEV = 640
CAP = 160
TREES = 8


def draw_parents(key, part):
    key = jax.random.fold_in(key, 11)
    column = jnp.arange(12, dtype=jnp.int32)
    lowest = jnp.where(column < 4, 0, 1).astype(jnp.int32)
    choices_each = jnp.where(column < 4, column + 1, 4).astype(jnp.int32)
    random_bits = jax.random.randint(key, (TREES, 12), 0, 1 << 20, dtype=jnp.int32)
    return (lowest[None, :] + random_bits % choices_each[None, :]).astype(jnp.int32)


def block_levels(stream_key, extent, shards, smallest, top_value):
    level = 1.0
    for position, blocks in shards:
        steps = jax.random.uniform(jax.random.fold_in(jax.random.fold_in(stream_key, 6), position), (blocks,), jnp.float32, smallest / len(shards), top_value / len(shards))
        level = level * jnp.repeat(jnp.exp(steps), extent[position] // blocks).reshape((-1,) + (1,) * (len(extent) - 1 - position))
    return level


def deal_out(key, own, number, rows, amount, top, reach, skew):
    order = jax.random.permutation(key, amount)
    crowded, usual = load_shares(amount, rows * top, reach, skew, True), load_shares(amount, rows * top, reach, skew, False)
    places = jnp.arange(amount)

    def named(sizes, turn):
        used = int((sizes > 0).sum())
        fixed = max(1, used // 4)
        shifted = fixed + (places - fixed + turn * (used - fixed)) % max(1, amount - fixed)
        return jnp.zeros((amount,), jnp.int32).at[order[jnp.where(places < fixed, places, shifted)]].set(jnp.asarray(sizes, jnp.int32))

    sizes = jnp.where(number % 4 == 0, named(crowded, number // 4), named(usual, number - number // 4 - 1))
    mixed = jax.random.permutation(jax.random.fold_in(own, 3), amount)
    giver, receiver = mixed[0:amount // 2 * 2:2], mixed[1:amount // 2 * 2:2]
    room = jnp.minimum(sizes[giver] - 1, reach - sizes[receiver]) // 2
    room = jnp.where((giver == order[0]) | (receiver == order[0]) | (sizes[receiver] == 0), 0, jnp.maximum(room, 0))
    shifted = jax.random.randint(jax.random.fold_in(own, 4), (amount // 2,), 0, 1 << 20) % (room + 1)
    sizes = sizes.at[giver].add(-shifted).at[receiver].add(shifted)
    members = jnp.searchsorted(jnp.cumsum(sizes), jnp.arange(rows * top), side="right").astype(jnp.int32)
    grid = members.reshape(top, rows).T
    grid = grid[jax.random.permutation(jax.random.fold_in(own, 1), rows)]
    turn = jax.random.randint(jax.random.fold_in(own, 2), (rows, 1), 0, top)
    return jnp.take_along_axis(grid, (jnp.arange(top)[None, :] + turn) % top, axis=1)


def load_shares(number_of, total, limit, lean, full):
    weights = [(1 << 20) // math.isqrt(grade ** lean) + 1 for grade in range(1, number_of + 1)]
    largest = limit if full else min(limit, max(-(-total // number_of), total * weights[0] // sum(weights)))
    least = 1 if total - largest >= number_of - 1 else 0
    counts, surplus = [largest] + [least] * (number_of - 1), total - largest - least * (number_of - 1)
    while surplus > 0:
        candidates = [i for i in range(1, number_of) if counts[i] < largest] or [i for i in range(1, number_of) if counts[i] < limit]
        whole, budget = sum([weights[i] for i in candidates]), surplus
        for i in candidates:
            extra = min(limit - counts[i], max(1, budget * weights[i] // whole), surplus)
            counts[i] = counts[i] + extra
            surplus = surplus - extra
    return np.array(counts)


def noise(rng, dims, spread, most, shards=(), kind=jnp.bfloat16):
    gain = block_levels(rng, dims, shards, -0.22, 0.18) if shards else 1.0
    result = jax.random.normal(rng, dims, jnp.float32) * spread * gain
    return jnp.minimum(jnp.maximum(result, -most), most).astype(kind)


def setup_inputs(seed: int = 0) -> dict:
    seeds = jax.random.split(jax.random.key(seed), 19)
    tokens = noise(seeds[0], (TREES, TREE_LEN, D), 1.0, 6.0, ((0, 8), (1, 4)))
    prior_logits = noise(seeds[1], (TREES, TREE_LEN, NEXP_ALL), 1.0, 6.0, ((0, 8), (1, 4)), jnp.float32)
    routes_keys = jax.random.split(jax.random.fold_in(seeds[2], 1), TREES * TREE_LEN // TOK_DEV)
    routes_turns = jax.random.permutation(jax.random.fold_in(seeds[2], 3), TREES * TREE_LEN // TOK_DEV)
    routes = jax.vmap(lambda own, number: deal_out(jax.random.fold_in(seeds[2], 2), own, number, TOK_DEV, NEXP_ALL, 2, CAP, 2))(routes_keys, routes_turns).reshape((TREES, TREE_LEN, 2))
    parents = draw_parents(jax.random.fold_in(seeds[18], 71), 0)
    cotangent = noise(seeds[4], (TREES, TREE_LEN, D), 1.0, 6.0, ((0, 8), (1, 4)))
    query_weight = noise(seeds[5], (D, D), (D // 2) ** -0.5, 0.3125)
    key_weight = noise(seeds[6], (D, D), D ** -0.5, 0.21875)
    value_weight = noise(seeds[7], (D, D), D ** -0.5, 0.21875)
    out_weight = noise(seeds[8], (D, D), (D // 16) ** -0.5, 0.875)
    attention_gain = jnp.clip(1.0 + 0.1 * jax.random.normal(seeds[9], (D,), jnp.float32), 0.5, 1.5)
    expert_gain = jnp.clip(1.0 + 0.1 * jax.random.normal(seeds[10], (D,), jnp.float32), 0.5, 1.5)
    router_weight = noise(seeds[11], (D, NEXP_ALL), (2 * D) ** -0.5, 0.15625)
    prior_weight = noise(seeds[12], (NEXP_ALL, NEXP_ALL), (4 * NEXP_ALL) ** -0.5, 0.875, (), jnp.float32)
    constant_weight = noise(seeds[13], (D, 4), D ** -0.5, 0.21875)
    constant_vector = noise(seeds[14], (2, D), 1.0, 6.0, (), jnp.float32)
    gate_weight = noise(seeds[15], (NFFN, D, FF), D ** -0.5, 0.21875, ((0, 4), (1, 8)))
    up_weight = noise(seeds[16], (NFFN, D, FF), D ** -0.5, 0.21875, ((0, 4), (1, 8)))
    down_weight = noise(seeds[17], (NFFN, FF, D), (FF // 4) ** -0.5, 0.25, ((0, 4), (1, 8)))
    return dict(tokens=tokens, prior_logits=prior_logits, routes=routes, parents=parents, cotangent=cotangent, query_weight=query_weight, key_weight=key_weight, value_weight=value_weight, out_weight=out_weight, attention_gain=attention_gain, expert_gain=expert_gain, router_weight=router_weight, prior_weight=prior_weight, constant_weight=constant_weight, constant_vector=constant_vector, gate_weight=gate_weight, up_weight=up_weight, down_weight=down_weight)


epsilon = 1e-06
masked_score = -1e+30
precise = lax.Precision.HIGHEST

@jax.custom_vjp
def low(v):
    return lax.optimization_barrier(v.astype(jnp.bfloat16)).astype(jnp.float32)

@jax.custom_vjp
def low_back(v):
    return v

def low_keep(v):
    return (low(v), None)

def low_pass(kept, grad):
    return (grad,)

def back_keep(v):
    return (v, None)

def back_low(kept, grad):
    return (low(grad),)
low.defvjp(low_keep, low_pass)
low_back.defvjp(back_keep, back_low)

def matmul(left, right):
    return jnp.dot(left, right, precision=precise)

def segment_of(token_ids):
    return jnp.where(token_ids < TRUNK, 0, 1 + (token_ids - TRUNK) // SEG).astype(jnp.int32)

def one_hot_segments(token_ids):
    return (segment_of(token_ids)[:, None] == jnp.arange(13, dtype=jnp.int32)[None, :]).astype(jnp.float32)

def lineage_of(parent_row):
    segment_total = parent_row.shape[0] + 1
    indices = jnp.arange(segment_total, dtype=jnp.int32)
    parent_all = jnp.concatenate([jnp.zeros((1,), jnp.int32), parent_row.astype(jnp.int32)])
    parent_step = ((parent_all[:, None] == indices[None, :]) & (indices[:, None] > 0)).astype(jnp.float32)
    identity = jnp.eye(segment_total, dtype=jnp.float32)
    lineage = identity
    for repeat in range(segment_total - 1):
        lineage = jnp.minimum(1.0, identity + matmul(parent_step, lineage))
    return lineage

def shift_table(lineage):
    counter = jnp.arange(13, dtype=jnp.int32)
    lengths = jnp.where(counter == 0, TRUNK, SEG).astype(jnp.float32)
    starts = jnp.where(counter == 0, 0, TRUNK + (counter - 1) * SEG).astype(jnp.float32)
    proper = lineage - jnp.eye(13, dtype=jnp.float32)
    return matmul(proper, lengths) - starts

def positions(token_ids, shifts):
    return matmul(one_hot_segments(token_ids), shifts) + token_ids.astype(jnp.float32)

def visible(query_ids, key_ids, lineage):
    reachable = matmul(matmul(one_hot_segments(query_ids), lineage), one_hot_segments(key_ids).T)
    return (reachable > 0.5) & (key_ids[None, :] <= query_ids[:, None])

def rotate(values, places, direction):
    half_size = values.shape[-1] // 2
    frequency = 10000.0 ** (-(jnp.arange(half_size, dtype=jnp.float32) * 2.0 / values.shape[-1]))
    angles = places[:, None] * frequency[None, :]
    cosine = jnp.cos(angles)[:, None, :]
    sine_part = direction * jnp.sin(angles)[:, None, :]
    first_half = values[..., :half_size]
    second = values[..., half_size:]
    return jnp.concatenate([first_half * cosine - second * sine_part, second * cosine + first_half * sine_part], -1)

def slot_tables(route_block, owners, capacity):
    row_count = route_block.shape[0]
    expert_ids = jnp.arange(NFFN, dtype=jnp.int32)
    matches = (route_block[:, :, None] == expert_ids[None, None, :]).astype(jnp.int32)
    per_row = lax.optimization_barrier(jnp.sum(matches, 1))
    before = jnp.cumsum(per_row, 0) - per_row
    ranking = lax.optimization_barrier(jnp.sum(matches * before[:, None, :], -1))
    per_owner = NFFN // owners
    target = jnp.minimum(route_block, NFFN - 1)
    spare_slot = NFFN * capacity
    flat_slots = target % per_owner * (owners * capacity) + target // per_owner * capacity + ranking
    flat_slots = jnp.where(route_block < NFFN, flat_slots, spare_slot).astype(jnp.int32)
    pair_ids = jnp.arange(2 * row_count, dtype=jnp.int32)
    slot_pairs = jnp.full((spare_slot,), 2 * row_count, jnp.int32).at[flat_slots.reshape(-1)].set(pair_ids, mode='drop')
    return (flat_slots, slot_pairs)

def tree_forward(params, inputs, prior_rows, route_rows, parent_row):
    query_weight, key_weight, value_weight, out_weight, attention_gain, expert_gain, router_weight, prior_weight, constant_weight, constant_vector, gate_weight, up_weight, down_weight = params
    length, model_width = inputs.shape
    head_count = model_width // HEAD_DIM
    lineage = lineage_of(parent_row)
    shifts = shift_table(lineage)
    token_ids = jnp.arange(length, dtype=jnp.int32)
    places = positions(token_ids, shifts)
    normed = low(inputs * lax.rsqrt(lax.optimization_barrier(jnp.mean(inputs * inputs, -1, keepdims=True)) + epsilon) * attention_gain)
    query_pre = low_back(matmul(normed, query_weight)).reshape(length, head_count, HEAD_DIM)
    key_pre = low_back(matmul(normed, key_weight)).reshape(length, head_count, HEAD_DIM)
    queries = low(rotate(query_pre, places, 1.0))
    keys = low(rotate(key_pre, places, 1.0))
    values = low(low_back(matmul(normed, value_weight))).reshape(length, head_count, HEAD_DIM)
    block_rows = 4 * SEG if 4 * SEG >= 512 else length

    def attend(item):
        query_block, query_ids = item
        allowed = visible(query_ids, token_ids, lineage)
        scores = low_back(jnp.einsum('qhd,khd->hqk', query_block, keys, precision=precise) * HEAD_DIM ** (-0.5))
        scores = jnp.where(allowed[None], scores, masked_score)
        peak = lax.optimization_barrier(jnp.max(scores, -1, keepdims=True))
        weights = jnp.where(allowed[None], jnp.exp(scores - peak), 0.0)
        weights = low(weights / lax.optimization_barrier(jnp.sum(weights, -1, keepdims=True)))
        return jnp.einsum('hqk,khd->qhd', weights, values, precision=precise)
    attended = lax.map(jax.checkpoint(attend), (queries.reshape(length // block_rows, block_rows, head_count, HEAD_DIM), token_ids.reshape(length // block_rows, block_rows)))
    attended = attended.reshape(length, model_width)
    resid = inputs + low_back(matmul(low(low_back(attended)), out_weight))
    hidden_in = resid * lax.rsqrt(lax.optimization_barrier(jnp.mean(resid * resid, -1, keepdims=True)) + epsilon) * expert_gain
    hidden_b = low(hidden_in)
    logits = matmul(hidden_b, router_weight) + matmul(prior_rows, prior_weight)
    picked = (route_rows[:, :, None] == jnp.arange(NFFN + 4, dtype=jnp.int32)[None, None, :]).astype(jnp.float32)
    chosen = jnp.einsum('lce,le->lc', picked, logits, precision=precise)
    gate_probs = jax.nn.softmax(chosen, -1)
    mixing = jax.nn.softmax(matmul(hidden_b, constant_weight).reshape(length, 2, 2), -1)
    constants = mixing[:, :, 0:1] * hidden_in[:, None, :] + mixing[:, :, 1:2] * constant_vector[None]
    owners = length // TOK_DEV
    local_experts = NFFN // owners
    route_blocks = route_rows.reshape(owners, TOK_DEV, 2)
    flat_slots, slot_pairs = jax.vmap(lambda block_routes: slot_tables(block_routes, owners, CAP))(route_blocks)
    padded = jnp.concatenate([hidden_b.reshape(owners, TOK_DEV, model_width), jnp.zeros((owners, 1, model_width), jnp.float32)], 1)
    outgoing = low_back(jax.vmap(lambda source, pairs: source[pairs // 2])(padded, slot_pairs))
    expert_rows = outgoing.reshape(owners, local_experts, owners, CAP, model_width).transpose(2, 1, 0, 3, 4)
    expert_rows = expert_rows.reshape(NFFN, owners * CAP, model_width)
    gate_pre = low_back(jnp.einsum('erd,edf->erf', expert_rows, gate_weight, precision=precise))
    up_pre = low_back(jnp.einsum('erd,edf->erf', expert_rows, up_weight, precision=precise))
    hidden_mid = low(jax.nn.silu(gate_pre) * up_pre)
    expert_out = low(low_back(jnp.einsum('erf,efd->erd', hidden_mid, down_weight, precision=precise)))
    returned = expert_out.reshape(owners, local_experts, owners, CAP, model_width).transpose(2, 1, 0, 3, 4)
    returned = returned.reshape(owners, NFFN * CAP, model_width)
    returned = jnp.concatenate([returned, jnp.zeros((owners, 1, model_width), jnp.float32)], 1)
    routed = jax.vmap(lambda source, slots: source[slots])(returned, flat_slots).reshape(length, 2, model_width)
    branches = routed + picked[:, :, NFFN + 1, None] * hidden_in[:, None, :] + picked[:, :, NFFN + 2, None] * constants[:, None, 0, :] + picked[:, :, NFFN + 3, None] * constants[:, None, 1, :]
    return resid + lax.optimization_barrier(jnp.sum(gate_probs[:, :, None] * branches, 1))

def reference(tokens, prior_logits, routes, parents, cotangent, query_weight, key_weight, value_weight, out_weight, attention_gain, expert_gain, router_weight, prior_weight, constant_weight, constant_vector, gate_weight, up_weight, down_weight):
    params = tuple((item.astype(jnp.float32) for item in (query_weight, key_weight, value_weight, out_weight, attention_gain, expert_gain, router_weight, prior_weight, constant_weight, constant_vector, gate_weight, up_weight, down_weight)))

    def forward(weights, inputs, prior):

        def one_tree(carry, item):
            tree_inputs, tree_prior, tree_routes, tree_parents = item
            return (carry, jax.checkpoint(tree_forward)(weights, tree_inputs, tree_prior, tree_routes, tree_parents))
        unused, outputs = lax.scan(one_tree, jnp.zeros((), jnp.float32), (inputs, prior, routes, parents))
        return outputs
    outputs, pull = jax.vjp(forward, params, tokens.astype(jnp.float32), prior_logits.astype(jnp.float32))
    grads, tokens_grad, prior_grad = pull(cotangent.astype(jnp.float32))
    return (outputs.astype(jnp.bfloat16), tokens_grad, prior_grad, grads[0], grads[1], grads[2], grads[3], grads[4], grads[5], grads[6], grads[7], grads[8], grads[9], grads[10], grads[11], grads[12])
```

```python
import jax
import jax.numpy as jnp
from jax import lax
from jax.experimental import pallas as pl
from jax.experimental.pallas import tpu as pltpu
from jax.sharding import Mesh
from jax.sharding import PartitionSpec as P

NFFN = 8
NEXP = 12
SEG = 128
HEAD_DIM = 64
TRUNK = 1024
TILE = 2 * SEG
LOG2E = 1.4426950408889634
masked_score = -1e30
MIB = 2**20
epsilon = 1e-06
precise = lax.Precision.HIGHEST


def dot_nt(left, right):
    return lax.dot_general(left, right, (((1,), (1,)), ((), ())), preferred_element_type=jnp.float32)


def dot_nn(left, right):
    return jnp.dot(left, right, preferred_element_type=jnp.float32)


def tile_parts(tile, start):
    trunk_tiles = TRUNK // TILE
    if tile is not None and tile < trunk_tiles:
        return [(k * TILE, False, k == tile) for k in range(tile + 1)]
    parts = [(k * TILE, False, False) for k in range(trunk_tiles)]
    branch_tiles = 2
    if tile is None:
        parts += [(TRUNK + k * TILE, True, False) for k in range(branch_tiles)]
    else:
        parts += [(TRUNK + k * TILE, True, False) for k in range(tile - trunk_tiles)]
    parts += [(start, True, True)]
    return parts


def causal_bias():
    key_ids = lax.broadcasted_iota(jnp.int32, (TILE, TILE), 0)
    query_ids = lax.broadcasted_iota(jnp.int32, (TILE, TILE), 1)
    return jnp.where(key_ids <= query_ids, 0.0, masked_score).astype(jnp.float32)


def part_scores(scores, part, columns, bias_ref, triangle):
    first, by_lineage, causal = part
    if by_lineage:
        segment = 1 + (first - TRUNK) // SEG
        rows = [bias_ref[pl.ds(segment + i, 1), columns] for i in range(TILE // SEG)]
        scores = jnp.concatenate(
            [scores[i * SEG : (i + 1) * SEG] + rows[i] for i in range(TILE // SEG)], 0
        )
    if causal:
        scores = scores + triangle[...]
    return scores


def for_tiles(length, body):
    trunk_tiles = TRUNK // TILE
    for tile in range(trunk_tiles + 2):
        body(tile, tile * TILE)
    first_leaf = trunk_tiles + 2

    @pl.loop(first_leaf, length // TILE)
    def _(tile):
        body(None, pl.multiple_of(tile * TILE, TILE))


def attend_kernel(bias_ref, qkv_ref, out_ref, lse_ref, q_ref, k_ref, v_ref, o_ref, s_ref, triangle):
    sources, _, rows = qkv_ref.shape
    length = sources * rows
    factor = HEAD_DIM ** (-0.5) * LOG2E
    triangle[...] = causal_bias()
    extra = lax.broadcasted_iota(jnp.int32, (16, length), 0)
    v_ref[HEAD_DIM:, :] = jnp.where(extra == 0, 1.0, 0.0).astype(jnp.bfloat16)
    for z in range(sources):
        span = pl.ds(z * rows, rows)
        q_ref[:, span] = qkv_ref[z, :HEAD_DIM]
        k_ref[span, :] = qkv_ref[z, HEAD_DIM : 2 * HEAD_DIM].astype(jnp.float32).T.astype(jnp.bfloat16)
        v_ref[:HEAD_DIM, span] = qkv_ref[z, 2 * HEAD_DIM :]

    def body(tile, start):
        columns = pl.ds(start, TILE)
        parts = tile_parts(tile, start)
        query = q_ref[:, columns]
        peak = None
        for i, part in enumerate(parts):
            scores = dot_nn(k_ref[pl.ds(part[0], TILE), :], query)
            scores = part_scores(scores, part, columns, bias_ref, triangle)
            s_ref[i * TILE : (i + 1) * TILE, :] = scores
            top = jnp.max(scores, 0, keepdims=True)
            peak = top if peak is None else jnp.maximum(peak, top)
        shift = peak * factor
        total = None
        for i, part in enumerate(parts):
            weights = jnp.exp2(s_ref[i * TILE : (i + 1) * TILE, :] * factor - shift)
            term = dot_nn(v_ref[:, pl.ds(part[0], TILE)], weights.astype(jnp.bfloat16))
            total = term if total is None else total + term
        norm = total[HEAD_DIM : HEAD_DIM + 1]
        o_ref[:, columns] = (total[:HEAD_DIM] / norm).astype(jnp.bfloat16)
        lse_ref[:, columns] = shift + jnp.log2(norm)

    for_tiles(length, body)
    for z in range(sources):
        out_ref[z] = o_ref[:, pl.ds(z * rows, rows)]


def attend(bias, qkv):
    sources, _, rows = qkv.shape
    length = sources * rows
    part_total = TRUNK // TILE + 3
    return pl.pallas_call(
        attend_kernel,
        out_shape=(
            jax.ShapeDtypeStruct((sources, HEAD_DIM, rows), jnp.bfloat16),
            jax.ShapeDtypeStruct((1, length), jnp.float32),
        ),
        scratch_shapes=[
            pltpu.VMEM((HEAD_DIM, length), jnp.bfloat16),
            pltpu.VMEM((length, HEAD_DIM), jnp.bfloat16),
            pltpu.VMEM((HEAD_DIM + 16, length), jnp.bfloat16),
            pltpu.VMEM((HEAD_DIM, length), jnp.bfloat16),
            pltpu.VMEM((part_total * TILE, TILE), jnp.float32),
            pltpu.VMEM((TILE, TILE), jnp.float32),
        ],
        compiler_params=pltpu.CompilerParams(vmem_limit_bytes=48 * MIB),
        cost_estimate=pl.CostEstimate(flops=2 * 10**9, bytes_accessed=4 * 10**6, transcendentals=3 * 10**6),
    )(bias, qkv)


def attend_back_kernel(
    bias_ref, cos_ref, sin_ref, qkv_ref, out_ref, lse_ref, grad_ref, back_ref,
    qt_ref, kt_ref, dt_ref, q_ref, k_ref, v_ref, d_ref, delta_ref, dq_ref, dk_ref, dv_ref, triangle,
):
    sources, _, rows = qkv_ref.shape
    length = sources * rows
    scaling = HEAD_DIM ** (-0.5)
    factor = scaling * LOG2E
    triangle[...] = causal_bias()

    def turned(values):
        return values.astype(jnp.float32).T.astype(jnp.bfloat16)

    for z in range(sources):
        span = pl.ds(z * rows, rows)
        query, key, value = (qkv_ref[z, i * HEAD_DIM : (i + 1) * HEAD_DIM] for i in range(3))
        grad = grad_ref[z]
        qt_ref[:, span] = query
        kt_ref[:, span] = key
        dt_ref[:, span] = grad
        q_ref[span, :] = turned(query)
        k_ref[span, :] = turned(key)
        v_ref[span, :] = turned(value)
        d_ref[span, :] = turned(grad)
        delta_ref[:, span] = jnp.sum(
            grad.astype(jnp.float32) * out_ref[z].astype(jnp.float32), 0, keepdims=True
        )
    dk_ref[...] = jnp.zeros_like(dk_ref)
    dv_ref[...] = jnp.zeros_like(dv_ref)

    def body(tile, start):
        columns = pl.ds(start, TILE)
        query_t, grad_t = qt_ref[:, columns], dt_ref[:, columns]
        query, grad = q_ref[columns, :], d_ref[columns, :]
        lse, delta = lse_ref[:, columns], delta_ref[:, columns]
        total = None
        for part in tile_parts(tile, start):
            span = pl.ds(part[0], TILE)
            scores = dot_nn(k_ref[span, :], query_t) * factor - lse
            scores = part_scores(scores, part, columns, bias_ref, triangle)
            weights = jnp.exp2(scores)
            weight_grads = dot_nn(v_ref[span, :], grad_t)
            score_grads = (weights * (weight_grads - delta)).astype(jnp.bfloat16)
            dv_ref[span, :] += dot_nn(weights.astype(jnp.bfloat16), grad)
            dk_ref[span, :] += dot_nn(score_grads, query)
            term = dot_nn(kt_ref[:, span], score_grads)
            total = term if total is None else total + term
        dq_ref[:, columns] = total

    for_tiles(length, body)
    half = HEAD_DIM // 2
    for z in range(sources):
        span = pl.ds(z * rows, rows)
        cosine, sine = cos_ref[:, span], sin_ref[:, span]
        for i, values in enumerate((dq_ref[:, span], dk_ref[span, :].T)):
            values = values * scaling
            first, second = values[:half], values[half:]
            back_ref[z, i * HEAD_DIM : (i + 1) * HEAD_DIM] = jnp.concatenate(
                [first * cosine + second * sine, second * cosine - first * sine], 0
            ).astype(jnp.bfloat16)
        back_ref[z, 2 * HEAD_DIM :] = dv_ref[span, :].T.astype(jnp.bfloat16)


def attend_back(bias, cosine, sine, qkv, out, lse, grad):
    sources, _, rows = qkv.shape
    length = sources * rows
    turned = pltpu.VMEM((HEAD_DIM, length), jnp.bfloat16)
    plain = pltpu.VMEM((length, HEAD_DIM), jnp.bfloat16)
    wide = pltpu.VMEM((length, HEAD_DIM), jnp.float32)
    return pl.pallas_call(
        attend_back_kernel,
        out_shape=jax.ShapeDtypeStruct((sources, 3 * HEAD_DIM, rows), jnp.bfloat16),
        scratch_shapes=[
            turned, turned, turned, plain, plain, plain, plain,
            pltpu.VMEM((1, length), jnp.float32),
            pltpu.VMEM((HEAD_DIM, length), jnp.float32),
            wide, wide,
            pltpu.VMEM((TILE, TILE), jnp.float32),
        ],
        compiler_params=pltpu.CompilerParams(vmem_limit_bytes=48 * MIB),
        cost_estimate=pl.CostEstimate(flops=5 * 10**9, bytes_accessed=6 * 10**6, transcendentals=3 * 10**6),
    )(bias, cosine, sine, qkv, out, lse, grad)


def params(limit):
    return pltpu.CompilerParams(vmem_limit_bytes=limit * MIB)


def cost(flops, moved):
    return pl.CostEstimate(flops=int(flops), bytes_accessed=int(moved), transcendentals=0)


def project_kernel(tokens_ref, gain_ref, query_ref, key_ref, value_ref, cos_ref, sin_ref, out_ref):
    inputs = tokens_ref[...].astype(jnp.float32)
    inverse = lax.rsqrt(jnp.mean(inputs * inputs, -1, keepdims=True) + epsilon)
    normed = (inputs * inverse * gain_ref[...]).astype(jnp.bfloat16)
    half = HEAD_DIM // 2
    cosine, sine = cos_ref[...], sin_ref[...]
    for i, weight in enumerate((query_ref, key_ref, value_ref)):
        turned = dot_nn(normed, weight[...]).T
        for z in range(out_ref.shape[0]):
            first = turned[z * HEAD_DIM : z * HEAD_DIM + half]
            second = turned[z * HEAD_DIM + half : (z + 1) * HEAD_DIM]
            if i < 2:
                first, second = first * cosine - second * sine, second * cosine + first * sine
            base = i * HEAD_DIM
            out_ref[z, base : base + half] = first.astype(jnp.bfloat16)
            out_ref[z, base + half : base + HEAD_DIM] = second.astype(jnp.bfloat16)


def project(chunk, owners, tokens, gain, weights, cosine, sine):
    rows, width = tokens.shape
    columns = owners * HEAD_DIM
    whole = lambda shape: pl.BlockSpec(shape, lambda i: (0,) * len(shape))
    part = pl.BlockSpec((width, columns), lambda i: (0, chunk))
    return pl.pallas_call(
        project_kernel,
        grid=(1,),
        in_specs=[whole((rows, width)), whole((1, width)), part, part, part]
        + [whole((HEAD_DIM // 2, rows))] * 2,
        out_specs=whole((owners, 3 * HEAD_DIM, rows)),
        out_shape=jax.ShapeDtypeStruct((owners, 3 * HEAD_DIM, rows), jnp.bfloat16),
        compiler_params=params(48),
        cost_estimate=cost(6 * rows * width * columns, 4e6),
    )(tokens, gain, *weights, cosine, sine)


def lane_pick(values, lanes, index):
    return jnp.sum(jnp.where(lanes == index, values, 0.0), -1, keepdims=True)


def middle_kernel(
    tokens_ref, a0_ref, a1_ref, a2_ref, out_weight_ref, gain_ref, mixer_ref, prior_ref, prior_weight_ref,
    routes_ref, codes_ref, resid_ref, small_ref, first_ref, second_ref, hidden_ref,
):
    rows, width = tokens_ref.shape

    @pl.loop(0, rows // SEG)
    def _(step):
        span = pl.ds(pl.multiple_of(step * SEG, SEG), SEG)
        attended = jnp.concatenate([ref[:, span] for ref in (a0_ref, a1_ref, a2_ref)], 0)
        attended = attended.astype(jnp.float32).T.astype(jnp.bfloat16)
        resid = tokens_ref[span, :].astype(jnp.float32) + dot_nn(attended, out_weight_ref[...])
        inverse = lax.rsqrt(jnp.mean(resid * resid, -1, keepdims=True) + epsilon)
        hidden = (resid * inverse * gain_ref[...]).astype(jnp.bfloat16)
        resid_ref[span, :] = resid
        hidden_ref[span, :] = hidden
        logits = dot_nn(hidden, mixer_ref[...])
        logits = logits + jnp.dot(
            prior_ref[span, :], prior_weight_ref[...], precision=precise, preferred_element_type=jnp.float32
        )
        lanes = lax.broadcasted_iota(jnp.int32, logits.shape, 1)
        routes = routes_ref[span, :]
        columns = []
        pairs = [[lane_pick(logits, lanes, routes[:, c : c + 1]) for c in range(2)]]
        pairs += [[logits[:, NEXP + 2 * m + c : NEXP + 2 * m + c + 1] for c in range(2)] for m in range(2)]
        for one, two in pairs:
            peak = jnp.maximum(one, two)
            one, two = jnp.exp(one - peak), jnp.exp(two - peak)
            columns += [one / (one + two), two / (one + two)]
        columns.append(inverse)
        small = jnp.zeros_like(logits)
        for i, column in enumerate(columns):
            small = jnp.where(lanes == i, column, small)
        small_ref[span, :] = small

    slots = first_ref.shape[0]
    for half, ref in enumerate((first_ref, second_ref)):
        index = lax.broadcasted_iota(jnp.int32, (slots, rows), 0) + half * slots
        chosen = (codes_ref[0:1, :] == index) | (codes_ref[1:2, :] == index)
        ref[...] = dot_nn(chosen.astype(jnp.bfloat16), hidden_ref[...]).astype(jnp.bfloat16)


def middle(tokens, attended, out_weight, gain, mixer, prior, prior_weight, routes, codes_row):
    rows, width = tokens.shape
    slots = rows
    return pl.pallas_call(
        middle_kernel,
        out_shape=(
            jax.ShapeDtypeStruct((rows, width), jnp.float32),
            jax.ShapeDtypeStruct((rows, 128), jnp.float32),
            jax.ShapeDtypeStruct((slots, width), jnp.bfloat16),
            jax.ShapeDtypeStruct((slots, width), jnp.bfloat16),
        ),
        scratch_shapes=[pltpu.VMEM((rows, width), jnp.bfloat16)],
        compiler_params=params(48),
        cost_estimate=cost(4 * rows * width * width + 4 * rows * rows * width, 1e7),
    )(tokens, *attended, out_weight, gain, mixer, prior, prior_weight, routes, codes_row)


def scatter_kernel(small_ref, grad_ref, codes_ref, first_ref, second_ref, scaled_ref):
    rows, width = grad_ref.shape
    small = small_ref[...]
    grad = grad_ref[...].astype(jnp.float32)
    for c in range(2):
        scaled_ref[c * rows : (c + 1) * rows, :] = (small[:, c : c + 1] * grad).astype(jnp.bfloat16)
    slots = first_ref.shape[0]
    for half, ref in enumerate((first_ref, second_ref)):
        index = lax.broadcasted_iota(jnp.int32, (slots, rows), 0) + half * slots
        chosen = jnp.concatenate([(codes_ref[c : c + 1, :] == index).astype(jnp.bfloat16) for c in range(2)], 1)
        ref[...] = dot_nn(chosen, scaled_ref[...]).astype(jnp.bfloat16)


def scatter(small, grad, codes_row):
    rows, width = grad.shape
    return pl.pallas_call(
        scatter_kernel,
        out_shape=(jax.ShapeDtypeStruct((rows, width), jnp.bfloat16),) * 2,
        scratch_shapes=[pltpu.VMEM((2 * rows, width), jnp.bfloat16)],
        compiler_params=params(48),
        cost_estimate=cost(8 * rows * rows * width, 4e6),
    )(small, grad, codes_row)


def expert_kernel(
    x_ref, d_ref, gate_ref, up_ref, down_ref, f_ref, back_ref, dots_ref, hid_ref, dg_ref, du_ref, f_sum, back_sum
):
    step = pl.program_id(0)
    rows = x_ref.shape[0]
    part = rows // 2
    for r in range(2):
        span = pl.ds(r * part, part)
        x, d = x_ref[span, :], d_ref[span, :]
        gate_pre = dot_nn(x, gate_ref[...])
        up_pre = dot_nn(x, up_ref[...])
        mid = dot_nt(d, down_ref[...])
        sigmoid = 1.0 / (1.0 + jnp.exp(-gate_pre))
        active = gate_pre * sigmoid
        hid = (active * up_pre).astype(jnp.bfloat16)
        du = (mid * active).astype(jnp.bfloat16)
        dg = (mid * up_pre * (sigmoid + active * (1.0 - sigmoid))).astype(jnp.bfloat16)
        hid_ref[span, :] = hid
        du_ref[span, :] = du
        dg_ref[span, :] = dg
        f_term = dot_nn(hid, down_ref[...])
        back_term = dot_nt(dg, gate_ref[...]) + dot_nt(du, up_ref[...])

        @pl.when(step == 0)
        def _():
            f_sum[span, :] = f_term
            back_sum[span, :] = back_term

        @pl.when(step > 0)
        def _():
            f_sum[span, :] += f_term
            back_sum[span, :] += back_term

    @pl.when(step == pl.num_programs(0) - 1)
    def _():
        back_ref[...] = back_sum[...].astype(jnp.bfloat16)
        f = f_sum[...].astype(jnp.bfloat16)
        f_ref[...] = f
        dots = jnp.sum(f.astype(jnp.float32) * d_ref[...].astype(jnp.float32), -1, keepdims=True)
        dots_ref[...] = jnp.broadcast_to(dots, (rows, 128)).T[:8]


def expert(x, d, gate, up, down):
    rows, width = x.shape
    units = gate.shape[1]
    part = 512
    whole = pl.BlockSpec((rows, width), lambda i: (0, 0))
    columns = pl.BlockSpec((width, part), lambda i: (0, i))
    mids = pl.BlockSpec((rows, part), lambda i: (0, i))
    return pl.pallas_call(
        expert_kernel,
        grid=(units // part,),
        in_specs=[whole, whole, columns, columns, pl.BlockSpec((part, width), lambda i: (i, 0))],
        out_specs=(whole, whole, pl.BlockSpec((8, rows), lambda i: (0, 0)), mids, mids, mids),
        out_shape=(
            jax.ShapeDtypeStruct((rows, width), jnp.bfloat16),
            jax.ShapeDtypeStruct((rows, width), jnp.bfloat16),
            jax.ShapeDtypeStruct((8, rows), jnp.float32),
        )
        + (jax.ShapeDtypeStruct((rows, units), jnp.bfloat16),) * 3,
        scratch_shapes=[pltpu.VMEM((rows, width), jnp.float32)] * 2,
        compiler_params=params(52),
        cost_estimate=cost(12 * rows * width * units, 3e7),
    )(x, d, gate, up, down)


def weights_kernel(
    xa_ref, xb_ref, da_ref, db_ref, ha_ref, hb_ref, ga_ref, gb_ref, ua_ref, ub_ref,
    gate_ref, up_ref, down_ref, x_turned, d_turned,
):
    rows = xa_ref.shape[0]

    @pl.when(pl.program_id(0) == 0)
    def _():
        for i, (x, d) in enumerate(((xa_ref, da_ref), (xb_ref, db_ref))):
            span = pl.ds(i * rows, rows)
            x_turned[:, span] = x[...].astype(jnp.float32).T.astype(jnp.bfloat16)
            d_turned[:, span] = d[...].astype(jnp.float32).T.astype(jnp.bfloat16)

    both = lambda one, two: jnp.concatenate([one[...], two[...]], 0)
    gate_ref[...] = dot_nn(x_turned[...], both(ga_ref, gb_ref)).astype(jnp.bfloat16)
    up_ref[...] = dot_nn(x_turned[...], both(ua_ref, ub_ref)).astype(jnp.bfloat16)
    down_ref[...] = dot_nn(d_turned[...], both(ha_ref, hb_ref)).T.astype(jnp.bfloat16)


def weight_grads(xs, ds, hids, gates, ups):
    rows, width = xs[0].shape
    units = hids[0].shape[1]
    part = 256
    whole = pl.BlockSpec((rows, width), lambda i: (0, 0))
    mids = pl.BlockSpec((rows, part), lambda i: (0, i))
    columns = pl.BlockSpec((width, part), lambda i: (0, i))
    return pl.pallas_call(
        weights_kernel,
        grid=(units // part,),
        in_specs=[whole] * 4 + [mids] * 6,
        out_specs=(columns, columns, pl.BlockSpec((part, width), lambda i: (i, 0))),
        out_shape=(
            jax.ShapeDtypeStruct((width, units), jnp.bfloat16),
            jax.ShapeDtypeStruct((width, units), jnp.bfloat16),
            jax.ShapeDtypeStruct((units, width), jnp.bfloat16),
        ),
        scratch_shapes=[pltpu.VMEM((width, 2 * rows), jnp.bfloat16)] * 2,
        compiler_params=params(52),
        cost_estimate=cost(12 * rows * width * units, 3e7),
    )(*xs, *ds, *hids, *gates, *ups)


def split_dot(dot, left, right):
    high = left.astype(jnp.bfloat16)
    low = (left - high.astype(jnp.float32)).astype(jnp.bfloat16)
    return dot(high, right) + dot(low, right)


def turn_kernel(
    resid_ref, small_ref, grad_ref, prior_ref, routes_ref, codes_ref, ra_ref, rb_ref, dots_ref, vector_ref,
    gain_ref, mixer_ref, prior_turned_ref, out_weight_ref, a0_ref, a1_ref, a2_ref,
    resid_grad_ref, g0_ref, g1_ref, g2_ref, out_grad_ref, sums_ref, prior_sums_ref, prior_grad_ref, back_ref,
):
    rows, width = resid_ref.shape
    slots = 2 * ra_ref.shape[0]
    sums_ref[...] = jnp.zeros_like(sums_ref)
    prior_sums_ref[...] = jnp.zeros_like(prior_sums_ref)

    @pl.loop(0, rows // SEG)
    def _(step):
        span = pl.ds(pl.multiple_of(step * SEG, SEG), SEG)
        small = small_ref[span, :]
        routes, codes = routes_ref[span, :], codes_ref[span, :]
        gates = [small[:, c : c + 1] for c in range(2)]
        mixing = [[small[:, 2 + 2 * m + c : 3 + 2 * m + c] for c in range(2)] for m in range(2)]
        inverse = small[:, 6:7]
        normed = resid_ref[span, :] * inverse
        hidden = normed * gain_ref[...]
        hidden_b = hidden.astype(jnp.bfloat16)
        grad_b = grad_ref[span, :]
        grad = grad_b.astype(jnp.float32)
        index = lax.broadcasted_iota(jnp.int32, (SEG, slots), 1)
        hits = [codes[:, c : c + 1] == index for c in range(2)]
        dots = dots_ref[...]
        terms = [jnp.sum(jnp.where(hit, dots, 0.0), -1, keepdims=True) for hit in hits]
        chosen = (hits[0] | hits[1]).astype(jnp.bfloat16)
        half = slots // 2
        routed = dot_nn(chosen[:, :half], ra_ref[...]) + dot_nn(chosen[:, half:], rb_ref[...])
        along = jnp.sum(grad * hidden, -1, keepdims=True)
        across = [jnp.sum(grad * vector_ref[m : m + 1, :], -1, keepdims=True) for m in range(2)]
        to_copy = 0.0
        to_mix = [0.0, 0.0]
        for c in range(2):
            route = routes[:, c : c + 1]
            copied = jnp.where(route == NFFN + 1, gates[c], 0.0)
            to_copy = to_copy + copied
            terms[c] = terms[c] + copied * along
            for m in range(2):
                mixed = jnp.where(route == NFFN + 2 + m, gates[c], 0.0)
                to_mix[m] = to_mix[m] + mixed
                terms[c] = terms[c] + mixed * (mixing[m][0] * along + mixing[m][1] * across[m])
        both = terms[0] + terms[1]
        lanes = lax.broadcasted_iota(jnp.int32, (SEG, 128), 1)
        logit_grads = jnp.zeros((SEG, 128), jnp.float32)
        for c in range(2):
            logit_grads = jnp.where(lanes == routes[:, c : c + 1], terms[c] - gates[c] * both, logit_grads)
        scores = logit_grads
        direct = to_copy
        for m in range(2):
            pair = (to_mix[m] * along, to_mix[m] * across[m])
            mean = mixing[m][0] * pair[0] + mixing[m][1] * pair[1]
            for c in range(2):
                scores = jnp.where(lanes == NEXP + 2 * m + c, mixing[m][c] * (pair[c] - mean), scores)
            direct = direct + mixing[m][0] * to_mix[m]
        prior_grad_ref[span, :] = jnp.dot(
            logit_grads, prior_turned_ref[...], precision=precise, preferred_element_type=jnp.float32
        )[:, : prior_grad_ref.shape[1]]
        hidden_grads = split_dot(dot_nn, scores, mixer_ref[...]) + direct * grad + routed
        scaled = hidden_grads * gain_ref[...]
        resid_grads = inverse * (scaled - normed * jnp.mean(scaled * normed, -1, keepdims=True)) + grad
        resid_grad_ref[span, :] = resid_grads
        back_ref[span, :] = resid_grads.astype(jnp.bfloat16)
        weights = jnp.zeros((SEG, 128), jnp.float32)
        for m in range(2):
            weights = jnp.where(lanes == m, mixing[m][1] * to_mix[m], weights)
        sums_ref[0:16, :] += split_dot(dot_nn, scores.T[0:16], hidden_b)
        sums_ref[16:24, :] += split_dot(dot_nn, weights.T[0:8], grad_b)
        sums_ref[24:32, :] += jnp.sum((hidden_grads * normed).reshape(SEG // 8, 8, width), 0)
        prior_sums_ref[...] += jnp.dot(
            prior_ref[span, :].T, logit_grads, precision=precise, preferred_element_type=jnp.float32
        )

    back = back_ref[...]
    part = a0_ref.shape[0]
    for j, (a_ref, g_ref) in enumerate(((a0_ref, g0_ref), (a1_ref, g1_ref), (a2_ref, g2_ref))):
        span = pl.ds(j * part, part)
        g_ref[...] = dot_nt(out_weight_ref[span, :], back).astype(jnp.bfloat16)
        out_grad_ref[span, :] = dot_nn(a_ref[...], back).astype(jnp.bfloat16)


def turn(resid, small, grad, prior, routes, codes, returned, dots, vector, gain, mixer_turned, prior_turned, out_weight, attended):
    rows, width = resid.shape
    part = attended[0].shape[0]
    return pl.pallas_call(
        turn_kernel,
        out_shape=(
            jax.ShapeDtypeStruct((rows, width), jnp.float32),
            *(jax.ShapeDtypeStruct((part, rows), jnp.bfloat16),) * 3,
            jax.ShapeDtypeStruct((width, width), jnp.bfloat16),
            jax.ShapeDtypeStruct((32, width), jnp.float32),
            jax.ShapeDtypeStruct((prior.shape[1], 128), jnp.float32),
            jax.ShapeDtypeStruct(prior.shape, jnp.float32),
        ),
        scratch_shapes=[pltpu.VMEM((rows, width), jnp.bfloat16)],
        compiler_params=params(56),
        cost_estimate=cost(4 * rows * width * width + 4 * rows * rows * width, 1.5e7),
    )(resid, small, grad, prior, routes, codes, *returned, dots, vector, gain, mixer_turned, prior_turned, out_weight, *attended)


def combine_kernel(resid_ref, small_ref, routes_ref, codes_ref, fa_ref, fb_ref, vector_ref, gain_ref, out_ref):
    rows, width = resid_ref.shape
    half = fa_ref.shape[0]

    @pl.loop(0, rows // SEG)
    def _(step):
        span = pl.ds(pl.multiple_of(step * SEG, SEG), SEG)
        small = small_ref[span, :]
        routes, codes = routes_ref[span, :], codes_ref[span, :]
        resid = resid_ref[span, :]
        hidden = resid * small[:, 6:7] * gain_ref[...]
        index = lax.broadcasted_iota(jnp.int32, (SEG, 2 * half), 1)
        total = resid
        direct = 0.0
        for c in range(2):
            gate, route = small[:, c : c + 1], routes[:, c : c + 1]
            chosen = (codes[:, c : c + 1] == index).astype(jnp.bfloat16)
            routed = dot_nn(chosen[:, :half], fa_ref[...]) + dot_nn(chosen[:, half:], fb_ref[...])
            total = total + gate * routed
            direct = direct + jnp.where(route == NFFN + 1, gate, 0.0)
            for m in range(2):
                mixed = jnp.where(route == NFFN + 2 + m, gate, 0.0)
                direct = direct + mixed * small[:, 2 + 2 * m : 3 + 2 * m]
                total = total + mixed * small[:, 3 + 2 * m : 4 + 2 * m] * vector_ref[m : m + 1, :]
        out_ref[span, :] = (total + direct * hidden).astype(jnp.bfloat16)


def combine(resid, small, routes, codes, outs, vector, gain):
    rows, width = resid.shape
    return pl.pallas_call(
        combine_kernel,
        out_shape=jax.ShapeDtypeStruct((rows, width), jnp.bfloat16),
        compiler_params=params(48),
        cost_estimate=cost(8 * rows * rows * width, 8e6),
    )(resid, small, routes, codes, *outs, vector, gain)


def last_kernel(
    tokens_ref, gain_ref, b0_ref, b1_ref, b2_ref, query_ref, key_ref, value_ref, resid_grad_ref,
    tokens_grad_ref, weight_grad_ref, normed_turned, back_turned,
):
    rows, width = tokens_ref.shape
    inputs = tokens_ref[...].astype(jnp.float32)
    inverse = lax.rsqrt(jnp.mean(inputs * inputs, -1, keepdims=True) + epsilon)
    normed = inputs * inverse
    normed_turned[...] = (normed * gain_ref[...]).T.astype(jnp.bfloat16)
    owners = b0_ref.shape[0]
    for i in range(3):
        for j, ref in enumerate((b0_ref, b1_ref, b2_ref)):
            for z in range(owners):
                head = j * owners + z
                back_turned[i, head * HEAD_DIM : (head + 1) * HEAD_DIM, :] = ref[z, i * HEAD_DIM : (i + 1) * HEAD_DIM]
    total = None
    for i, ref in enumerate((query_ref, key_ref, value_ref)):
        term = dot_nn(ref[...], back_turned[i])
        total = term if total is None else total + term
        weight_grad_ref[:, i * width : (i + 1) * width] = dot_nt(normed_turned[...], back_turned[i]).astype(jnp.bfloat16)
    first_grads = total.T
    summed = jnp.sum((first_grads * normed).reshape(rows // 8, 8, width), 0)
    column = jnp.sum(summed.T, -1, keepdims=True)
    weight_grad_ref[:, 3 * width :] = jnp.broadcast_to(column, (width, 128)).astype(jnp.bfloat16)
    scaled = first_grads * gain_ref[...]
    tokens_grad_ref[...] = (
        inverse * (scaled - normed * jnp.mean(scaled * normed, -1, keepdims=True)) + resid_grad_ref[...]
    )


def last(tokens, gain, backs, weights, resid_grads):
    rows, width = tokens.shape
    return pl.pallas_call(
        last_kernel,
        out_shape=(
            jax.ShapeDtypeStruct((rows, width), jnp.float32),
            jax.ShapeDtypeStruct((width, 3 * width + 128), jnp.bfloat16),
        ),
        scratch_shapes=[
            pltpu.VMEM((width, rows), jnp.bfloat16),
            pltpu.VMEM((3, width, rows), jnp.bfloat16),
        ],
        compiler_params=params(56),
        cost_estimate=cost(12 * rows * width * width, 2e7),
    )(tokens, gain, *backs, *weights, resid_grads)


def lineage_of(parent_row):
    segment_total = parent_row.shape[0] + 1
    indices = jnp.arange(segment_total, dtype=jnp.int32)
    parent_all = jnp.concatenate([jnp.full((1,), -1, jnp.int32), parent_row])
    reach = (parent_all[:, None] == indices[None, :]) | (indices[:, None] == indices[None, :])
    for repeat in range(3):
        reach = jnp.any(reach[:, :, None] & reach[None, :, :], 1)
    return reach


def slot_codes(routes, half_slots):
    rows = routes.shape[0]
    experts = jnp.arange(NFFN, dtype=jnp.int32)
    matches = routes[:, :, None] == experts
    per_row = jnp.sum(matches.astype(jnp.float32), 1)
    earlier = jnp.arange(rows)[:, None] > jnp.arange(rows)[None, :]
    before = jnp.dot(
        earlier.astype(jnp.bfloat16), per_row.astype(jnp.bfloat16), preferred_element_type=jnp.float32
    )
    rank = jnp.sum(jnp.where(matches, before[:, None, :], 0.0), -1).astype(jnp.int32)
    late = (rank >= half_slots).astype(jnp.int32)
    code = late * (NFFN * half_slots) + routes * half_slots + rank - late * half_slots
    return jnp.where(routes < NFFN, code, 4 * NFFN * half_slots)


def per_device(
    tokens, prior_logits, routes, parents, cotangent, query_weight, key_weight, value_weight, out_weight,
    attention_gain, expert_gain, router_weight, prior_weight, constant_weight, constant_vector,
    gate_weight, up_weight, down_weight,
):
    owners = lax.axis_size("expert")
    member = lax.axis_index("expert")
    core = lax.axis_index("core")
    tokens, prior, routes, grad = tokens[0], prior_logits[0], routes[0], cotangent[0]
    rows, width = tokens.shape
    length = rows * owners
    chunks = width // HEAD_DIM // owners
    half_slots = rows // 8
    planes, everyone = ("expert", "core"), ("expert", "xy", "core")

    def swap(values):
        return lax.ppermute(values, "core", [(0, 1), (1, 0)])

    def exchange(values, axes):
        return lax.all_to_all(values, axes, split_axis=0, concat_axis=0, tiled=True)

    def gather_weight(weight):
        mine = jnp.where(core == 0, weight[0], weight[1])
        other = swap(jnp.where(core == 0, weight[1], weight[0]))
        pair = jnp.concatenate([jnp.where(core == 0, mine, other), jnp.where(core == 0, other, mine)], 0)
        return lax.all_gather(pair, "xy", axis=0, tiled=True)

    def scatter_weight(grads):
        part = lax.psum_scatter(grads, "xy", scatter_dimension=0, tiled=True)
        part = part.reshape(2, part.shape[0] // 2, part.shape[1])
        mine = jnp.where(core == 0, part[0], part[1])
        other = swap(jnp.where(core == 0, part[1], part[0]))
        return jnp.stack(
            [jnp.where(core == 0, mine, other), jnp.where(core == 0, other, mine)], 0
        ).astype(jnp.float32)

    lineage = lineage_of(parents[0])
    segments = lineage.shape[0]
    lengths = jnp.where(jnp.arange(segments) == 0, TRUNK, SEG)
    begins = jnp.where(jnp.arange(segments) == 0, 0, TRUNK + (jnp.arange(segments) - 1) * SEG)
    shifts = jnp.sum(jnp.where(lineage, lengths[None, :], 0), 1) - lengths - begins
    ids = jnp.arange(length, dtype=jnp.int32)
    segment = jnp.where(ids < TRUNK, 0, 1 + (ids - TRUNK) // SEG)
    own = segment[None, :] == jnp.arange(segments)[:, None]
    places = (jnp.sum(jnp.where(own, shifts[:, None], 0), 0) + ids).astype(jnp.float32)
    reach = jnp.any(own[:, None, :] & lineage[:, :, None], 0)
    bias = jnp.where(reach, 0.0, masked_score).astype(jnp.float32)
    bias = jnp.concatenate([bias, jnp.zeros((16 - segments, length), jnp.float32)], 0)
    frequency = 10000.0 ** (-(jnp.arange(HEAD_DIM // 2, dtype=jnp.float32) * 2.0 / HEAD_DIM))
    angles = frequency[:, None] * places[None, :]
    cosine, sine = jnp.cos(angles), jnp.sin(angles)
    own_cosine, own_sine = (lax.dynamic_slice_in_dim(table, member * rows, rows, 1) for table in (cosine, sine))

    attention_row, expert_row = attention_gain[None], expert_gain[None]
    qkv_weights = (query_weight, key_weight, value_weight)
    sent = [project(j, owners, tokens, attention_row, qkv_weights, own_cosine, own_sine) for j in range(chunks)]
    heads = [exchange(chunk, "expert") for chunk in sent]
    gate, up, down = (gather_weight(weight) for weight in (gate_weight, up_weight, down_weight))
    codes = slot_codes(routes, half_slots)
    codes_row = codes.T

    attended, logs, outs = [], [], []
    for chunk in heads:
        out, log = attend(bias, chunk)
        outs.append(out)
        logs.append(log)
        attended.append(exchange(out, "expert").reshape(owners * HEAD_DIM, rows))

    mixer = jnp.concatenate(
        [router_weight, constant_weight, jnp.zeros((width, 128 - NEXP - 4), jnp.bfloat16)], 1
    )
    prior_wide = jnp.pad(prior_weight, ((0, 0), (0, 128 - NEXP)))
    prior_turned = jnp.pad(prior_weight.T, ((0, 128 - NEXP), (0, 128 - NEXP)))
    resid, small, *x_out = middle(
        tokens, attended, out_weight, expert_row, mixer, prior, prior_wide, routes, codes_row
    )
    d_out = scatter(small, grad, codes_row)

    def to_experts(values):
        return exchange(values.reshape(NFFN, half_slots, -1), planes).reshape(values.shape)

    xs, ds, fs, backs, dots, hids, gates, ups = ([] for _ in range(8))
    for x_part, d_part in zip(x_out, d_out):
        x, d = to_experts(x_part), to_experts(d_part)
        f, back, dot, hid, dg, du = expert(x, d, gate, up, down)
        backs.append(to_experts(back))
        dots.append(exchange(dot[0].reshape(NFFN, half_slots), planes).reshape(1, rows))
        for kept, item in zip((xs, ds, fs, hids, gates, ups), (x, d, to_experts(f), hid, dg, du)):
            kept.append(item)
    gate_part, up_part, down_part = (
        scatter_weight(grads) for grads in weight_grads(xs, ds, hids, gates, ups)
    )

    vector = jnp.concatenate([constant_vector, jnp.zeros((6, width), jnp.float32)], 0)
    resid_grads, *grads_out, out_grad, sums, prior_sums, prior_grad = turn(
        resid, small, grad, prior, routes, codes, backs, jnp.concatenate(dots, 1), vector, expert_row,
        mixer.T, prior_turned, out_weight, attended,
    )
    result = combine(resid, small, routes, codes, fs, vector, expert_row)

    own_backs = []
    for j in range(chunks):
        head_grads = exchange(grads_out[j].reshape(owners, HEAD_DIM, rows), "expert")
        back = attend_back(bias, cosine, sine, heads[j], outs[j], logs[j], head_grads)
        own_backs.append(exchange(back, "expert"))
    tokens_grad, qkv_grads = last(tokens, attention_row, own_backs, qkv_weights, resid_grads)

    def reduce_rows(partial):
        part = lax.psum_scatter(partial, ("xy", "core"), scatter_dimension=1, tiled=True)
        part = lax.psum_scatter(part, "expert", scatter_dimension=0, tiled=True)
        return lax.all_gather(part, ("xy", "core"), axis=1, tiled=True).astype(jnp.float32)

    out_total = reduce_rows(out_grad)
    qkv_total = reduce_rows(qkv_grads)
    sums, prior_sums = lax.psum((sums, prior_sums), everyone)
    share = width // owners
    mine = lax.dynamic_slice_in_dim(sums, member * share, share, 1)
    return (
        result[None],
        tokens_grad[None],
        prior_grad[None],
        *(qkv_total[:, i * width : (i + 1) * width] for i in range(3)),
        out_total,
        qkv_total[:, 3 * width],
        jnp.sum(mine[24:32], 0),
        mine[:NEXP].T,
        lax.dynamic_slice_in_dim(prior_sums, member * (NEXP // owners), NEXP // owners, 0)[:, :NEXP],
        mine[NEXP : NEXP + 4].T,
        mine[16:18],
        gate_part,
        up_part,
        down_part,
    )


def solution(mesh):
    owners, copies = mesh.shape["expert"], mesh.shape["dp"]
    cores = 2
    mesh = Mesh(mesh.devices.reshape(owners, copies // cores, cores), ("expert", "xy", "core"))
    dp = ("xy", "core")
    rows = P(dp, "expert", None)
    shard = P("expert", dp, None)
    in_specs = (rows, rows, rows, P(dp, None), rows) + (P(),) * 10 + (shard,) * 3
    out_specs = (
        (rows,) * 3
        + (P("expert", None),) * 4
        + (P("expert"),) * 2
        + (P("expert", None),) * 3
        + (P(None, "expert"),)
        + (shard,) * 3
    )
    return jax.shard_map(per_device, mesh=mesh, in_specs=in_specs, out_specs=out_specs, check_vma=False)
```

```python
import jax
import jax.numpy as jnp
from jax import lax
from jax.experimental import pallas as pl
from jax.experimental.pallas import tpu as pltpu
from jax.sharding import Mesh
from jax.sharding import PartitionSpec as P

NFFN = 8
NEXP = 12
SEG = 128
HEAD_DIM = 64
TRUNK = 1024
TILE = 2 * SEG
LOG2E = 1.4426950408889634
masked_score = -1e30
MIB = 2**20
epsilon = 1e-06
precise = lax.Precision.HIGHEST


def dot_nt(left, right):
    return lax.dot_general(left, right, (((1,), (1,)), ((), ())), preferred_element_type=jnp.float32)


def dot_nn(left, right):
    return jnp.dot(left, right, preferred_element_type=jnp.float32)


def tile_parts(tile, start):
    trunk_tiles = TRUNK // TILE
    if tile is not None and tile < trunk_tiles:
        return [(k * TILE, False, k == tile) for k in range(tile + 1)]
    parts = [(k * TILE, False, False) for k in range(trunk_tiles)]
    branch_tiles = 2
    if tile is None:
        parts += [(TRUNK + k * TILE, True, False) for k in range(branch_tiles)]
    else:
        parts += [(TRUNK + k * TILE, True, False) for k in range(tile - trunk_tiles)]
    parts += [(start, True, True)]
    return parts


def causal_bias():
    key_ids = lax.broadcasted_iota(jnp.int32, (TILE, TILE), 0)
    query_ids = lax.broadcasted_iota(jnp.int32, (TILE, TILE), 1)
    return jnp.where(key_ids <= query_ids, 0.0, masked_score).astype(jnp.float32)


def part_scores(scores, part, columns, bias_ref, triangle):
    first, by_lineage, causal = part
    if by_lineage:
        segment = 1 + (first - TRUNK) // SEG
        rows = [bias_ref[pl.ds(segment + i, 1), columns] for i in range(TILE // SEG)]
        scores = jnp.concatenate(
            [scores[i * SEG : (i + 1) * SEG] + rows[i] for i in range(TILE // SEG)], 0
        )
    if causal:
        scores = scores + triangle[...]
    return scores


def for_tiles(length, body):
    trunk_tiles = TRUNK // TILE
    for tile in range(trunk_tiles + 2):
        body(tile, tile * TILE)
    first_leaf = trunk_tiles + 2

    @pl.loop(first_leaf, length // TILE)
    def _(tile):
        body(None, pl.multiple_of(tile * TILE, TILE))


def attend_head(bias_ref, qkv_ref, out_ref, lse_ref, q_ref, k_ref, v_ref, o_ref, s_ref, triangle):
    sources, _, rows = qkv_ref.shape
    length = sources * rows
    factor = HEAD_DIM ** (-0.5) * LOG2E
    triangle[...] = causal_bias()
    extra = lax.broadcasted_iota(jnp.int32, (16, length), 0)
    v_ref[HEAD_DIM:, :] = jnp.where(extra == 0, 1.0, 0.0).astype(jnp.bfloat16)
    for z in range(sources):
        span = pl.ds(z * rows, rows)
        q_ref[:, span] = qkv_ref[z, :HEAD_DIM]
        k_ref[span, :] = qkv_ref[z, HEAD_DIM : 2 * HEAD_DIM].astype(jnp.float32).T.astype(jnp.bfloat16)
        v_ref[:HEAD_DIM, span] = qkv_ref[z, 2 * HEAD_DIM :]

    def body(tile, start):
        columns = pl.ds(start, TILE)
        parts = tile_parts(tile, start)
        query = q_ref[:, columns]
        peak = None
        for i, part in enumerate(parts):
            scores = dot_nn(k_ref[pl.ds(part[0], TILE), :], query)
            scores = part_scores(scores, part, columns, bias_ref, triangle)
            s_ref[i * TILE : (i + 1) * TILE, :] = scores
            top = jnp.max(scores, 0, keepdims=True)
            peak = top if peak is None else jnp.maximum(peak, top)
        shift = peak * factor
        total = None
        for i, part in enumerate(parts):
            weights = jnp.exp2(s_ref[i * TILE : (i + 1) * TILE, :] * factor - shift)
            term = dot_nn(v_ref[:, pl.ds(part[0], TILE)], weights.astype(jnp.bfloat16))
            total = term if total is None else total + term
        norm = total[HEAD_DIM : HEAD_DIM + 1]
        o_ref[:, columns] = (total[:HEAD_DIM] / norm).astype(jnp.bfloat16)
        lse_ref[:, columns] = shift + jnp.log2(norm)

    for_tiles(length, body)
    for z in range(sources):
        out_ref[z] = o_ref[:, pl.ds(z * rows, rows)]


def attend_back_kernel(
    bias_ref, cos_ref, sin_ref, qkv_ref, out_ref, lse_ref, grad_ref, back_ref,
    qt_ref, kt_ref, dt_ref, q_ref, k_ref, v_ref, d_ref, delta_ref, dq_ref, dk_ref, dv_ref, triangle,
):
    sources, _, rows = qkv_ref.shape
    length = sources * rows
    scaling = HEAD_DIM ** (-0.5)
    factor = scaling * LOG2E
    triangle[...] = causal_bias()

    def turned(values):
        return values.astype(jnp.float32).T.astype(jnp.bfloat16)

    for z in range(sources):
        span = pl.ds(z * rows, rows)
        query, key, value = (qkv_ref[z, i * HEAD_DIM : (i + 1) * HEAD_DIM] for i in range(3))
        grad = grad_ref[z]
        qt_ref[:, span] = query
        kt_ref[:, span] = key
        dt_ref[:, span] = grad
        q_ref[span, :] = turned(query)
        k_ref[span, :] = turned(key)
        v_ref[span, :] = turned(value)
        d_ref[span, :] = turned(grad)
        delta_ref[:, span] = jnp.sum(
            grad.astype(jnp.float32) * out_ref[z].astype(jnp.float32), 0, keepdims=True
        )
    dk_ref[...] = jnp.zeros_like(dk_ref)
    dv_ref[...] = jnp.zeros_like(dv_ref)

    def body(tile, start):
        columns = pl.ds(start, TILE)
        query_t, grad_t = qt_ref[:, columns], dt_ref[:, columns]
        query, grad = q_ref[columns, :], d_ref[columns, :]
        lse, delta = lse_ref[:, columns], delta_ref[:, columns]
        total = None
        for part in tile_parts(tile, start):
            span = pl.ds(part[0], TILE)
            scores = dot_nn(k_ref[span, :], query_t) * factor - lse
            scores = part_scores(scores, part, columns, bias_ref, triangle)
            weights = jnp.exp2(scores)
            weight_grads = dot_nn(v_ref[span, :], grad_t)
            score_grads = (weights * (weight_grads - delta)).astype(jnp.bfloat16)
            dv_ref[span, :] += dot_nn(weights.astype(jnp.bfloat16), grad)
            dk_ref[span, :] += dot_nn(score_grads, query)
            term = dot_nn(kt_ref[:, span], score_grads)
            total = term if total is None else total + term
        dq_ref[:, columns] = total

    for_tiles(length, body)
    half = HEAD_DIM // 2
    for z in range(sources):
        span = pl.ds(z * rows, rows)
        cosine, sine = cos_ref[:, span], sin_ref[:, span]
        for i, values in enumerate((dq_ref[:, span], dk_ref[span, :].T)):
            values = values * scaling
            first, second = values[:half], values[half:]
            back_ref[z, i * HEAD_DIM : (i + 1) * HEAD_DIM] = jnp.concatenate(
                [first * cosine + second * sine, second * cosine - first * sine], 0
            ).astype(jnp.bfloat16)
        back_ref[z, 2 * HEAD_DIM :] = dv_ref[span, :].T.astype(jnp.bfloat16)


def attend_back(bias, cosine, sine, qkv, out, lse, grad):
    sources, _, rows = qkv.shape
    length = sources * rows
    turned = pltpu.VMEM((HEAD_DIM, length), jnp.bfloat16)
    plain = pltpu.VMEM((length, HEAD_DIM), jnp.bfloat16)
    wide = pltpu.VMEM((length, HEAD_DIM), jnp.float32)
    return pl.pallas_call(
        attend_back_kernel,
        out_shape=jax.ShapeDtypeStruct((sources, 3 * HEAD_DIM, rows), jnp.bfloat16),
        scratch_shapes=[
            turned, turned, turned, plain, plain, plain, plain,
            pltpu.VMEM((1, length), jnp.float32),
            pltpu.VMEM((HEAD_DIM, length), jnp.float32),
            wide, wide,
            pltpu.VMEM((TILE, TILE), jnp.float32),
        ],
        compiler_params=pltpu.CompilerParams(vmem_limit_bytes=48 * MIB),
        cost_estimate=pl.CostEstimate(flops=5 * 10**9, bytes_accessed=6 * 10**6, transcendentals=3 * 10**6),
    )(bias, cosine, sine, qkv, out, lse, grad)


def params(limit):
    return pltpu.CompilerParams(vmem_limit_bytes=limit * MIB)


def cost(flops, moved):
    return pl.CostEstimate(flops=int(flops), bytes_accessed=int(moved), transcendentals=0)


def greet(ring, copies):
    barrier = pltpu.get_barrier_semaphore()
    for target in ring + copies:
        pl.semaphore_signal(barrier, inc=1, device_id=target, device_id_type=pl.DeviceIdType.MESH)
    pl.semaphore_wait(barrier, len(ring) + len(copies))


def ring_partners(owners):
    member = lax.axis_index("expert")
    result = []
    for step in sorted(range(1, owners), key=lambda k: -min(k, owners - k)):
        index = lax.rem(member + step, owners)
        result.append((step, index, {"expert": index}))
    return result


def copy_partners(total):
    place = lax.axis_index("xy") * 2 + lax.axis_index("core")
    result = []
    for step in sorted(range(1, total), key=lambda k: -(k % 8 in (6, 2, 4))):
        index = lax.rem(place + step, total)
        result.append((step, lax.rem(index, 2), {"xy": index // 2, "core": lax.rem(index, 2)}))
    return result


def remote(source, target, send, receive, device):
    return pltpu.make_async_remote_copy(
        src_ref=source, dst_ref=target, send_sem=send, recv_sem=receive,
        device_id=device, device_id_type=pl.DeviceIdType.MESH,
    )


def attend_phase_kernel(
    tokens_ref, gain_ref, query_ref, key_ref, value_ref, cos_ref, sin_ref, bias_ref, gate_ref, up_ref, down_ref,
    attended_ref, lse_ref, heads_ref, outs_ref, gate_full, up_full, down_full,
    normed_ref, qkv_sent, qkv_got, out_sent, out_got, q_ref, k_ref, v_ref, o_ref, s_ref, triangle,
    qkv_send, qkv_recv, out_send, out_recv, weight_send, weight_recv, local_sem,
):
    chunks, owners, _, rows = qkv_sent.shape
    member = lax.axis_index("expert")
    copies = gate_full.shape[0]
    ring, others = ring_partners(owners), copy_partners(copies)
    greet([item[2] for item in ring], [item[2] for item in others])
    weights = ((gate_ref, gate_full), (up_ref, up_full), (down_ref, down_full))
    place = lax.axis_index("xy") * 2 + lax.axis_index("core")
    core = lax.axis_index("core")
    started = []

    inputs = tokens_ref[...].astype(jnp.float32)
    inverse = lax.rsqrt(jnp.mean(inputs * inputs, -1, keepdims=True) + epsilon)
    normed_ref[...] = (inputs * inverse * gain_ref[...]).astype(jnp.bfloat16)
    half = HEAD_DIM // 2
    span_width = owners * HEAD_DIM
    qkv_copies = []
    for j in range(chunks):
        for i, weight in enumerate((query_ref, key_ref, value_ref)):
            turned = dot_nn(normed_ref[...], weight[:, j * span_width : (j + 1) * span_width]).T
            base = i * HEAD_DIM
            for z in range(owners):
                first = turned[z * HEAD_DIM : z * HEAD_DIM + half]
                second = turned[z * HEAD_DIM + half : (z + 1) * HEAD_DIM]
                if i < 2:
                    cosine, sine = cos_ref[...], sin_ref[...]
                    first, second = first * cosine - second * sine, second * cosine + first * sine
                qkv_sent[j, z, base : base + half] = first.astype(jnp.bfloat16)
                qkv_sent[j, z, base + half : base + HEAD_DIM] = second.astype(jnp.bfloat16)
        local = pltpu.make_async_copy(qkv_sent.at[j, member], qkv_got.at[j, member], local_sem.at[j])
        local.start()
        group = []
        for step, index, device in ring:
            copy = remote(
                qkv_sent.at[j, index], qkv_got.at[j, member],
                qkv_send.at[j, step - 1], qkv_recv.at[j, step - 1], device,
            )
            copy.start()
            group.append(copy)
        qkv_copies.append((local, group))
        if j == 0:
            for i, (shard, full) in enumerate(weights):
                local = pltpu.make_async_copy(shard.at[core], full.at[place], weight_send.at[i, 0])
                local.start()
                started.append((local, None))
                for step, other_core, device in others:
                    copy = remote(
                        shard.at[other_core], full.at[place], weight_send.at[i, step], weight_recv.at[i, step], device
                    )
                    copy.start()
                    started.append((None, copy))

    out_copies = []
    kept = []
    for j in range(chunks):
        local, group = qkv_copies[j]
        local.wait()
        for copy in group:
            copy.wait_recv()
        keep = pltpu.make_async_copy(qkv_got.at[j], heads_ref.at[j], local_sem.at[chunks + j])
        keep.start()
        kept.append(keep)
        attend_head(
            bias_ref, qkv_got.at[j], out_sent.at[j], lse_ref.at[j : j + 1], q_ref, k_ref, v_ref, o_ref, s_ref, triangle
        )
        local = pltpu.make_async_copy(out_sent.at[j, member], out_got.at[j, member], local_sem.at[2 * chunks + j])
        local.start()
        keep = pltpu.make_async_copy(out_sent.at[j], outs_ref.at[j], local_sem.at[3 * chunks + j])
        keep.start()
        kept += [local, keep]
        for step, index, device in ring:
            copy = remote(
                out_sent.at[j, index], out_got.at[j, member],
                out_send.at[j, step - 1], out_recv.at[j, step - 1], device,
            )
            copy.start()
            out_copies.append(copy)
    for copy in out_copies:
        copy.wait_recv()
    for copy in kept:
        copy.wait()
    attended_ref[...] = out_got[...]
    for local, group in qkv_copies:
        for copy in group:
            copy.wait_send()
    for copy in out_copies:
        copy.wait_send()
    for local, copy in started:
        if copy is None:
            local.wait()
        else:
            copy.wait()


def attend_phase(tokens, gain, weights, cosine, sine, bias, shards, copies):
    rows, width = tokens.shape
    owners = lax.axis_size("expert")
    length = rows * owners
    chunks = width // HEAD_DIM // owners
    head = (chunks, owners, 3 * HEAD_DIM, rows)
    out = (chunks, owners, HEAD_DIM, rows)
    vmem, hbm = pl.BlockSpec(memory_space=pltpu.VMEM), pl.BlockSpec(memory_space=pl.ANY)
    fulls = [jax.ShapeDtypeStruct((copies, *shard.shape[1:]), shard.dtype) for shard in shards]
    part_total = TRUNK // TILE + 3
    sems = lambda *shape: pltpu.SemaphoreType.DMA(shape)
    return pl.pallas_call(
        attend_phase_kernel,
        in_specs=[vmem] * 8 + [hbm] * 3,
        out_specs=(vmem, vmem, hbm, hbm, hbm, hbm, hbm),
        out_shape=(
            jax.ShapeDtypeStruct(out, jnp.bfloat16),
            jax.ShapeDtypeStruct((8, length), jnp.float32),
            jax.ShapeDtypeStruct(head, jnp.bfloat16),
            jax.ShapeDtypeStruct(out, jnp.bfloat16),
            *fulls,
        ),
        scratch_shapes=[
            pltpu.VMEM((rows, width), jnp.bfloat16),
            pltpu.VMEM(head, jnp.bfloat16),
            pltpu.VMEM(head, jnp.bfloat16),
            pltpu.VMEM(out, jnp.bfloat16),
            pltpu.VMEM(out, jnp.bfloat16),
            pltpu.VMEM((HEAD_DIM, length), jnp.bfloat16),
            pltpu.VMEM((length, HEAD_DIM), jnp.bfloat16),
            pltpu.VMEM((HEAD_DIM + 16, length), jnp.bfloat16),
            pltpu.VMEM((HEAD_DIM, length), jnp.bfloat16),
            pltpu.VMEM((part_total * TILE, TILE), jnp.float32),
            pltpu.VMEM((TILE, TILE), jnp.float32),
            sems(chunks, owners - 1), sems(chunks, owners - 1), sems(chunks, owners - 1), sems(chunks, owners - 1),
            sems(3, copies), sems(3, copies), sems(4 * chunks),
        ],
        compiler_params=pltpu.CompilerParams(vmem_limit_bytes=56 * MIB, collective_id=1, has_side_effects=True),
        cost_estimate=cost(1e10, 5e7),
    )(tokens, gain, *weights, cosine, sine, bias, *shards)


def lane_pick(values, lanes, index):
    return jnp.sum(jnp.where(lanes == index, values, 0.0), -1, keepdims=True)


def middle_kernel(
    tokens_ref, a0_ref, a1_ref, a2_ref, out_weight_ref, gain_ref, mixer_ref, prior_ref, prior_weight_ref,
    routes_ref, codes_ref, resid_ref, small_ref, first_ref, second_ref, hidden_ref,
):
    rows, width = tokens_ref.shape

    @pl.loop(0, rows // SEG)
    def _(step):
        span = pl.ds(pl.multiple_of(step * SEG, SEG), SEG)
        attended = jnp.concatenate([ref[:, span] for ref in (a0_ref, a1_ref, a2_ref)], 0)
        attended = attended.astype(jnp.float32).T.astype(jnp.bfloat16)
        resid = tokens_ref[span, :].astype(jnp.float32) + dot_nn(attended, out_weight_ref[...])
        inverse = lax.rsqrt(jnp.mean(resid * resid, -1, keepdims=True) + epsilon)
        hidden = (resid * inverse * gain_ref[...]).astype(jnp.bfloat16)
        resid_ref[span, :] = resid
        hidden_ref[span, :] = hidden
        logits = dot_nn(hidden, mixer_ref[...])
        logits = logits + jnp.dot(
            prior_ref[span, :], prior_weight_ref[...], precision=precise, preferred_element_type=jnp.float32
        )
        lanes = lax.broadcasted_iota(jnp.int32, logits.shape, 1)
        routes = routes_ref[span, :]
        columns = []
        pairs = [[lane_pick(logits, lanes, routes[:, c : c + 1]) for c in range(2)]]
        pairs += [[logits[:, NEXP + 2 * m + c : NEXP + 2 * m + c + 1] for c in range(2)] for m in range(2)]
        for one, two in pairs:
            peak = jnp.maximum(one, two)
            one, two = jnp.exp(one - peak), jnp.exp(two - peak)
            columns += [one / (one + two), two / (one + two)]
        columns.append(inverse)
        small = jnp.zeros_like(logits)
        for i, column in enumerate(columns):
            small = jnp.where(lanes == i, column, small)
        small_ref[span, :] = small

    slots = first_ref.shape[0]
    for half, ref in enumerate((first_ref, second_ref)):
        index = lax.broadcasted_iota(jnp.int32, (slots, rows), 0) + half * slots
        chosen = (codes_ref[0:1, :] == index) | (codes_ref[1:2, :] == index)
        ref[...] = dot_nn(chosen.astype(jnp.bfloat16), hidden_ref[...]).astype(jnp.bfloat16)


def middle(tokens, attended, out_weight, gain, mixer, prior, prior_weight, routes, codes_row):
    rows, width = tokens.shape
    slots = rows
    return pl.pallas_call(
        middle_kernel,
        out_shape=(
            jax.ShapeDtypeStruct((rows, width), jnp.float32),
            jax.ShapeDtypeStruct((rows, 128), jnp.float32),
            jax.ShapeDtypeStruct((slots, width), jnp.bfloat16),
            jax.ShapeDtypeStruct((slots, width), jnp.bfloat16),
        ),
        scratch_shapes=[pltpu.VMEM((rows, width), jnp.bfloat16)],
        compiler_params=params(48),
        cost_estimate=cost(4 * rows * width * width + 4 * rows * rows * width, 1e7),
    )(tokens, *attended, out_weight, gain, mixer, prior, prior_weight, routes, codes_row)


def scatter_kernel(small_ref, grad_ref, codes_ref, first_ref, second_ref, scaled_ref):
    rows, width = grad_ref.shape
    small = small_ref[...]
    grad = grad_ref[...].astype(jnp.float32)
    for c in range(2):
        scaled_ref[c * rows : (c + 1) * rows, :] = (small[:, c : c + 1] * grad).astype(jnp.bfloat16)
    slots = first_ref.shape[0]
    for half, ref in enumerate((first_ref, second_ref)):
        index = lax.broadcasted_iota(jnp.int32, (slots, rows), 0) + half * slots
        chosen = jnp.concatenate([(codes_ref[c : c + 1, :] == index).astype(jnp.bfloat16) for c in range(2)], 1)
        ref[...] = dot_nn(chosen, scaled_ref[...]).astype(jnp.bfloat16)


def scatter(small, grad, codes_row):
    rows, width = grad.shape
    return pl.pallas_call(
        scatter_kernel,
        out_shape=(jax.ShapeDtypeStruct((rows, width), jnp.bfloat16),) * 2,
        scratch_shapes=[pltpu.VMEM((2 * rows, width), jnp.bfloat16)],
        compiler_params=params(48),
        cost_estimate=cost(8 * rows * rows * width, 4e6),
    )(small, grad, codes_row)


def expert_kernel(
    x_ref, d_ref, gate_ref, up_ref, down_ref, f_ref, back_ref, dots_ref, hid_ref, dg_ref, du_ref, f_sum, back_sum
):
    step = pl.program_id(0)
    rows = x_ref.shape[0]
    part = rows // 2
    for r in range(2):
        span = pl.ds(r * part, part)
        x, d = x_ref[span, :], d_ref[span, :]
        gate_pre = dot_nn(x, gate_ref[...])
        up_pre = dot_nn(x, up_ref[...])
        mid = dot_nt(d, down_ref[...])
        sigmoid = 1.0 / (1.0 + jnp.exp(-gate_pre))
        active = gate_pre * sigmoid
        hid = (active * up_pre).astype(jnp.bfloat16)
        du = (mid * active).astype(jnp.bfloat16)
        dg = (mid * up_pre * (sigmoid + active * (1.0 - sigmoid))).astype(jnp.bfloat16)
        hid_ref[span, :] = hid
        du_ref[span, :] = du
        dg_ref[span, :] = dg
        f_term = dot_nn(hid, down_ref[...])
        back_term = dot_nt(dg, gate_ref[...]) + dot_nt(du, up_ref[...])

        @pl.when(step == 0)
        def _():
            f_sum[span, :] = f_term
            back_sum[span, :] = back_term

        @pl.when(step > 0)
        def _():
            f_sum[span, :] += f_term
            back_sum[span, :] += back_term

    @pl.when(step == pl.num_programs(0) - 1)
    def _():
        back_ref[...] = back_sum[...].astype(jnp.bfloat16)
        f = f_sum[...].astype(jnp.bfloat16)
        f_ref[...] = f
        dots = jnp.sum(f.astype(jnp.float32) * d_ref[...].astype(jnp.float32), -1, keepdims=True)
        dots_ref[...] = jnp.broadcast_to(dots, (rows, 128)).T[:8]


def expert(x, d, gate, up, down):
    rows, width = x.shape
    units = gate.shape[1]
    part = 512
    whole = pl.BlockSpec((rows, width), lambda i: (0, 0))
    columns = pl.BlockSpec((width, part), lambda i: (0, i))
    mids = pl.BlockSpec((rows, part), lambda i: (0, i))
    return pl.pallas_call(
        expert_kernel,
        grid=(units // part,),
        in_specs=[whole, whole, columns, columns, pl.BlockSpec((part, width), lambda i: (i, 0))],
        out_specs=(whole, whole, pl.BlockSpec((8, rows), lambda i: (0, 0)), mids, mids, mids),
        out_shape=(
            jax.ShapeDtypeStruct((rows, width), jnp.bfloat16),
            jax.ShapeDtypeStruct((rows, width), jnp.bfloat16),
            jax.ShapeDtypeStruct((8, rows), jnp.float32),
        )
        + (jax.ShapeDtypeStruct((rows, units), jnp.bfloat16),) * 3,
        scratch_shapes=[pltpu.VMEM((rows, width), jnp.float32)] * 2,
        compiler_params=params(52),
        cost_estimate=cost(12 * rows * width * units, 3e7),
    )(x, d, gate, up, down)


def weights_kernel(
    xa_ref, xb_ref, da_ref, db_ref, ha_ref, hb_ref, ga_ref, gb_ref, ua_ref, ub_ref,
    gate_ref, up_ref, down_ref, x_turned, d_turned,
):
    rows = xa_ref.shape[0]

    @pl.when(pl.program_id(0) == 0)
    def _():
        for i, (x, d) in enumerate(((xa_ref, da_ref), (xb_ref, db_ref))):
            span = pl.ds(i * rows, rows)
            x_turned[:, span] = x[...].astype(jnp.float32).T.astype(jnp.bfloat16)
            d_turned[:, span] = d[...].astype(jnp.float32).T.astype(jnp.bfloat16)

    both = lambda one, two: jnp.concatenate([one[...], two[...]], 0)
    gate_ref[...] = dot_nn(x_turned[...], both(ga_ref, gb_ref)).astype(jnp.bfloat16)
    up_ref[...] = dot_nn(x_turned[...], both(ua_ref, ub_ref)).astype(jnp.bfloat16)
    down_ref[...] = dot_nn(d_turned[...], both(ha_ref, hb_ref)).T.astype(jnp.bfloat16)


def weight_grads(xs, ds, hids, gates, ups):
    rows, width = xs[0].shape
    units = hids[0].shape[1]
    part = 256
    whole = pl.BlockSpec((rows, width), lambda i: (0, 0))
    mids = pl.BlockSpec((rows, part), lambda i: (0, i))
    columns = pl.BlockSpec((width, part), lambda i: (0, i))
    return pl.pallas_call(
        weights_kernel,
        grid=(units // part,),
        in_specs=[whole] * 4 + [mids] * 6,
        out_specs=(columns, columns, pl.BlockSpec((part, width), lambda i: (i, 0))),
        out_shape=(
            jax.ShapeDtypeStruct((width, units), jnp.bfloat16),
            jax.ShapeDtypeStruct((width, units), jnp.bfloat16),
            jax.ShapeDtypeStruct((units, width), jnp.bfloat16),
        ),
        scratch_shapes=[pltpu.VMEM((width, 2 * rows), jnp.bfloat16)] * 2,
        compiler_params=params(52),
        cost_estimate=cost(12 * rows * width * units, 3e7),
    )(*xs, *ds, *hids, *gates, *ups)


def split_dot(dot, left, right):
    high = left.astype(jnp.bfloat16)
    low = (left - high.astype(jnp.float32)).astype(jnp.bfloat16)
    return dot(high, right) + dot(low, right)


def turn_kernel(
    resid_ref, small_ref, grad_ref, prior_ref, routes_ref, codes_ref, ra_ref, rb_ref, dots_ref, vector_ref,
    gain_ref, mixer_ref, prior_turned_ref, out_weight_ref, a0_ref, a1_ref, a2_ref,
    resid_grad_ref, g0_ref, g1_ref, g2_ref, out_grad_ref, prior_grad_ref, back_ref, sums_ref, prior_sums_ref, extra_ref,
):
    rows, width = resid_ref.shape
    slots = 2 * ra_ref.shape[0]
    sums_ref[...] = jnp.zeros_like(sums_ref)
    prior_sums_ref[...] = jnp.zeros_like(prior_sums_ref)

    @pl.loop(0, rows // SEG)
    def _(step):
        span = pl.ds(pl.multiple_of(step * SEG, SEG), SEG)
        small = small_ref[span, :]
        routes, codes = routes_ref[span, :], codes_ref[span, :]
        gates = [small[:, c : c + 1] for c in range(2)]
        mixing = [[small[:, 2 + 2 * m + c : 3 + 2 * m + c] for c in range(2)] for m in range(2)]
        inverse = small[:, 6:7]
        normed = resid_ref[span, :] * inverse
        hidden = normed * gain_ref[...]
        hidden_b = hidden.astype(jnp.bfloat16)
        grad_b = grad_ref[span, :]
        grad = grad_b.astype(jnp.float32)
        index = lax.broadcasted_iota(jnp.int32, (SEG, slots), 1)
        hits = [codes[:, c : c + 1] == index for c in range(2)]
        dots = dots_ref[...]
        terms = [jnp.sum(jnp.where(hit, dots, 0.0), -1, keepdims=True) for hit in hits]
        chosen = (hits[0] | hits[1]).astype(jnp.bfloat16)
        half = slots // 2
        routed = dot_nn(chosen[:, :half], ra_ref[...]) + dot_nn(chosen[:, half:], rb_ref[...])
        along = jnp.sum(grad * hidden, -1, keepdims=True)
        across = [jnp.sum(grad * vector_ref[m : m + 1, :], -1, keepdims=True) for m in range(2)]
        to_copy = 0.0
        to_mix = [0.0, 0.0]
        for c in range(2):
            route = routes[:, c : c + 1]
            copied = jnp.where(route == NFFN + 1, gates[c], 0.0)
            to_copy = to_copy + copied
            terms[c] = terms[c] + copied * along
            for m in range(2):
                mixed = jnp.where(route == NFFN + 2 + m, gates[c], 0.0)
                to_mix[m] = to_mix[m] + mixed
                terms[c] = terms[c] + mixed * (mixing[m][0] * along + mixing[m][1] * across[m])
        both = terms[0] + terms[1]
        lanes = lax.broadcasted_iota(jnp.int32, (SEG, 128), 1)
        logit_grads = jnp.zeros((SEG, 128), jnp.float32)
        for c in range(2):
            logit_grads = jnp.where(lanes == routes[:, c : c + 1], terms[c] - gates[c] * both, logit_grads)
        scores = logit_grads
        direct = to_copy
        for m in range(2):
            pair = (to_mix[m] * along, to_mix[m] * across[m])
            mean = mixing[m][0] * pair[0] + mixing[m][1] * pair[1]
            for c in range(2):
                scores = jnp.where(lanes == NEXP + 2 * m + c, mixing[m][c] * (pair[c] - mean), scores)
            direct = direct + mixing[m][0] * to_mix[m]
        prior_grad_ref[span, :] = jnp.dot(
            logit_grads, prior_turned_ref[...], precision=precise, preferred_element_type=jnp.float32
        )[:, : prior_grad_ref.shape[1]]
        hidden_grads = split_dot(dot_nn, scores, mixer_ref[...]) + direct * grad + routed
        scaled = hidden_grads * gain_ref[...]
        resid_grads = inverse * (scaled - normed * jnp.mean(scaled * normed, -1, keepdims=True)) + grad
        resid_grad_ref[span, :] = resid_grads
        back_ref[span, :] = resid_grads.astype(jnp.bfloat16)
        weights = jnp.zeros((SEG, 128), jnp.float32)
        for m in range(2):
            weights = jnp.where(lanes == m, mixing[m][1] * to_mix[m], weights)
        sums_ref[0:16, :] += split_dot(dot_nn, scores.T[0:16], hidden_b)
        sums_ref[16:24, :] += split_dot(dot_nn, weights.T[0:8], grad_b)
        sums_ref[24:32, :] += jnp.sum((hidden_grads * normed).reshape(SEG // 8, 8, width), 0)
        prior_sums_ref[...] += jnp.dot(
            prior_ref[span, :].T,
            jnp.concatenate([logit_grads[:, 96:], logit_grads[:, :96]], 1),
            precision=precise,
            preferred_element_type=jnp.float32,
        )

    sums_ref[24:25, :] = jnp.sum(sums_ref[24:32, :], 0, keepdims=True)
    extra_ref[...] = jnp.concatenate([sums_ref[...], jnp.zeros((96, width), jnp.float32)], 0).T
    owners = a0_ref.shape[0] // HEAD_DIM
    kept = NEXP // owners
    for z in range(owners):
        extra_ref[pl.ds(z * (width // owners), kept), :] += prior_sums_ref[z * kept : (z + 1) * kept, :]
    out_grad_ref[:, width:] = extra_ref[...].astype(jnp.bfloat16)
    back = back_ref[...]
    part = a0_ref.shape[0]
    for j, (a_ref, g_ref) in enumerate(((a0_ref, g0_ref), (a1_ref, g1_ref), (a2_ref, g2_ref))):
        span = pl.ds(j * part, part)
        g_ref[...] = dot_nt(out_weight_ref[span, :], back).astype(jnp.bfloat16)
        out_grad_ref[span, :width] = dot_nn(a_ref[...], back).astype(jnp.bfloat16)


def turn(resid, small, grad, prior, routes, codes, returned, dots, vector, gain, mixer_turned, prior_turned, out_weight, attended):
    rows, width = resid.shape
    part = attended[0].shape[0]
    return pl.pallas_call(
        turn_kernel,
        out_shape=(
            jax.ShapeDtypeStruct((rows, width), jnp.float32),
            *(jax.ShapeDtypeStruct((part, rows), jnp.bfloat16),) * 3,
            jax.ShapeDtypeStruct((width, width + 128), jnp.bfloat16),
            jax.ShapeDtypeStruct(prior.shape, jnp.float32),
        ),
        scratch_shapes=[
            pltpu.VMEM((rows, width), jnp.bfloat16),
            pltpu.VMEM((32, width), jnp.float32),
            pltpu.VMEM((prior.shape[1], 128), jnp.float32),
            pltpu.VMEM((width, 128), jnp.float32),
        ],
        compiler_params=params(56),
        cost_estimate=cost(4 * rows * width * width + 4 * rows * rows * width, 1.5e7),
    )(resid, small, grad, prior, routes, codes, *returned, dots, vector, gain, mixer_turned, prior_turned, out_weight, *attended)


def combine_kernel(resid_ref, small_ref, routes_ref, codes_ref, fa_ref, fb_ref, vector_ref, gain_ref, out_ref):
    rows, width = resid_ref.shape
    half = fa_ref.shape[0]

    @pl.loop(0, rows // SEG)
    def _(step):
        span = pl.ds(pl.multiple_of(step * SEG, SEG), SEG)
        small = small_ref[span, :]
        routes, codes = routes_ref[span, :], codes_ref[span, :]
        resid = resid_ref[span, :]
        hidden = resid * small[:, 6:7] * gain_ref[...]
        index = lax.broadcasted_iota(jnp.int32, (SEG, 2 * half), 1)
        total = resid
        direct = 0.0
        for c in range(2):
            gate, route = small[:, c : c + 1], routes[:, c : c + 1]
            chosen = (codes[:, c : c + 1] == index).astype(jnp.bfloat16)
            routed = dot_nn(chosen[:, :half], fa_ref[...]) + dot_nn(chosen[:, half:], fb_ref[...])
            total = total + gate * routed
            direct = direct + jnp.where(route == NFFN + 1, gate, 0.0)
            for m in range(2):
                mixed = jnp.where(route == NFFN + 2 + m, gate, 0.0)
                direct = direct + mixed * small[:, 2 + 2 * m : 3 + 2 * m]
                total = total + mixed * small[:, 3 + 2 * m : 4 + 2 * m] * vector_ref[m : m + 1, :]
        out_ref[span, :] = (total + direct * hidden).astype(jnp.bfloat16)


def combine(resid, small, routes, codes, outs, vector, gain):
    rows, width = resid.shape
    return pl.pallas_call(
        combine_kernel,
        out_shape=jax.ShapeDtypeStruct((rows, width), jnp.bfloat16),
        compiler_params=params(48),
        cost_estimate=cost(8 * rows * rows * width, 8e6),
    )(resid, small, routes, codes, *outs, vector, gain)


def head_grads_kernel(tokens_ref, gain_ref, back_ref, out_ref, turned_ref):
    inputs = tokens_ref[...].astype(jnp.float32)
    inverse = lax.rsqrt(jnp.mean(inputs * inputs, -1, keepdims=True) + epsilon)
    normed = (inputs * inverse * gain_ref[...]).T.astype(jnp.bfloat16)
    owners = back_ref.shape[0]
    for i in range(3):
        for z in range(owners):
            row = (i * owners + z) * HEAD_DIM
            turned_ref[row : row + HEAD_DIM, :] = back_ref[z, i * HEAD_DIM : (i + 1) * HEAD_DIM]
    out_ref[...] = dot_nt(normed, turned_ref[...]).astype(jnp.bfloat16)


def head_grads(tokens, gain, back):
    rows, width = tokens.shape
    columns = back.shape[0] * back.shape[1]
    return pl.pallas_call(
        head_grads_kernel,
        out_shape=jax.ShapeDtypeStruct((width, columns), jnp.bfloat16),
        scratch_shapes=[pltpu.VMEM((columns, rows), jnp.bfloat16)],
        compiler_params=params(48),
        cost_estimate=cost(2 * rows * width * columns, 4e6),
    )(tokens, gain, back)


def last_kernel(
    tokens_ref, gain_ref, b0_ref, b1_ref, b2_ref, query_ref, key_ref, value_ref, resid_grad_ref,
    tokens_grad_ref, gain_grad_ref, back_turned,
):
    rows, width = tokens_ref.shape
    inputs = tokens_ref[...].astype(jnp.float32)
    inverse = lax.rsqrt(jnp.mean(inputs * inputs, -1, keepdims=True) + epsilon)
    normed = inputs * inverse
    owners = b0_ref.shape[0]
    for i in range(3):
        for j, ref in enumerate((b0_ref, b1_ref, b2_ref)):
            for z in range(owners):
                head = j * owners + z
                back_turned[i, head * HEAD_DIM : (head + 1) * HEAD_DIM, :] = ref[z, i * HEAD_DIM : (i + 1) * HEAD_DIM]
    total = None
    for i, ref in enumerate((query_ref, key_ref, value_ref)):
        term = dot_nn(ref[...], back_turned[i])
        total = term if total is None else total + term
    first_grads = total.T
    summed = jnp.sum((first_grads * normed).reshape(rows // 8, 8, width), 0)
    column = jnp.sum(summed.T, -1, keepdims=True)
    gain_grad_ref[...] = jnp.broadcast_to(column, (width, 128)).astype(jnp.bfloat16)
    scaled = first_grads * gain_ref[...]
    tokens_grad_ref[...] = (
        inverse * (scaled - normed * jnp.mean(scaled * normed, -1, keepdims=True)) + resid_grad_ref[...]
    )


def last(tokens, gain, backs, weights, resid_grads):
    rows, width = tokens.shape
    return pl.pallas_call(
        last_kernel,
        out_shape=(
            jax.ShapeDtypeStruct((rows, width), jnp.float32),
            jax.ShapeDtypeStruct((width, 128), jnp.bfloat16),
        ),
        scratch_shapes=[pltpu.VMEM((3, width, rows), jnp.bfloat16)],
        compiler_params=params(56),
        cost_estimate=cost(6 * rows * width * width, 2e7),
    )(tokens, gain, *backs, *weights, resid_grads)


def lineage_of(parent_row):
    segment_total = parent_row.shape[0] + 1
    indices = jnp.arange(segment_total, dtype=jnp.int32)
    parent_all = jnp.concatenate([jnp.full((1,), -1, jnp.int32), parent_row])
    reach = (parent_all[:, None] == indices[None, :]) | (indices[:, None] == indices[None, :])
    for repeat in range(3):
        reach = jnp.any(reach[:, :, None] & reach[None, :, :], 1)
    return reach


def slot_codes(routes, half_slots):
    rows = routes.shape[0]
    experts = jnp.arange(NFFN, dtype=jnp.int32)
    matches = routes[:, :, None] == experts
    per_row = jnp.sum(matches.astype(jnp.float32), 1)
    earlier = jnp.arange(rows)[:, None] > jnp.arange(rows)[None, :]
    before = jnp.dot(
        earlier.astype(jnp.bfloat16), per_row.astype(jnp.bfloat16), preferred_element_type=jnp.float32
    )
    rank = jnp.sum(jnp.where(matches, before[:, None, :], 0.0), -1).astype(jnp.int32)
    late = (rank >= half_slots).astype(jnp.int32)
    code = late * (NFFN * half_slots) + routes * half_slots + rank - late * half_slots
    return jnp.where(routes < NFFN, code, 4 * NFFN * half_slots)


def per_device(
    tokens, prior_logits, routes, parents, cotangent, query_weight, key_weight, value_weight, out_weight,
    attention_gain, expert_gain, router_weight, prior_weight, constant_weight, constant_vector,
    gate_weight, up_weight, down_weight,
):
    owners = lax.axis_size("expert")
    member = lax.axis_index("expert")
    core = lax.axis_index("core")
    tokens, prior, routes, grad = tokens[0], prior_logits[0], routes[0], cotangent[0]
    rows, width = tokens.shape
    copies = lax.axis_size("xy") * lax.axis_size("core")
    length = rows * owners
    chunks = width // HEAD_DIM // owners
    half_slots = rows // 8
    planes, everyone = ("expert", "core"), ("expert", "xy", "core")

    def swap(values):
        return lax.ppermute(values, "core", [(0, 1), (1, 0)])

    def exchange(values, axes):
        return lax.all_to_all(values, axes, split_axis=0, concat_axis=0, tiled=True)

    def gather_weight(weight):
        mine = jnp.where(core == 0, weight[0], weight[1])
        other = swap(jnp.where(core == 0, weight[1], weight[0]))
        pair = jnp.concatenate([jnp.where(core == 0, mine, other), jnp.where(core == 0, other, mine)], 0)
        return lax.all_gather(pair, "xy", axis=0, tiled=True)

    def scatter_weight(grads):
        part = lax.psum_scatter(grads, "xy", scatter_dimension=0, tiled=True)
        part = part.reshape(2, part.shape[0] // 2, part.shape[1])
        mine = jnp.where(core == 0, part[0], part[1])
        other = swap(jnp.where(core == 0, part[1], part[0]))
        return jnp.stack(
            [jnp.where(core == 0, mine, other), jnp.where(core == 0, other, mine)], 0
        ).astype(jnp.float32)

    lineage = lineage_of(parents[0])
    segments = lineage.shape[0]
    lengths = jnp.where(jnp.arange(segments) == 0, TRUNK, SEG)
    begins = jnp.where(jnp.arange(segments) == 0, 0, TRUNK + (jnp.arange(segments) - 1) * SEG)
    shifts = jnp.sum(jnp.where(lineage, lengths[None, :], 0), 1) - lengths - begins
    ids = jnp.arange(length, dtype=jnp.int32)
    segment = jnp.where(ids < TRUNK, 0, 1 + (ids - TRUNK) // SEG)
    own = segment[None, :] == jnp.arange(segments)[:, None]
    places = (jnp.sum(jnp.where(own, shifts[:, None], 0), 0) + ids).astype(jnp.float32)
    reach = jnp.any(own[:, None, :] & lineage[:, :, None], 0)
    bias = jnp.where(reach, 0.0, masked_score).astype(jnp.float32)
    bias = jnp.concatenate([bias, jnp.zeros((16 - segments, length), jnp.float32)], 0)
    frequency = 10000.0 ** (-(jnp.arange(HEAD_DIM // 2, dtype=jnp.float32) * 2.0 / HEAD_DIM))
    angles = frequency[:, None] * places[None, :]
    cosine, sine = jnp.cos(angles), jnp.sin(angles)
    own_cosine, own_sine = (lax.dynamic_slice_in_dim(table, member * rows, rows, 1) for table in (cosine, sine))

    attention_row, expert_row = attention_gain[None], expert_gain[None]
    qkv_weights = (query_weight, key_weight, value_weight)
    attended, logs, heads, outs, gate, up, down = attend_phase(
        tokens, attention_row, qkv_weights, own_cosine, own_sine, bias, (gate_weight, up_weight, down_weight), copies
    )
    attended = [attended[j].reshape(owners * HEAD_DIM, rows) for j in range(chunks)]
    gate, up, down = (full.reshape(-1, full.shape[-1]) for full in (gate, up, down))
    codes = slot_codes(routes, half_slots)
    codes_row = codes.T

    mixer = jnp.concatenate(
        [router_weight, constant_weight, jnp.zeros((width, 128 - NEXP - 4), jnp.bfloat16)], 1
    )
    prior_wide = jnp.pad(prior_weight, ((0, 0), (0, 128 - NEXP)))
    prior_turned = jnp.pad(prior_weight.T, ((0, 128 - NEXP), (0, 128 - NEXP)))
    resid, small, *x_out = middle(
        tokens, attended, out_weight, expert_row, mixer, prior, prior_wide, routes, codes_row
    )
    d_out = scatter(small, grad, codes_row)

    def to_experts(values):
        return exchange(values.reshape(NFFN, half_slots, -1), planes).reshape(values.shape)

    xs, ds, fs, backs, dots, hids, gates, ups = ([] for _ in range(8))
    for x_part, d_part in zip(x_out, d_out):
        x, d = to_experts(x_part), to_experts(d_part)
        f, back, dot, hid, dg, du = expert(x, d, gate, up, down)
        backs.append(to_experts(back))
        dots.append(exchange(dot[0].reshape(NFFN, half_slots), planes).reshape(1, rows))
        for kept, item in zip((xs, ds, fs, hids, gates, ups), (x, d, f, hid, dg, du)):
            kept.append(item)
    *backs, grads_gate, grads_up, grads_down = lax.optimization_barrier(
        (*backs, *weight_grads(xs, ds, hids, gates, ups))
    )
    gate_part, up_part, down_part = (scatter_weight(grads) for grads in (grads_gate, grads_up, grads_down))

    vector = jnp.concatenate([constant_vector, jnp.zeros((6, width), jnp.float32)], 0)
    resid_grads, *grads_out, out_grad, prior_grad = turn(
        resid, small, grad, prior, routes, codes, backs, jnp.concatenate(dots, 1), vector, expert_row,
        mixer.T, prior_turned, out_weight, attended,
    )
    fs[0], grads_out[0] = lax.optimization_barrier((fs[0], grads_out[0]))

    def over_copies(partial):
        return lax.psum_scatter(partial, ("xy", "core"), scatter_dimension=1, tiled=True)

    out_grad, gate_part = lax.optimization_barrier((out_grad, gate_part))
    own_backs, parts = [], [over_copies(out_grad)]
    for j in range(chunks):
        grads_in = exchange(grads_out[j].reshape(owners, HEAD_DIM, rows), "expert")
        back = exchange(attend_back(bias, cosine, sine, heads[j], outs[j], logs[j : j + 1], grads_in), "expert")
        own_backs.append(back)
        parts.append(over_copies(head_grads(tokens, attention_row, back)))
    fs[1], own_backs[0] = lax.optimization_barrier((fs[1], own_backs[0]))
    result = combine(resid, small, routes, codes, [to_experts(f) for f in fs], vector, expert_row)
    tokens_grad, gain_grads = last(tokens, attention_row, own_backs, qkv_weights, resid_grads)
    parts.append(over_copies(gain_grads))
    sizes = [part.shape[1] for part in parts]
    share = width // owners
    joined = jnp.concatenate(parts, 1)
    joined = exchange(joined.reshape(owners, share, joined.shape[1]), "expert")
    joined = jnp.sum(joined.astype(jnp.float32), 0).astype(jnp.bfloat16)
    joined = lax.all_gather(joined, ("xy", "core"), axis=0, tiled=False)
    totals, begin = [], 0
    for size in sizes:
        part = joined[:, :, begin : begin + size].transpose(1, 0, 2).reshape(share, -1)
        totals.append(part.astype(jnp.float32))
        begin += size
    out_total, *head_totals, gain_total = totals
    span = owners * HEAD_DIM
    qkv_totals = [
        jnp.concatenate([part[:, i * span : (i + 1) * span] for part in head_totals], 1) for i in range(3)
    ]
    small_total = out_total[:, width:]
    return (
        result[None],
        tokens_grad[None],
        prior_grad[None],
        *qkv_totals,
        out_total[:, :width],
        gain_total[:, 0],
        small_total[:, 24],
        small_total[:, :NEXP],
        small_total[: NEXP // owners, 32 : 32 + NEXP],
        small_total[:, NEXP : NEXP + 4],
        small_total[:, 16:18].T,
        gate_part,
        up_part,
        down_part,
    )


def solution(mesh):
    owners, copies = mesh.shape["expert"], mesh.shape["dp"]
    cores = 2
    mesh = Mesh(mesh.devices.reshape(owners, copies // cores, cores), ("expert", "xy", "core"))
    dp = ("xy", "core")
    rows = P(dp, "expert", None)
    shard = P("expert", dp, None)
    in_specs = (rows, rows, rows, P(dp, None), rows) + (P(),) * 10 + (shard,) * 3
    out_specs = (
        (rows,) * 3
        + (P("expert", None),) * 4
        + (P("expert"),) * 2
        + (P("expert", None),) * 3
        + (P(None, "expert"),)
        + (shard,) * 3
    )
    return jax.shard_map(per_device, mesh=mesh, in_specs=in_specs, out_specs=out_specs, check_vma=False)
```

```python
import functools

import jax
import jax.numpy as jnp
from jax import lax
from jax.experimental import pallas as pl
from jax.experimental.pallas import tpu as pltpu
from jax.sharding import Mesh
from jax.sharding import PartitionSpec as P

NFFN = 8
NEXP = 12
SEG = 128
HEAD_DIM = 64
TRUNK = 1024
TILE = 2 * SEG
LOG2E = 1.4426950408889634
masked_score = -1e30
MIB = 2**20
epsilon = 1e-06
precise = lax.Precision.HIGHEST


def dot_nt(left, right):
    return lax.dot_general(left, right, (((1,), (1,)), ((), ())), preferred_element_type=jnp.float32)


def dot_nn(left, right):
    return jnp.dot(left, right, preferred_element_type=jnp.float32)


def tile_parts(tile, start):
    trunk_tiles = TRUNK // TILE
    if tile is not None and tile < trunk_tiles:
        return [(k * TILE, False, k == tile) for k in range(tile + 1)]
    parts = [(k * TILE, False, False) for k in range(trunk_tiles)]
    branch_tiles = 2
    if tile is None:
        parts += [(TRUNK + k * TILE, True, False) for k in range(branch_tiles)]
    else:
        parts += [(TRUNK + k * TILE, True, False) for k in range(tile - trunk_tiles)]
    parts += [(start, True, True)]
    return parts


def causal_bias():
    key_ids = lax.broadcasted_iota(jnp.int32, (TILE, TILE), 0)
    query_ids = lax.broadcasted_iota(jnp.int32, (TILE, TILE), 1)
    return jnp.where(key_ids <= query_ids, 0.0, masked_score).astype(jnp.float32)


def part_scores(scores, part, columns, bias_ref, triangle):
    first, by_lineage, causal = part
    if by_lineage:
        segment = 1 + (first - TRUNK) // SEG
        rows = [bias_ref[pl.ds(segment + i, 1), columns] for i in range(TILE // SEG)]
        scores = jnp.concatenate(
            [scores[i * SEG : (i + 1) * SEG] + rows[i] for i in range(TILE // SEG)], 0
        )
    if causal:
        scores = scores + triangle[...]
    return scores


def for_tiles(length, body):
    trunk_tiles = TRUNK // TILE
    for tile in range(trunk_tiles + 2):
        body(tile, tile * TILE)
    first_leaf = trunk_tiles + 2

    @pl.loop(first_leaf, length // TILE)
    def _(tile):
        body(None, pl.multiple_of(tile * TILE, TILE))


def attend_head(bias_ref, qkv_ref, out_ref, lse_ref, q_ref, k_ref, v_ref, o_ref, s_ref, triangle):
    sources, _, rows = qkv_ref.shape
    length = sources * rows
    factor = HEAD_DIM ** (-0.5) * LOG2E
    triangle[...] = causal_bias()
    extra = lax.broadcasted_iota(jnp.int32, (16, length), 0)
    v_ref[HEAD_DIM:, :] = jnp.where(extra == 0, 1.0, 0.0).astype(jnp.bfloat16)
    for z in range(sources):
        span = pl.ds(z * rows, rows)
        q_ref[:, span] = qkv_ref[z, :HEAD_DIM]
        k_ref[span, :] = qkv_ref[z, HEAD_DIM : 2 * HEAD_DIM].astype(jnp.float32).T.astype(jnp.bfloat16)
        v_ref[:HEAD_DIM, span] = qkv_ref[z, 2 * HEAD_DIM :]

    def body(tile, start):
        columns = pl.ds(start, TILE)
        parts = tile_parts(tile, start)
        query = q_ref[:, columns]
        peak = None
        for i, part in enumerate(parts):
            scores = dot_nn(k_ref[pl.ds(part[0], TILE), :], query)
            scores = part_scores(scores, part, columns, bias_ref, triangle)
            s_ref[i * TILE : (i + 1) * TILE, :] = scores
            top = jnp.max(scores, 0, keepdims=True)
            peak = top if peak is None else jnp.maximum(peak, top)
        shift = peak * factor
        total = None
        for i, part in enumerate(parts):
            weights = jnp.exp2(s_ref[i * TILE : (i + 1) * TILE, :] * factor - shift)
            term = dot_nn(v_ref[:, pl.ds(part[0], TILE)], weights.astype(jnp.bfloat16))
            total = term if total is None else total + term
        norm = total[HEAD_DIM : HEAD_DIM + 1]
        o_ref[:, columns] = (total[:HEAD_DIM] / norm).astype(jnp.bfloat16)
        lse_ref[:, columns] = shift + jnp.log2(norm)

    for_tiles(length, body)
    for z in range(sources):
        out_ref[z] = o_ref[:, pl.ds(z * rows, rows)]


def attend_back_head(
    bias_ref, cos_ref, sin_ref, qkv_ref, out_ref, lse_ref, grad_ref, back_ref,
    qt_ref, kt_ref, dt_ref, q_ref, k_ref, v_ref, d_ref, delta_ref, dq_ref, dk_ref, dv_ref, triangle,
):
    sources, _, rows = qkv_ref.shape
    length = sources * rows
    scaling = HEAD_DIM ** (-0.5)
    factor = scaling * LOG2E
    triangle[...] = causal_bias()

    def turned(values):
        return values.astype(jnp.float32).T.astype(jnp.bfloat16)

    for z in range(sources):
        span = pl.ds(z * rows, rows)
        query, key, value = (qkv_ref[z, i * HEAD_DIM : (i + 1) * HEAD_DIM] for i in range(3))
        grad = grad_ref[z]
        qt_ref[:, span] = query
        kt_ref[:, span] = key
        dt_ref[:, span] = grad
        q_ref[span, :] = turned(query)
        k_ref[span, :] = turned(key)
        v_ref[span, :] = turned(value)
        d_ref[span, :] = turned(grad)
        delta_ref[:, span] = jnp.sum(
            grad.astype(jnp.float32) * out_ref[z].astype(jnp.float32), 0, keepdims=True
        )
    dk_ref[...] = jnp.zeros_like(dk_ref)
    dv_ref[...] = jnp.zeros_like(dv_ref)

    def body(tile, start):
        columns = pl.ds(start, TILE)
        query_t, grad_t = qt_ref[:, columns], dt_ref[:, columns]
        query, grad = q_ref[columns, :], d_ref[columns, :]
        lse, delta = lse_ref[:, columns], delta_ref[:, columns]
        total = None
        for part in tile_parts(tile, start):
            span = pl.ds(part[0], TILE)
            scores = dot_nn(k_ref[span, :], query_t) * factor - lse
            scores = part_scores(scores, part, columns, bias_ref, triangle)
            weights = jnp.exp2(scores)
            weight_grads = dot_nn(v_ref[span, :], grad_t)
            score_grads = (weights * (weight_grads - delta)).astype(jnp.bfloat16)
            dv_ref[span, :] += dot_nn(weights.astype(jnp.bfloat16), grad)
            dk_ref[span, :] += dot_nn(score_grads, query)
            term = dot_nn(kt_ref[:, span], score_grads)
            total = term if total is None else total + term
        dq_ref[:, columns] = total

    for_tiles(length, body)
    half = HEAD_DIM // 2
    for z in range(sources):
        span = pl.ds(z * rows, rows)
        cosine, sine = cos_ref[:, span], sin_ref[:, span]
        for i, values in enumerate((dq_ref[:, span], dk_ref[span, :].T)):
            values = values * scaling
            first, second = values[:half], values[half:]
            back_ref[z, i * HEAD_DIM : (i + 1) * HEAD_DIM] = jnp.concatenate(
                [first * cosine + second * sine, second * cosine - first * sine], 0
            ).astype(jnp.bfloat16)
        back_ref[z, 2 * HEAD_DIM :] = dv_ref[span, :].T.astype(jnp.bfloat16)


def params(limit):
    return pltpu.CompilerParams(vmem_limit_bytes=limit * MIB)


def cost(flops, moved):
    return pl.CostEstimate(flops=int(flops), bytes_accessed=int(moved), transcendentals=0)


def greet(ring, copies):
    barrier = pltpu.get_barrier_semaphore()
    for target in ring + copies:
        pl.semaphore_signal(barrier, inc=1, device_id=target, device_id_type=pl.DeviceIdType.MESH)
    pl.semaphore_wait(barrier, len(ring) + len(copies))


def ring_partners(owners):
    member = lax.axis_index("expert")
    result = []
    for step in sorted(range(1, owners), key=lambda k: -min(k, owners - k)):
        index = lax.rem(member + step, owners)
        result.append((step, index, {"expert": index}))
    return result


def copy_partners(total):
    place = lax.axis_index("xy") * 2 + lax.axis_index("core")
    result = []
    for step in sorted(range(1, total), key=lambda k: -(k % 8 in (6, 2, 4))):
        index = lax.rem(place + step, total)
        result.append((step, lax.rem(index, 2), {"xy": index // 2, "core": lax.rem(index, 2)}))
    return result


def remote(source, target, send, receive, device):
    return pltpu.make_async_remote_copy(
        src_ref=source, dst_ref=target, send_sem=send, recv_sem=receive,
        device_id=device, device_id_type=pl.DeviceIdType.MESH,
    )


def attend_phase_kernel(
    tokens_ref, gain_ref, query_ref, key_ref, value_ref, cos_ref, sin_ref, bias_ref, gate_ref, up_ref, down_ref,
    attended_ref, lse_ref, heads_ref, outs_ref, gate_full, up_full, down_full,
    normed_ref, qkv_sent, qkv_got, out_sent, out_got, q_ref, k_ref, v_ref, o_ref, s_ref, triangle,
    qkv_send, qkv_recv, out_send, out_recv, weight_send, weight_recv, local_sem,
):
    chunks, owners, _, rows = qkv_sent.shape
    member = lax.axis_index("expert")
    copies = gate_full.shape[0]
    ring, others = ring_partners(owners), copy_partners(copies)
    greet([item[2] for item in ring], [item[2] for item in others])
    weights = ((gate_ref, gate_full), (up_ref, up_full), (down_ref, down_full))
    place = lax.axis_index("xy") * 2 + lax.axis_index("core")
    core = lax.axis_index("core")
    started = []

    inputs = tokens_ref[...].astype(jnp.float32)
    inverse = lax.rsqrt(jnp.mean(inputs * inputs, -1, keepdims=True) + epsilon)
    normed_ref[...] = (inputs * inverse * gain_ref[...]).astype(jnp.bfloat16)
    half = HEAD_DIM // 2
    span_width = owners * HEAD_DIM
    qkv_copies = []
    for j in range(chunks):
        for i, weight in enumerate((query_ref, key_ref, value_ref)):
            turned = dot_nn(normed_ref[...], weight[:, j * span_width : (j + 1) * span_width]).T
            base = i * HEAD_DIM
            for z in range(owners):
                first = turned[z * HEAD_DIM : z * HEAD_DIM + half]
                second = turned[z * HEAD_DIM + half : (z + 1) * HEAD_DIM]
                if i < 2:
                    cosine, sine = cos_ref[...], sin_ref[...]
                    first, second = first * cosine - second * sine, second * cosine + first * sine
                qkv_sent[j, z, base : base + half] = first.astype(jnp.bfloat16)
                qkv_sent[j, z, base + half : base + HEAD_DIM] = second.astype(jnp.bfloat16)
        local = pltpu.make_async_copy(qkv_sent.at[j, member], qkv_got.at[j, member], local_sem.at[j])
        local.start()
        group = []
        for step, index, device in ring:
            copy = remote(
                qkv_sent.at[j, index], qkv_got.at[j, member],
                qkv_send.at[j, step - 1], qkv_recv.at[j, step - 1], device,
            )
            copy.start()
            group.append(copy)
        qkv_copies.append((local, group))
        if j == 0:
            for i, (shard, full) in enumerate(weights):
                local = pltpu.make_async_copy(shard.at[core], full.at[place], weight_send.at[i, 0])
                local.start()
                started.append((local, None))
                for step, other_core, device in others:
                    copy = remote(
                        shard.at[other_core], full.at[place], weight_send.at[i, step], weight_recv.at[i, step], device
                    )
                    copy.start()
                    started.append((None, copy))

    out_copies = []
    kept = []
    for j in range(chunks):
        local, group = qkv_copies[j]
        local.wait()
        for copy in group:
            copy.wait_recv()
        keep = pltpu.make_async_copy(qkv_got.at[j], heads_ref.at[j], local_sem.at[chunks + j])
        keep.start()
        kept.append(keep)
        attend_head(
            bias_ref, qkv_got.at[j], out_sent.at[j], lse_ref.at[j : j + 1], q_ref, k_ref, v_ref, o_ref, s_ref, triangle
        )
        local = pltpu.make_async_copy(out_sent.at[j, member], out_got.at[j, member], local_sem.at[2 * chunks + j])
        local.start()
        keep = pltpu.make_async_copy(out_sent.at[j], outs_ref.at[j], local_sem.at[3 * chunks + j])
        keep.start()
        kept += [local, keep]
        for step, index, device in ring:
            copy = remote(
                out_sent.at[j, index], out_got.at[j, member],
                out_send.at[j, step - 1], out_recv.at[j, step - 1], device,
            )
            copy.start()
            out_copies.append(copy)
    for copy in out_copies:
        copy.wait_recv()
    for copy in kept:
        copy.wait()
    attended_ref[...] = out_got[...]
    for local, group in qkv_copies:
        for copy in group:
            copy.wait_send()
    for copy in out_copies:
        copy.wait_send()
    for local, copy in started:
        if copy is None:
            local.wait()
        else:
            copy.wait()


def attend_phase(tokens, gain, weights, cosine, sine, bias, shards, copies):
    rows, width = tokens.shape
    owners = lax.axis_size("expert")
    length = rows * owners
    chunks = width // HEAD_DIM // owners
    head = (chunks, owners, 3 * HEAD_DIM, rows)
    out = (chunks, owners, HEAD_DIM, rows)
    vmem, hbm = pl.BlockSpec(memory_space=pltpu.VMEM), pl.BlockSpec(memory_space=pl.ANY)
    fulls = [jax.ShapeDtypeStruct((copies, *shard.shape[1:]), shard.dtype) for shard in shards]
    part_total = TRUNK // TILE + 3
    sems = lambda *shape: pltpu.SemaphoreType.DMA(shape)
    return pl.pallas_call(
        attend_phase_kernel,
        in_specs=[vmem] * 8 + [hbm] * 3,
        out_specs=(vmem, vmem, hbm, hbm, hbm, hbm, hbm),
        out_shape=(
            jax.ShapeDtypeStruct(out, jnp.bfloat16),
            jax.ShapeDtypeStruct((8, length), jnp.float32),
            jax.ShapeDtypeStruct(head, jnp.bfloat16),
            jax.ShapeDtypeStruct(out, jnp.bfloat16),
            *fulls,
        ),
        scratch_shapes=[
            pltpu.VMEM((rows, width), jnp.bfloat16),
            pltpu.VMEM(head, jnp.bfloat16),
            pltpu.VMEM(head, jnp.bfloat16),
            pltpu.VMEM(out, jnp.bfloat16),
            pltpu.VMEM(out, jnp.bfloat16),
            pltpu.VMEM((HEAD_DIM, length), jnp.bfloat16),
            pltpu.VMEM((length, HEAD_DIM), jnp.bfloat16),
            pltpu.VMEM((HEAD_DIM + 16, length), jnp.bfloat16),
            pltpu.VMEM((HEAD_DIM, length), jnp.bfloat16),
            pltpu.VMEM((part_total * TILE, TILE), jnp.float32),
            pltpu.VMEM((TILE, TILE), jnp.float32),
            sems(chunks, owners - 1), sems(chunks, owners - 1), sems(chunks, owners - 1), sems(chunks, owners - 1),
            sems(3, copies), sems(3, copies), sems(4 * chunks),
        ],
        compiler_params=pltpu.CompilerParams(vmem_limit_bytes=56 * MIB, collective_id=1, has_side_effects=True),
        cost_estimate=cost(1e10, 5e7),
    )(tokens, gain, *weights, cosine, sine, bias, *shards)


def lane_pick(values, lanes, index):
    return jnp.sum(jnp.where(lanes == index, values, 0.0), -1, keepdims=True)


def middle_kernel(
    tokens_ref, attended_ref, out_weight_ref, gain_ref, mixer_ref, prior_ref, prior_weight_ref,
    routes_ref, codes_ref, resid_ref, small_ref, first_ref, second_ref, hidden_ref,
):
    rows, width = tokens_ref.shape

    @pl.loop(0, rows // SEG)
    def _(step):
        span = pl.ds(pl.multiple_of(step * SEG, SEG), SEG)
        attended = attended_ref[:, span].astype(jnp.float32).T.astype(jnp.bfloat16)
        resid = tokens_ref[span, :].astype(jnp.float32) + dot_nn(attended, out_weight_ref[...])
        inverse = lax.rsqrt(jnp.mean(resid * resid, -1, keepdims=True) + epsilon)
        hidden = (resid * inverse * gain_ref[...]).astype(jnp.bfloat16)
        resid_ref[span, :] = resid
        hidden_ref[span, :] = hidden
        logits = dot_nn(hidden, mixer_ref[...])
        logits = logits + jnp.dot(
            prior_ref[span, :], prior_weight_ref[...], precision=precise, preferred_element_type=jnp.float32
        )
        lanes = lax.broadcasted_iota(jnp.int32, logits.shape, 1)
        routes = routes_ref[span, :]
        columns = []
        pairs = [[lane_pick(logits, lanes, routes[:, c : c + 1]) for c in range(2)]]
        pairs += [[logits[:, NEXP + 2 * m + c : NEXP + 2 * m + c + 1] for c in range(2)] for m in range(2)]
        for one, two in pairs:
            peak = jnp.maximum(one, two)
            one, two = jnp.exp(one - peak), jnp.exp(two - peak)
            columns += [one / (one + two), two / (one + two)]
        columns.append(inverse)
        small = jnp.zeros_like(logits)
        for i, column in enumerate(columns):
            small = jnp.where(lanes == i, column, small)
        small_ref[span, :] = small

    slots = first_ref.shape[0]
    for half, ref in enumerate((first_ref, second_ref)):
        index = lax.broadcasted_iota(jnp.int32, (slots, rows), 0) + half * slots
        chosen = (codes_ref[0:1, :] == index) | (codes_ref[1:2, :] == index)
        ref[...] = dot_nn(chosen.astype(jnp.bfloat16), hidden_ref[...]).astype(jnp.bfloat16)


def middle(tokens, attended, out_weight, gain, mixer, prior, prior_weight, routes, codes_row):
    rows, width = tokens.shape
    slots = rows
    return pl.pallas_call(
        middle_kernel,
        out_shape=(
            jax.ShapeDtypeStruct((rows, width), jnp.float32),
            jax.ShapeDtypeStruct((rows, 128), jnp.float32),
            jax.ShapeDtypeStruct((slots, width), jnp.bfloat16),
            jax.ShapeDtypeStruct((slots, width), jnp.bfloat16),
        ),
        scratch_shapes=[pltpu.VMEM((rows, width), jnp.bfloat16)],
        compiler_params=params(48),
        cost_estimate=cost(4 * rows * width * width + 4 * rows * rows * width, 1e7),
    )(tokens, attended, out_weight, gain, mixer, prior, prior_weight, routes, codes_row)


def plane_partners(owners):
    total = 2 * owners
    place = lax.axis_index("expert") * 2 + lax.axis_index("core")
    result = []
    for step in sorted(range(1, total), key=lambda k: -min(k, total - k)):
        index = lax.rem(place + step, total)
        result.append((step, index, {"expert": index // 2, "core": lax.rem(index, 2)}))
    return result


def expert_phase_kernel(
    xa_ref, xb_ref, small_ref, grad_ref, codes_ref, gate_hbm, up_hbm, down_hbm,
    back_out, dots_out, f_out, gate_grad, up_grad, down_grad,
    gate_ref, up_ref, down_ref, scaled_ref, d_sent, x_got, d_got, back_sent, back_got, dots_sent, dots_got,
    f_sum, back_sum, hid_ref, one_ref, two_ref, x_turned, d_turned, stage, stage_down,
    x_send, x_recv, d_send, d_recv, back_send, back_recv, dots_send, dots_recv, local_sem, stage_sem,
):
    experts, slots, width = x_got.shape[1:]
    rows = experts * slots
    units = gate_ref.shape[1]
    owners = experts // 2
    place = lax.axis_index("expert") * 2 + lax.axis_index("core")
    partners = plane_partners(owners)
    greet([item[2] for item in partners], [])
    loads = [
        pltpu.make_async_copy(source, target, local_sem.at[i])
        for i, (source, target) in enumerate(((gate_hbm, gate_ref), (up_hbm, up_ref), (down_hbm, down_ref)))
    ]
    for load in loads:
        load.start()

    def send(source, target, sends, receives, half, locals_at):
        copies = []
        local = pltpu.make_async_copy(source(place), target.at[half, place], local_sem.at[locals_at + half])
        local.start()
        for step, index, device in partners:
            copy = remote(source(index), target.at[half, place], sends.at[half, step], receives.at[half, step], device)
            copy.start()
            copies.append(copy)
        return local, copies

    def arrive(group):
        group[0].wait()
        for copy in group[1]:
            copy.wait_recv()

    x_refs = (xa_ref, xb_ref)
    x_groups = [send(lambda e, ref=ref: ref.at[e], x_got, x_send, x_recv, h, 3) for h, ref in enumerate(x_refs)]
    for c in range(2):
        scaled_ref[c * rows : (c + 1) * rows, :] = (
            small_ref[:, c : c + 1] * grad_ref[...].astype(jnp.float32)
        ).astype(jnp.bfloat16)
    d_groups = []
    for half in range(2):
        index = lax.broadcasted_iota(jnp.int32, (rows, rows), 0) + half * rows
        chosen = jnp.concatenate([(codes_ref[c : c + 1, :] == index).astype(jnp.bfloat16) for c in range(2)], 1)
        d_sent[half] = dot_nn(chosen, scaled_ref[...]).astype(jnp.bfloat16).reshape(experts, slots, width)
        d_groups.append(send(lambda e, half=half: d_sent.at[half, e], d_got, d_send, d_recv, half, 5))
    for load in loads:
        load.wait()

    part = 512
    tile = rows // 2

    def forward(half):
        x = x_got[half].reshape(rows, width)
        f_sum[...] = jnp.zeros_like(f_sum)
        x_turned[:, half * rows : (half + 1) * rows] = x.astype(jnp.float32).T.astype(jnp.bfloat16)

        @pl.loop(0, units // part)
        def _(step):
            columns = pl.ds(pl.multiple_of(step * part, part), part)
            for r in range(2):
                near = slice(r * tile, (r + 1) * tile)
                far = pl.ds(half * rows + r * tile, tile)
                gate_pre = dot_nn(x[near], gate_ref[:, columns])
                up_pre = dot_nn(x[near], up_ref[:, columns])
                sigmoid = 1.0 / (1.0 + jnp.exp(-gate_pre))
                active = gate_pre * sigmoid
                hid = (active * up_pre).astype(jnp.bfloat16)
                hid_ref[far, columns] = hid
                one_ref[far, columns] = (up_pre * (sigmoid + active * (1.0 - sigmoid))).astype(jnp.bfloat16)
                two_ref[far, columns] = active.astype(jnp.bfloat16)
                f_sum[near, :] += dot_nn(hid, down_ref[columns, :])

        f_out[half] = f_sum[...].astype(jnp.bfloat16).reshape(experts, slots, width)

    def backward(half):
        d = d_got[half].reshape(rows, width)
        back_sum[...] = jnp.zeros_like(back_sum)
        d_turned[:, half * rows : (half + 1) * rows] = d.astype(jnp.float32).T.astype(jnp.bfloat16)

        @pl.loop(0, units // part)
        def _(step):
            columns = pl.ds(pl.multiple_of(step * part, part), part)
            for r in range(2):
                near = slice(r * tile, (r + 1) * tile)
                far = pl.ds(half * rows + r * tile, tile)
                mid = dot_nt(d[near], down_ref[columns, :])
                dg = (mid * one_ref[far, columns].astype(jnp.float32)).astype(jnp.bfloat16)
                du = (mid * two_ref[far, columns].astype(jnp.float32)).astype(jnp.bfloat16)
                one_ref[far, columns] = dg
                two_ref[far, columns] = du
                back_sum[near, :] += dot_nt(dg, gate_ref[:, columns]) + dot_nt(du, up_ref[:, columns])

        back_sent[half] = back_sum[...].astype(jnp.bfloat16).reshape(experts, slots, width)

    def dots(half):
        ones = jnp.ones((8, width), jnp.float32)
        for e in range(experts):
            product = f_out[half, e].astype(jnp.float32) * d_got[half, e].astype(jnp.float32)
            total = lax.dot_general(
                ones, product, (((1,), (1,)), ((), ())), precision=precise, preferred_element_type=jnp.float32
            )
            dots_sent[half, e] = jnp.concatenate([total, jnp.zeros((8, 128 - slots), jnp.float32)], 1)

    for half in range(2):
        arrive(x_groups[half])
        forward(half)
    back_groups, dots_groups = [], []
    for half in range(2):
        arrive(d_groups[half])
        backward(half)
        back_groups.append(send(lambda e, half=half: back_sent.at[half, e], back_got, back_send, back_recv, half, 7))
        dots(half)
        dots_groups.append(send(lambda e, half=half: dots_sent.at[half, e], dots_got, dots_send, dots_recv, half, 9))

    piece = 256
    steps = units // piece

    def stores(step, slot):
        columns = pl.ds(pl.multiple_of(step * piece, piece), piece)
        return [
            pltpu.make_async_copy(stage.at[0, slot], gate_grad.at[:, columns], stage_sem.at[0, slot]),
            pltpu.make_async_copy(stage.at[1, slot], up_grad.at[:, columns], stage_sem.at[1, slot]),
            pltpu.make_async_copy(stage_down.at[slot], down_grad.at[columns, :], stage_sem.at[2, slot]),
        ]

    @pl.loop(0, steps // 2)
    def _(pair):
        for slot in range(2):
            step = pair * 2 + slot
            columns = pl.ds(pl.multiple_of(step * piece, piece), piece)

            @pl.when(pair > 0)
            def _():
                for store in stores(step, slot):
                    store.wait()

            stage[0, slot] = dot_nn(x_turned[...], one_ref[:, columns]).astype(jnp.bfloat16)
            stage[1, slot] = dot_nn(x_turned[...], two_ref[:, columns]).astype(jnp.bfloat16)
            stage_down[slot] = dot_nn(d_turned[...], hid_ref[:, columns]).T.astype(jnp.bfloat16)
            for store in stores(step, slot):
                store.start()

    for slot in range(2):
        for store in stores(steps - 2 + slot, slot):
            store.wait()
    for group in back_groups + dots_groups:
        arrive(group)
    back_out[...] = back_got[...]
    dots_out[...] = dots_got[...]
    for group in x_groups + d_groups + back_groups + dots_groups:
        for copy in group[1]:
            copy.wait_send()


def expert_phase(x_parts, small, grad, codes_row, gate, up, down):
    rows, width = grad.shape
    units = gate.shape[1]
    slots = rows // NFFN
    both = (2, NFFN, slots, width)
    dots = (2, NFFN, 8, 128)
    vmem, hbm = pl.BlockSpec(memory_space=pltpu.VMEM), pl.BlockSpec(memory_space=pl.ANY)
    sems = pltpu.SemaphoreType.DMA((2, NFFN))
    wide = pltpu.VMEM((rows, width), jnp.float32)
    mids = pltpu.VMEM((2 * rows, units), jnp.bfloat16)
    turned = pltpu.VMEM((width, 2 * rows), jnp.bfloat16)
    moved = pltpu.VMEM(both, jnp.bfloat16)
    return pl.pallas_call(
        expert_phase_kernel,
        in_specs=[vmem] * 5 + [hbm] * 3,
        out_specs=(vmem, vmem, vmem, hbm, hbm, hbm),
        out_shape=(
            jax.ShapeDtypeStruct(both, jnp.bfloat16),
            jax.ShapeDtypeStruct(dots, jnp.float32),
            jax.ShapeDtypeStruct(both, jnp.bfloat16),
            jax.ShapeDtypeStruct(gate.shape, jnp.bfloat16),
            jax.ShapeDtypeStruct(up.shape, jnp.bfloat16),
            jax.ShapeDtypeStruct(down.shape, jnp.bfloat16),
        ),
        scratch_shapes=[
            pltpu.VMEM(gate.shape, jnp.bfloat16),
            pltpu.VMEM(up.shape, jnp.bfloat16),
            pltpu.VMEM(down.shape, jnp.bfloat16),
            pltpu.VMEM((2 * rows, width), jnp.bfloat16),
            moved, moved, moved, moved, moved,
            pltpu.VMEM(dots, jnp.float32),
            pltpu.VMEM(dots, jnp.float32),
            wide, wide, mids, mids, mids, turned, turned,
            pltpu.VMEM((2, 2, width, 256), jnp.bfloat16),
            pltpu.VMEM((2, 256, width), jnp.bfloat16),
            *(sems,) * 8,
            pltpu.SemaphoreType.DMA((11,)),
            pltpu.SemaphoreType.DMA((3, 2)),
        ],
        compiler_params=pltpu.CompilerParams(vmem_limit_bytes=63 * MIB, collective_id=2, has_side_effects=True),
        cost_estimate=cost(36 * rows * width * units, 5e7),
    )(*(part.reshape(NFFN, slots, width) for part in x_parts), small, grad, codes_row, gate, up, down)


def split_dot(dot, left, right):
    high = left.astype(jnp.bfloat16)
    low = (left - high.astype(jnp.float32)).astype(jnp.bfloat16)
    return dot(high, right) + dot(low, right)


def turn_kernel(
    resid_ref, small_ref, grad_ref, prior_ref, routes_ref, codes_ref, ra_ref, rb_ref, dots_ref, vector_ref,
    gain_ref, mixer_ref, prior_turned_ref, out_weight_ref, attended_ref,
    resid_grad_ref, grads_ref, out_grad_ref, prior_grad_ref, back_ref, sums_ref, prior_sums_ref, extra_ref, *, owners,
):
    rows, width = resid_ref.shape
    slots = 2 * ra_ref.shape[0]
    sums_ref[...] = jnp.zeros_like(sums_ref)
    prior_sums_ref[...] = jnp.zeros_like(prior_sums_ref)

    @pl.loop(0, rows // SEG)
    def _(step):
        span = pl.ds(pl.multiple_of(step * SEG, SEG), SEG)
        small = small_ref[span, :]
        routes, codes = routes_ref[span, :], codes_ref[span, :]
        gates = [small[:, c : c + 1] for c in range(2)]
        mixing = [[small[:, 2 + 2 * m + c : 3 + 2 * m + c] for c in range(2)] for m in range(2)]
        inverse = small[:, 6:7]
        normed = resid_ref[span, :] * inverse
        hidden = normed * gain_ref[...]
        hidden_b = hidden.astype(jnp.bfloat16)
        grad_b = grad_ref[span, :]
        grad = grad_b.astype(jnp.float32)
        index = lax.broadcasted_iota(jnp.int32, (SEG, slots), 1)
        hits = [codes[:, c : c + 1] == index for c in range(2)]
        dots = dots_ref[...]
        terms = [jnp.sum(jnp.where(hit, dots, 0.0), -1, keepdims=True) for hit in hits]
        chosen = (hits[0] | hits[1]).astype(jnp.bfloat16)
        half = slots // 2
        routed = dot_nn(chosen[:, :half], ra_ref[...]) + dot_nn(chosen[:, half:], rb_ref[...])
        along = jnp.sum(grad * hidden, -1, keepdims=True)
        across = [jnp.sum(grad * vector_ref[m : m + 1, :], -1, keepdims=True) for m in range(2)]
        to_copy = 0.0
        to_mix = [0.0, 0.0]
        for c in range(2):
            route = routes[:, c : c + 1]
            copied = jnp.where(route == NFFN + 1, gates[c], 0.0)
            to_copy = to_copy + copied
            terms[c] = terms[c] + copied * along
            for m in range(2):
                mixed = jnp.where(route == NFFN + 2 + m, gates[c], 0.0)
                to_mix[m] = to_mix[m] + mixed
                terms[c] = terms[c] + mixed * (mixing[m][0] * along + mixing[m][1] * across[m])
        both = terms[0] + terms[1]
        lanes = lax.broadcasted_iota(jnp.int32, (SEG, 128), 1)
        logit_grads = jnp.zeros((SEG, 128), jnp.float32)
        for c in range(2):
            logit_grads = jnp.where(lanes == routes[:, c : c + 1], terms[c] - gates[c] * both, logit_grads)
        scores = logit_grads
        direct = to_copy
        for m in range(2):
            pair = (to_mix[m] * along, to_mix[m] * across[m])
            mean = mixing[m][0] * pair[0] + mixing[m][1] * pair[1]
            for c in range(2):
                scores = jnp.where(lanes == NEXP + 2 * m + c, mixing[m][c] * (pair[c] - mean), scores)
            direct = direct + mixing[m][0] * to_mix[m]
        prior_grad_ref[span, :] = jnp.dot(
            logit_grads, prior_turned_ref[...], precision=precise, preferred_element_type=jnp.float32
        )[:, : prior_grad_ref.shape[1]]
        hidden_grads = split_dot(dot_nn, scores, mixer_ref[...]) + direct * grad + routed
        scaled = hidden_grads * gain_ref[...]
        resid_grads = inverse * (scaled - normed * jnp.mean(scaled * normed, -1, keepdims=True)) + grad
        resid_grad_ref[span, :] = resid_grads
        back_ref[span, :] = resid_grads.astype(jnp.bfloat16)
        weights = jnp.zeros((SEG, 128), jnp.float32)
        for m in range(2):
            weights = jnp.where(lanes == m, mixing[m][1] * to_mix[m], weights)
        sums_ref[0:16, :] += split_dot(dot_nn, scores.T[0:16], hidden_b)
        sums_ref[16:24, :] += split_dot(dot_nn, weights.T[0:8], grad_b)
        sums_ref[24:32, :] += jnp.sum((hidden_grads * normed).reshape(SEG // 8, 8, width), 0)
        prior_sums_ref[...] += jnp.dot(
            prior_ref[span, :].T,
            jnp.concatenate([logit_grads[:, 96:], logit_grads[:, :96]], 1),
            precision=precise,
            preferred_element_type=jnp.float32,
        )

    sums_ref[24:25, :] = jnp.sum(sums_ref[24:32, :], 0, keepdims=True)
    extra_ref[...] = jnp.concatenate([sums_ref[...], jnp.zeros((96, width), jnp.float32)], 0).T
    kept = NEXP // owners
    for z in range(owners):
        extra_ref[pl.ds(z * (width // owners), kept), :] += prior_sums_ref[z * kept : (z + 1) * kept, :]
    out_grad_ref[:, width : width + 128] = extra_ref[...].astype(jnp.bfloat16)
    out_grad_ref[:, width + 128 :] = jnp.zeros((width, 128), jnp.bfloat16)
    back = back_ref[...]
    grads_ref[...] = dot_nt(out_weight_ref[...], back).astype(jnp.bfloat16)
    out_grad_ref[:, :width] = dot_nn(attended_ref[...], back).astype(jnp.bfloat16)


def turn(resid, small, grad, prior, routes, codes, returned, dots, vector, gain, mixer_turned, prior_turned, out_weight, attended):
    rows, width = resid.shape
    return pl.pallas_call(
        functools.partial(turn_kernel, owners=lax.axis_size("expert")),
        out_shape=(
            jax.ShapeDtypeStruct((rows, width), jnp.float32),
            jax.ShapeDtypeStruct((width, rows), jnp.bfloat16),
            jax.ShapeDtypeStruct((width, width + 256), jnp.bfloat16),
            jax.ShapeDtypeStruct(prior.shape, jnp.float32),
        ),
        scratch_shapes=[
            pltpu.VMEM((rows, width), jnp.bfloat16),
            pltpu.VMEM((32, width), jnp.float32),
            pltpu.VMEM((prior.shape[1], 128), jnp.float32),
            pltpu.VMEM((width, 128), jnp.float32),
        ],
        compiler_params=params(56),
        cost_estimate=cost(4 * rows * width * width + 4 * rows * rows * width, 1.5e7),
    )(resid, small, grad, prior, routes, codes, *returned, dots, vector, gain, mixer_turned, prior_turned, out_weight, attended)


def combine_kernel(resid_ref, small_ref, routes_ref, codes_ref, fa_ref, fb_ref, vector_ref, gain_ref, out_ref):
    rows, width = resid_ref.shape
    half = fa_ref.shape[0]

    @pl.loop(0, rows // SEG)
    def _(step):
        span = pl.ds(pl.multiple_of(step * SEG, SEG), SEG)
        small = small_ref[span, :]
        routes, codes = routes_ref[span, :], codes_ref[span, :]
        resid = resid_ref[span, :]
        hidden = resid * small[:, 6:7] * gain_ref[...]
        index = lax.broadcasted_iota(jnp.int32, (SEG, 2 * half), 1)
        total = resid
        direct = 0.0
        for c in range(2):
            gate, route = small[:, c : c + 1], routes[:, c : c + 1]
            chosen = (codes[:, c : c + 1] == index).astype(jnp.bfloat16)
            routed = dot_nn(chosen[:, :half], fa_ref[...]) + dot_nn(chosen[:, half:], fb_ref[...])
            total = total + gate * routed
            direct = direct + jnp.where(route == NFFN + 1, gate, 0.0)
            for m in range(2):
                mixed = jnp.where(route == NFFN + 2 + m, gate, 0.0)
                direct = direct + mixed * small[:, 2 + 2 * m : 3 + 2 * m]
                total = total + mixed * small[:, 3 + 2 * m : 4 + 2 * m] * vector_ref[m : m + 1, :]
        out_ref[span, :] = (total + direct * hidden).astype(jnp.bfloat16)


def combine(resid, small, routes, codes, outs, vector, gain):
    rows, width = resid.shape
    return pl.pallas_call(
        combine_kernel,
        out_shape=jax.ShapeDtypeStruct((rows, width), jnp.bfloat16),
        compiler_params=params(48),
        cost_estimate=cost(8 * rows * rows * width, 8e6),
    )(resid, small, routes, codes, *outs, vector, gain)


def attend_back_phase_kernel(
    grads_ref, heads_ref, outs_ref, lse_ref, bias_ref, cos_ref, sin_ref, tokens_ref, gain_ref,
    query_ref, key_ref, value_ref, resid_grad_ref, out_part_ref, f_ref, gate_ref, up_ref, down_ref,
    tokens_grad_ref, f_got, gate_got, up_got, down_got, *rest, reduce,
):
    if reduce:
        total_ref, *rest = rest
    else:
        parts_ref, *rest = rest
    (
        d_got, back_sent, back_got, normed_turned, turned_ref, back_sum,
        qt_ref, kt_ref, dt_ref, q_ref, k_ref, v_ref, d_ref, delta_ref, dq_ref, dk_ref, dv_ref, triangle,
        d_send, d_recv, back_send, back_recv, weight_send, weight_recv, f_send, f_recv, local_sem, *rest,
    ) = rest
    if reduce:
        (
            parts_ref, half_got, half_sum, chip_got, chip_sum, ring_got, ring_sum, all_got,
            half_send, half_recv, chip_send, chip_recv, ring_send, ring_recv, all_send, all_recv,
        ) = rest
    chunks, owners, _, rows = grads_ref.shape
    width = tokens_ref.shape[1]
    copies = gate_ref.shape[0]
    member, xy, core = (lax.axis_index(name) for name in ("expert", "xy", "core"))
    place = xy * 2 + core
    ring, others, planes = ring_partners(owners), copy_partners(copies), plane_partners(owners)
    greet([item[2] for item in planes], [item[2] for item in others])

    d_groups = []
    for j in range(chunks):
        local = pltpu.make_async_copy(grads_ref.at[j, member], d_got.at[j, member], local_sem.at[j])
        local.start()
        group = []
        for step, index, device in ring:
            copy = remote(
                grads_ref.at[j, index], d_got.at[j, member], d_send.at[j, step - 1], d_recv.at[j, step - 1], device
            )
            copy.start()
            group.append(copy)
        d_groups.append((local, group))

    inputs = tokens_ref[...].astype(jnp.float32)
    inverse = lax.rsqrt(jnp.mean(inputs * inputs, -1, keepdims=True) + epsilon)
    normed_turned[...] = (inputs * inverse * gain_ref[...]).T.astype(jnp.bfloat16)
    share = width // owners
    part_shape = (owners, share // 48, 48)

    def fill(p, values, begin, size):
        if reduce:
            parts_ref[p, :, :, :, begin : begin + size] = values.reshape(*part_shape, size)
        else:
            parts_ref[p, :, begin : begin + size] = values

    fill(0, out_part_ref[...], 0, out_part_ref.shape[1])
    columns_total = out_part_ref.shape[1]
    for p in range(1, chunks + 1):
        fill(p, jnp.zeros((width, columns_total - width), jnp.bfloat16), width, columns_total - width)

    stages = {}

    def over_cores(p):
        half = columns_total // 2
        away = pl.ds(pl.multiple_of((1 - core) * half, half), half)
        copy = remote(
            parts_ref.at[p, :, :, :, away], half_got.at[p], half_send.at[p], half_recv.at[p], {"core": 1 - core}
        )
        copy.start()
        stages[p, 0] = [copy]

    def over_chips(p):
        for copy in stages[p, 0]:
            copy.wait_recv()
        half = columns_total // 2
        mine = pl.ds(pl.multiple_of(core * half, half), half)
        half_sum[p] = (
            parts_ref[p, :, :, :, mine].astype(jnp.float32) + half_got[p].astype(jnp.float32)
        ).astype(jnp.bfloat16)
        stages[p, 1] = []
        for step in (3, 1, 2):
            index = lax.rem(xy + step, 4)
            copy = remote(
                half_sum.at[p, :, index], chip_got.at[p, xy], chip_send.at[p, step - 1], chip_recv.at[p, step - 1],
                {"xy": index},
            )
            copy.start()
            stages[p, 1].append(copy)
        chip_got[p, xy] = half_sum[p, :, xy]

    def over_owners(p):
        for copy in stages[p, 1]:
            copy.wait_recv()
        chip_sum[p] = jnp.sum(chip_got[p].astype(jnp.float32), 0).astype(jnp.bfloat16)
        stages[p, 2] = []
        for step, index, device in ring:
            copy = remote(
                chip_sum.at[p, index], ring_got.at[p, member], ring_send.at[p, step - 1], ring_recv.at[p, step - 1],
                device,
            )
            copy.start()
            stages[p, 2].append(copy)
        ring_got[p, member] = chip_sum[p, member]

    def to_copies(p):
        for copy in stages[p, 2]:
            copy.wait_recv()
        half = columns_total // 2
        mine = pl.ds(pl.multiple_of(core * half, half), half)
        ring_sum[p] = jnp.sum(ring_got[p].astype(jnp.float32), 0).astype(jnp.bfloat16)
        stages[p, 3] = []
        for step, _, device in others:
            copy = remote(
                ring_sum.at[p], all_got.at[p, xy, :, mine], all_send.at[p, step - 1], all_recv.at[p, step - 1], device
            )
            copy.start()
            stages[p, 3].append(copy)
        all_got[p, xy, :, mine] = ring_sum[p]

    def advance(*pairs):
        if reduce:
            for stage, p in pairs:
                (over_cores, over_chips, over_owners, to_copies)[stage](p)

    advance((0, 0))

    background = []
    for i, (source, target) in enumerate(((gate_ref, gate_got), (up_ref, up_got), (down_ref, down_got))):
        local = pltpu.make_async_copy(source.at[place], target.at[place], weight_send.at[i, 0])
        local.start()
        background.append((local, None))
        for step, index, device in others:
            copy = remote(
                source.at[2 * device["xy"] + device["core"]], target.at[place],
                weight_send.at[i, step], weight_recv.at[i, step], device,
            )
            copy.start()
            background.append((None, copy))

    def head(j):
        local, group = d_groups[j]
        local.wait()
        for copy in group:
            copy.wait_recv()
        attend_back_head(
            bias_ref, cos_ref, sin_ref, heads_ref.at[j], outs_ref.at[j], lse_ref.at[j : j + 1], d_got.at[j],
            back_sent.at[j], qt_ref, kt_ref, dt_ref, q_ref, k_ref, v_ref, d_ref, delta_ref, dq_ref, dk_ref, dv_ref,
            triangle,
        )
        local = pltpu.make_async_copy(back_sent.at[j, member], back_got.at[j, member], local_sem.at[chunks + j])
        local.start()
        group = []
        for step, index, device in ring:
            copy = remote(
                back_sent.at[j, index], back_got.at[j, member],
                back_send.at[j, step - 1], back_recv.at[j, step - 1], device,
            )
            copy.start()
            group.append(copy)
        return local, group

    span_width = owners * HEAD_DIM

    def weights_of(j, group):
        local, copies_in = group
        local.wait()
        for copy in copies_in:
            copy.wait_recv()
        for i in range(3):
            for z in range(owners):
                row = i * span_width + z * HEAD_DIM
                turned_ref[row : row + HEAD_DIM, :] = back_got[j, z, i * HEAD_DIM : (i + 1) * HEAD_DIM]
        total = None
        for i, weight in enumerate((query_ref, key_ref, value_ref)):
            term = dot_nn(weight[:, j * span_width : (j + 1) * span_width], turned_ref[i * span_width : (i + 1) * span_width, :])
            total = term if total is None else total + term
        back_sum[...] = total if j == 0 else back_sum[...] + total
        fill(j + 1, dot_nt(normed_turned[...], turned_ref[...]).astype(jnp.bfloat16), 0, 3 * span_width)

    groups = [head(0)]
    advance((1, 0))
    groups.append(head(1))
    weights_of(0, groups[0])
    advance((2, 0), (0, 1))
    groups.append(head(2))
    for half in range(2):
        expert = member * 2 + core
        local = pltpu.make_async_copy(f_ref.at[half, expert], f_got.at[half, expert], f_send.at[half, 0])
        local.start()
        background.append((local, None))
        for step, index, device in planes:
            copy = remote(
                f_ref.at[half, index], f_got.at[half, expert], f_send.at[half, step], f_recv.at[half, step], device
            )
            copy.start()
            background.append((None, copy))
    advance((3, 0), (1, 1))
    weights_of(1, groups[1])
    advance((0, 2), (2, 1), (1, 2))
    weights_of(2, groups[2])
    normed = inputs * inverse
    first_grads = back_sum[...].T
    summed = jnp.sum((first_grads * normed).reshape(rows // 8, 8, width), 0)
    column = jnp.sum(summed.T, -1, keepdims=True)
    fill(chunks, jnp.broadcast_to(column, (width, 128)).astype(jnp.bfloat16), width, 128)
    advance((0, 3), (3, 1), (2, 2))
    scaled = first_grads * gain_ref[...]
    tokens_grad_ref[...] = (
        inverse * (scaled - normed * jnp.mean(scaled * normed, -1, keepdims=True)) + resid_grad_ref[...]
    )
    advance((1, 3), (3, 2), (2, 3), (3, 3))
    if reduce:
        for p in range(chunks + 1):
            for copy in stages[p, 3]:
                copy.wait_recv()
            total_ref[p] = all_got[p].astype(jnp.float32).reshape(share, columns_total)
            for stage in range(4):
                for copy in stages[p, stage]:
                    copy.wait_send()
    for local, group in d_groups + groups:
        for copy in group:
            copy.wait_send()
    for local, copy in background:
        if copy is None:
            local.wait()
        else:
            copy.wait()


def attend_back_phase(
    grads, heads, outs, lse, bias, cosine, sine, tokens, gain, weights, resid_grads, out_part, fs, expert_grads, copies
):
    chunks, owners, _, rows = grads.shape
    width = tokens.shape[1]
    length = owners * rows
    head = (chunks, owners, 3 * HEAD_DIM, rows)
    columns = out_part.shape[1]
    share = width // owners
    total = chunks + 1
    reduce = copies == 8 and share == 4 * 48
    vmem, hbm = pl.BlockSpec(memory_space=pltpu.VMEM), pl.BlockSpec(memory_space=pl.ANY)
    pieces = [item.reshape(copies, -1, item.shape[-1]) for item in expert_grads]
    turned = pltpu.VMEM((HEAD_DIM, length), jnp.bfloat16)
    plain = pltpu.VMEM((length, HEAD_DIM), jnp.bfloat16)
    wide = pltpu.VMEM((length, HEAD_DIM), jnp.float32)
    sems = lambda *shape: pltpu.SemaphoreType.DMA(shape)
    scratch = [
        pltpu.VMEM(grads.shape, jnp.bfloat16),
        pltpu.VMEM(head, jnp.bfloat16),
        pltpu.VMEM(head, jnp.bfloat16),
        pltpu.VMEM((width, rows), jnp.bfloat16),
        pltpu.VMEM((3 * owners * HEAD_DIM, rows), jnp.bfloat16),
        pltpu.VMEM((width, rows), jnp.float32),
        turned, turned, turned, plain, plain, plain, plain,
        pltpu.VMEM((1, length), jnp.float32),
        pltpu.VMEM((HEAD_DIM, length), jnp.float32),
        wide, wide,
        pltpu.VMEM((TILE, TILE), jnp.float32),
        *(sems(chunks, owners - 1),) * 4,
        sems(3, copies), sems(3, copies), sems(2, 2 * owners), sems(2, 2 * owners), sems(2 * chunks),
    ]
    if reduce:
        half = columns // 2
        low = lambda *shape: pltpu.VMEM(shape, jnp.bfloat16)
        scratch += [
            low(total, owners, 4, 48, columns),
            low(total, owners, 4, 48, half),
            low(total, owners, 4, 48, half),
            low(total, 4, owners, 48, half),
            low(total, owners, 48, half),
            low(total, owners, 48, half),
            low(total, 48, half),
            low(total, 4, 48, columns),
            sems(total), sems(total), sems(total, 3), sems(total, 3),
            sems(total, owners - 1), sems(total, owners - 1), sems(total, copies - 1), sems(total, copies - 1),
        ]
        last_spec, last_shape = vmem, jax.ShapeDtypeStruct((total, share, columns), jnp.float32)
    else:
        last_spec, last_shape = vmem, jax.ShapeDtypeStruct((total, width, columns), jnp.bfloat16)
    *result, totals = pl.pallas_call(
        functools.partial(attend_back_phase_kernel, reduce=reduce),
        in_specs=[vmem] * 14 + [hbm] * 4,
        out_specs=(vmem, hbm, hbm, hbm, hbm, last_spec),
        out_shape=(
            jax.ShapeDtypeStruct((rows, width), jnp.float32),
            jax.ShapeDtypeStruct(fs.shape, fs.dtype),
            *(jax.ShapeDtypeStruct(piece.shape, piece.dtype) for piece in pieces),
            last_shape,
        ),
        scratch_shapes=scratch,
        compiler_params=pltpu.CompilerParams(vmem_limit_bytes=63 * MIB, collective_id=3, has_side_effects=True),
        cost_estimate=cost(2e10, 5e7),
    )(grads, heads, outs, lse, bias, cosine, sine, tokens, gain, *weights, resid_grads, out_part, fs, *pieces)
    if not reduce:
        totals = lax.psum_scatter(totals, "expert", scatter_dimension=1, tiled=True)
        totals = lax.psum(totals, ("xy", "core")).astype(jnp.float32)
    return (*result, totals)


def lineage_of(parent_row):
    segment_total = parent_row.shape[0] + 1
    indices = jnp.arange(segment_total, dtype=jnp.int32)
    parent_all = jnp.concatenate([jnp.full((1,), -1, jnp.int32), parent_row])
    reach = (parent_all[:, None] == indices[None, :]) | (indices[:, None] == indices[None, :])
    for repeat in range(3):
        reach = jnp.any(reach[:, :, None] & reach[None, :, :], 1)
    return reach


def slot_codes(routes, half_slots):
    rows = routes.shape[0]
    experts = jnp.arange(NFFN, dtype=jnp.int32)
    matches = routes[:, :, None] == experts
    per_row = jnp.sum(matches.astype(jnp.float32), 1)
    earlier = jnp.arange(rows)[:, None] > jnp.arange(rows)[None, :]
    before = jnp.dot(
        earlier.astype(jnp.bfloat16), per_row.astype(jnp.bfloat16), preferred_element_type=jnp.float32
    )
    rank = jnp.sum(jnp.where(matches, before[:, None, :], 0.0), -1).astype(jnp.int32)
    late = (rank >= half_slots).astype(jnp.int32)
    code = late * (NFFN * half_slots) + routes * half_slots + rank - late * half_slots
    return jnp.where(routes < NFFN, code, 4 * NFFN * half_slots)


def per_device(
    tokens, prior_logits, routes, parents, cotangent, query_weight, key_weight, value_weight, out_weight,
    attention_gain, expert_gain, router_weight, prior_weight, constant_weight, constant_vector,
    gate_weight, up_weight, down_weight,
):
    owners = lax.axis_size("expert")
    member = lax.axis_index("expert")
    core = lax.axis_index("core")
    tokens, prior, routes, grad = tokens[0], prior_logits[0], routes[0], cotangent[0]
    rows, width = tokens.shape
    copies = lax.axis_size("xy") * lax.axis_size("core")
    length = rows * owners
    chunks = width // HEAD_DIM // owners
    half_slots = rows // 8

    def own_sum(got):
        return jnp.sum(got.reshape(copies // 2, 2, *got.shape[1:]).astype(jnp.float32), 0)

    lineage = lineage_of(parents[0])
    segments = lineage.shape[0]
    lengths = jnp.where(jnp.arange(segments) == 0, TRUNK, SEG)
    begins = jnp.where(jnp.arange(segments) == 0, 0, TRUNK + (jnp.arange(segments) - 1) * SEG)
    shifts = jnp.sum(jnp.where(lineage, lengths[None, :], 0), 1) - lengths - begins
    ids = jnp.arange(length, dtype=jnp.int32)
    segment = jnp.where(ids < TRUNK, 0, 1 + (ids - TRUNK) // SEG)
    own = segment[None, :] == jnp.arange(segments)[:, None]
    places = (jnp.sum(jnp.where(own, shifts[:, None], 0), 0) + ids).astype(jnp.float32)
    reach = jnp.any(own[:, None, :] & lineage[:, :, None], 0)
    bias = jnp.where(reach, 0.0, masked_score).astype(jnp.float32)
    bias = jnp.concatenate([bias, jnp.zeros((16 - segments, length), jnp.float32)], 0)
    frequency = 10000.0 ** (-(jnp.arange(HEAD_DIM // 2, dtype=jnp.float32) * 2.0 / HEAD_DIM))
    angles = frequency[:, None] * places[None, :]
    cosine, sine = jnp.cos(angles), jnp.sin(angles)
    own_cosine, own_sine = (lax.dynamic_slice_in_dim(table, member * rows, rows, 1) for table in (cosine, sine))

    attention_row, expert_row = attention_gain[None], expert_gain[None]
    qkv_weights = (query_weight, key_weight, value_weight)
    attended, logs, heads, outs, gate, up, down = attend_phase(
        tokens, attention_row, qkv_weights, own_cosine, own_sine, bias, (gate_weight, up_weight, down_weight), copies
    )
    attended = attended.reshape(width, rows)
    gate, up, down = (full.reshape(-1, full.shape[-1]) for full in (gate, up, down))
    codes = slot_codes(routes, half_slots)
    codes_row = codes.T

    mixer = jnp.concatenate(
        [router_weight, constant_weight, jnp.zeros((width, 128 - NEXP - 4), jnp.bfloat16)], 1
    )
    prior_wide = jnp.pad(prior_weight, ((0, 0), (0, 128 - NEXP)))
    prior_turned = jnp.pad(prior_weight.T, ((0, 128 - NEXP), (0, 128 - NEXP)))
    resid, small, *x_out = middle(
        tokens, attended, out_weight, expert_row, mixer, prior, prior_wide, routes, codes_row
    )
    backs, dots, fs, grads_gate, grads_up, grads_down = expert_phase(x_out, small, grad, codes_row, gate, up, down)
    dots = dots[:, :, 0, :half_slots].reshape(1, 2 * rows)
    backs = backs.reshape(2, rows, width)
    vector = jnp.concatenate([constant_vector, jnp.zeros((6, width), jnp.float32)], 0)
    resid_grads, grads_out, out_part, prior_grad = turn(
        resid, small, grad, prior, routes, codes, backs, dots, vector, expert_row,
        mixer.T, prior_turned, out_weight, attended,
    )
    tokens_grad, fs, gate_got, up_got, down_got, totals = attend_back_phase(
        grads_out.reshape(chunks, owners, HEAD_DIM, rows), heads, outs, logs, bias, cosine, sine, tokens,
        attention_row, qkv_weights, resid_grads, out_part, fs, (grads_gate, grads_up, grads_down), copies,
    )
    result = combine(resid, small, routes, codes, fs.reshape(2, rows, width), vector, expert_row)
    gate_part, up_part, down_part = (own_sum(got) for got in (gate_got, up_got, down_got))
    span = owners * HEAD_DIM
    qkv_totals = [
        jnp.concatenate([part[:, i * span : (i + 1) * span] for part in totals[1:]], 1) for i in range(3)
    ]
    small_total = totals[0, :, width:]
    return (
        result[None],
        tokens_grad[None],
        prior_grad[None],
        *qkv_totals,
        totals[0, :, :width],
        totals[chunks, :, width],
        small_total[:, 24],
        small_total[:, :NEXP],
        small_total[: NEXP // owners, 32 : 32 + NEXP],
        small_total[:, NEXP : NEXP + 4],
        small_total[:, 16:18].T,
        gate_part,
        up_part,
        down_part,
    )


def solution(mesh):
    owners, copies = mesh.shape["expert"], mesh.shape["dp"]
    cores = 2
    mesh = Mesh(mesh.devices.reshape(owners, copies // cores, cores), ("expert", "xy", "core"))
    dp = ("xy", "core")
    rows = P(dp, "expert", None)
    shard = P("expert", dp, None)
    in_specs = (rows, rows, rows, P(dp, None), rows) + (P(),) * 10 + (shard,) * 3
    out_specs = (
        (rows,) * 3
        + (P("expert", None),) * 4
        + (P("expert"),) * 2
        + (P("expert", None),) * 3
        + (P(None, "expert"),)
        + (shard,) * 3
    )
    return jax.shard_map(per_device, mesh=mesh, in_specs=in_specs, out_specs=out_specs, check_vma=False)
```

```python
import functools

import jax
import jax.numpy as jnp
from jax import lax
from jax.experimental import pallas as pl
from jax.experimental.pallas import tpu as pltpu
from jax.sharding import Mesh
from jax.sharding import PartitionSpec as P

NFFN = 8
NEXP = 12
SEG = 128
HEAD_DIM = 64
TRUNK = 1024
TILE = 2 * SEG
LOG2E = 1.4426950408889634
masked_score = -1e30
MIB = 2**20
epsilon = 1e-06
precise = lax.Precision.HIGHEST


def dot_nt(left, right):
    return lax.dot_general(left, right, (((1,), (1,)), ((), ())), preferred_element_type=jnp.float32)


def dot_nn(left, right):
    return jnp.dot(left, right, preferred_element_type=jnp.float32)


def tile_parts(tile, start):
    trunk_tiles = TRUNK // TILE
    if tile is not None and tile < trunk_tiles:
        return [(k * TILE, False, k == tile) for k in range(tile + 1)]
    parts = [(k * TILE, False, False) for k in range(trunk_tiles)]
    branch_tiles = 2
    if tile is None:
        parts += [(TRUNK + k * TILE, True, False) for k in range(branch_tiles)]
    else:
        parts += [(TRUNK + k * TILE, True, False) for k in range(tile - trunk_tiles)]
    parts += [(start, True, True)]
    return parts


def causal_bias():
    key_ids = lax.broadcasted_iota(jnp.int32, (TILE, TILE), 0)
    query_ids = lax.broadcasted_iota(jnp.int32, (TILE, TILE), 1)
    return jnp.where(key_ids <= query_ids, 0.0, masked_score).astype(jnp.float32)


def part_scores(scores, part, columns, bias_ref, triangle):
    first, by_lineage, causal = part
    if by_lineage:
        segment = 1 + (first - TRUNK) // SEG
        rows = [bias_ref[pl.ds(segment + i, 1), columns] for i in range(TILE // SEG)]
        scores = jnp.concatenate(
            [scores[i * SEG : (i + 1) * SEG] + rows[i] for i in range(TILE // SEG)], 0
        )
    if causal:
        scores = scores + triangle[...]
    return scores


def for_tiles(length, body):
    trunk_tiles = TRUNK // TILE
    for tile in range(trunk_tiles + 2):
        body(tile, tile * TILE)
    first_leaf = trunk_tiles + 2

    @pl.loop(first_leaf, length // TILE)
    def _(tile):
        body(None, pl.multiple_of(tile * TILE, TILE))


def attend_head(bias_ref, qkv_ref, out_ref, lse_ref, q_ref, k_ref, v_ref, o_ref, s_ref, triangle):
    sources, _, rows = qkv_ref.shape
    length = sources * rows
    factor = HEAD_DIM ** (-0.5) * LOG2E
    triangle[...] = causal_bias()
    extra = lax.broadcasted_iota(jnp.int32, (16, length), 0)
    v_ref[HEAD_DIM:, :] = jnp.where(extra == 0, 1.0, 0.0).astype(jnp.bfloat16)
    for z in range(sources):
        span = pl.ds(z * rows, rows)
        q_ref[:, span] = qkv_ref[z, :HEAD_DIM]
        k_ref[span, :] = qkv_ref[z, HEAD_DIM : 2 * HEAD_DIM].astype(jnp.float32).T.astype(jnp.bfloat16)
        v_ref[:HEAD_DIM, span] = qkv_ref[z, 2 * HEAD_DIM :]

    def body(tile, start):
        columns = pl.ds(start, TILE)
        parts = tile_parts(tile, start)
        query = q_ref[:, columns]
        peak = None
        for i, part in enumerate(parts):
            scores = dot_nn(k_ref[pl.ds(part[0], TILE), :], query)
            scores = part_scores(scores, part, columns, bias_ref, triangle)
            s_ref[i * TILE : (i + 1) * TILE, :] = scores
            top = jnp.max(scores, 0, keepdims=True)
            peak = top if peak is None else jnp.maximum(peak, top)
        shift = peak * factor
        total = None
        for i, part in enumerate(parts):
            weights = jnp.exp2(s_ref[i * TILE : (i + 1) * TILE, :] * factor - shift)
            term = dot_nn(v_ref[:, pl.ds(part[0], TILE)], weights.astype(jnp.bfloat16))
            total = term if total is None else total + term
        norm = total[HEAD_DIM : HEAD_DIM + 1]
        o_ref[:, columns] = (total[:HEAD_DIM] / norm).astype(jnp.bfloat16)
        lse_ref[:, columns] = shift + jnp.log2(norm)

    for_tiles(length, body)
    for z in range(sources):
        out_ref[z] = o_ref[:, pl.ds(z * rows, rows)]


def attend_back_head(
    bias_ref, cos_ref, sin_ref, qkv_ref, out_ref, lse_ref, grad_ref, back_ref,
    qt_ref, kt_ref, dt_ref, q_ref, k_ref, v_ref, d_ref, delta_ref, dq_ref, dk_ref, dv_ref, triangle,
):
    sources, _, rows = qkv_ref.shape
    length = sources * rows
    scaling = HEAD_DIM ** (-0.5)
    factor = scaling * LOG2E
    triangle[...] = causal_bias()

    def turned(values):
        return values.astype(jnp.float32).T.astype(jnp.bfloat16)

    for z in range(sources):
        span = pl.ds(z * rows, rows)
        query, key, value = (qkv_ref[z, i * HEAD_DIM : (i + 1) * HEAD_DIM] for i in range(3))
        grad = grad_ref[z]
        qt_ref[:, span] = query
        kt_ref[:, span] = key
        dt_ref[:, span] = grad
        q_ref[span, :] = turned(query)
        k_ref[span, :] = turned(key)
        v_ref[span, :] = turned(value)
        d_ref[span, :] = turned(grad)
        delta_ref[:, span] = jnp.sum(
            grad.astype(jnp.float32) * out_ref[z].astype(jnp.float32), 0, keepdims=True
        )
    dk_ref[...] = jnp.zeros_like(dk_ref)
    dv_ref[...] = jnp.zeros_like(dv_ref)

    def body(tile, start):
        columns = pl.ds(start, TILE)
        query_t, grad_t = qt_ref[:, columns], dt_ref[:, columns]
        query, grad = q_ref[columns, :], d_ref[columns, :]
        lse, delta = lse_ref[:, columns], delta_ref[:, columns]
        total = None
        for part in tile_parts(tile, start):
            span = pl.ds(part[0], TILE)
            scores = dot_nn(k_ref[span, :], query_t) * factor - lse
            scores = part_scores(scores, part, columns, bias_ref, triangle)
            weights = jnp.exp2(scores)
            weight_grads = dot_nn(v_ref[span, :], grad_t)
            score_grads = (weights * (weight_grads - delta)).astype(jnp.bfloat16)
            dv_ref[span, :] += dot_nn(weights.astype(jnp.bfloat16), grad)
            dk_ref[span, :] += dot_nn(score_grads, query)
            term = dot_nn(kt_ref[:, span], score_grads)
            total = term if total is None else total + term
        dq_ref[:, columns] = total

    for_tiles(length, body)
    half = HEAD_DIM // 2
    for z in range(sources):
        span = pl.ds(z * rows, rows)
        cosine, sine = cos_ref[:, span], sin_ref[:, span]
        for i, values in enumerate((dq_ref[:, span], dk_ref[span, :].T)):
            values = values * scaling
            first, second = values[:half], values[half:]
            back_ref[z, i * HEAD_DIM : (i + 1) * HEAD_DIM] = jnp.concatenate(
                [first * cosine + second * sine, second * cosine - first * sine], 0
            ).astype(jnp.bfloat16)
        back_ref[z, 2 * HEAD_DIM :] = dv_ref[span, :].T.astype(jnp.bfloat16)


def params(limit):
    return pltpu.CompilerParams(vmem_limit_bytes=limit * MIB)


def cost(flops, moved):
    return pl.CostEstimate(flops=int(flops), bytes_accessed=int(moved), transcendentals=0)


def greet(ring, copies):
    barrier = pltpu.get_barrier_semaphore()
    for target in ring + copies:
        pl.semaphore_signal(barrier, inc=1, device_id=target, device_id_type=pl.DeviceIdType.MESH)
    pl.semaphore_wait(barrier, len(ring) + len(copies))


def ring_partners(owners):
    member = lax.axis_index("expert")
    result = []
    for step in sorted(range(1, owners), key=lambda k: -min(k, owners - k)):
        index = lax.rem(member + step, owners)
        result.append((step, index, {"expert": index}))
    return result


def copy_partners(total):
    place = lax.axis_index("xy") * 2 + lax.axis_index("core")
    result = []
    for step in sorted(range(1, total), key=lambda k: -(k % 8 in (6, 2, 4))):
        index = lax.rem(place + step, total)
        result.append((step, lax.rem(index, 2), {"xy": index // 2, "core": lax.rem(index, 2)}))
    return result


def plane_chips(xy):
    return xy + 1 - 2 * lax.rem(xy, 2), lax.rem(xy + 2, 4), 3 - xy


def first_hops(beside, behind, across):
    return (
        (across * 2, 2, beside), (across * 2 + 1, 3, behind), (beside * 2, 0, beside), (behind * 2 + 1, 1, behind),
    )


def relayed(copies):
    return copies == 8


def remote(source, target, send, receive, device):
    return pltpu.make_async_remote_copy(
        src_ref=source, dst_ref=target, send_sem=send, recv_sem=receive,
        device_id=device, device_id_type=pl.DeviceIdType.MESH,
    )


def reach_of(parents):
    shape = (128, 128)
    one, two = lax.broadcasted_iota(jnp.int32, shape, 0), lax.broadcasted_iota(jnp.int32, shape, 1)
    count = parents.shape[1]
    none = lambda size: jnp.full((1, size), -1, jnp.int32)
    parent_row = jnp.concatenate([none(1), parents, none(127 - count)], 1)
    reach = jnp.where((one == two) | (one == parent_row), 1.0, 0.0).astype(jnp.bfloat16)
    for _ in range(3):
        reach = jnp.minimum(dot_nn(reach, reach), 1.0).astype(jnp.bfloat16)
    return reach


def place_tables(reach, first, size):
    ids = lax.broadcasted_iota(jnp.int32, (1, size), 1) + first
    later = ids - TRUNK
    segment = jnp.where(later < 0, 0, 1 + lax.shift_right_arithmetic(later, 7))
    inside = jnp.where(later < 0, later, (later & (SEG - 1)) - SEG)
    own = jnp.where(segment == lax.broadcasted_iota(jnp.int32, (128, size), 0), 1.0, 0.0).astype(jnp.bfloat16)
    seen = dot_nn(reach[:16], own)
    index = lax.broadcasted_iota(jnp.int32, (16, 1), 0)
    lengths = jnp.where(index == 0, float(TRUNK), float(SEG))
    places = jnp.sum(seen * lengths, 0, keepdims=True) + inside.astype(jnp.float32)
    turn = lax.broadcasted_iota(jnp.int32, (HEAD_DIM // 2, 1), 0).astype(jnp.float32)
    angles = jnp.exp(turn * (-2.0 / HEAD_DIM * 9.210340371976184)) * places
    return seen, jnp.cos(angles), jnp.sin(angles)


def slot_codes(routes_ref, codes_ref, codes_row_ref):
    rows = routes_ref.shape[0]
    half_slots = rows // NFFN
    routes = routes_ref[...]
    lanes = lax.broadcasted_iota(jnp.int32, (rows, 128), 1)
    matches = [
        jnp.where((lanes == routes[:, c : c + 1]) & (lanes < NFFN), 1.0, 0.0).astype(jnp.float32) for c in range(2)
    ]
    square = (rows, rows)
    earlier = lax.broadcasted_iota(jnp.int32, square, 0) > lax.broadcasted_iota(jnp.int32, square, 1)
    before = dot_nn(
        jnp.where(earlier, 1.0, 0.0).astype(jnp.bfloat16), (matches[0] + matches[1]).astype(jnp.bfloat16)
    )
    codes = jnp.zeros((rows, 128), jnp.float32)
    for c in range(2):
        rank = jnp.sum(matches[c] * before, -1, keepdims=True)
        route = routes[:, c : c + 1].astype(jnp.float32)
        late = jnp.where(rank >= half_slots, float((NFFN - 1) * half_slots), 0.0)
        code = jnp.where(route < NFFN, route * half_slots + rank + late, float(4 * rows))
        codes = jnp.where(lanes == c, code, codes)
    codes_ref[...] = codes.astype(jnp.int32)
    codes_row_ref[...] = codes.T[:8].astype(jnp.int32)


def attend_phase_kernel(
    tokens_ref, table_ref, query_ref, key_ref, value_ref, parents_ref, routes_ref, gate_ref, up_ref, down_ref,
    attended_ref, lse_ref, bias_ref, cos_ref, sin_ref, codes_ref, codes_row_ref, heads_ref, outs_ref,
    gate_full, up_full, down_full,
    normed_ref, qkv_sent, qkv_got, out_sent, out_got, q_ref, k_ref, v_ref, o_ref, s_ref, triangle,
    qkv_send, qkv_recv, out_send, out_recv, weight_send, weight_recv, local_sem,
):
    chunks, owners, _, rows = qkv_sent.shape
    member = lax.axis_index("expert")
    copies = gate_full.shape[0]
    ring, others = ring_partners(owners), copy_partners(copies)
    greet([item[2] for item in ring], [item[2] for item in others])
    weights = ((gate_ref, gate_full), (up_ref, up_full), (down_ref, down_full))
    place = lax.axis_index("xy") * 2 + lax.axis_index("core")
    core = lax.axis_index("core")
    started = []

    relays = relayed(copies)
    xy = lax.axis_index("xy")
    beside, behind, across = plane_chips(xy)
    arrivals = {}

    def send_weight(i):
        shard, full = weights[i]
        local = pltpu.make_async_copy(shard.at[core], full.at[place], weight_send.at[i, 0])
        local.start()
        started.append(local.wait)
        if relays:
            targets = [(2, beside, 0), (4, behind, 0), (2, beside, 1), (4, behind, 1)]
            targets = [(1, 1 - core, {"core": 1 - core})] + [
                (base + core, other, {"xy": chip, "core": other}) for base, chip, other in targets
            ]
            for n, (slot, other, device) in enumerate(targets):
                copy = remote(
                    shard.at[other], full.at[place], weight_send.at[i, 1 + n], weight_recv.at[i, slot], device
                )
                copy.start()
                started.append(copy.wait_send)
            for slot in range(1, 8):
                arrivals[i, slot] = remote(
                    shard.at[core], full.at[place], weight_send.at[i, 0], weight_recv.at[i, slot], {"core": 1 - core}
                )
        else:
            for step, other_core, device in others:
                copy = remote(
                    shard.at[other_core], full.at[place], weight_send.at[i, step], weight_recv.at[i, step], device
                )
                copy.start()
                started.append(copy.wait)

    def relay_weight(i):
        full = weights[i][1]
        for slot, piece, chip, landing in ((4, behind * 2, beside, 6), (3, beside * 2 + 1, behind, 7)):
            arrivals.pop((i, slot)).wait_recv()
            copy = remote(
                full.at[piece], full.at[piece], weight_send.at[i, landing], weight_recv.at[i, landing], {"xy": chip}
            )
            copy.start()
            started.append(copy.wait_send)

    for i in range(3):
        send_weight(i)

    inputs = tokens_ref[...].astype(jnp.float32)
    inverse = lax.rsqrt(jnp.mean(inputs * inputs, -1, keepdims=True) + epsilon)
    normed_ref[...] = (inputs * inverse * table_ref[0:1, :]).astype(jnp.bfloat16)
    reach = reach_of(parents_ref[...])
    _, cosine, sine = place_tables(reach, member * rows, rows)
    half = HEAD_DIM // 2
    span_width = owners * HEAD_DIM
    qkv_copies = []
    for j in range(chunks):
        for i, weight in enumerate((query_ref, key_ref, value_ref)):
            turned = dot_nn(normed_ref[...], weight[:, j * span_width : (j + 1) * span_width]).T
            base = i * HEAD_DIM
            for z in range(owners):
                first = turned[z * HEAD_DIM : z * HEAD_DIM + half]
                second = turned[z * HEAD_DIM + half : (z + 1) * HEAD_DIM]
                if i < 2:
                    first, second = first * cosine - second * sine, second * cosine + first * sine
                qkv_sent[j, z, base : base + half] = first.astype(jnp.bfloat16)
                qkv_sent[j, z, base + half : base + HEAD_DIM] = second.astype(jnp.bfloat16)
        local = pltpu.make_async_copy(qkv_sent.at[j, member], qkv_got.at[j, member], local_sem.at[j])
        local.start()
        group = []
        for step, index, device in ring:
            copy = remote(
                qkv_sent.at[j, index], qkv_got.at[j, member],
                qkv_send.at[j, step - 1], qkv_recv.at[j, step - 1], device,
            )
            copy.start()
            group.append(copy)
        qkv_copies.append((local, group))
    seen, whole_cosine, whole_sine = place_tables(reach, 0, owners * rows)
    bias_ref[...] = jnp.where(seen > 0.5, 0.0, masked_score)
    cos_ref[...] = whole_cosine
    sin_ref[...] = whole_sine
    slot_codes(routes_ref, codes_ref, codes_row_ref)

    out_copies = []
    kept = []
    for j in range(chunks):
        local, group = qkv_copies[j]
        local.wait()
        for copy in group:
            copy.wait_recv()
        keep = pltpu.make_async_copy(qkv_got.at[j], heads_ref.at[j], local_sem.at[chunks + j])
        keep.start()
        kept.append(keep)
        attend_head(
            bias_ref, qkv_got.at[j], out_sent.at[j], lse_ref.at[j : j + 1], q_ref, k_ref, v_ref, o_ref, s_ref, triangle
        )
        local = pltpu.make_async_copy(out_sent.at[j, member], out_got.at[j, member], local_sem.at[2 * chunks + j])
        local.start()
        keep = pltpu.make_async_copy(out_sent.at[j], outs_ref.at[j], local_sem.at[3 * chunks + j])
        keep.start()
        kept += [local, keep]
        for step, index, device in ring:
            copy = remote(
                out_sent.at[j, index], out_got.at[j, member],
                out_send.at[j, step - 1], out_recv.at[j, step - 1], device,
            )
            copy.start()
            out_copies.append(copy)
        if relays and j == 1:
            for i in range(3):
                relay_weight(i)
    for copy in out_copies:
        copy.wait_recv()
    for copy in kept:
        copy.wait()
    attended_ref[...] = out_got[...]
    for local, group in qkv_copies:
        for copy in group:
            copy.wait_send()
    for copy in out_copies:
        copy.wait_send()
    for copy in arrivals.values():
        copy.wait_recv()
    for wait in started:
        wait()


def attend_phase(tokens, table, weights, parents, routes, shards, copies):
    rows, width = tokens.shape
    owners = lax.axis_size("expert")
    length = rows * owners
    chunks = width // HEAD_DIM // owners
    head = (chunks, owners, 3 * HEAD_DIM, rows)
    out = (chunks, owners, HEAD_DIM, rows)
    vmem, hbm = pl.BlockSpec(memory_space=pltpu.VMEM), pl.BlockSpec(memory_space=pl.ANY)
    fulls = [jax.ShapeDtypeStruct((copies, *shard.shape[1:]), shard.dtype) for shard in shards]
    part_total = TRUNK // TILE + 3
    sems = lambda *shape: pltpu.SemaphoreType.DMA(shape)
    return pl.pallas_call(
        attend_phase_kernel,
        in_specs=[vmem] * 7 + [hbm] * 3,
        out_specs=(vmem,) * 7 + (hbm,) * 5,
        out_shape=(
            jax.ShapeDtypeStruct(out, jnp.bfloat16),
            jax.ShapeDtypeStruct((8, length), jnp.float32),
            jax.ShapeDtypeStruct((16, length), jnp.float32),
            *(jax.ShapeDtypeStruct((HEAD_DIM // 2, length), jnp.float32),) * 2,
            jax.ShapeDtypeStruct((rows, 128), jnp.int32),
            jax.ShapeDtypeStruct((8, rows), jnp.int32),
            jax.ShapeDtypeStruct(head, jnp.bfloat16),
            jax.ShapeDtypeStruct(out, jnp.bfloat16),
            *fulls,
        ),
        scratch_shapes=[
            pltpu.VMEM((rows, width), jnp.bfloat16),
            pltpu.VMEM(head, jnp.bfloat16),
            pltpu.VMEM(head, jnp.bfloat16),
            pltpu.VMEM(out, jnp.bfloat16),
            pltpu.VMEM(out, jnp.bfloat16),
            pltpu.VMEM((HEAD_DIM, length), jnp.bfloat16),
            pltpu.VMEM((length, HEAD_DIM), jnp.bfloat16),
            pltpu.VMEM((HEAD_DIM + 16, length), jnp.bfloat16),
            pltpu.VMEM((HEAD_DIM, length), jnp.bfloat16),
            pltpu.VMEM((part_total * TILE, TILE), jnp.float32),
            pltpu.VMEM((TILE, TILE), jnp.float32),
            sems(chunks, owners - 1), sems(chunks, owners - 1), sems(chunks, owners - 1), sems(chunks, owners - 1),
            sems(3, copies), sems(3, copies), sems(4 * chunks),
        ],
        compiler_params=pltpu.CompilerParams(vmem_limit_bytes=56 * MIB, collective_id=1, has_side_effects=True),
        cost_estimate=cost(1e10, 5e7),
    )(tokens, table, *weights, parents, routes, *shards)


def lane_pick(values, lanes, index):
    return jnp.sum(jnp.where(lanes == index, values, 0.0), -1, keepdims=True)


def middle_kernel(
    tokens_ref, attended_ref, out_weight_ref, table_ref, router_ref, constant_ref, prior_ref, prior_weight_ref,
    routes_ref, codes_ref, resid_ref, small_ref, first_ref, second_ref, mixer_ref, hidden_ref,
):
    rows, width = tokens_ref.shape
    mixer_ref[...] = jnp.concatenate(
        [router_ref[...], constant_ref[...], jnp.zeros((width, 128 - NEXP - 4), jnp.bfloat16)], 1
    )

    @pl.loop(0, rows // SEG)
    def _(step):
        span = pl.ds(pl.multiple_of(step * SEG, SEG), SEG)
        attended = attended_ref[:, span].astype(jnp.float32).T.astype(jnp.bfloat16)
        resid = tokens_ref[span, :].astype(jnp.float32) + dot_nn(attended, out_weight_ref[...])
        inverse = lax.rsqrt(jnp.mean(resid * resid, -1, keepdims=True) + epsilon)
        hidden = (resid * inverse * table_ref[1:2, :]).astype(jnp.bfloat16)
        resid_ref[span, :] = resid
        hidden_ref[span, :] = hidden
        logits = dot_nn(hidden, mixer_ref[...])
        carried = jnp.dot(
            prior_ref[span, :], prior_weight_ref[...], precision=precise, preferred_element_type=jnp.float32
        )
        logits = logits + jnp.concatenate([carried, jnp.zeros((SEG, 128 - NEXP), jnp.float32)], 1)
        lanes = lax.broadcasted_iota(jnp.int32, logits.shape, 1)
        routes = routes_ref[span, :]
        columns = []
        pairs = [[lane_pick(logits, lanes, routes[:, c : c + 1]) for c in range(2)]]
        pairs += [[logits[:, NEXP + 2 * m + c : NEXP + 2 * m + c + 1] for c in range(2)] for m in range(2)]
        for one, two in pairs:
            peak = jnp.maximum(one, two)
            one, two = jnp.exp(one - peak), jnp.exp(two - peak)
            columns += [one / (one + two), two / (one + two)]
        columns.append(inverse)
        small = jnp.zeros_like(logits)
        for i, column in enumerate(columns):
            small = jnp.where(lanes == i, column, small)
        small_ref[span, :] = small

    slots = first_ref.shape[0]
    for half, ref in enumerate((first_ref, second_ref)):
        index = lax.broadcasted_iota(jnp.int32, (slots, rows), 0) + half * slots
        chosen = (codes_ref[0:1, :] == index) | (codes_ref[1:2, :] == index)
        ref[...] = dot_nn(chosen.astype(jnp.bfloat16), hidden_ref[...]).astype(jnp.bfloat16)


def middle(tokens, attended, out_weight, table, router, constant, prior, prior_weight, routes, codes_row):
    rows, width = tokens.shape
    slots = rows
    return pl.pallas_call(
        middle_kernel,
        out_shape=(
            jax.ShapeDtypeStruct((rows, width), jnp.float32),
            jax.ShapeDtypeStruct((rows, 128), jnp.float32),
            jax.ShapeDtypeStruct((slots, width), jnp.bfloat16),
            jax.ShapeDtypeStruct((slots, width), jnp.bfloat16),
            jax.ShapeDtypeStruct((width, 128), jnp.bfloat16),
        ),
        scratch_shapes=[pltpu.VMEM((rows, width), jnp.bfloat16)],
        compiler_params=params(48),
        cost_estimate=cost(4 * rows * width * width + 4 * rows * rows * width, 1e7),
    )(tokens, attended, out_weight, table, router, constant, prior, prior_weight, routes, codes_row)


def plane_partners(owners):
    total = 2 * owners
    place = lax.axis_index("expert") * 2 + lax.axis_index("core")
    result = []
    for step in sorted(range(1, total), key=lambda k: -min(k, total - k)):
        index = lax.rem(place + step, total)
        result.append((step, index, {"expert": index // 2, "core": lax.rem(index, 2)}))
    return result


def expert_phase_kernel(
    xa_ref, xb_ref, small_ref, grad_ref, codes_ref, gate_hbm, up_hbm, down_hbm,
    back_out, dots_out, fa_out, fb_out, gate_grad, up_grad, down_grad,
    gate_ref, up_ref, down_ref, scaled_ref, d_sent, x_got, d_got, back_sent, back_got, dots_sent, dots_got,
    f_sum, back_sum, hid_ref, one_ref, two_ref, x_turned, d_turned, stage, stage_down,
    x_send, x_recv, d_send, d_recv, back_send, back_recv, dots_send, dots_recv, local_sem, stage_sem,
):
    experts, slots, width = x_got.shape[1:]
    rows = experts * slots
    units = gate_ref.shape[1]
    owners = experts // 2
    place = lax.axis_index("expert") * 2 + lax.axis_index("core")
    partners = plane_partners(owners)
    greet([item[2] for item in partners], [])
    loads = [
        pltpu.make_async_copy(source, target, local_sem.at[i])
        for i, (source, target) in enumerate(((gate_hbm, gate_ref), (up_hbm, up_ref), (down_hbm, down_ref)))
    ]
    for load in loads:
        load.start()

    def send(source, target, sends, receives, half, locals_at):
        copies = []
        local = pltpu.make_async_copy(source(place), target.at[half, place], local_sem.at[locals_at + half])
        local.start()
        for step, index, device in partners:
            copy = remote(source(index), target.at[half, place], sends.at[half, step], receives.at[half, step], device)
            copy.start()
            copies.append(copy)
        return local, copies

    def arrive(group):
        group[0].wait()
        for copy in group[1]:
            copy.wait_recv()

    x_refs = (xa_ref, xb_ref)
    x_groups = [send(lambda e, ref=ref: ref.at[e], x_got, x_send, x_recv, h, 3) for h, ref in enumerate(x_refs)]
    for c in range(2):
        scaled_ref[c * rows : (c + 1) * rows, :] = (
            small_ref[:, c : c + 1] * grad_ref[...].astype(jnp.float32)
        ).astype(jnp.bfloat16)
    d_groups = []
    for half in range(2):
        index = lax.broadcasted_iota(jnp.int32, (rows, rows), 0) + half * rows
        chosen = jnp.concatenate([(codes_ref[c : c + 1, :] == index).astype(jnp.bfloat16) for c in range(2)], 1)
        d_sent[half] = dot_nn(chosen, scaled_ref[...]).astype(jnp.bfloat16).reshape(experts, slots, width)
        d_groups.append(send(lambda e, half=half: d_sent.at[half, e], d_got, d_send, d_recv, half, 5))
    for load in loads:
        load.wait()

    part = 512
    tile = rows // 2

    def forward(half):
        x = x_got[half].reshape(rows, width)
        f_sum[...] = jnp.zeros_like(f_sum)
        x_turned[:, half * rows : (half + 1) * rows] = x.astype(jnp.float32).T.astype(jnp.bfloat16)

        @pl.loop(0, units // part)
        def _(step):
            columns = pl.ds(pl.multiple_of(step * part, part), part)
            for r in range(2):
                near = slice(r * tile, (r + 1) * tile)
                far = pl.ds(half * rows + r * tile, tile)
                gate_pre = dot_nn(x[near], gate_ref[:, columns])
                up_pre = dot_nn(x[near], up_ref[:, columns])
                sigmoid = 1.0 / (1.0 + jnp.exp(-gate_pre))
                active = gate_pre * sigmoid
                hid = (active * up_pre).astype(jnp.bfloat16)
                hid_ref[far, columns] = hid
                one_ref[far, columns] = (up_pre * (sigmoid + active * (1.0 - sigmoid))).astype(jnp.bfloat16)
                two_ref[far, columns] = active.astype(jnp.bfloat16)
                f_sum[near, :] += dot_nn(hid, down_ref[columns, :])

        (fa_out, fb_out)[half][...] = f_sum[...].astype(jnp.bfloat16).reshape(experts, slots, width)

    def backward(half):
        d = d_got[half].reshape(rows, width)
        back_sum[...] = jnp.zeros_like(back_sum)
        d_turned[:, half * rows : (half + 1) * rows] = d.astype(jnp.float32).T.astype(jnp.bfloat16)

        @pl.loop(0, units // part)
        def _(step):
            columns = pl.ds(pl.multiple_of(step * part, part), part)
            for r in range(2):
                near = slice(r * tile, (r + 1) * tile)
                far = pl.ds(half * rows + r * tile, tile)
                mid = dot_nt(d[near], down_ref[columns, :])
                dg = (mid * one_ref[far, columns].astype(jnp.float32)).astype(jnp.bfloat16)
                du = (mid * two_ref[far, columns].astype(jnp.float32)).astype(jnp.bfloat16)
                one_ref[far, columns] = dg
                two_ref[far, columns] = du
                back_sum[near, :] += dot_nt(dg, gate_ref[:, columns]) + dot_nt(du, up_ref[:, columns])

        back_sent[half] = back_sum[...].astype(jnp.bfloat16).reshape(experts, slots, width)

    def dots(half):
        ones = jnp.ones((8, width), jnp.float32)
        for e in range(experts):
            product = (fa_out, fb_out)[half][e].astype(jnp.float32) * d_got[half, e].astype(jnp.float32)
            total = lax.dot_general(
                ones, product, (((1,), (1,)), ((), ())), precision=precise, preferred_element_type=jnp.float32
            )
            dots_sent[half, e] = jnp.concatenate([total, jnp.zeros((8, 128 - slots), jnp.float32)], 1)

    for half in range(2):
        arrive(x_groups[half])
        forward(half)
    back_groups, dots_groups = [], []
    for half in range(2):
        arrive(d_groups[half])
        backward(half)
        back_groups.append(send(lambda e, half=half: back_sent.at[half, e], back_got, back_send, back_recv, half, 7))
        dots(half)
        dots_groups.append(send(lambda e, half=half: dots_sent.at[half, e], dots_got, dots_send, dots_recv, half, 9))

    piece = 256
    steps = units // piece

    def stores(step, slot):
        columns = pl.ds(pl.multiple_of(step * piece, piece), piece)
        return [
            pltpu.make_async_copy(stage.at[0, slot], gate_grad.at[:, columns], stage_sem.at[0, slot]),
            pltpu.make_async_copy(stage.at[1, slot], up_grad.at[:, columns], stage_sem.at[1, slot]),
            pltpu.make_async_copy(stage_down.at[slot], down_grad.at[columns, :], stage_sem.at[2, slot]),
        ]

    @pl.loop(0, steps // 2)
    def _(pair):
        for slot in range(2):
            step = pair * 2 + slot
            columns = pl.ds(pl.multiple_of(step * piece, piece), piece)

            @pl.when(pair > 0)
            def _():
                for store in stores(step, slot):
                    store.wait()

            stage[0, slot] = dot_nn(x_turned[...], one_ref[:, columns]).astype(jnp.bfloat16)
            stage[1, slot] = dot_nn(x_turned[...], two_ref[:, columns]).astype(jnp.bfloat16)
            stage_down[slot] = dot_nn(d_turned[...], hid_ref[:, columns]).T.astype(jnp.bfloat16)
            for store in stores(step, slot):
                store.start()

    for slot in range(2):
        for store in stores(steps - 2 + slot, slot):
            store.wait()
    for group in back_groups + dots_groups:
        arrive(group)
    back_out[...] = back_got[...]
    dots_out[...] = dots_got[...]
    for group in x_groups + d_groups + back_groups + dots_groups:
        for copy in group[1]:
            copy.wait_send()


def expert_phase(x_parts, small, grad, codes_row, gate, up, down):
    rows, width = grad.shape
    units = gate.shape[1]
    slots = rows // NFFN
    both = (2, NFFN, slots, width)
    dots = (2, NFFN, 8, 128)
    vmem, hbm = pl.BlockSpec(memory_space=pltpu.VMEM), pl.BlockSpec(memory_space=pl.ANY)
    sems = pltpu.SemaphoreType.DMA((2, NFFN))
    wide = pltpu.VMEM((rows, width), jnp.float32)
    mids = pltpu.VMEM((2 * rows, units), jnp.bfloat16)
    turned = pltpu.VMEM((width, 2 * rows), jnp.bfloat16)
    moved = pltpu.VMEM(both, jnp.bfloat16)
    return pl.pallas_call(
        expert_phase_kernel,
        in_specs=[vmem] * 5 + [hbm] * 3,
        out_specs=(vmem, vmem, vmem, vmem, hbm, hbm, hbm),
        out_shape=(
            jax.ShapeDtypeStruct(both, jnp.bfloat16),
            jax.ShapeDtypeStruct(dots, jnp.float32),
            *(jax.ShapeDtypeStruct(both[1:], jnp.bfloat16),) * 2,
            jax.ShapeDtypeStruct(gate.shape, jnp.bfloat16),
            jax.ShapeDtypeStruct(up.shape, jnp.bfloat16),
            jax.ShapeDtypeStruct(down.shape, jnp.bfloat16),
        ),
        scratch_shapes=[
            pltpu.VMEM(gate.shape, jnp.bfloat16),
            pltpu.VMEM(up.shape, jnp.bfloat16),
            pltpu.VMEM(down.shape, jnp.bfloat16),
            pltpu.VMEM((2 * rows, width), jnp.bfloat16),
            moved, moved, moved, moved, moved,
            pltpu.VMEM(dots, jnp.float32),
            pltpu.VMEM(dots, jnp.float32),
            wide, wide, mids, mids, mids, turned, turned,
            pltpu.VMEM((2, 2, width, 256), jnp.bfloat16),
            pltpu.VMEM((2, 256, width), jnp.bfloat16),
            *(sems,) * 8,
            pltpu.SemaphoreType.DMA((11,)),
            pltpu.SemaphoreType.DMA((3, 2)),
        ],
        compiler_params=pltpu.CompilerParams(vmem_limit_bytes=63 * MIB, collective_id=2, has_side_effects=True),
        cost_estimate=cost(36 * rows * width * units, 5e7),
    )(*(part.reshape(NFFN, slots, width) for part in x_parts), small, grad, codes_row, gate, up, down)


def split_dot(dot, left, right):
    high = left.astype(jnp.bfloat16)
    low = (left - high.astype(jnp.float32)).astype(jnp.bfloat16)
    return dot(high, right) + dot(low, right)


def turn_kernel(
    resid_ref, small_ref, grad_ref, prior_ref, routes_ref, codes_ref, returned_ref, dots_ref, table_ref,
    mixer_ref, prior_weight_ref, out_weight_ref, attended_ref, f_ref, gate_ref,
    resid_grad_ref, grads_ref, out_grad_ref, prior_grad_ref, f_got, gate_first,
    back_ref, sums_ref, prior_sums_ref, extra_ref, f_send, f_recv, gate_send, gate_recv, *, owners, reduce,
):
    rows, width = resid_ref.shape
    planes = plane_partners(owners)
    beside, behind, across = plane_chips(lax.axis_index("xy"))
    greet([item[2] for item in planes], [{"xy": beside}, {"xy": behind}] if reduce else [])
    expert = lax.axis_index("expert") * 2 + lax.axis_index("core")
    copies = [pltpu.make_async_copy(f_ref.at[expert], f_got.at[expert], f_send.at[0])]
    copies += [
        remote(f_ref.at[index], f_got.at[expert], f_send.at[step], f_recv.at[step], device)
        for step, index, device in planes
    ]
    if reduce:
        for piece, landing, chip in first_hops(beside, behind, across):
            copies.append(
                remote(
                    gate_ref.at[piece], gate_first.at[landing], gate_send.at[landing], gate_recv.at[landing],
                    {"xy": chip},
                )
            )
    for copy in copies:
        copy.start()
    slots = returned_ref.shape[0]
    sums_ref[...] = jnp.zeros_like(sums_ref)
    prior_sums_ref[...] = jnp.zeros_like(prior_sums_ref)

    @pl.loop(0, rows // SEG)
    def _(step):
        span = pl.ds(pl.multiple_of(step * SEG, SEG), SEG)
        small = small_ref[span, :]
        routes, codes = routes_ref[span, :], codes_ref[span, :]
        gates = [small[:, c : c + 1] for c in range(2)]
        mixing = [[small[:, 2 + 2 * m + c : 3 + 2 * m + c] for c in range(2)] for m in range(2)]
        inverse = small[:, 6:7]
        normed = resid_ref[span, :] * inverse
        gain = table_ref[1:2, :]
        hidden = normed * gain
        hidden_b = hidden.astype(jnp.bfloat16)
        grad_b = grad_ref[span, :]
        grad = grad_b.astype(jnp.float32)
        index = lax.broadcasted_iota(jnp.int32, (SEG, slots), 1)
        hits = [codes[:, c : c + 1] == index for c in range(2)]
        dots = dots_ref[...]
        terms = [jnp.sum(jnp.where(hit, dots, 0.0), -1, keepdims=True) for hit in hits]
        chosen = (hits[0] | hits[1]).astype(jnp.bfloat16)
        routed = dot_nn(chosen, returned_ref[...])
        along = jnp.sum(grad * hidden, -1, keepdims=True)
        across = [jnp.sum(grad * table_ref[2 + m : 3 + m, :], -1, keepdims=True) for m in range(2)]
        to_copy = 0.0
        to_mix = [0.0, 0.0]
        for c in range(2):
            route = routes[:, c : c + 1]
            copied = jnp.where(route == NFFN + 1, gates[c], 0.0)
            to_copy = to_copy + copied
            terms[c] = terms[c] + copied * along
            for m in range(2):
                mixed = jnp.where(route == NFFN + 2 + m, gates[c], 0.0)
                to_mix[m] = to_mix[m] + mixed
                terms[c] = terms[c] + mixed * (mixing[m][0] * along + mixing[m][1] * across[m])
        both = terms[0] + terms[1]
        lanes = lax.broadcasted_iota(jnp.int32, (SEG, 128), 1)
        logit_grads = jnp.zeros((SEG, 128), jnp.float32)
        for c in range(2):
            logit_grads = jnp.where(lanes == routes[:, c : c + 1], terms[c] - gates[c] * both, logit_grads)
        scores = logit_grads
        direct = to_copy
        for m in range(2):
            pair = (to_mix[m] * along, to_mix[m] * across[m])
            mean = mixing[m][0] * pair[0] + mixing[m][1] * pair[1]
            for c in range(2):
                scores = jnp.where(lanes == NEXP + 2 * m + c, mixing[m][c] * (pair[c] - mean), scores)
            direct = direct + mixing[m][0] * to_mix[m]
        prior_grad_ref[span, :] = lax.dot_general(
            logit_grads[:, :NEXP], prior_weight_ref[...], (((1,), (1,)), ((), ())),
            precision=precise, preferred_element_type=jnp.float32,
        )
        hidden_grads = split_dot(dot_nt, scores, mixer_ref[...]) + direct * grad + routed
        scaled = hidden_grads * gain
        resid_grads = inverse * (scaled - normed * jnp.mean(scaled * normed, -1, keepdims=True)) + grad
        resid_grad_ref[span, :] = resid_grads
        back_ref[span, :] = resid_grads.astype(jnp.bfloat16)
        weights = jnp.zeros((SEG, 128), jnp.float32)
        for m in range(2):
            weights = jnp.where(lanes == m, mixing[m][1] * to_mix[m], weights)
        sums_ref[0:16, :] += split_dot(dot_nn, scores.T[0:16], hidden_b)
        sums_ref[16:24, :] += split_dot(dot_nn, weights.T[0:8], grad_b)
        sums_ref[24:32, :] += jnp.sum((hidden_grads * normed).reshape(SEG // 8, 8, width), 0)
        prior_sums_ref[...] += jnp.dot(
            prior_ref[span, :].T,
            jnp.concatenate([logit_grads[:, 96:], logit_grads[:, :96]], 1),
            precision=precise,
            preferred_element_type=jnp.float32,
        )

    sums_ref[24:25, :] = jnp.sum(sums_ref[24:32, :], 0, keepdims=True)
    extra_ref[...] = jnp.concatenate([sums_ref[...], jnp.zeros((96, width), jnp.float32)], 0).T
    kept = NEXP // owners
    for z in range(owners):
        extra_ref[pl.ds(z * (width // owners), kept), :] += prior_sums_ref[z * kept : (z + 1) * kept, :]
    out_grad_ref[:, width : width + 128] = extra_ref[...].astype(jnp.bfloat16)
    out_grad_ref[:, width + 128 :] = jnp.zeros((width, 128), jnp.bfloat16)
    back = back_ref[...]
    grads_ref[...] = dot_nt(out_weight_ref[...], back).astype(jnp.bfloat16)
    out_grad_ref[:, :width] = dot_nn(attended_ref[...], back).astype(jnp.bfloat16)
    for copy in copies:
        copy.wait()


def turn(resid, small, grad, prior, routes, codes, returned, dots, table, mixer, prior_weight, out_weight, attended, f, gate):
    rows, width = resid.shape
    owners = lax.axis_size("expert")
    vmem, hbm = pl.BlockSpec(memory_space=pltpu.VMEM), pl.BlockSpec(memory_space=pl.ANY)
    return pl.pallas_call(
        functools.partial(turn_kernel, owners=owners, reduce=relayed(gate.shape[0])),
        in_specs=[vmem] * 13 + [hbm] * 2,
        out_specs=(vmem, vmem, vmem, vmem, hbm, hbm),
        out_shape=(
            jax.ShapeDtypeStruct((rows, width), jnp.float32),
            jax.ShapeDtypeStruct((width, rows), jnp.bfloat16),
            jax.ShapeDtypeStruct((width, width + 256), jnp.bfloat16),
            jax.ShapeDtypeStruct(prior.shape, jnp.float32),
            jax.ShapeDtypeStruct(f.shape, f.dtype),
            jax.ShapeDtypeStruct((4, *gate.shape[1:]), gate.dtype),
        ),
        scratch_shapes=[
            pltpu.VMEM((rows, width), jnp.bfloat16),
            pltpu.VMEM((32, width), jnp.float32),
            pltpu.VMEM((prior.shape[1], 128), jnp.float32),
            pltpu.VMEM((width, 128), jnp.float32),
            pltpu.SemaphoreType.DMA((2 * owners,)),
            pltpu.SemaphoreType.DMA((2 * owners,)),
            pltpu.SemaphoreType.DMA((4,)),
            pltpu.SemaphoreType.DMA((4,)),
        ],
        compiler_params=pltpu.CompilerParams(vmem_limit_bytes=60 * MIB, collective_id=4, has_side_effects=True),
        cost_estimate=cost(4 * rows * width * width + 4 * rows * rows * width, 1.5e7),
    )(resid, small, grad, prior, routes, codes, returned, dots, table, mixer, prior_weight, out_weight, attended, f, gate)


def finish_kernel(
    resid_ref, small_ref, routes_ref, codes_ref, fa_ref, fb_ref, table_ref, totals_ref, *refs, owners
):
    count = (len(refs) - 11) // 3
    sources, targets, refs = refs[:count], refs[count : 2 * count], refs[2 * count :]
    out_ref, *weight_refs, router_ref, prior_ref, constant_ref, rows_ref = refs[:9]
    held, (load_sem, store_sem) = refs[9:-2], refs[-2:]
    loads = [pltpu.make_async_copy(one, two, load_sem.at[i]) for i, (one, two) in enumerate(zip(sources, held))]
    stores = [pltpu.make_async_copy(one, two, store_sem.at[i]) for i, (one, two) in enumerate(zip(held, targets))]
    for move in loads:
        move.start()
    rows, width = resid_ref.shape
    half = fa_ref.shape[0]

    @pl.loop(0, rows // SEG)
    def _(step):
        span = pl.ds(pl.multiple_of(step * SEG, SEG), SEG)
        small = small_ref[span, :]
        routes, codes = routes_ref[span, :], codes_ref[span, :]
        resid = resid_ref[span, :]
        hidden = resid * small[:, 6:7] * table_ref[1:2, :]
        index = lax.broadcasted_iota(jnp.int32, (SEG, 2 * half), 1)
        total = resid
        direct = 0.0
        for c in range(2):
            gate, route = small[:, c : c + 1], routes[:, c : c + 1]
            chosen = (codes[:, c : c + 1] == index).astype(jnp.bfloat16)
            routed = dot_nn(chosen[:, :half], fa_ref[...]) + dot_nn(chosen[:, half:], fb_ref[...])
            total = total + gate * routed
            direct = direct + jnp.where(route == NFFN + 1, gate, 0.0)
            for m in range(2):
                mixed = jnp.where(route == NFFN + 2 + m, gate, 0.0)
                direct = direct + mixed * small[:, 2 + 2 * m : 3 + 2 * m]
                total = total + mixed * small[:, 3 + 2 * m : 4 + 2 * m] * table_ref[2 + m : 3 + m, :]
        out_ref[span, :] = (total + direct * hidden).astype(jnp.bfloat16)

    for load, store in zip(loads, stores):
        load.wait()
        store.start()
    heads_width = owners * HEAD_DIM
    for i, ref in enumerate(weight_refs[:3]):
        for p in range(1, totals_ref.shape[0]):
            ref[:, (p - 1) * heads_width : p * heads_width] = totals_ref[
                p, :, i * heads_width : (i + 1) * heads_width
            ].astype(jnp.float32)
    weight_refs[3][...] = totals_ref[0, :, :width].astype(jnp.float32)
    extra = totals_ref[0, :, width : width + 128].astype(jnp.float32)
    router_ref[...] = extra[:, :NEXP]
    constant_ref[...] = extra[:, NEXP : NEXP + 4]
    prior_ref[...] = extra[: NEXP // owners, 32 : 32 + NEXP]
    turned = extra.T
    gains = totals_ref[totals_ref.shape[0] - 1, :, width : width + 128].astype(jnp.float32).T
    rows_ref[0:2, :] = turned[16:18]
    rows_ref[2:3, :] = turned[24:25]
    rows_ref[3:4, :] = gains[0:1]
    rows_ref[4:8, :] = jnp.zeros((4, rows_ref.shape[1]), jnp.float32)
    for move in stores:
        move.wait()


def finish(resid, small, routes, codes, outs, table, totals, moved):
    rows, width = resid.shape
    owners = lax.axis_size("expert")
    share = width // owners
    vmem, hbm = pl.BlockSpec(memory_space=pltpu.VMEM), pl.BlockSpec(memory_space=pl.ANY)
    shape = lambda *dims: jax.ShapeDtypeStruct(dims, jnp.float32)
    count = len(moved)
    return pl.pallas_call(
        functools.partial(finish_kernel, owners=owners),
        in_specs=[vmem] * 8 + [hbm] * count,
        out_specs=(hbm,) * count + (vmem,) * 9,
        out_shape=(
            *(jax.ShapeDtypeStruct(item.shape, item.dtype) for item in moved),
            jax.ShapeDtypeStruct((rows, width), jnp.bfloat16),
            *(shape(share, width),) * 4,
            shape(share, NEXP), shape(NEXP // owners, NEXP), shape(share, 4), shape(8, share),
        ),
        scratch_shapes=[
            *(pltpu.VMEM(item.shape, item.dtype) for item in moved),
            pltpu.SemaphoreType.DMA((count,)),
            pltpu.SemaphoreType.DMA((count,)),
        ],
        compiler_params=params(48),
        cost_estimate=cost(8 * rows * rows * width, 8e6),
    )(resid, small, routes, codes, *outs, table, totals, *moved)


def attend_back_phase_kernel(
    grads_ref, heads_ref, outs_ref, lse_ref, bias_ref, cos_ref, sin_ref, tokens_ref, table_ref,
    query_ref, key_ref, value_ref, resid_grad_ref, out_part_ref, f_ref, gate_ref, up_ref, down_ref, gate_first,
    tokens_grad_ref, f_got, gate_got, up_got, down_got, *rest, reduce,
):
    if reduce:
        total_ref, gate_out, up_out, down_out, *rest = rest
    else:
        parts_ref, *rest = rest
    (
        d_got, back_sent, back_got, normed_turned, turned_ref, back_sum, column_ref,
        qt_ref, kt_ref, dt_ref, q_ref, k_ref, v_ref, d_ref, delta_ref, dq_ref, dk_ref, dv_ref, triangle,
        d_send, d_recv, back_send, back_recv, weight_send, weight_recv, f_send, f_recv, local_sem, early_sem, *rest,
    ) = rest
    if reduce:
        (
            parts_ref, half_got, chip_got, chip_sum, ring_got, ring_sum, all_got,
            half_send, half_recv, chip_send, chip_recv, ring_send, ring_recv, all_send, all_recv,
            gate_work, gate_sums, up_sums, gate_wide, down_work, down_sums, down_wide, work_sem, wide_sem,
        ) = rest
    chunks, owners, _, rows = grads_ref.shape
    width = tokens_ref.shape[1]
    copies = gate_ref.shape[0]
    member, xy, core = (lax.axis_index(name) for name in ("expert", "xy", "core"))
    place = xy * 2 + core
    ring, others, planes = ring_partners(owners), copy_partners(copies), plane_partners(owners)
    greet([item[2] for item in planes], [item[2] for item in others])

    d_groups = []
    for j in range(chunks):
        local = pltpu.make_async_copy(grads_ref.at[j, member], d_got.at[j, member], local_sem.at[j])
        local.start()
        group = []
        for step, index, device in ring:
            copy = remote(
                grads_ref.at[j, index], d_got.at[j, member], d_send.at[j, step - 1], d_recv.at[j, step - 1], device
            )
            copy.start()
            group.append(copy)
        d_groups.append((local, group))

    inputs = tokens_ref[...].astype(jnp.float32)
    inverse = lax.rsqrt(jnp.mean(inputs * inputs, -1, keepdims=True) + epsilon)
    normed_turned[...] = (inputs * inverse * table_ref[0:1, :]).T.astype(jnp.bfloat16)
    share = width // owners
    part_shape = (owners, share // 48, 48)

    def fill(p, values, begin, size):
        if reduce:
            parts_ref[p, :, :, :, begin : begin + size] = values.reshape(*part_shape, size)
        else:
            parts_ref[p, :, begin : begin + size] = values

    columns_total = parts_ref.shape[-1]
    early = [
        pltpu.make_async_copy(resid_grad_ref, tokens_grad_ref, early_sem.at[0]),
        pltpu.make_async_copy(out_part_ref, parts_ref.at[0], early_sem.at[1]),
    ]
    for copy in early:
        copy.start()
    fill(chunks, jnp.zeros((width, 128), jnp.bfloat16), width + 128, columns_total - width - 128)

    stages = {}

    def half_of(p):
        return (columns_total if p in (0, chunks) else width) // 2

    def over_cores(p):
        half = half_of(p)
        away = pl.ds(pl.multiple_of((1 - core) * half, 128), half)
        copy = remote(
            parts_ref.at[p, :, :, :, away], half_got.at[p, :, :, :, pl.ds(0, half)], half_send.at[p], half_recv.at[p], {"core": 1 - core}
        )
        copy.start()
        stages[p, 0] = [copy]

    def over_chips(p):
        for copy in stages[p, 0]:
            copy.wait_recv()
        half = half_of(p)
        mine, near = pl.ds(pl.multiple_of(core * half, 128), half), pl.ds(0, half)
        half_got[p, :, :, :, near] = (
            parts_ref[p, :, :, :, mine].astype(jnp.float32) + half_got[p, :, :, :, near].astype(jnp.float32)
        ).astype(jnp.bfloat16)
        stages[p, 1] = []
        for step in (3, 1, 2):
            index = lax.rem(xy + step, 4)
            copy = remote(
                half_got.at[p, :, index, :, near], chip_got.at[p, xy, :, :, near], chip_send.at[p, step - 1], chip_recv.at[p, step - 1],
                {"xy": index},
            )
            copy.start()
            stages[p, 1].append(copy)
        chip_got[p, xy, :, :, near] = half_got[p, :, xy, :, near]

    def over_owners(p):
        for copy in stages[p, 1]:
            copy.wait_recv()
        near = pl.ds(0, half_of(p))
        chip_sum[p, :, :, near] = jnp.sum(chip_got[p, :, :, :, near].astype(jnp.float32), 0).astype(jnp.bfloat16)
        stages[p, 2] = []
        for step, index, device in ring:
            copy = remote(
                chip_sum.at[p, index, :, near], ring_got.at[p, member, :, near], ring_send.at[p, step - 1], ring_recv.at[p, step - 1],
                device,
            )
            copy.start()
            stages[p, 2].append(copy)
        ring_got[p, member, :, near] = chip_sum[p, member, :, near]

    def to_copies(p):
        for copy in stages[p, 2]:
            copy.wait_recv()
        half = half_of(p)
        mine, near = pl.ds(pl.multiple_of(core * half, 128), half), pl.ds(0, half)
        ring_sum[p, :, near] = jnp.sum(ring_got[p, :, :, near].astype(jnp.float32), 0).astype(jnp.bfloat16)
        stages[p, 3] = []
        for step, _, device in others:
            copy = remote(
                ring_sum.at[p, :, near], all_got.at[p, xy, :, mine], all_send.at[p, step - 1], all_recv.at[p, step - 1], device
            )
            copy.start()
            stages[p, 3].append(copy)
        all_got[p, xy, :, mine] = ring_sum[p, :, near]

    def advance(*pairs):
        if reduce:
            for stage, p in pairs:
                (over_cores, over_chips, over_owners, to_copies)[stage](p)

    for copy in early:
        copy.wait()
    advance((0, 0))

    background = []

    pieces = ((gate_ref, gate_got), (up_ref, up_got), (down_ref, down_got))

    def send_experts():
        for i, (source, target) in enumerate(pieces):
            local = pltpu.make_async_copy(source.at[place], target.at[place], weight_send.at[i, 0])
            local.start()
            background.append(local.wait)
            for step, index, device in others:
                copy = remote(
                    source.at[2 * device["xy"] + device["core"]], target.at[place],
                    weight_send.at[i, step], weight_recv.at[i, step], device,
                )
                copy.start()
                background.append(copy.wait)

    beside, behind, across = plane_chips(xy)
    landed = {}

    def relay(i, source, landing, device):
        target = landing_ref(i, landing)
        copy = remote(source, target, weight_send.at[i, landing], weight_recv.at[i, landing], device)
        copy.start()
        landed[i, landing] = copy

    def landing_ref(i, landing):
        return gate_first.at[landing] if i == 0 and landing < 4 else pieces[i][1].at[landing]

    def arrive(i, *landings):
        for landing in landings:
            if (i, landing) in landed:
                landed[i, landing].wait_recv()

    def first_hop(i):
        for piece, landing, chip in first_hops(beside, behind, across):
            relay(i, pieces[i][0].at[piece], landing, {"xy": chip})

    def buffers(i):
        if i < 2:
            return gate_work, (gate_sums, up_sums)[i], gate_wide, (gate_out, up_out)[i]
        return down_work, down_sums, down_wide, down_out

    def load(i, items):
        work = buffers(i)[0]
        loads = [pltpu.make_async_copy(ref, work.at[n], work_sem.at[n]) for n, ref in enumerate(items)]
        for item in loads:
            item.start()
        for item in loads:
            item.wait()

    def second_hop(i):
        source = pieces[i][0]
        work, sums = buffers(i)[:2]
        arrive(i, 2, 3)
        load(i, (source.at[behind * 2], landing_ref(i, 2), source.at[beside * 2 + 1], landing_ref(i, 3)))
        for n, device in enumerate(({"xy": behind}, {"xy": beside})):
            sums[n] = (work[2 * n].astype(jnp.float32) + work[2 * n + 1].astype(jnp.float32)).astype(jnp.bfloat16)
            relay(i, sums.at[n], 4 + n, device)

    def core_hop(i):
        source = pieces[i][0]
        work, sums, wide, out = buffers(i)
        arrive(i, 0, 1, 4, 5)
        got = [landing_ref(i, landing) for landing in (0, 4, 1, 5)]
        load(i, (source.at[xy * 2], got[0], got[1], source.at[xy * 2 + 1], got[2], got[3]))
        if i == 1:
            store(0).wait()
        totals = [jnp.sum(work[3 * n : 3 * n + 3].astype(jnp.float32), 0) for n in range(2)]
        wide[core] = jnp.where(core == 0, totals[0], totals[1])
        sums[2] = jnp.where(core == 0, totals[1], totals[0]).astype(jnp.bfloat16)
        relay(i, sums.at[2], 6, {"core": 1 - core})

    def store(i):
        wide, out = buffers(i)[2:]
        return pltpu.make_async_copy(wide, out, wide_sem.at[i])

    def finish(i):
        work, sums, wide, out = buffers(i)
        arrive(i, 6)
        load(i, (landing_ref(i, 6),))
        wide[1 - core] = work[0].astype(jnp.float32)
        store(i).start()

    if reduce:
        for i in (1, 2):
            first_hop(i)
    else:
        send_experts()

    def head(j):
        local, group = d_groups[j]
        local.wait()
        for copy in group:
            copy.wait_recv()
        attend_back_head(
            bias_ref, cos_ref, sin_ref, heads_ref.at[j], outs_ref.at[j], lse_ref.at[j : j + 1], d_got.at[j],
            back_sent.at[j], qt_ref, kt_ref, dt_ref, q_ref, k_ref, v_ref, d_ref, delta_ref, dq_ref, dk_ref, dv_ref,
            triangle,
        )
        local = pltpu.make_async_copy(back_sent.at[j, member], back_got.at[j, member], local_sem.at[chunks + j])
        local.start()
        group = []
        for step, index, device in ring:
            copy = remote(
                back_sent.at[j, index], back_got.at[j, member],
                back_send.at[j, step - 1], back_recv.at[j, step - 1], device,
            )
            copy.start()
            group.append(copy)
        return local, group

    span_width = owners * HEAD_DIM

    def weights_of(j, group):
        local, copies_in = group
        local.wait()
        for copy in copies_in:
            copy.wait_recv()
        for i in range(3):
            for z in range(owners):
                row = i * span_width + z * HEAD_DIM
                turned_ref[row : row + HEAD_DIM, :] = back_got[j, z, i * HEAD_DIM : (i + 1) * HEAD_DIM]
        total = None
        for i, weight in enumerate((query_ref, key_ref, value_ref)):
            term = dot_nn(weight[:, j * span_width : (j + 1) * span_width], turned_ref[i * span_width : (i + 1) * span_width, :])
            total = term if total is None else total + term
        back_sum[...] = total if j == 0 else back_sum[...] + total
        column = jnp.sum(total * normed_turned[...].astype(jnp.float32), -1, keepdims=True)
        column_ref[...] = column if j == 0 else column_ref[...] + column
        if j == chunks - 1:
            fill(chunks, jnp.broadcast_to(column_ref[...], (width, 128)).astype(jnp.bfloat16), width, 128)
        fill(j + 1, dot_nt(normed_turned[...], turned_ref[...]).astype(jnp.bfloat16), 0, 3 * span_width)

    def send_f():
        expert = member * 2 + core
        local = pltpu.make_async_copy(f_ref.at[expert], f_got.at[expert], f_send.at[0])
        local.start()
        background.append(local.wait)
        for step, index, device in planes:
            copy = remote(f_ref.at[index], f_got.at[expert], f_send.at[step], f_recv.at[step], device)
            copy.start()
            background.append(copy.wait)

    def expert_step(step, i):
        if reduce:
            step(i)

    groups = [head(0)]
    expert_step(second_hop, 0)
    groups.append(head(1))
    advance((1, 0))
    expert_step(second_hop, 1)
    groups.append(head(2))
    expert_step(second_hop, 2)
    advance((2, 0))
    weights_of(0, groups[0])
    advance((0, 1), (3, 0))
    expert_step(core_hop, 0)
    weights_of(1, groups[1])
    advance((0, 2), (1, 1))
    expert_step(finish, 0)
    expert_step(core_hop, 1)
    advance((1, 2), (2, 1))
    weights_of(2, groups[2])
    advance((0, 3))
    send_f()
    normed = inputs * inverse
    first_grads = back_sum[...].T
    advance((1, 3))
    expert_step(core_hop, 2)
    advance((2, 2), (3, 1))
    expert_step(finish, 1)
    scaled = first_grads * table_ref[0:1, :]
    tokens_grad_ref[...] += inverse * (scaled - normed * jnp.mean(scaled * normed, -1, keepdims=True))
    advance((2, 3), (3, 2))
    expert_step(finish, 2)
    advance((3, 3))
    if reduce:
        for p in range(chunks + 1):
            for copy in stages[p, 3]:
                copy.wait_recv()
            size = 2 * half_of(p)
            total_ref[p, :, :size] = all_got[p, :, :, :size].reshape(share, size)
            for stage in range(4):
                for copy in stages[p, stage]:
                    copy.wait_send()
        for copy in landed.values():
            copy.wait_send()
        for i in range(1, 3):
            store(i).wait()
    for local, group in d_groups + groups:
        for copy in group:
            copy.wait_send()
    for wait in background:
        wait()


def attend_back_phase(
    grads, heads, outs, lse, bias, cosine, sine, tokens, table, weights, resid_grads, out_part, f, pieces, gate_first, copies
):
    chunks, owners, _, rows = grads.shape
    width = tokens.shape[1]
    length = owners * rows
    head = (chunks, owners, 3 * HEAD_DIM, rows)
    columns = out_part.shape[1]
    share = width // owners
    total = chunks + 1
    reduce = relayed(copies)
    vmem, hbm = pl.BlockSpec(memory_space=pltpu.VMEM), pl.BlockSpec(memory_space=pl.ANY)
    gate_shape, down_shape = pieces[0].shape[1:], pieces[2].shape[1:]
    turned = pltpu.VMEM((HEAD_DIM, length), jnp.bfloat16)
    plain = pltpu.VMEM((length, HEAD_DIM), jnp.bfloat16)
    wide = pltpu.VMEM((length, HEAD_DIM), jnp.float32)
    sems = lambda *shape: pltpu.SemaphoreType.DMA(shape)
    scratch = [
        pltpu.VMEM(grads.shape, jnp.bfloat16),
        pltpu.VMEM(head, jnp.bfloat16),
        pltpu.VMEM(head, jnp.bfloat16),
        pltpu.VMEM((width, rows), jnp.bfloat16),
        pltpu.VMEM((3 * owners * HEAD_DIM, rows), jnp.bfloat16),
        pltpu.VMEM((width, rows), jnp.float32),
        pltpu.VMEM((width, 1), jnp.float32),
        turned, turned, turned, plain, plain, plain, plain,
        pltpu.VMEM((1, length), jnp.float32),
        pltpu.VMEM((HEAD_DIM, length), jnp.float32),
        wide, wide,
        pltpu.VMEM((TILE, TILE), jnp.float32),
        *(sems(chunks, owners - 1),) * 4,
        sems(3, copies), sems(3, copies), sems(2 * owners), sems(2 * owners), sems(2 * chunks), sems(2),
    ]
    if reduce:
        half = columns // 2
        low = lambda *shape: pltpu.VMEM(shape, jnp.bfloat16)
        scratch += [
            low(total, owners, 4, 48, columns),
            low(total, owners, 4, 48, half),
            low(total, 4, owners, 48, half),
            low(total, owners, 48, half),
            low(total, owners, 48, half),
            low(total, 48, half),
            low(total, 4, 48, columns),
            sems(total), sems(total), sems(total, 3), sems(total, 3),
            sems(total, owners - 1), sems(total, owners - 1), sems(total, copies - 1), sems(total, copies - 1),
            low(6, *gate_shape), low(3, *gate_shape), low(3, *gate_shape), pltpu.VMEM((2, *gate_shape), jnp.float32),
            low(6, *down_shape), low(3, *down_shape), pltpu.VMEM((2, *down_shape), jnp.float32),
            sems(6), sems(3),
        ]
        out_part = out_part.reshape(owners, 4, 48, columns)
        last_specs = (vmem, hbm, hbm, hbm)
        last_shapes = (
            jax.ShapeDtypeStruct((total, share, columns), jnp.bfloat16),
            *(jax.ShapeDtypeStruct((2, *piece.shape[1:]), jnp.float32) for piece in pieces),
        )
    else:
        last_specs, last_shapes = (vmem,), (jax.ShapeDtypeStruct((total, width, columns), jnp.bfloat16),)
    tokens_grad, f_got, gate_got, up_got, down_got, totals, *sums = pl.pallas_call(
        functools.partial(attend_back_phase_kernel, reduce=reduce),
        in_specs=[vmem] * 12 + [hbm] * 7,
        out_specs=(vmem, hbm, hbm, hbm, hbm, *last_specs),
        out_shape=(
            jax.ShapeDtypeStruct((rows, width), jnp.float32),
            jax.ShapeDtypeStruct(f.shape, f.dtype),
            *(jax.ShapeDtypeStruct(piece.shape, piece.dtype) for piece in pieces),
            *last_shapes,
        ),
        scratch_shapes=scratch,
        compiler_params=pltpu.CompilerParams(vmem_limit_bytes=63 * MIB, collective_id=3, has_side_effects=True),
        cost_estimate=cost(2e10, 5e7),
    )(grads, heads, outs, lse, bias, cosine, sine, tokens, table, *weights, resid_grads, out_part, f, *pieces, gate_first)
    if not reduce:
        totals = lax.psum_scatter(totals, "expert", scatter_dimension=1, tiled=True)
        totals = lax.psum(totals, ("xy", "core"))
        sums = [
            jnp.sum(got.reshape(copies // 2, 2, *got.shape[1:]).astype(jnp.float32), 0)
            for got in (gate_got, up_got, down_got)
        ]
    return (tokens_grad, f_got, totals, *sums)


def per_device(
    tokens, prior_logits, routes, parents, cotangent, query_weight, key_weight, value_weight, out_weight,
    attention_gain, expert_gain, router_weight, prior_weight, constant_weight, constant_vector,
    gate_weight, up_weight, down_weight,
):
    owners = lax.axis_size("expert")
    member = lax.axis_index("expert")
    tokens, prior, routes, grad = tokens[0], prior_logits[0], routes[0], cotangent[0]
    rows, width = tokens.shape
    copies = lax.axis_size("xy") * lax.axis_size("core")
    chunks = width // HEAD_DIM // owners
    zeros = jnp.zeros((4, width), jnp.float32)
    table = jnp.concatenate([attention_gain[None], expert_gain[None], constant_vector, zeros], 0)
    qkv_weights = (query_weight, key_weight, value_weight)
    attended, logs, bias, cosine, sine, codes, codes_row, heads, outs, gate, up, down = attend_phase(
        tokens, table, qkv_weights, parents, routes, (gate_weight, up_weight, down_weight), copies
    )
    attended = attended.reshape(width, rows)
    gate, up, down = (full.reshape(-1, full.shape[-1]) for full in (gate, up, down))
    resid, small, *x_out, mixer = middle(
        tokens, attended, out_weight, table, router_weight, constant_weight, prior, prior_weight, routes, codes_row
    )
    backs, dots, fa, fb, *grads = expert_phase(x_out, small, grad, codes_row, gate, up, down)
    pieces = [item.reshape(copies, -1, item.shape[-1]) for item in grads]
    dots = dots[:, :, 0, : rows // NFFN].reshape(1, 2 * rows)
    resid_grads, grads_out, out_part, prior_grad, fa, gate_first = turn(
        resid, small, grad, prior, routes, codes, backs.reshape(2 * rows, width), dots, table, mixer, prior_weight,
        out_weight, attended, fa, pieces[0],
    )
    tokens_grad, fb, totals, *sums = attend_back_phase(
        grads_out.reshape(chunks, owners, HEAD_DIM, rows), heads, outs, logs, bias, cosine, sine, tokens,
        table, qkv_weights, resid_grads, out_part, fb, pieces, gate_first, copies,
    )
    fs = [f.reshape(rows, width) for f in (fa, fb)]
    (
        tokens_grad, gate_part, up_part, down_part, result, *qkv_out_grads, router_grad, prior_weight_grad,
        constant_weight_grad, row_grads,
    ) = finish(resid, small, routes, codes, fs, table, totals, (tokens_grad, *sums))
    share = width // owners
    own_gain = lax.dynamic_slice_in_dim(attention_gain, member * share, share)
    return (
        result[None],
        tokens_grad[None],
        prior_grad[None],
        *qkv_out_grads,
        row_grads[3] / own_gain,
        row_grads[2],
        router_grad,
        prior_weight_grad,
        constant_weight_grad,
        row_grads[:2],
        gate_part,
        up_part,
        down_part,
    )


def solution(mesh):
    owners, copies = mesh.shape["expert"], mesh.shape["dp"]
    cores = 2
    mesh = Mesh(mesh.devices.reshape(owners, copies // cores, cores), ("expert", "xy", "core"))
    dp = ("xy", "core")
    rows = P(dp, "expert", None)
    shard = P("expert", dp, None)
    in_specs = (rows, rows, rows, P(dp, None), rows) + (P(),) * 10 + (shard,) * 3
    out_specs = (
        (rows,) * 3
        + (P("expert", None),) * 4
        + (P("expert"),) * 2
        + (P("expert", None),) * 3
        + (P(None, "expert"),)
        + (shard,) * 3
    )
    return jax.shard_map(per_device, mesh=mesh, in_specs=in_specs, out_specs=out_specs, check_vma=False)
```

```python
import functools

import jax
import jax.numpy as jnp
from jax import lax
from jax.experimental import pallas as pl
from jax.experimental.pallas import tpu as pltpu
from jax.sharding import Mesh
from jax.sharding import PartitionSpec as P

NFFN = 8
NEXP = 12
SEG = 128
HEAD_DIM = 64
TRUNK = 1024
TILE = 2 * SEG
LOG2E = 1.4426950408889634
masked_score = -1e30
MIB = 2**20
epsilon = 1e-06
precise = lax.Precision.HIGHEST


def dot_nt(left, right):
    return lax.dot_general(left, right, (((1,), (1,)), ((), ())), preferred_element_type=jnp.float32)


def dot_nn(left, right):
    return jnp.dot(left, right, preferred_element_type=jnp.float32)


def tile_parts(tile, start):
    trunk_tiles = TRUNK // TILE
    if tile is not None and tile < trunk_tiles:
        return [(k * TILE, False, k == tile) for k in range(tile + 1)]
    parts = [(k * TILE, False, False) for k in range(trunk_tiles)]
    branch_tiles = 2
    if tile is None:
        parts += [(TRUNK + k * TILE, True, False) for k in range(branch_tiles)]
    else:
        parts += [(TRUNK + k * TILE, True, False) for k in range(tile - trunk_tiles)]
    parts += [(start, True, True)]
    return parts


def causal_bias():
    key_ids = lax.broadcasted_iota(jnp.int32, (TILE, TILE), 0)
    query_ids = lax.broadcasted_iota(jnp.int32, (TILE, TILE), 1)
    return jnp.where(key_ids <= query_ids, 0.0, masked_score).astype(jnp.float32)


def part_scores(scores, part, columns, bias_ref, triangle):
    first, by_lineage, causal = part
    if by_lineage:
        segment = 1 + (first - TRUNK) // SEG
        rows = [bias_ref[pl.ds(segment + i, 1), columns] for i in range(TILE // SEG)]
        scores = jnp.concatenate(
            [scores[i * SEG : (i + 1) * SEG] + rows[i] for i in range(TILE // SEG)], 0
        )
    if causal:
        scores = scores + triangle[...]
    return scores


def for_tiles(length, body):
    trunk_tiles = TRUNK // TILE
    for tile in range(trunk_tiles + 2):
        body(tile, tile * TILE)
    first_leaf = trunk_tiles + 2

    @pl.loop(first_leaf, length // TILE)
    def _(tile):
        body(None, pl.multiple_of(tile * TILE, TILE))


def attend_head(bias_ref, qkv_ref, out_ref, lse_ref, q_ref, k_ref, v_ref, o_ref, s_ref, triangle):
    sources, _, rows = qkv_ref.shape
    length = sources * rows
    factor = HEAD_DIM ** (-0.5) * LOG2E
    triangle[...] = causal_bias()
    extra = lax.broadcasted_iota(jnp.int32, (16, length), 0)
    v_ref[HEAD_DIM:, :] = jnp.where(extra == 0, 1.0, 0.0).astype(jnp.bfloat16)
    for z in range(sources):
        span = pl.ds(z * rows, rows)
        q_ref[:, span] = qkv_ref[z, :HEAD_DIM]
        k_ref[span, :] = qkv_ref[z, HEAD_DIM : 2 * HEAD_DIM].astype(jnp.float32).T.astype(jnp.bfloat16)
        v_ref[:HEAD_DIM, span] = qkv_ref[z, 2 * HEAD_DIM :]

    def body(tile, start):
        columns = pl.ds(start, TILE)
        parts = tile_parts(tile, start)
        query = q_ref[:, columns]
        peak = None
        for i, part in enumerate(parts):
            scores = dot_nn(k_ref[pl.ds(part[0], TILE), :], query)
            scores = part_scores(scores, part, columns, bias_ref, triangle)
            s_ref[i * TILE : (i + 1) * TILE, :] = scores
            top = jnp.max(scores, 0, keepdims=True)
            peak = top if peak is None else jnp.maximum(peak, top)
        shift = peak * factor
        total = None
        for i, part in enumerate(parts):
            weights = jnp.exp2(s_ref[i * TILE : (i + 1) * TILE, :] * factor - shift)
            term = dot_nn(v_ref[:, pl.ds(part[0], TILE)], weights.astype(jnp.bfloat16))
            total = term if total is None else total + term
        norm = total[HEAD_DIM : HEAD_DIM + 1]
        o_ref[:, columns] = (total[:HEAD_DIM] / norm).astype(jnp.bfloat16)
        lse_ref[:, columns] = shift + jnp.log2(norm)

    for_tiles(length, body)
    for z in range(sources):
        out_ref[z] = o_ref[:, pl.ds(z * rows, rows)]


def attend_back_head(
    bias_ref, cos_ref, sin_ref, qkv_ref, out_ref, lse_ref, grad_ref, back_ref,
    qt_ref, kt_ref, dt_ref, q_ref, k_ref, v_ref, d_ref, delta_ref, dq_ref, dk_ref, dv_ref, triangle,
):
    sources, _, rows = qkv_ref.shape
    length = sources * rows
    scaling = HEAD_DIM ** (-0.5)
    factor = scaling * LOG2E
    triangle[...] = causal_bias()

    def turned(values):
        return values.astype(jnp.float32).T.astype(jnp.bfloat16)

    for z in range(sources):
        span = pl.ds(z * rows, rows)
        query, key, value = (qkv_ref[z, i * HEAD_DIM : (i + 1) * HEAD_DIM] for i in range(3))
        grad = grad_ref[z]
        qt_ref[:, span] = query
        kt_ref[:, span] = key
        dt_ref[:, span] = grad
        q_ref[span, :] = turned(query)
        k_ref[span, :] = turned(key)
        v_ref[span, :] = turned(value)
        d_ref[span, :] = turned(grad)
        delta_ref[:, span] = jnp.sum(
            grad.astype(jnp.float32) * out_ref[z].astype(jnp.float32), 0, keepdims=True
        )
    dk_ref[...] = jnp.zeros_like(dk_ref)
    dv_ref[...] = jnp.zeros_like(dv_ref)

    def body(tile, start):
        columns = pl.ds(start, TILE)
        query_t, grad_t = qt_ref[:, columns], dt_ref[:, columns]
        query, grad = q_ref[columns, :], d_ref[columns, :]
        lse, delta = lse_ref[:, columns], delta_ref[:, columns]
        total = None
        for part in tile_parts(tile, start):
            span = pl.ds(part[0], TILE)
            scores = dot_nn(k_ref[span, :], query_t) * factor - lse
            scores = part_scores(scores, part, columns, bias_ref, triangle)
            weights = jnp.exp2(scores)
            weight_grads = dot_nn(v_ref[span, :], grad_t)
            score_grads = (weights * (weight_grads - delta)).astype(jnp.bfloat16)
            dv_ref[span, :] += dot_nn(weights.astype(jnp.bfloat16), grad)
            dk_ref[span, :] += dot_nn(score_grads, query)
            term = dot_nn(kt_ref[:, span], score_grads)
            total = term if total is None else total + term
        dq_ref[:, columns] = total

    for_tiles(length, body)
    half = HEAD_DIM // 2
    for z in range(sources):
        span = pl.ds(z * rows, rows)
        cosine, sine = cos_ref[:, span], sin_ref[:, span]
        for i, values in enumerate((dq_ref[:, span], dk_ref[span, :].T)):
            values = values * scaling
            first, second = values[:half], values[half:]
            back_ref[z, i * HEAD_DIM : (i + 1) * HEAD_DIM] = jnp.concatenate(
                [first * cosine + second * sine, second * cosine - first * sine], 0
            ).astype(jnp.bfloat16)
        back_ref[z, 2 * HEAD_DIM :] = dv_ref[span, :].T.astype(jnp.bfloat16)


def params(limit):
    return pltpu.CompilerParams(vmem_limit_bytes=limit * MIB)


def cost(flops, moved):
    return pl.CostEstimate(flops=int(flops), bytes_accessed=int(moved), transcendentals=0)


def greet(ring, copies):
    barrier = pltpu.get_barrier_semaphore()
    for target in ring + copies:
        pl.semaphore_signal(barrier, inc=1, device_id=target, device_id_type=pl.DeviceIdType.MESH)
    pl.semaphore_wait(barrier, len(ring) + len(copies))


def ring_partners(owners):
    member = lax.axis_index("expert")
    result = []
    for step in sorted(range(1, owners), key=lambda k: -min(k, owners - k)):
        index = lax.rem(member + step, owners)
        result.append((step, index, {"expert": index}))
    return result


def copy_partners(total):
    place = lax.axis_index("xy") * 2 + lax.axis_index("core")
    result = []
    for step in sorted(range(1, total), key=lambda k: -(k % 8 in (6, 2, 4))):
        index = lax.rem(place + step, total)
        result.append((step, lax.rem(index, 2), {"xy": index // 2, "core": lax.rem(index, 2)}))
    return result


def plane_chips(xy):
    return xy + 1 - 2 * lax.rem(xy, 2), lax.rem(xy + 2, 4), 3 - xy


def first_hops(beside, behind, across):
    return (
        (across * 2, 2, beside), (across * 2 + 1, 3, behind), (beside * 2, 0, beside), (behind * 2 + 1, 1, behind),
    )


def relayed(copies):
    return copies == 8


def remote(source, target, send, receive, device):
    return pltpu.make_async_remote_copy(
        src_ref=source, dst_ref=target, send_sem=send, recv_sem=receive,
        device_id=device, device_id_type=pl.DeviceIdType.MESH,
    )


def reach_of(parents):
    shape = (128, 128)
    one, two = lax.broadcasted_iota(jnp.int32, shape, 0), lax.broadcasted_iota(jnp.int32, shape, 1)
    count = parents.shape[1]
    none = lambda size: jnp.full((1, size), -1, jnp.int32)
    parent_row = jnp.concatenate([none(1), parents, none(127 - count)], 1)
    reach = jnp.where((one == two) | (one == parent_row), 1.0, 0.0).astype(jnp.bfloat16)
    for _ in range(3):
        reach = jnp.minimum(dot_nn(reach, reach), 1.0).astype(jnp.bfloat16)
    return reach


def place_tables(reach, first, size):
    ids = lax.broadcasted_iota(jnp.int32, (1, size), 1) + first
    later = ids - TRUNK
    segment = jnp.where(later < 0, 0, 1 + lax.shift_right_arithmetic(later, 7))
    inside = jnp.where(later < 0, later, (later & (SEG - 1)) - SEG)
    own = jnp.where(segment == lax.broadcasted_iota(jnp.int32, (128, size), 0), 1.0, 0.0).astype(jnp.bfloat16)
    seen = dot_nn(reach[:16], own)
    index = lax.broadcasted_iota(jnp.int32, (16, 1), 0)
    lengths = jnp.where(index == 0, float(TRUNK), float(SEG))
    places = jnp.sum(seen * lengths, 0, keepdims=True) + inside.astype(jnp.float32)
    turn = lax.broadcasted_iota(jnp.int32, (HEAD_DIM // 2, 1), 0).astype(jnp.float32)
    angles = jnp.exp(turn * (-2.0 / HEAD_DIM * 9.210340371976184)) * places
    return seen, jnp.cos(angles), jnp.sin(angles)


def slot_codes(routes_ref, codes_ref, codes_row_ref):
    rows = routes_ref.shape[1]
    half_slots = rows // NFFN
    turned = jnp.concatenate([routes_ref[...].astype(jnp.float32), jnp.zeros((126, rows), jnp.float32)], 0).T
    routes = turned.astype(jnp.int32)
    lanes = lax.broadcasted_iota(jnp.int32, (rows, 128), 1)
    matches = [
        jnp.where((lanes == routes[:, c : c + 1]) & (lanes < NFFN), 1.0, 0.0).astype(jnp.float32) for c in range(2)
    ]
    square = (rows, rows)
    earlier = lax.broadcasted_iota(jnp.int32, square, 0) > lax.broadcasted_iota(jnp.int32, square, 1)
    before = dot_nn(
        jnp.where(earlier, 1.0, 0.0).astype(jnp.bfloat16), (matches[0] + matches[1]).astype(jnp.bfloat16)
    )
    codes = jnp.zeros((rows, 128), jnp.float32)
    for c in range(2):
        rank = jnp.sum(matches[c] * before, -1, keepdims=True)
        route = routes[:, c : c + 1].astype(jnp.float32)
        late = jnp.where(rank >= half_slots, float((NFFN - 1) * half_slots), 0.0)
        code = jnp.where(route < NFFN, route * half_slots + rank + late, float(4 * rows))
        codes = jnp.where(lanes == c, code, jnp.where(lanes == 2 + c, route, codes))
    codes_ref[...] = codes.astype(jnp.int32)
    codes_row_ref[...] = codes.T[:8].astype(jnp.int32)


def attend_phase_kernel(
    tokens_ref, table_ref, query_ref, key_ref, value_ref, parents_ref, routes_ref, gate_ref, up_ref, down_ref,
    attended_ref, lse_ref, bias_ref, cos_ref, sin_ref, codes_ref, codes_row_ref, heads_ref, outs_ref,
    gate_full, up_full, down_full,
    normed_ref, qkv_sent, qkv_got, out_sent, out_got, q_ref, k_ref, v_ref, o_ref, s_ref, triangle,
    qkv_send, qkv_recv, out_send, out_recv, weight_send, weight_recv, local_sem,
):
    chunks, owners, _, rows = qkv_sent.shape
    member = lax.axis_index("expert")
    copies = gate_full.shape[0]
    ring, others = ring_partners(owners), copy_partners(copies)
    greet([item[2] for item in ring], [item[2] for item in others])
    weights = ((gate_ref, gate_full), (up_ref, up_full), (down_ref, down_full))
    place = lax.axis_index("xy") * 2 + lax.axis_index("core")
    core = lax.axis_index("core")
    started = []

    relays = relayed(copies)
    xy = lax.axis_index("xy")
    beside, behind, across = plane_chips(xy)
    arrivals = {}

    def send_weight(i):
        shard, full = weights[i]
        local = pltpu.make_async_copy(shard.at[core], full.at[place], weight_send.at[i, 0])
        local.start()
        started.append(local.wait)
        if relays:
            targets = [(2, beside, 0), (4, behind, 0), (2, beside, 1), (4, behind, 1)]
            targets = [(1, 1 - core, {"core": 1 - core})] + [
                (base + core, other, {"xy": chip, "core": other}) for base, chip, other in targets
            ]
            for n, (slot, other, device) in enumerate(targets):
                copy = remote(
                    shard.at[other], full.at[place], weight_send.at[i, 1 + n], weight_recv.at[i, slot], device
                )
                copy.start()
                started.append(copy.wait_send)
            for slot in range(1, 8):
                arrivals[i, slot] = remote(
                    shard.at[core], full.at[place], weight_send.at[i, 0], weight_recv.at[i, slot], {"core": 1 - core}
                )
        else:
            for step, other_core, device in others:
                copy = remote(
                    shard.at[other_core], full.at[place], weight_send.at[i, step], weight_recv.at[i, step], device
                )
                copy.start()
                started.append(copy.wait)

    def relay_weight(i):
        full = weights[i][1]
        for slot, piece, chip, landing in ((4, behind * 2, beside, 6), (3, beside * 2 + 1, behind, 7)):
            arrivals.pop((i, slot)).wait_recv()
            copy = remote(
                full.at[piece], full.at[piece], weight_send.at[i, landing], weight_recv.at[i, landing], {"xy": chip}
            )
            copy.start()
            started.append(copy.wait_send)

    for i in range(3):
        send_weight(i)

    inputs = tokens_ref[...].astype(jnp.float32)
    inverse = lax.rsqrt(jnp.mean(inputs * inputs, -1, keepdims=True) + epsilon)
    normed_ref[...] = (inputs * inverse * table_ref[0:1, :]).astype(jnp.bfloat16)
    reach = reach_of(parents_ref[...])
    _, cosine, sine = place_tables(reach, member * rows, rows)
    half = HEAD_DIM // 2
    span_width = owners * HEAD_DIM
    qkv_copies = []
    for j in range(chunks):
        for i, weight in enumerate((query_ref, key_ref, value_ref)):
            turned = dot_nn(normed_ref[...], weight[:, j * span_width : (j + 1) * span_width]).T
            base = i * HEAD_DIM
            for z in range(owners):
                first = turned[z * HEAD_DIM : z * HEAD_DIM + half]
                second = turned[z * HEAD_DIM + half : (z + 1) * HEAD_DIM]
                if i < 2:
                    first, second = first * cosine - second * sine, second * cosine + first * sine
                qkv_sent[j, z, base : base + half] = first.astype(jnp.bfloat16)
                qkv_sent[j, z, base + half : base + HEAD_DIM] = second.astype(jnp.bfloat16)
        local = pltpu.make_async_copy(qkv_sent.at[j, member], qkv_got.at[j, member], local_sem.at[j])
        local.start()
        group = []
        for step, index, device in ring:
            copy = remote(
                qkv_sent.at[j, index], qkv_got.at[j, member],
                qkv_send.at[j, step - 1], qkv_recv.at[j, step - 1], device,
            )
            copy.start()
            group.append(copy)
        qkv_copies.append((local, group))
    seen, whole_cosine, whole_sine = place_tables(reach, 0, owners * rows)
    bias_ref[...] = jnp.where(seen > 0.5, 0.0, masked_score)
    cos_ref[...] = whole_cosine
    sin_ref[...] = whole_sine
    slot_codes(routes_ref, codes_ref, codes_row_ref)

    out_copies = []
    kept = []
    for j in range(chunks):
        local, group = qkv_copies[j]
        local.wait()
        for copy in group:
            copy.wait_recv()
        keep = pltpu.make_async_copy(qkv_got.at[j], heads_ref.at[j], local_sem.at[chunks + j])
        keep.start()
        kept.append(keep)
        attend_head(
            bias_ref, qkv_got.at[j], out_sent.at[j], lse_ref.at[j : j + 1], q_ref, k_ref, v_ref, o_ref, s_ref, triangle
        )
        local = pltpu.make_async_copy(out_sent.at[j, member], out_got.at[j, member], local_sem.at[2 * chunks + j])
        local.start()
        keep = pltpu.make_async_copy(out_sent.at[j], outs_ref.at[j], local_sem.at[3 * chunks + j])
        keep.start()
        kept += [local, keep]
        for step, index, device in ring:
            copy = remote(
                out_sent.at[j, index], out_got.at[j, member],
                out_send.at[j, step - 1], out_recv.at[j, step - 1], device,
            )
            copy.start()
            out_copies.append(copy)
        if relays and j == 1:
            for i in range(3):
                relay_weight(i)
    for copy in out_copies:
        copy.wait_recv()
    for copy in kept:
        copy.wait()
    attended_ref[...] = out_got[...]
    for local, group in qkv_copies:
        for copy in group:
            copy.wait_send()
    for copy in out_copies:
        copy.wait_send()
    for copy in arrivals.values():
        copy.wait_recv()
    for wait in started:
        wait()


def attend_phase(tokens, table, weights, parents, routes, shards, copies):
    rows, width = tokens.shape
    owners = lax.axis_size("expert")
    length = rows * owners
    chunks = width // HEAD_DIM // owners
    head = (chunks, owners, 3 * HEAD_DIM, rows)
    out = (chunks, owners, HEAD_DIM, rows)
    vmem, hbm = pl.BlockSpec(memory_space=pltpu.VMEM), pl.BlockSpec(memory_space=pl.ANY)
    fulls = [jax.ShapeDtypeStruct((copies, *shard.shape[1:]), shard.dtype) for shard in shards]
    part_total = TRUNK // TILE + 3
    sems = lambda *shape: pltpu.SemaphoreType.DMA(shape)
    return pl.pallas_call(
        attend_phase_kernel,
        in_specs=[vmem] * 7 + [hbm] * 3,
        out_specs=(vmem,) * 7 + (hbm,) * 5,
        out_shape=(
            jax.ShapeDtypeStruct(out, jnp.bfloat16),
            jax.ShapeDtypeStruct((8, length), jnp.float32),
            jax.ShapeDtypeStruct((16, length), jnp.float32),
            *(jax.ShapeDtypeStruct((HEAD_DIM // 2, length), jnp.float32),) * 2,
            jax.ShapeDtypeStruct((rows, 128), jnp.int32),
            jax.ShapeDtypeStruct((8, rows), jnp.int32),
            jax.ShapeDtypeStruct(head, jnp.bfloat16),
            jax.ShapeDtypeStruct(out, jnp.bfloat16),
            *fulls,
        ),
        scratch_shapes=[
            pltpu.VMEM((rows, width), jnp.bfloat16),
            pltpu.VMEM(head, jnp.bfloat16),
            pltpu.VMEM(head, jnp.bfloat16),
            pltpu.VMEM(out, jnp.bfloat16),
            pltpu.VMEM(out, jnp.bfloat16),
            pltpu.VMEM((HEAD_DIM, length), jnp.bfloat16),
            pltpu.VMEM((length, HEAD_DIM), jnp.bfloat16),
            pltpu.VMEM((HEAD_DIM + 16, length), jnp.bfloat16),
            pltpu.VMEM((HEAD_DIM, length), jnp.bfloat16),
            pltpu.VMEM((part_total * TILE, TILE), jnp.float32),
            pltpu.VMEM((TILE, TILE), jnp.float32),
            sems(chunks, owners - 1), sems(chunks, owners - 1), sems(chunks, owners - 1), sems(chunks, owners - 1),
            sems(3, copies), sems(3, copies), sems(4 * chunks),
        ],
        compiler_params=pltpu.CompilerParams(vmem_limit_bytes=63 * MIB, collective_id=1, has_side_effects=True),
        cost_estimate=cost(1e10, 5e7),
    )(tokens, table, *weights, parents, routes, *shards)


def lane_pick(values, lanes, index):
    return jnp.sum(jnp.where(lanes == index, values, 0.0), -1, keepdims=True)


def middle_kernel(
    tokens_ref, attended_ref, out_weight_ref, table_ref, router_ref, constant_ref, prior_ref, prior_weight_ref,
    codes_ref, codes_row_ref, resid_ref, small_ref, first_ref, second_ref, mixer_ref, hidden_ref,
):
    rows, width = tokens_ref.shape
    mixer = [ref[...].astype(jnp.float32) for ref in (router_ref, constant_ref)]
    mixer_ref[...] = jnp.concatenate([*mixer, jnp.zeros((128 - NEXP - 4, width), jnp.float32)], 0).astype(jnp.bfloat16)
    missing = jnp.zeros((16 - NEXP, SEG), jnp.float32)

    @pl.loop(0, rows // SEG)
    def _(step):
        span = pl.ds(pl.multiple_of(step * SEG, SEG), SEG)
        attended = attended_ref[:, span].astype(jnp.float32).T.astype(jnp.bfloat16)
        resid = tokens_ref[span, :].astype(jnp.float32) + dot_nn(attended, out_weight_ref[...])
        inverse = lax.rsqrt(jnp.mean(resid * resid, -1, keepdims=True) + epsilon)
        hidden = (resid * inverse * table_ref[1:2, :]).astype(jnp.bfloat16)
        resid_ref[span, :] = resid
        hidden_ref[span, :] = hidden
        logits = dot_nt(hidden, mixer_ref[...])
        prior = jnp.concatenate([prior_ref[:, span], missing], 0).T[:, :NEXP]
        carried = jnp.dot(prior, prior_weight_ref[...], precision=precise, preferred_element_type=jnp.float32)
        logits = logits + jnp.concatenate([carried, jnp.zeros((SEG, 128 - NEXP), jnp.float32)], 1)
        lanes = lax.broadcasted_iota(jnp.int32, logits.shape, 1)
        routes = codes_ref[span, 2:4]
        columns = []
        pairs = [[lane_pick(logits, lanes, routes[:, c : c + 1]) for c in range(2)]]
        pairs += [[logits[:, NEXP + 2 * m + c : NEXP + 2 * m + c + 1] for c in range(2)] for m in range(2)]
        for one, two in pairs:
            peak = jnp.maximum(one, two)
            one, two = jnp.exp(one - peak), jnp.exp(two - peak)
            columns += [one / (one + two), two / (one + two)]
        columns.append(inverse)
        small = jnp.zeros_like(logits)
        for i, column in enumerate(columns):
            small = jnp.where(lanes == i, column, small)
        small_ref[span, :] = small

    slots = first_ref.shape[0]
    for half, ref in enumerate((first_ref, second_ref)):
        index = lax.broadcasted_iota(jnp.int32, (slots, rows), 0) + half * slots
        chosen = (codes_row_ref[0:1, :] == index) | (codes_row_ref[1:2, :] == index)
        ref[...] = dot_nn(chosen.astype(jnp.bfloat16), hidden_ref[...]).astype(jnp.bfloat16)


def middle(tokens, attended, out_weight, table, router, constant, prior, prior_weight, codes, codes_row):
    rows, width = tokens.shape
    slots = rows
    return pl.pallas_call(
        middle_kernel,
        out_shape=(
            jax.ShapeDtypeStruct((rows, width), jnp.float32),
            jax.ShapeDtypeStruct((rows, 128), jnp.float32),
            jax.ShapeDtypeStruct((slots, width), jnp.bfloat16),
            jax.ShapeDtypeStruct((slots, width), jnp.bfloat16),
            jax.ShapeDtypeStruct((128, width), jnp.bfloat16),
        ),
        scratch_shapes=[pltpu.VMEM((rows, width), jnp.bfloat16)],
        compiler_params=params(63),
        cost_estimate=cost(4 * rows * width * width + 4 * rows * rows * width, 1e7),
    )(tokens, attended, out_weight, table, router, constant, prior, prior_weight, codes, codes_row)


def plane_partners(owners):
    total = 2 * owners
    place = lax.axis_index("expert") * 2 + lax.axis_index("core")
    result = []
    for step in sorted(range(1, total), key=lambda k: -min(k, total - k)):
        index = lax.rem(place + step, total)
        result.append((step, index, {"expert": index // 2, "core": lax.rem(index, 2)}))
    return result


def expert_phase_kernel(
    xa_ref, xb_ref, small_ref, grad_ref, codes_ref, gate_hbm, up_hbm, down_hbm,
    back_out, dots_out, fa_out, fb_out, gate_grad, up_grad, down_grad,
    gate_ref, up_ref, down_ref, scaled_ref, d_sent, x_got, d_got, back_sent, back_got, dots_sent, dots_got,
    f_sum, back_sum, hid_ref, one_ref, two_ref, x_turned, d_turned, stage, stage_down,
    x_send, x_recv, d_send, d_recv, back_send, back_recv, dots_send, dots_recv, local_sem, stage_sem,
):
    experts, slots, width = x_got.shape[1:]
    rows = experts * slots
    units = gate_ref.shape[1]
    owners = experts // 2
    place = lax.axis_index("expert") * 2 + lax.axis_index("core")
    partners = plane_partners(owners)
    greet([item[2] for item in partners], [])
    loads = [
        pltpu.make_async_copy(source, target, local_sem.at[i])
        for i, (source, target) in enumerate(((gate_hbm, gate_ref), (up_hbm, up_ref), (down_hbm, down_ref)))
    ]
    for load in loads:
        load.start()

    def send(source, target, sends, receives, half, locals_at):
        copies = []
        local = pltpu.make_async_copy(source(place), target.at[half, place], local_sem.at[locals_at + half])
        local.start()
        for step, index, device in partners:
            copy = remote(source(index), target.at[half, place], sends.at[half, step], receives.at[half, step], device)
            copy.start()
            copies.append(copy)
        return local, copies

    def arrive(group):
        group[0].wait()
        for copy in group[1]:
            copy.wait_recv()

    x_refs = (xa_ref, xb_ref)
    x_groups = [send(lambda e, ref=ref: ref.at[e], x_got, x_send, x_recv, h, 3) for h, ref in enumerate(x_refs)]
    for c in range(2):
        scaled_ref[c * rows : (c + 1) * rows, :] = (
            small_ref[:, c : c + 1] * grad_ref[...].astype(jnp.float32)
        ).astype(jnp.bfloat16)
    d_groups = []
    for half in range(2):
        index = lax.broadcasted_iota(jnp.int32, (rows, rows), 0) + half * rows
        chosen = jnp.concatenate([(codes_ref[c : c + 1, :] == index).astype(jnp.bfloat16) for c in range(2)], 1)
        d_sent[half] = dot_nn(chosen, scaled_ref[...]).astype(jnp.bfloat16).reshape(experts, slots, width)
        d_groups.append(send(lambda e, half=half: d_sent.at[half, e], d_got, d_send, d_recv, half, 5))
    for load in loads:
        load.wait()

    part = 512
    tile = rows // 2

    def forward(half):
        x = x_got[half].reshape(rows, width)
        f_sum[...] = jnp.zeros_like(f_sum)
        x_turned[:, half * rows : (half + 1) * rows] = x.astype(jnp.float32).T.astype(jnp.bfloat16)

        @pl.loop(0, units // part)
        def _(step):
            columns = pl.ds(pl.multiple_of(step * part, part), part)
            for r in range(2):
                near = slice(r * tile, (r + 1) * tile)
                far = pl.ds(half * rows + r * tile, tile)
                gate_pre = dot_nn(x[near], gate_ref[:, columns])
                up_pre = dot_nn(x[near], up_ref[:, columns])
                sigmoid = 1.0 / (1.0 + jnp.exp(-gate_pre))
                active = gate_pre * sigmoid
                hid = (active * up_pre).astype(jnp.bfloat16)
                hid_ref[far, columns] = hid
                one_ref[far, columns] = (up_pre * (sigmoid + active * (1.0 - sigmoid))).astype(jnp.bfloat16)
                two_ref[far, columns] = active.astype(jnp.bfloat16)
                f_sum[near, :] += dot_nn(hid, down_ref[columns, :])

        (fa_out, fb_out)[half][...] = f_sum[...].astype(jnp.bfloat16).reshape(experts, slots, width)

    def backward(half):
        d = d_got[half].reshape(rows, width)
        back_sum[...] = jnp.zeros_like(back_sum)
        d_turned[:, half * rows : (half + 1) * rows] = d.astype(jnp.float32).T.astype(jnp.bfloat16)

        @pl.loop(0, units // part)
        def _(step):
            columns = pl.ds(pl.multiple_of(step * part, part), part)
            for r in range(2):
                near = slice(r * tile, (r + 1) * tile)
                far = pl.ds(half * rows + r * tile, tile)
                mid = dot_nt(d[near], down_ref[columns, :])
                dg = (mid * one_ref[far, columns].astype(jnp.float32)).astype(jnp.bfloat16)
                du = (mid * two_ref[far, columns].astype(jnp.float32)).astype(jnp.bfloat16)
                one_ref[far, columns] = dg
                two_ref[far, columns] = du
                back_sum[near, :] += dot_nt(dg, gate_ref[:, columns]) + dot_nt(du, up_ref[:, columns])

        back_sent[half] = back_sum[...].astype(jnp.bfloat16).reshape(experts, slots, width)

    def dots(half):
        ones = jnp.ones((8, width), jnp.float32)
        for e in range(experts):
            product = (fa_out, fb_out)[half][e].astype(jnp.float32) * d_got[half, e].astype(jnp.float32)
            total = lax.dot_general(
                ones, product, (((1,), (1,)), ((), ())), precision=precise, preferred_element_type=jnp.float32
            )
            dots_sent[half, e] = jnp.concatenate([total, jnp.zeros((8, 128 - slots), jnp.float32)], 1)

    for half in range(2):
        arrive(x_groups[half])
        forward(half)
    back_groups, dots_groups = [], []
    for half in range(2):
        arrive(d_groups[half])
        backward(half)
        back_groups.append(send(lambda e, half=half: back_sent.at[half, e], back_got, back_send, back_recv, half, 7))
        dots(half)
        dots_groups.append(send(lambda e, half=half: dots_sent.at[half, e], dots_got, dots_send, dots_recv, half, 9))

    piece = 256
    steps = units // piece

    def stores(step, slot):
        columns = pl.ds(pl.multiple_of(step * piece, piece), piece)
        return [
            pltpu.make_async_copy(stage.at[0, slot], gate_grad.at[:, columns], stage_sem.at[0, slot]),
            pltpu.make_async_copy(stage.at[1, slot], up_grad.at[:, columns], stage_sem.at[1, slot]),
            pltpu.make_async_copy(stage_down.at[slot], down_grad.at[columns, :], stage_sem.at[2, slot]),
        ]

    @pl.loop(0, steps // 2)
    def _(pair):
        for slot in range(2):
            step = pair * 2 + slot
            columns = pl.ds(pl.multiple_of(step * piece, piece), piece)

            @pl.when(pair > 0)
            def _():
                for store in stores(step, slot):
                    store.wait()

            stage[0, slot] = dot_nn(x_turned[...], one_ref[:, columns]).astype(jnp.bfloat16)
            stage[1, slot] = dot_nn(x_turned[...], two_ref[:, columns]).astype(jnp.bfloat16)
            stage_down[slot] = dot_nn(d_turned[...], hid_ref[:, columns]).T.astype(jnp.bfloat16)
            for store in stores(step, slot):
                store.start()

    for slot in range(2):
        for store in stores(steps - 2 + slot, slot):
            store.wait()
    for group in back_groups + dots_groups:
        arrive(group)
    back_out[...] = back_got[...]
    dots_out[...] = dots_got[...]
    for group in x_groups + d_groups + back_groups + dots_groups:
        for copy in group[1]:
            copy.wait_send()


def expert_phase(x_parts, small, grad, codes_row, gate, up, down):
    rows, width = grad.shape
    units = gate.shape[1]
    slots = rows // NFFN
    both = (2, NFFN, slots, width)
    dots = (2, NFFN, 8, 128)
    vmem, hbm = pl.BlockSpec(memory_space=pltpu.VMEM), pl.BlockSpec(memory_space=pl.ANY)
    sems = pltpu.SemaphoreType.DMA((2, NFFN))
    wide = pltpu.VMEM((rows, width), jnp.float32)
    mids = pltpu.VMEM((2 * rows, units), jnp.bfloat16)
    turned = pltpu.VMEM((width, 2 * rows), jnp.bfloat16)
    moved = pltpu.VMEM(both, jnp.bfloat16)
    return pl.pallas_call(
        expert_phase_kernel,
        in_specs=[vmem] * 5 + [hbm] * 3,
        out_specs=(vmem, vmem, vmem, vmem, hbm, hbm, hbm),
        out_shape=(
            jax.ShapeDtypeStruct(both, jnp.bfloat16),
            jax.ShapeDtypeStruct(dots, jnp.float32),
            *(jax.ShapeDtypeStruct(both[1:], jnp.bfloat16),) * 2,
            jax.ShapeDtypeStruct(gate.shape, jnp.bfloat16),
            jax.ShapeDtypeStruct(up.shape, jnp.bfloat16),
            jax.ShapeDtypeStruct(down.shape, jnp.bfloat16),
        ),
        scratch_shapes=[
            pltpu.VMEM(gate.shape, jnp.bfloat16),
            pltpu.VMEM(up.shape, jnp.bfloat16),
            pltpu.VMEM(down.shape, jnp.bfloat16),
            pltpu.VMEM((2 * rows, width), jnp.bfloat16),
            moved, moved, moved, moved, moved,
            pltpu.VMEM(dots, jnp.float32),
            pltpu.VMEM(dots, jnp.float32),
            wide, wide, mids, mids, mids, turned, turned,
            pltpu.VMEM((2, 2, width, 256), jnp.bfloat16),
            pltpu.VMEM((2, 256, width), jnp.bfloat16),
            *(sems,) * 8,
            pltpu.SemaphoreType.DMA((11,)),
            pltpu.SemaphoreType.DMA((3, 2)),
        ],
        compiler_params=pltpu.CompilerParams(vmem_limit_bytes=63 * MIB, collective_id=2, has_side_effects=True),
        cost_estimate=cost(36 * rows * width * units, 5e7),
    )(*(part.reshape(NFFN, slots, width) for part in x_parts), small, grad, codes_row, gate, up, down)


def split_dot(dot, left, right):
    high = left.astype(jnp.bfloat16)
    low = (left - high.astype(jnp.float32)).astype(jnp.bfloat16)
    return dot(high, right) + dot(low, right)


def put_part(ref, values, begin):
    _, chips, owners, tall, half = ref.shape
    end = begin + values.shape[1]
    for core in range(2):
        low, high = max(begin, core * half), min(end, (core + 1) * half)
        if low < high:
            for z in range(owners):
                for chip in range(chips):
                    row = (z * chips + chip) * tall
                    ref[core, chip, z, :, low - core * half : high - core * half] = values[
                        row : row + tall, low - begin : high - begin
                    ]


def turn_kernel(
    resid_ref, small_ref, grad_ref, prior_ref, codes_ref, returned_ref, dots_ref, table_ref,
    mixer_ref, prior_weight_ref, out_weight_ref, attended_ref, f_ref, gate_ref,
    resid_grad_ref, grads_ref, out_grad_ref, prior_grad_ref, f_got, gate_first,
    back_ref, sums_ref, prior_sums_ref, extra_ref, f_send, f_recv, gate_send, gate_recv, *, owners, reduce,
):
    rows, width = resid_ref.shape
    planes = plane_partners(owners)
    beside, behind, across = plane_chips(lax.axis_index("xy"))
    greet([item[2] for item in planes], [{"xy": beside}, {"xy": behind}] if reduce else [])
    expert = lax.axis_index("expert") * 2 + lax.axis_index("core")
    copies = [pltpu.make_async_copy(f_ref.at[expert], f_got.at[expert], f_send.at[0])]
    copies += [
        remote(f_ref.at[index], f_got.at[expert], f_send.at[step], f_recv.at[step], device)
        for step, index, device in planes
    ]
    if reduce:
        for piece, landing, chip in first_hops(beside, behind, across):
            copies.append(
                remote(
                    gate_ref.at[piece], gate_first.at[landing], gate_send.at[landing], gate_recv.at[landing],
                    {"xy": chip},
                )
            )
    for copy in copies:
        copy.start()
    slots = returned_ref.shape[0]
    sums_ref[...] = jnp.zeros_like(sums_ref)
    prior_sums_ref[...] = jnp.zeros_like(prior_sums_ref)

    @pl.loop(0, rows // SEG)
    def _(step):
        span = pl.ds(pl.multiple_of(step * SEG, SEG), SEG)
        small = small_ref[span, :]
        codes = codes_ref[span, :]
        routes = codes[:, 2:4]
        gates = [small[:, c : c + 1] for c in range(2)]
        mixing = [[small[:, 2 + 2 * m + c : 3 + 2 * m + c] for c in range(2)] for m in range(2)]
        inverse = small[:, 6:7]
        normed = resid_ref[span, :] * inverse
        gain = table_ref[1:2, :]
        hidden = normed * gain
        hidden_b = hidden.astype(jnp.bfloat16)
        grad_b = grad_ref[span, :]
        grad = grad_b.astype(jnp.float32)
        index = lax.broadcasted_iota(jnp.int32, (SEG, slots), 1)
        hits = [codes[:, c : c + 1] == index for c in range(2)]
        dots = dots_ref[...]
        terms = [jnp.sum(jnp.where(hit, dots, 0.0), -1, keepdims=True) for hit in hits]
        chosen = (hits[0] | hits[1]).astype(jnp.bfloat16)
        routed = dot_nn(chosen, returned_ref[...])
        along = jnp.sum(grad * hidden, -1, keepdims=True)
        across = [jnp.sum(grad * table_ref[2 + m : 3 + m, :], -1, keepdims=True) for m in range(2)]
        to_copy = 0.0
        to_mix = [0.0, 0.0]
        for c in range(2):
            route = routes[:, c : c + 1]
            copied = jnp.where(route == NFFN + 1, gates[c], 0.0)
            to_copy = to_copy + copied
            terms[c] = terms[c] + copied * along
            for m in range(2):
                mixed = jnp.where(route == NFFN + 2 + m, gates[c], 0.0)
                to_mix[m] = to_mix[m] + mixed
                terms[c] = terms[c] + mixed * (mixing[m][0] * along + mixing[m][1] * across[m])
        both = terms[0] + terms[1]
        lanes = lax.broadcasted_iota(jnp.int32, (SEG, 128), 1)
        logit_grads = jnp.zeros((SEG, 128), jnp.float32)
        for c in range(2):
            logit_grads = jnp.where(lanes == routes[:, c : c + 1], terms[c] - gates[c] * both, logit_grads)
        scores = logit_grads
        direct = to_copy
        for m in range(2):
            pair = (to_mix[m] * along, to_mix[m] * across[m])
            mean = mixing[m][0] * pair[0] + mixing[m][1] * pair[1]
            for c in range(2):
                scores = jnp.where(lanes == NEXP + 2 * m + c, mixing[m][c] * (pair[c] - mean), scores)
            direct = direct + mixing[m][0] * to_mix[m]
        prior_grad_ref[:, span] = lax.dot_general(
            prior_weight_ref[...], logit_grads[:, :NEXP], (((1,), (1,)), ((), ())),
            precision=precise, preferred_element_type=jnp.float32,
        )
        hidden_grads = split_dot(dot_nn, scores, mixer_ref[...]) + direct * grad + routed
        scaled = hidden_grads * gain
        resid_grads = inverse * (scaled - normed * jnp.mean(scaled * normed, -1, keepdims=True)) + grad
        resid_grad_ref[span, :] = resid_grads
        back_ref[span, :] = resid_grads.astype(jnp.bfloat16)
        weights = jnp.zeros((SEG, 128), jnp.float32)
        for m in range(2):
            weights = jnp.where(lanes == m, mixing[m][1] * to_mix[m], weights)
        sums_ref[0:16, :] += split_dot(dot_nn, scores.T[0:16], hidden_b)
        sums_ref[16:24, :] += split_dot(dot_nn, weights.T[0:8], grad_b)
        sums_ref[24:32, :] += jnp.sum((hidden_grads * normed).reshape(SEG // 8, 8, width), 0)
        prior_sums_ref[...] += jnp.dot(
            prior_ref[:, span],
            jnp.concatenate([logit_grads[:, 96:], logit_grads[:, :96]], 1),
            precision=precise,
            preferred_element_type=jnp.float32,
        )

    sums_ref[24:25, :] = jnp.sum(sums_ref[24:32, :], 0, keepdims=True)
    extra_ref[...] = jnp.concatenate([sums_ref[...], jnp.zeros((96, width), jnp.float32)], 0).T
    kept = NEXP // owners
    for z in range(owners):
        extra_ref[pl.ds(z * (width // owners), kept), :] += prior_sums_ref[z * kept : (z + 1) * kept, :]
    small_part = jnp.concatenate([extra_ref[...], jnp.zeros((width, 128), jnp.float32)], 1).astype(jnp.bfloat16)
    put_part(out_grad_ref, small_part, width)
    back = back_ref[...]
    grads_ref[...] = dot_nt(out_weight_ref[...], back).astype(jnp.bfloat16)
    put_part(out_grad_ref, dot_nn(attended_ref[...], back).astype(jnp.bfloat16), 0)
    for copy in copies:
        copy.wait()


def turn(resid, small, grad, prior, codes, returned, dots, table, mixer, prior_weight, out_weight, attended, f, gate):
    rows, width = resid.shape
    owners = lax.axis_size("expert")
    vmem, hbm = pl.BlockSpec(memory_space=pltpu.VMEM), pl.BlockSpec(memory_space=pl.ANY)
    return pl.pallas_call(
        functools.partial(turn_kernel, owners=owners, reduce=relayed(gate.shape[0])),
        in_specs=[vmem] * 12 + [hbm] * 2,
        out_specs=(vmem, vmem, vmem, vmem, hbm, hbm),
        out_shape=(
            jax.ShapeDtypeStruct((rows, width), jnp.float32),
            jax.ShapeDtypeStruct((width, rows), jnp.bfloat16),
            jax.ShapeDtypeStruct((2, 4, owners, width // owners // 4, (width + 256) // 2), jnp.bfloat16),
            jax.ShapeDtypeStruct(prior.shape, jnp.float32),
            jax.ShapeDtypeStruct(f.shape, f.dtype),
            jax.ShapeDtypeStruct((4, *gate.shape[1:]), gate.dtype),
        ),
        scratch_shapes=[
            pltpu.VMEM((rows, width), jnp.bfloat16),
            pltpu.VMEM((32, width), jnp.float32),
            pltpu.VMEM((prior.shape[0], 128), jnp.float32),
            pltpu.VMEM((width, 128), jnp.float32),
            pltpu.SemaphoreType.DMA((2 * owners,)),
            pltpu.SemaphoreType.DMA((2 * owners,)),
            pltpu.SemaphoreType.DMA((4,)),
            pltpu.SemaphoreType.DMA((4,)),
        ],
        compiler_params=pltpu.CompilerParams(vmem_limit_bytes=63 * MIB, collective_id=4, has_side_effects=True),
        cost_estimate=cost(4 * rows * width * width + 4 * rows * rows * width, 1.5e7),
    )(resid, small, grad, prior, codes, returned, dots, table, mixer, prior_weight, out_weight, attended, f, gate)


def finish_kernel(
    resid_ref, small_ref, codes_ref, fa_ref, fb_ref, table_ref, totals_ref, tokens_grad_ref, *refs, owners, count, reduce
):
    experts, refs = refs[: 3 * count], refs[3 * count :]
    tokens_grad_out, *expert_outs = refs[:4]
    out_ref, *weight_refs, router_ref, prior_ref, constant_ref, vector_ref, gains_ref = refs[4:14]
    held, *work = refs[14:-2]
    load_sem, store_sem = refs[-2:]
    core = lax.axis_index("core")
    place = lax.axis_index("xy") * 2 + core
    load = pltpu.make_async_copy(tokens_grad_ref, held, load_sem.at[0])
    loads = []
    for i in range(3):
        if reduce:
            piece, first, got = experts[3 * i : 3 * i + 3]
            items = (piece.at[place], first.at[core], got.at[4 + core], got.at[6], got.at[7], got.at[5 - core])
        else:
            items = (experts[i],)
        for n, item in enumerate(items):
            target = work[2 * i].at[n] if reduce else work[2 * i + 1]
            loads.append((i, pltpu.make_async_copy(item, target, load_sem.at[1 + 6 * i + n])))
    load.start()
    for _, item in loads:
        item.start()
    stores = [pltpu.make_async_copy(held, tokens_grad_out, store_sem.at[0])]
    stores += [pltpu.make_async_copy(work[2 * i + 1], expert_outs[i], store_sem.at[1 + i]) for i in range(3)]
    rows, width = resid_ref.shape
    half = fa_ref.shape[0]

    @pl.loop(0, rows // SEG)
    def _(step):
        span = pl.ds(pl.multiple_of(step * SEG, SEG), SEG)
        small = small_ref[span, :]
        codes = codes_ref[span, :]
        routes = codes[:, 2:4]
        resid = resid_ref[span, :]
        hidden = resid * small[:, 6:7] * table_ref[1:2, :]
        index = lax.broadcasted_iota(jnp.int32, (SEG, 2 * half), 1)
        total = resid
        direct = 0.0
        for c in range(2):
            gate, route = small[:, c : c + 1], routes[:, c : c + 1]
            chosen = (codes[:, c : c + 1] == index).astype(jnp.bfloat16)
            routed = dot_nn(chosen[:, :half], fa_ref[...]) + dot_nn(chosen[:, half:], fb_ref[...])
            total = total + gate * routed
            direct = direct + jnp.where(route == NFFN + 1, gate, 0.0)
            for m in range(2):
                mixed = jnp.where(route == NFFN + 2 + m, gate, 0.0)
                direct = direct + mixed * small[:, 2 + 2 * m : 3 + 2 * m]
                total = total + mixed * small[:, 3 + 2 * m : 4 + 2 * m] * table_ref[2 + m : 3 + m, :]
        out_ref[span, :] = (total + direct * hidden).astype(jnp.bfloat16)

    load.wait()
    stores[0].start()
    for i in range(3):
        for index, item in loads:
            if index == i:
                item.wait()
        if reduce:
            wide = work[2 * i + 1]
            for n in range(2):
                wide[core if n == 0 else 1 - core] = jnp.sum(work[2 * i][3 * n : 3 * n + 3].astype(jnp.float32), 0)
        stores[1 + i].start()
    span = owners * HEAD_DIM
    chunks = width // span
    offsets, _ = part_columns(width, chunks)
    for i, ref in enumerate(weight_refs[:3]):
        for j in range(chunks):
            begin = offsets[j + 1] + i * span if j < chunks - 1 or i < 2 else offsets[-1]
            ref[:, j * span : (j + 1) * span] = totals_ref[:, begin : begin + span].astype(jnp.float32)
    weight_refs[3][...] = totals_ref[:, :width].astype(jnp.float32)
    extra = totals_ref[:, width : width + 128].astype(jnp.float32)
    prior_ref[...] = extra[: NEXP // owners, 32 : 32 + NEXP]
    turned = extra.T
    router_ref[...] = turned[:NEXP]
    constant_ref[...] = turned[NEXP : NEXP + 4]
    vector_ref[...] = turned[16:18]
    begin = offsets[-1] + span
    gains = totals_ref[:, begin : begin + 128].astype(jnp.float32).T
    member = lax.axis_index("expert")
    share = router_ref.shape[1]
    own_gain = table_ref[0:1, :share]
    for z in range(1, owners):
        own_gain = jnp.where(member == z, table_ref[0:1, z * share : (z + 1) * share], own_gain)
    gains_ref[0:1, :] = gains[0:1] / own_gain
    gains_ref[1:2, :] = turned[24:25]
    for move in stores:
        move.wait()


def finish(resid, small, codes, outs, table, totals, tokens_grad, experts, reduce):
    rows, width = resid.shape
    owners = lax.axis_size("expert")
    share = width // owners
    vmem, hbm = pl.BlockSpec(memory_space=pltpu.VMEM), pl.BlockSpec(memory_space=pl.ANY)
    shape = lambda *dims: jax.ShapeDtypeStruct(dims, jnp.float32)
    count = 3 if reduce else 1
    shapes = [item.shape[1:] for item in experts[count - 1 :: count]]
    work = []
    for dims in shapes:
        work += [pltpu.VMEM((6 if reduce else 1, *dims), jnp.bfloat16), pltpu.VMEM((2, *dims), jnp.float32)]
    return pl.pallas_call(
        functools.partial(finish_kernel, owners=owners, count=count, reduce=reduce),
        in_specs=[vmem] * 7 + [hbm] * (1 + len(experts)),
        out_specs=(hbm,) * 4 + (vmem,) * 10,
        out_shape=(
            shape(rows, width),
            *(shape(2, *dims) for dims in shapes),
            jax.ShapeDtypeStruct((rows, width), jnp.bfloat16),
            *(shape(share, width),) * 4,
            shape(NEXP, share), shape(NEXP // owners, NEXP), shape(4, share), shape(2, share), shape(2, share),
        ),
        scratch_shapes=[
            pltpu.VMEM((rows, width), jnp.float32), *work,
            pltpu.SemaphoreType.DMA((19,)), pltpu.SemaphoreType.DMA((4,)),
        ],
        compiler_params=params(63),
        cost_estimate=cost(8 * rows * rows * width, 8e6),
    )(resid, small, codes, *outs, table, totals, tokens_grad, *experts)


def attend_back_phase_kernel(
    grads_ref, heads_ref, outs_ref, lse_ref, bias_ref, cos_ref, sin_ref, tokens_ref, table_ref,
    query_ref, key_ref, value_ref, resid_grad_ref, out_part_ref, f_ref, gate_ref, up_ref, down_ref, gate_first,
    tokens_grad_ref, f_got, gate_got, up_got, down_got, *rest, reduce,
):
    chunks, owners, _, rows = grads_ref.shape
    width = tokens_ref.shape[1]
    if reduce:
        total_ref, *rest = rest
    else:
        flat_ref, *rest = rest
    (
        d_got, back_sent, back_got, normed_turned, turned_ref, back_sum, column_ref,
        qt_ref, kt_ref, dt_ref, q_ref, k_ref, v_ref, d_ref, delta_ref, dq_ref, dk_ref, dv_ref, triangle,
        d_send, d_recv, back_send, back_recv, weight_send, weight_recv, f_send, f_recv, local_sem, early_sem, *rest,
    ) = rest
    if reduce:
        (
            half_send, half_recv, chip_send, chip_recv, ring_send, ring_recv, all_send, all_recv,
            gate_work, gate_sums, up_sums, down_work, down_sums, work_sem, *rest,
        ) = rest
        count = len(part_columns(width, chunks)[1])
        own_parts, half_got, chip_got, chip_sum, ring_got, ring_sum, all_got = (
            rest[max(0, n * count - 1) : (n + 1) * count - 1] for n in range(7)
        )
        parts = [out_part_ref, *own_parts]
    copies = gate_ref.shape[0]
    member, xy, core = (lax.axis_index(name) for name in ("expert", "xy", "core"))
    place = xy * 2 + core
    ring, others, planes = ring_partners(owners), copy_partners(copies), plane_partners(owners)
    greet([item[2] for item in planes], [item[2] for item in others])

    d_groups = []
    for j in range(chunks):
        local = pltpu.make_async_copy(grads_ref.at[j, member], d_got.at[j, member], local_sem.at[j])
        local.start()
        group = []
        for step, index, device in ring:
            copy = remote(
                grads_ref.at[j, index], d_got.at[j, member], d_send.at[j, step - 1], d_recv.at[j, step - 1], device
            )
            copy.start()
            group.append(copy)
        d_groups.append((local, group))

    inputs = tokens_ref[...].astype(jnp.float32)
    inverse = lax.rsqrt(jnp.mean(inputs * inputs, -1, keepdims=True) + epsilon)
    normed_turned[...] = (inputs * inverse * table_ref[0:1, :]).T.astype(jnp.bfloat16)
    share = width // owners

    offsets, sizes = part_columns(width, chunks)

    def fill(p, values, begin, size):
        if reduce:
            put_part(parts[p], values, begin)
        else:
            begin = offsets[p] + begin
            flat_ref[:, begin : begin + size] = values

    early = pltpu.make_async_copy(resid_grad_ref, tokens_grad_ref, early_sem.at[0])
    early.start()
    last_part = len(sizes) - 1
    fill(last_part, jnp.zeros((width, 128), jnp.bfloat16), sizes[-1] - 128, 128)

    stages = {}

    def over_cores(p):
        copy = remote(parts[p].at[1 - core], half_got[p], half_send.at[p], half_recv.at[p], {"core": 1 - core})
        copy.start()
        stages[p, 0] = [copy]

    def over_chips(p):
        for copy in stages[p, 0]:
            copy.wait_recv()
        half_got[p][...] = (parts[p][core].astype(jnp.float32) + half_got[p][...].astype(jnp.float32)).astype(
            jnp.bfloat16
        )
        stages[p, 1] = []
        for step in (3, 1, 2):
            index = lax.rem(xy + step, 4)
            copy = remote(
                half_got[p].at[index], chip_got[p].at[xy],
                chip_send.at[p, step - 1], chip_recv.at[p, step - 1], {"xy": index},
            )
            copy.start()
            stages[p, 1].append(copy)
        chip_got[p][xy] = half_got[p][xy]

    def over_owners(p):
        for copy in stages[p, 1]:
            copy.wait_recv()
        chip_sum[p][...] = jnp.sum(chip_got[p][...].astype(jnp.float32), 0).astype(jnp.bfloat16)
        stages[p, 2] = []
        for step, index, device in ring:
            copy = remote(
                chip_sum[p].at[index], ring_got[p].at[member],
                ring_send.at[p, step - 1], ring_recv.at[p, step - 1], device,
            )
            copy.start()
            stages[p, 2].append(copy)
        ring_got[p][member] = chip_sum[p][member]

    def to_copies(p):
        for copy in stages[p, 2]:
            copy.wait_recv()
        ring_sum[p][...] = jnp.sum(ring_got[p][...].astype(jnp.float32), 0).astype(jnp.bfloat16)
        stages[p, 3] = []
        for step, _, device in others:
            copy = remote(
                ring_sum[p], all_got[p].at[xy, core], all_send.at[p, step - 1], all_recv.at[p, step - 1], device
            )
            copy.start()
            stages[p, 3].append(copy)
        all_got[p][xy, core] = ring_sum[p][...]

    def advance(*pairs):
        if reduce:
            for stage, p in pairs:
                (over_cores, over_chips, over_owners, to_copies)[stage](p)

    advance((0, 0))

    background = []

    pieces = ((gate_ref, gate_got), (up_ref, up_got), (down_ref, down_got))

    def send_experts():
        for i, (source, target) in enumerate(pieces):
            local = pltpu.make_async_copy(source.at[place], target.at[place], weight_send.at[i, 0])
            local.start()
            background.append(local.wait)
            for step, index, device in others:
                copy = remote(
                    source.at[2 * device["xy"] + device["core"]], target.at[place],
                    weight_send.at[i, step], weight_recv.at[i, step], device,
                )
                copy.start()
                background.append(copy.wait)

    beside, behind, across = plane_chips(xy)
    landed = {}
    sent = []

    def relay(i, source, landing, device):
        copy = remote(
            source, landing_ref(i, landing), weight_send.at[i, landing], weight_recv.at[i, landing], device
        )
        copy.start()
        landed[i, landing] = copy
        sent.append(copy)

    def landing_ref(i, landing):
        return gate_first.at[landing] if i == 0 and landing < 4 else pieces[i][1].at[landing]

    def arrive(i, *landings):
        for landing in landings:
            if (i, landing) in landed:
                landed[i, landing].wait_recv()

    def first_hop(i):
        for piece, landing, chip in first_hops(beside, behind, across):
            relay(i, pieces[i][0].at[piece], landing, {"xy": chip})

    def second_hop(i):
        source, target = pieces[i]
        work, sums = (gate_work, (gate_sums, up_sums)[i]) if i < 2 else (down_work, down_sums)
        arrive(i, 2, 3)
        items = (source.at[behind * 2], landing_ref(i, 2), source.at[beside * 2 + 1], landing_ref(i, 3))
        loads = [pltpu.make_async_copy(ref, work.at[n], work_sem.at[n]) for n, ref in enumerate(items)]
        for item in loads:
            item.start()
        arrive(i, 0, 1)
        other = {"core": 1 - core}
        relay(i, source.at[xy * 2 + 1 - core], 6, other)
        relay(i, (gate_first if i == 0 else target).at[1 - core], 7, other)
        for item in loads:
            item.wait()
        for n, device in enumerate(({"xy": behind, "core": 0}, {"xy": beside, "core": 1})):
            sums[n] = (work[2 * n].astype(jnp.float32) + work[2 * n + 1].astype(jnp.float32)).astype(jnp.bfloat16)
            copy = remote(
                sums.at[n], target.at[4 + core], weight_send.at[i, 4 + n], weight_recv.at[i, 4 + core], device
            )
            copy.start()
            sent.append(copy)
            landed[i, 4 + n] = remote(
                sums.at[n], target.at[4 + n], weight_send.at[i, 4 + n], weight_recv.at[i, 4 + n], device
            )

    if reduce:
        for i in (1, 2):
            first_hop(i)
    else:
        send_experts()

    def head(j):
        local, group = d_groups[j]
        local.wait()
        for copy in group:
            copy.wait_recv()
        attend_back_head(
            bias_ref, cos_ref, sin_ref, heads_ref.at[j], outs_ref.at[j], lse_ref.at[j : j + 1], d_got.at[j],
            back_sent.at[j], qt_ref, kt_ref, dt_ref, q_ref, k_ref, v_ref, d_ref, delta_ref, dq_ref, dk_ref, dv_ref,
            triangle,
        )

    def send_back(j, cuts):
        local = None
        if cuts[0][1] == 0:
            local = pltpu.make_async_copy(back_sent.at[j, member], back_got.at[j, member], local_sem.at[chunks + j])
            local.start()
        groups = []
        for slot, begin, size in cuts:
            span = pl.ds(begin, size)
            group = []
            for step, index, device in ring:
                copy = remote(
                    back_sent.at[j, index, span], back_got.at[j, member, span],
                    back_send.at[slot, step - 1], back_recv.at[slot, step - 1], device,
                )
                copy.start()
                group.append(copy)
            groups.append(group)
        return local, groups

    span_width = owners * HEAD_DIM

    def weights_of(j, group, types=(0, 1, 2)):
        local, copies_in = group
        if 0 in types:
            local.wait()
        for copy in copies_in[1 if 0 not in types else 0]:
            copy.wait_recv()
        total = None
        for i in types:
            for z in range(owners):
                row = i * span_width + z * HEAD_DIM
                turned_ref[row : row + HEAD_DIM, :] = back_got[j, z, i * HEAD_DIM : (i + 1) * HEAD_DIM]
            weight = (query_ref, key_ref, value_ref)[i]
            term = dot_nn(
                weight[:, j * span_width : (j + 1) * span_width], turned_ref[i * span_width : (i + 1) * span_width, :]
            )
            total = term if total is None else total + term
        first = j == 0 and 0 in types
        back_sum[...] = total if first else back_sum[...] + total
        column = jnp.sum(total * normed_turned[...].astype(jnp.float32), -1, keepdims=True)
        column_ref[...] = column if first else column_ref[...] + column
        begin, size = types[0] * span_width, len(types) * span_width
        part = j + 1 if 0 in types else j + 2
        if part == last_part:
            fill(part, jnp.broadcast_to(column_ref[...], (width, 128)).astype(jnp.bfloat16), span_width, 128)
        fill(part, dot_nt(normed_turned[...], turned_ref[begin : begin + size, :]).astype(jnp.bfloat16), 0, size)

    expert = member * 2 + core

    def send_f(distance):
        if distance == 0:
            local = pltpu.make_async_copy(f_ref.at[expert], f_got.at[expert], f_send.at[0])
            local.start()
            background.append(local.wait)
        for step, index, device in planes[3 * distance : 3 * distance + 3]:
            copy = remote(f_ref.at[index], f_got.at[expert], f_send.at[step], f_recv.at[step], device)
            copy.start()
            background.append(copy.wait)

    def expert_step(step, i):
        if reduce:
            step(i)

    part_k, part_v = chunks, chunks + 1
    both = 2 * HEAD_DIM
    head(0)
    groups = [send_back(0, [(0, 0, 3 * HEAD_DIM)])]
    expert_step(second_hop, 0)
    advance((1, 0))
    head(1)
    advance((2, 0))
    groups.append(send_back(1, [(1, 0, 3 * HEAD_DIM)]))
    expert_step(second_hop, 1)
    expert_step(second_hop, 2)
    head(2)
    groups.append(send_back(2, [(2, 0, both), (3, both, HEAD_DIM)]))
    weights_of(0, groups[0])
    advance((0, 1), (3, 0))
    weights_of(1, groups[1])
    advance((1, 1), (0, 2))
    weights_of(2, groups[2], (0, 1))
    advance((0, part_k), (1, 2), (2, 1))
    weights_of(2, groups[2], (2,))
    advance((0, part_v), (1, part_k), (2, 2))
    send_f(0)
    advance((1, part_v), (2, part_k))
    send_f(1)
    normed = inputs * inverse
    first_grads = back_sum[...].T
    advance((2, part_v))
    send_f(2)
    scaled = first_grads * table_ref[0:1, :]
    early.wait()
    tokens_grad_ref[...] += inverse * (scaled - normed * jnp.mean(scaled * normed, -1, keepdims=True))
    advance((3, 1), (3, 2), (3, part_k), (3, part_v))
    if reduce:
        for p in range(len(sizes)):
            for copy in stages[p, 3]:
                copy.wait_recv()
            for stage in range(4):
                for copy in stages[p, stage]:
                    copy.wait_send()
            _, _, tall, half = all_got[p].shape
            for chip in range(4):
                for side in range(2):
                    begin = offsets[p] + side * half
                    total_ref[chip * tall : (chip + 1) * tall, begin : begin + half] = all_got[p][chip, side]
        for i in range(3):
            arrive(i, 4, 5, 6, 7)
        for copy in sent:
            copy.wait_send()
    for local, group in d_groups:
        for copy in group:
            copy.wait_send()
    for local, items in groups:
        for group in items:
            for copy in group:
                copy.wait_send()
    for wait in background:
        wait()


def part_columns(width, chunks):
    sizes = [width + 256] + [width] * (chunks - 1) + [width // 3 * 2, width // 3 + 256]
    return [sum(sizes[:p]) for p in range(len(sizes))], sizes


def attend_back_phase(
    grads, heads, outs, lse, bias, cosine, sine, tokens, table, weights, resid_grads, out_part, f, pieces, gate_first, copies
):
    chunks, owners, _, rows = grads.shape
    width = tokens.shape[1]
    length = owners * rows
    head = (chunks, owners, 3 * HEAD_DIM, rows)
    sizes = part_columns(width, chunks)[1]
    columns, total = sum(sizes), len(sizes)
    share = width // owners
    reduce = relayed(copies)
    vmem, hbm = pl.BlockSpec(memory_space=pltpu.VMEM), pl.BlockSpec(memory_space=pl.ANY)
    gate_shape, down_shape = pieces[0].shape[1:], pieces[2].shape[1:]
    turned = pltpu.VMEM((HEAD_DIM, length), jnp.bfloat16)
    plain = pltpu.VMEM((length, HEAD_DIM), jnp.bfloat16)
    wide = pltpu.VMEM((length, HEAD_DIM), jnp.float32)
    sems = lambda *shape: pltpu.SemaphoreType.DMA(shape)
    scratch = [
        pltpu.VMEM(grads.shape, jnp.bfloat16),
        pltpu.VMEM(head, jnp.bfloat16),
        pltpu.VMEM(head, jnp.bfloat16),
        pltpu.VMEM((width, rows), jnp.bfloat16),
        pltpu.VMEM((3 * owners * HEAD_DIM, rows), jnp.bfloat16),
        pltpu.VMEM((width, rows), jnp.float32),
        pltpu.VMEM((width, 1), jnp.float32),
        turned, turned, turned, plain, plain, plain, plain,
        pltpu.VMEM((1, length), jnp.float32),
        pltpu.VMEM((HEAD_DIM, length), jnp.float32),
        wide, wide,
        pltpu.VMEM((TILE, TILE), jnp.float32),
        *(sems(chunks, owners - 1),) * 2,
        *(sems(chunks + 1, owners - 1),) * 2,
        sems(3, copies), sems(3, copies), sems(2 * owners), sems(2 * owners), sems(2 * chunks), sems(2),
    ]
    if reduce:
        low = lambda *shape: pltpu.VMEM(shape, jnp.bfloat16)
        scratch += [
            sems(total), sems(total), sems(total, 3), sems(total, 3),
            sems(total, owners - 1), sems(total, owners - 1), sems(total, copies - 1), sems(total, copies - 1),
            low(4, *gate_shape), low(2, *gate_shape), low(2, *gate_shape), low(4, *down_shape), low(2, *down_shape),
            sems(4),
        ]
        tall, halves = share // 4, [size // 2 for size in sizes]
        for shape in (
            (2, 4, owners, tall), (4, owners, tall), (4, owners, tall), (owners, tall), (owners, tall), (tall,), (4, 2, tall)
        ):
            scratch += [low(*shape, half) for half in (halves[1:] if len(shape) == 4 and shape[0] == 2 else halves)]
        last_specs, last_shapes = (vmem,), (jax.ShapeDtypeStruct((share, columns), jnp.bfloat16),)
    else:
        last_specs, last_shapes = (vmem,), (jax.ShapeDtypeStruct((width, columns), jnp.bfloat16),)
    tokens_grad, f_got, *gots, totals = pl.pallas_call(
        functools.partial(attend_back_phase_kernel, reduce=reduce),
        in_specs=[vmem] * 12 + [hbm, vmem] + [hbm] * 5,
        out_specs=(vmem, hbm, hbm, hbm, hbm, *last_specs),
        out_shape=(
            jax.ShapeDtypeStruct((rows, width), jnp.float32),
            jax.ShapeDtypeStruct(f.shape, f.dtype),
            *(jax.ShapeDtypeStruct(piece.shape, piece.dtype) for piece in pieces),
            *last_shapes,
        ),
        scratch_shapes=scratch,
        compiler_params=pltpu.CompilerParams(vmem_limit_bytes=63 * MIB, collective_id=3, has_side_effects=True),
        cost_estimate=cost(2e10, 5e7),
    )(grads, heads, outs, lse, bias, cosine, sine, tokens, table, *weights, resid_grads, out_part, f, *pieces, gate_first)
    if not reduce:
        out_part = out_part.transpose(2, 1, 3, 0, 4).reshape(width, sizes[0])
        totals = jnp.concatenate([out_part, totals[:, sizes[0] :]], 1)
        totals = lax.psum_scatter(totals, "expert", scatter_dimension=0, tiled=True)
        totals = lax.psum(totals, ("xy", "core"))
        gots = [jnp.sum(got.reshape(copies // 2, 2, *got.shape[1:]).astype(jnp.float32), 0) for got in gots]
    return (tokens_grad, f_got, totals, gots)


def per_device(
    tokens, prior_logits, routes, parents, cotangent, query_weight, key_weight, value_weight, out_weight,
    attention_gain, expert_gain, router_weight, prior_weight, constant_weight, constant_vector,
    gate_weight, up_weight, down_weight,
):
    owners = lax.axis_size("expert")
    member = lax.axis_index("expert")
    tokens, prior, routes, grad = tokens[0], prior_logits[0].T, routes[0].T, cotangent[0]
    rows, width = tokens.shape
    copies = lax.axis_size("xy") * lax.axis_size("core")
    chunks = width // HEAD_DIM // owners
    zeros = jnp.zeros((4, width), jnp.float32)
    table = jnp.concatenate([attention_gain[None], expert_gain[None], constant_vector, zeros], 0)
    qkv_weights = (query_weight, key_weight, value_weight)
    attended, logs, bias, cosine, sine, codes, codes_row, heads, outs, gate, up, down = attend_phase(
        tokens, table, qkv_weights, parents, routes, (gate_weight, up_weight, down_weight), copies
    )
    attended = attended.reshape(width, rows)
    gate, up, down = (full.reshape(-1, full.shape[-1]) for full in (gate, up, down))
    resid, small, *x_out, mixer = middle(
        tokens, attended, out_weight, table, router_weight.T, constant_weight.T, prior, prior_weight, codes, codes_row
    )
    backs, dots, fa, fb, *grads = expert_phase(x_out, small, grad, codes_row, gate, up, down)
    pieces = [item.reshape(copies, -1, item.shape[-1]) for item in grads]
    dots = dots[:, :, 0, : rows // NFFN].reshape(1, 2 * rows)
    resid_grads, grads_out, out_part, prior_grad, fa, gate_first = turn(
        resid, small, grad, prior, codes, backs.reshape(2 * rows, width), dots, table, mixer, prior_weight,
        out_weight, attended, fa, pieces[0],
    )
    tokens_grad, fb, totals, gots = attend_back_phase(
        grads_out.reshape(chunks, owners, HEAD_DIM, rows), heads, outs, logs, bias, cosine, sine, tokens,
        table, qkv_weights, resid_grads, out_part, fb, pieces, gate_first, copies,
    )
    fs = [f.reshape(rows, width) for f in (fa, fb)]
    reduce = relayed(copies)
    experts = gots
    if reduce:
        experts = [item for i in range(3) for item in (pieces[i], gate_first if i == 0 else gots[i], gots[i])]
    (
        tokens_grad, gate_part, up_part, down_part, result, *qkv_out_grads, router_grad, prior_weight_grad,
        constant_weight_grad, vector_grad, gain_grads,
    ) = finish(resid, small, codes, fs, table, totals, tokens_grad, experts, reduce)
    return (
        result[None],
        tokens_grad[None],
        prior_grad.T[None],
        *qkv_out_grads,
        gain_grads[0],
        gain_grads[1],
        router_grad.T,
        prior_weight_grad,
        constant_weight_grad.T,
        vector_grad,
        gate_part,
        up_part,
        down_part,
    )


def solution(mesh):
    owners, copies = mesh.shape["expert"], mesh.shape["dp"]
    cores = 2
    mesh = Mesh(mesh.devices.reshape(owners, copies // cores, cores), ("expert", "xy", "core"))
    dp = ("xy", "core")
    rows = P(dp, "expert", None)
    shard = P("expert", dp, None)
    in_specs = (rows, rows, rows, P(dp, None), rows) + (P(),) * 10 + (shard,) * 3
    out_specs = (
        (rows,) * 3
        + (P("expert", None),) * 4
        + (P("expert"),) * 2
        + (P("expert", None),) * 3
        + (P(None, "expert"),)
        + (shard,) * 3
    )
    return jax.shard_map(per_device, mesh=mesh, in_specs=in_specs, out_specs=out_specs, check_vma=False)
```

```python
import functools

import jax
import jax.numpy as jnp
from jax import lax
from jax.experimental import pallas as pl
from jax.experimental.pallas import tpu as pltpu
from jax.sharding import Mesh
from jax.sharding import PartitionSpec as P

NFFN = 8
NEXP = 12
SEG = 128
HEAD_DIM = 64
TRUNK = 1024
TILE = 2 * SEG
LOG2E = 1.4426950408889634
masked_score = -1e30
MIB = 2**20
epsilon = 1e-06
precise = lax.Precision.HIGHEST


def dot_nt(left, right):
    return lax.dot_general(left, right, (((1,), (1,)), ((), ())), preferred_element_type=jnp.float32)


def dot_nn(left, right):
    return jnp.dot(left, right, preferred_element_type=jnp.float32)


def tile_parts(tile, start):
    trunk_tiles = TRUNK // TILE
    if tile is not None and tile < trunk_tiles:
        return [(k * TILE, False, k == tile) for k in range(tile + 1)]
    parts = [(k * TILE, False, False) for k in range(trunk_tiles)]
    branch_tiles = 2
    if tile is None:
        parts += [(TRUNK + k * TILE, True, False) for k in range(branch_tiles)]
    else:
        parts += [(TRUNK + k * TILE, True, False) for k in range(tile - trunk_tiles)]
    parts += [(start, True, True)]
    return parts


def causal_bias():
    key_ids = lax.broadcasted_iota(jnp.int32, (TILE, TILE), 0)
    query_ids = lax.broadcasted_iota(jnp.int32, (TILE, TILE), 1)
    return jnp.where(key_ids <= query_ids, 0.0, masked_score).astype(jnp.float32)


def part_scores(scores, part, columns, bias_ref, triangle):
    first, by_lineage, causal = part
    if by_lineage:
        segment = 1 + (first - TRUNK) // SEG
        rows = [bias_ref[pl.ds(segment + i, 1), columns] for i in range(TILE // SEG)]
        scores = jnp.concatenate(
            [scores[i * SEG : (i + 1) * SEG] + rows[i] for i in range(TILE // SEG)], 0
        )
    if causal:
        scores = scores + triangle[...]
    return scores


def for_tiles(length, body):
    trunk_tiles = TRUNK // TILE
    for tile in range(trunk_tiles + 2):
        body(tile, tile * TILE)
    first_leaf = trunk_tiles + 2

    @pl.loop(first_leaf, length // TILE)
    def _(tile):
        body(None, pl.multiple_of(tile * TILE, TILE))


def attend_head(bias_ref, qkv_ref, out_ref, lse_ref, q_ref, k_ref, v_ref, o_ref, s_ref, triangle):
    sources, _, rows = qkv_ref.shape
    length = sources * rows
    factor = HEAD_DIM ** (-0.5) * LOG2E
    triangle[...] = causal_bias()
    extra = lax.broadcasted_iota(jnp.int32, (16, length), 0)
    v_ref[HEAD_DIM:, :] = jnp.where(extra == 0, 1.0, 0.0).astype(jnp.bfloat16)
    for z in range(sources):
        span = pl.ds(z * rows, rows)
        q_ref[:, span] = qkv_ref[z, :HEAD_DIM]
        k_ref[span, :] = qkv_ref[z, HEAD_DIM : 2 * HEAD_DIM].astype(jnp.float32).T.astype(jnp.bfloat16)
        v_ref[:HEAD_DIM, span] = qkv_ref[z, 2 * HEAD_DIM :]

    def body(tile, start):
        columns = pl.ds(start, TILE)
        parts = tile_parts(tile, start)
        query = q_ref[:, columns]
        peak = None
        for i, part in enumerate(parts):
            scores = dot_nn(k_ref[pl.ds(part[0], TILE), :], query)
            scores = part_scores(scores, part, columns, bias_ref, triangle)
            s_ref[i * TILE : (i + 1) * TILE, :] = scores
            top = jnp.max(scores, 0, keepdims=True)
            peak = top if peak is None else jnp.maximum(peak, top)
        shift = peak * factor
        total = None
        for i, part in enumerate(parts):
            weights = jnp.exp2(s_ref[i * TILE : (i + 1) * TILE, :] * factor - shift)
            term = dot_nn(v_ref[:, pl.ds(part[0], TILE)], weights.astype(jnp.bfloat16))
            total = term if total is None else total + term
        norm = total[HEAD_DIM : HEAD_DIM + 1]
        o_ref[:, columns] = (total[:HEAD_DIM] / norm).astype(jnp.bfloat16)
        lse_ref[:, columns] = shift + jnp.log2(norm)

    for_tiles(length, body)
    for z in range(sources):
        out_ref[z] = o_ref[:, pl.ds(z * rows, rows)]


def attend_back_head(
    bias_ref, cos_ref, sin_ref, qkv_ref, out_ref, lse_ref, grad_ref, back_ref,
    qt_ref, kt_ref, dt_ref, q_ref, k_ref, v_ref, d_ref, delta_ref, dq_ref, dk_ref, dv_ref, triangle,
):
    sources, _, rows = qkv_ref.shape
    length = sources * rows
    scaling = HEAD_DIM ** (-0.5)
    factor = scaling * LOG2E
    triangle[...] = causal_bias()

    def turned(values):
        return values.astype(jnp.float32).T.astype(jnp.bfloat16)

    for z in range(sources):
        span = pl.ds(z * rows, rows)
        query, key, value = (qkv_ref[z, i * HEAD_DIM : (i + 1) * HEAD_DIM] for i in range(3))
        grad = grad_ref[z]
        qt_ref[:, span] = query
        kt_ref[:, span] = key
        dt_ref[:, span] = grad
        q_ref[span, :] = turned(query)
        k_ref[span, :] = turned(key)
        v_ref[span, :] = turned(value)
        d_ref[span, :] = turned(grad)
        delta_ref[:, span] = jnp.sum(
            grad.astype(jnp.float32) * out_ref[z].astype(jnp.float32), 0, keepdims=True
        )
    dk_ref[...] = jnp.zeros_like(dk_ref)
    dv_ref[...] = jnp.zeros_like(dv_ref)

    def body(tile, start):
        columns = pl.ds(start, TILE)
        query_t, grad_t = qt_ref[:, columns], dt_ref[:, columns]
        query, grad = q_ref[columns, :], d_ref[columns, :]
        lse, delta = lse_ref[:, columns], delta_ref[:, columns]
        total = None
        for part in tile_parts(tile, start):
            span = pl.ds(part[0], TILE)
            scores = dot_nn(k_ref[span, :], query_t) * factor - lse
            scores = part_scores(scores, part, columns, bias_ref, triangle)
            weights = jnp.exp2(scores)
            weight_grads = dot_nn(v_ref[span, :], grad_t)
            score_grads = (weights * (weight_grads - delta)).astype(jnp.bfloat16)
            dv_ref[span, :] += dot_nn(weights.astype(jnp.bfloat16), grad)
            dk_ref[span, :] += dot_nn(score_grads, query)
            term = dot_nn(kt_ref[:, span], score_grads)
            total = term if total is None else total + term
        dq_ref[:, columns] = total

    for_tiles(length, body)
    half = HEAD_DIM // 2
    for z in range(sources):
        span = pl.ds(z * rows, rows)
        cosine, sine = cos_ref[:, span], sin_ref[:, span]
        for i, values in enumerate((dq_ref[:, span], dk_ref[span, :].T)):
            values = values * scaling
            first, second = values[:half], values[half:]
            back_ref[z, i * HEAD_DIM : (i + 1) * HEAD_DIM] = jnp.concatenate(
                [first * cosine + second * sine, second * cosine - first * sine], 0
            ).astype(jnp.bfloat16)
        back_ref[z, 2 * HEAD_DIM :] = dv_ref[span, :].T.astype(jnp.bfloat16)


def params(limit):
    return pltpu.CompilerParams(vmem_limit_bytes=limit * MIB)


def cost(flops, moved):
    return pl.CostEstimate(flops=int(flops), bytes_accessed=int(moved), transcendentals=0)


def greet(ring, copies):
    barrier = pltpu.get_barrier_semaphore()
    for target in ring + copies:
        pl.semaphore_signal(barrier, inc=1, device_id=target, device_id_type=pl.DeviceIdType.MESH)
    pl.semaphore_wait(barrier, len(ring) + len(copies))


def ring_partners(owners):
    member = lax.axis_index("expert")
    result = []
    for step in sorted(range(1, owners), key=lambda k: -min(k, owners - k)):
        index = lax.rem(member + step, owners)
        result.append((step, index, {"expert": index}))
    return result


def copy_partners(total):
    place = lax.axis_index("xy") * 2 + lax.axis_index("core")
    result = []
    for step in sorted(range(1, total), key=lambda k: -(k % 8 in (6, 2, 4))):
        index = lax.rem(place + step, total)
        result.append((step, lax.rem(index, 2), {"xy": index // 2, "core": lax.rem(index, 2)}))
    return result


def plane_chips(xy):
    return xy + 1 - 2 * lax.rem(xy, 2), lax.rem(xy + 2, 4), 3 - xy


def first_hops(beside, behind, across):
    return (
        (across * 2, 2, beside), (across * 2 + 1, 3, behind), (beside * 2, 0, beside), (behind * 2 + 1, 1, behind),
    )


def relayed(copies):
    return copies == 8


def remote(source, target, send, receive, device):
    return pltpu.make_async_remote_copy(
        src_ref=source, dst_ref=target, send_sem=send, recv_sem=receive,
        device_id=device, device_id_type=pl.DeviceIdType.MESH,
    )


def reach_of(parents):
    shape = (128, 128)
    one, two = lax.broadcasted_iota(jnp.int32, shape, 0), lax.broadcasted_iota(jnp.int32, shape, 1)
    count = parents.shape[1]
    none = lambda size: jnp.full((1, size), -1, jnp.int32)
    parent_row = jnp.concatenate([none(1), parents, none(127 - count)], 1)
    reach = jnp.where((one == two) | (one == parent_row), 1.0, 0.0).astype(jnp.bfloat16)
    for _ in range(3):
        reach = jnp.minimum(dot_nn(reach, reach), 1.0).astype(jnp.bfloat16)
    return reach


def place_tables(reach, first, size):
    ids = lax.broadcasted_iota(jnp.int32, (1, size), 1) + first
    later = ids - TRUNK
    segment = jnp.where(later < 0, 0, 1 + lax.shift_right_arithmetic(later, 7))
    inside = jnp.where(later < 0, later, (later & (SEG - 1)) - SEG)
    own = jnp.where(segment == lax.broadcasted_iota(jnp.int32, (128, size), 0), 1.0, 0.0).astype(jnp.bfloat16)
    seen = dot_nn(reach[:16], own)
    index = lax.broadcasted_iota(jnp.int32, (16, 1), 0)
    lengths = jnp.where(index == 0, float(TRUNK), float(SEG))
    places = jnp.sum(seen * lengths, 0, keepdims=True) + inside.astype(jnp.float32)
    turn = lax.broadcasted_iota(jnp.int32, (HEAD_DIM // 2, 1), 0).astype(jnp.float32)
    angles = jnp.exp(turn * (-2.0 / HEAD_DIM * 9.210340371976184)) * places
    return seen, jnp.cos(angles), jnp.sin(angles)


def slot_codes(routes_ref, codes_ref, codes_row_ref):
    rows = routes_ref.shape[1]
    half_slots = rows // NFFN
    turned = jnp.concatenate([routes_ref[...].astype(jnp.float32), jnp.zeros((126, rows), jnp.float32)], 0).T
    routes = turned.astype(jnp.int32)
    lanes = lax.broadcasted_iota(jnp.int32, (rows, 128), 1)
    matches = [
        jnp.where((lanes == routes[:, c : c + 1]) & (lanes < NFFN), 1.0, 0.0).astype(jnp.float32) for c in range(2)
    ]
    square = (rows, rows)
    earlier = lax.broadcasted_iota(jnp.int32, square, 0) > lax.broadcasted_iota(jnp.int32, square, 1)
    before = dot_nn(
        jnp.where(earlier, 1.0, 0.0).astype(jnp.bfloat16), (matches[0] + matches[1]).astype(jnp.bfloat16)
    )
    codes = jnp.zeros((rows, 128), jnp.float32)
    for c in range(2):
        rank = jnp.sum(matches[c] * before, -1, keepdims=True)
        route = routes[:, c : c + 1].astype(jnp.float32)
        late = jnp.where(rank >= half_slots, float((NFFN - 1) * half_slots), 0.0)
        code = jnp.where(route < NFFN, route * half_slots + rank + late, float(4 * rows))
        codes = jnp.where(lanes == c, code, jnp.where(lanes == 2 + c, route, codes))
    codes_ref[...] = codes.astype(jnp.int32)
    codes_row_ref[...] = codes.T[:8].astype(jnp.int32)


def attend_phase_kernel(
    tokens_ref, table_ref, query_ref, key_ref, value_ref, parents_ref, routes_ref, gate_ref, up_ref, down_ref,
    attended_ref, lse_ref, bias_ref, cos_ref, sin_ref, codes_ref, codes_row_ref, heads_ref, outs_ref,
    gate_full, up_full, down_full,
    normed_ref, qkv_sent, qkv_got, out_sent, out_got, q_ref, k_ref, v_ref, o_ref, s_ref, triangle,
    qkv_send, qkv_recv, out_send, out_recv, weight_send, weight_recv, local_sem,
):
    chunks, owners, _, rows = qkv_sent.shape
    member = lax.axis_index("expert")
    copies = gate_full.shape[0]
    ring, others = ring_partners(owners), copy_partners(copies)
    greet([item[2] for item in ring], [item[2] for item in others])
    weights = ((gate_ref, gate_full), (up_ref, up_full), (down_ref, down_full))
    place = lax.axis_index("xy") * 2 + lax.axis_index("core")
    core = lax.axis_index("core")
    started = []

    relays = relayed(copies)
    xy = lax.axis_index("xy")
    beside, behind, across = plane_chips(xy)
    arrivals = {}

    def send_weight(i):
        shard, full = weights[i]
        local = pltpu.make_async_copy(shard.at[core], full.at[place], weight_send.at[i, 0])
        local.start()
        started.append(local.wait)
        if relays:
            targets = [(2, beside, 0), (4, behind, 0), (2, beside, 1), (4, behind, 1)]
            targets = [(1, 1 - core, {"core": 1 - core})] + [
                (base + core, other, {"xy": chip, "core": other}) for base, chip, other in targets
            ]
            for n, (slot, other, device) in enumerate(targets):
                copy = remote(
                    shard.at[other], full.at[place], weight_send.at[i, 1 + n], weight_recv.at[i, slot], device
                )
                copy.start()
                started.append(copy.wait_send)
            for slot in range(1, 8):
                arrivals[i, slot] = remote(
                    shard.at[core], full.at[place], weight_send.at[i, 0], weight_recv.at[i, slot], {"core": 1 - core}
                )
        else:
            for step, other_core, device in others:
                copy = remote(
                    shard.at[other_core], full.at[place], weight_send.at[i, step], weight_recv.at[i, step], device
                )
                copy.start()
                started.append(copy.wait)

    def relay_weight(i):
        full = weights[i][1]
        for slot, piece, chip, landing in ((4, behind * 2, beside, 6), (3, beside * 2 + 1, behind, 7)):
            arrivals.pop((i, slot)).wait_recv()
            copy = remote(
                full.at[piece], full.at[piece], weight_send.at[i, landing], weight_recv.at[i, landing], {"xy": chip}
            )
            copy.start()
            started.append(copy.wait_send)

    for i in range(3):
        send_weight(i)

    inputs = tokens_ref[...].astype(jnp.float32)
    inverse = lax.rsqrt(jnp.mean(inputs * inputs, -1, keepdims=True) + epsilon)
    normed_ref[...] = (inputs * inverse * table_ref[0:1, :]).astype(jnp.bfloat16)
    reach = reach_of(parents_ref[...])
    _, cosine, sine = place_tables(reach, member * rows, rows)
    half = HEAD_DIM // 2
    span_width = owners * HEAD_DIM
    qkv_copies = []
    for j in range(chunks):
        for i, weight in enumerate((query_ref, key_ref, value_ref)):
            turned = dot_nn(normed_ref[...], weight[:, j * span_width : (j + 1) * span_width]).T
            base = i * HEAD_DIM
            for z in range(owners):
                first = turned[z * HEAD_DIM : z * HEAD_DIM + half]
                second = turned[z * HEAD_DIM + half : (z + 1) * HEAD_DIM]
                if i < 2:
                    first, second = first * cosine - second * sine, second * cosine + first * sine
                qkv_sent[j, z, base : base + half] = first.astype(jnp.bfloat16)
                qkv_sent[j, z, base + half : base + HEAD_DIM] = second.astype(jnp.bfloat16)
        local = pltpu.make_async_copy(qkv_sent.at[j, member], qkv_got.at[j, member], local_sem.at[j])
        local.start()
        group = []
        for step, index, device in ring:
            copy = remote(
                qkv_sent.at[j, index], qkv_got.at[j, member],
                qkv_send.at[j, step - 1], qkv_recv.at[j, step - 1], device,
            )
            copy.start()
            group.append(copy)
        qkv_copies.append((local, group))
    seen, whole_cosine, whole_sine = place_tables(reach, 0, owners * rows)
    bias_ref[...] = jnp.where(seen > 0.5, 0.0, masked_score)
    cos_ref[...] = whole_cosine
    sin_ref[...] = whole_sine
    slot_codes(routes_ref, codes_ref, codes_row_ref)

    out_copies = []
    kept = []
    for j in range(chunks):
        local, group = qkv_copies[j]
        local.wait()
        for copy in group:
            copy.wait_recv()
        keep = pltpu.make_async_copy(qkv_got.at[j], heads_ref.at[j], local_sem.at[chunks + j])
        keep.start()
        kept.append(keep)
        attend_head(
            bias_ref, qkv_got.at[j], out_sent.at[j], lse_ref.at[j : j + 1], q_ref, k_ref, v_ref, o_ref, s_ref, triangle
        )
        local = pltpu.make_async_copy(out_sent.at[j, member], out_got.at[j, member], local_sem.at[2 * chunks + j])
        local.start()
        keep = pltpu.make_async_copy(out_sent.at[j], outs_ref.at[j], local_sem.at[3 * chunks + j])
        keep.start()
        kept += [local, keep]
        for step, index, device in ring:
            copy = remote(
                out_sent.at[j, index], out_got.at[j, member],
                out_send.at[j, step - 1], out_recv.at[j, step - 1], device,
            )
            copy.start()
            out_copies.append(copy)
        if relays and j == 1:
            for i in range(3):
                relay_weight(i)
    for copy in out_copies:
        copy.wait_recv()
    for copy in kept:
        copy.wait()
    attended_ref[...] = out_got[...]
    for local, group in qkv_copies:
        for copy in group:
            copy.wait_send()
    for copy in out_copies:
        copy.wait_send()
    for copy in arrivals.values():
        copy.wait_recv()
    for wait in started:
        wait()


def attend_phase(tokens, table, weights, parents, routes, shards, copies):
    rows, width = tokens.shape
    owners = lax.axis_size("expert")
    length = rows * owners
    chunks = width // HEAD_DIM // owners
    head = (chunks, owners, 3 * HEAD_DIM, rows)
    out = (chunks, owners, HEAD_DIM, rows)
    vmem, hbm = pl.BlockSpec(memory_space=pltpu.VMEM), pl.BlockSpec(memory_space=pl.ANY)
    fulls = [jax.ShapeDtypeStruct((copies, *shard.shape[1:]), shard.dtype) for shard in shards]
    part_total = TRUNK // TILE + 3
    sems = lambda *shape: pltpu.SemaphoreType.DMA(shape)
    return pl.pallas_call(
        attend_phase_kernel,
        in_specs=[vmem] * 7 + [hbm] * 3,
        out_specs=(vmem,) * 7 + (hbm,) * 5,
        out_shape=(
            jax.ShapeDtypeStruct(out, jnp.bfloat16),
            jax.ShapeDtypeStruct((8, length), jnp.float32),
            jax.ShapeDtypeStruct((16, length), jnp.float32),
            *(jax.ShapeDtypeStruct((HEAD_DIM // 2, length), jnp.float32),) * 2,
            jax.ShapeDtypeStruct((rows, 128), jnp.int32),
            jax.ShapeDtypeStruct((8, rows), jnp.int32),
            jax.ShapeDtypeStruct(head, jnp.bfloat16),
            jax.ShapeDtypeStruct(out, jnp.bfloat16),
            *fulls,
        ),
        scratch_shapes=[
            pltpu.VMEM((rows, width), jnp.bfloat16),
            pltpu.VMEM(head, jnp.bfloat16),
            pltpu.VMEM(head, jnp.bfloat16),
            pltpu.VMEM(out, jnp.bfloat16),
            pltpu.VMEM(out, jnp.bfloat16),
            pltpu.VMEM((HEAD_DIM, length), jnp.bfloat16),
            pltpu.VMEM((length, HEAD_DIM), jnp.bfloat16),
            pltpu.VMEM((HEAD_DIM + 16, length), jnp.bfloat16),
            pltpu.VMEM((HEAD_DIM, length), jnp.bfloat16),
            pltpu.VMEM((part_total * TILE, TILE), jnp.float32),
            pltpu.VMEM((TILE, TILE), jnp.float32),
            sems(chunks, owners - 1), sems(chunks, owners - 1), sems(chunks, owners - 1), sems(chunks, owners - 1),
            sems(3, copies), sems(3, copies), sems(4 * chunks),
        ],
        compiler_params=pltpu.CompilerParams(vmem_limit_bytes=63 * MIB, collective_id=1, has_side_effects=True),
        cost_estimate=cost(1e10, 5e7),
    )(tokens, table, *weights, parents, routes, *shards)


def lane_pick(values, lanes, index):
    return jnp.sum(jnp.where(lanes == index, values, 0.0), -1, keepdims=True)


def middle_kernel(
    tokens_ref, attended_ref, out_weight_ref, table_ref, router_ref, constant_ref, prior_ref, prior_weight_ref,
    codes_ref, codes_row_ref, resid_ref, small_ref, first_ref, second_ref, mixer_ref, hidden_ref,
):
    rows, width = tokens_ref.shape
    mixer = [ref[...].astype(jnp.float32) for ref in (router_ref, constant_ref)]
    mixer_ref[...] = jnp.concatenate([*mixer, jnp.zeros((128 - NEXP - 4, width), jnp.float32)], 0).astype(jnp.bfloat16)
    missing = jnp.zeros((16 - NEXP, SEG), jnp.float32)

    @pl.loop(0, rows // SEG)
    def _(step):
        span = pl.ds(pl.multiple_of(step * SEG, SEG), SEG)
        attended = attended_ref[:, span].astype(jnp.float32).T.astype(jnp.bfloat16)
        resid = tokens_ref[span, :].astype(jnp.float32) + dot_nn(attended, out_weight_ref[...])
        inverse = lax.rsqrt(jnp.mean(resid * resid, -1, keepdims=True) + epsilon)
        hidden = (resid * inverse * table_ref[1:2, :]).astype(jnp.bfloat16)
        resid_ref[span, :] = resid
        hidden_ref[span, :] = hidden
        logits = dot_nt(hidden, mixer_ref[...])
        prior = jnp.concatenate([prior_ref[:, span], missing], 0).T[:, :NEXP]
        carried = jnp.dot(prior, prior_weight_ref[...], precision=precise, preferred_element_type=jnp.float32)
        logits = logits + jnp.concatenate([carried, jnp.zeros((SEG, 128 - NEXP), jnp.float32)], 1)
        lanes = lax.broadcasted_iota(jnp.int32, logits.shape, 1)
        routes = codes_ref[span, 2:4]
        columns = []
        pairs = [[lane_pick(logits, lanes, routes[:, c : c + 1]) for c in range(2)]]
        pairs += [[logits[:, NEXP + 2 * m + c : NEXP + 2 * m + c + 1] for c in range(2)] for m in range(2)]
        for one, two in pairs:
            peak = jnp.maximum(one, two)
            one, two = jnp.exp(one - peak), jnp.exp(two - peak)
            columns += [one / (one + two), two / (one + two)]
        columns.append(inverse)
        small = jnp.zeros_like(logits)
        for i, column in enumerate(columns):
            small = jnp.where(lanes == i, column, small)
        small_ref[span, :] = small

    slots = first_ref.shape[0]
    for half, ref in enumerate((first_ref, second_ref)):
        index = lax.broadcasted_iota(jnp.int32, (slots, rows), 0) + half * slots
        chosen = (codes_row_ref[0:1, :] == index) | (codes_row_ref[1:2, :] == index)
        ref[...] = dot_nn(chosen.astype(jnp.bfloat16), hidden_ref[...]).astype(jnp.bfloat16)


def middle(tokens, attended, out_weight, table, router, constant, prior, prior_weight, codes, codes_row):
    rows, width = tokens.shape
    slots = rows
    return pl.pallas_call(
        middle_kernel,
        out_shape=(
            jax.ShapeDtypeStruct((rows, width), jnp.float32),
            jax.ShapeDtypeStruct((rows, 128), jnp.float32),
            jax.ShapeDtypeStruct((slots, width), jnp.bfloat16),
            jax.ShapeDtypeStruct((slots, width), jnp.bfloat16),
            jax.ShapeDtypeStruct((128, width), jnp.bfloat16),
        ),
        scratch_shapes=[pltpu.VMEM((rows, width), jnp.bfloat16)],
        compiler_params=params(63),
        cost_estimate=cost(4 * rows * width * width + 4 * rows * rows * width, 1e7),
    )(tokens, attended, out_weight, table, router, constant, prior, prior_weight, codes, codes_row)


def plane_partners(owners):
    total = 2 * owners
    place = lax.axis_index("expert") * 2 + lax.axis_index("core")
    result = []
    for step in sorted(range(1, total), key=lambda k: -min(k, total - k)):
        index = lax.rem(place + step, total)
        result.append((step, index, {"expert": index // 2, "core": lax.rem(index, 2)}))
    return result


def expert_phase_kernel(
    xa_ref, xb_ref, small_ref, grad_ref, codes_ref, gate_hbm, up_hbm, down_hbm,
    back_out, dots_out, fa_out, fb_out, gate_grad, up_grad, down_grad,
    gate_ref, up_ref, down_ref, scaled_ref, d_sent, x_got, d_got, back_sent, back_got, dots_sent, dots_got,
    f_sum, back_sum, hid_ref, one_ref, two_ref, x_turned, d_turned, stage, stage_down,
    x_send, x_recv, d_send, d_recv, back_send, back_recv, dots_send, dots_recv, local_sem, stage_sem,
):
    experts, slots, width = x_got.shape[1:]
    rows = experts * slots
    units = gate_ref.shape[1]
    owners = experts // 2
    place = lax.axis_index("expert") * 2 + lax.axis_index("core")
    partners = plane_partners(owners)
    greet([item[2] for item in partners], [])
    loads = [
        pltpu.make_async_copy(source, target, local_sem.at[i])
        for i, (source, target) in enumerate(((gate_hbm, gate_ref), (up_hbm, up_ref), (down_hbm, down_ref)))
    ]
    for load in loads:
        load.start()

    def send(source, target, sends, receives, half, locals_at):
        copies = []
        local = pltpu.make_async_copy(source(place), target.at[half, place], local_sem.at[locals_at + half])
        local.start()
        for step, index, device in partners:
            copy = remote(source(index), target.at[half, place], sends.at[half, step], receives.at[half, step], device)
            copy.start()
            copies.append(copy)
        return local, copies

    def arrive(group):
        group[0].wait()
        for copy in group[1]:
            copy.wait_recv()

    x_refs = (xa_ref, xb_ref)
    x_groups = [send(lambda e, ref=ref: ref.at[e], x_got, x_send, x_recv, h, 3) for h, ref in enumerate(x_refs)]
    for c in range(2):
        scaled_ref[c * rows : (c + 1) * rows, :] = (
            small_ref[:, c : c + 1] * grad_ref[...].astype(jnp.float32)
        ).astype(jnp.bfloat16)
    d_groups = []
    for half in range(2):
        index = lax.broadcasted_iota(jnp.int32, (rows, rows), 0) + half * rows
        chosen = jnp.concatenate([(codes_ref[c : c + 1, :] == index).astype(jnp.bfloat16) for c in range(2)], 1)
        d_sent[half] = dot_nn(chosen, scaled_ref[...]).astype(jnp.bfloat16).reshape(experts, slots, width)
        d_groups.append(send(lambda e, half=half: d_sent.at[half, e], d_got, d_send, d_recv, half, 5))
    for load in loads:
        load.wait()

    part = 512
    tile = rows // 2

    def forward(half):
        x = x_got[half].reshape(rows, width)
        f_sum[...] = jnp.zeros_like(f_sum)
        x_turned[:, half * rows : (half + 1) * rows] = x.astype(jnp.float32).T.astype(jnp.bfloat16)

        @pl.loop(0, units // part)
        def _(step):
            columns = pl.ds(pl.multiple_of(step * part, part), part)
            for r in range(2):
                near = slice(r * tile, (r + 1) * tile)
                far = pl.ds(half * rows + r * tile, tile)
                gate_pre = dot_nn(x[near], gate_ref[:, columns])
                up_pre = dot_nn(x[near], up_ref[:, columns])
                sigmoid = 1.0 / (1.0 + jnp.exp(-gate_pre))
                active = gate_pre * sigmoid
                hid = (active * up_pre).astype(jnp.bfloat16)
                hid_ref[far, columns] = hid
                one_ref[far, columns] = (up_pre * (sigmoid + active * (1.0 - sigmoid))).astype(jnp.bfloat16)
                two_ref[far, columns] = active.astype(jnp.bfloat16)
                f_sum[near, :] += dot_nn(hid, down_ref[columns, :])

        (fa_out, fb_out)[half][...] = f_sum[...].astype(jnp.bfloat16).reshape(experts, slots, width)

    def backward(half):
        d = d_got[half].reshape(rows, width)
        back_sum[...] = jnp.zeros_like(back_sum)
        d_turned[:, half * rows : (half + 1) * rows] = d.astype(jnp.float32).T.astype(jnp.bfloat16)

        @pl.loop(0, units // part)
        def _(step):
            columns = pl.ds(pl.multiple_of(step * part, part), part)
            for r in range(2):
                near = slice(r * tile, (r + 1) * tile)
                far = pl.ds(half * rows + r * tile, tile)
                mid = dot_nt(d[near], down_ref[columns, :])
                dg = (mid * one_ref[far, columns].astype(jnp.float32)).astype(jnp.bfloat16)
                du = (mid * two_ref[far, columns].astype(jnp.float32)).astype(jnp.bfloat16)
                one_ref[far, columns] = dg
                two_ref[far, columns] = du
                back_sum[near, :] += dot_nt(dg, gate_ref[:, columns]) + dot_nt(du, up_ref[:, columns])

        back_sent[half] = back_sum[...].astype(jnp.bfloat16).reshape(experts, slots, width)

    def dots(half):
        ones = jnp.ones((8, width), jnp.float32)
        for e in range(experts):
            product = (fa_out, fb_out)[half][e].astype(jnp.float32) * d_got[half, e].astype(jnp.float32)
            total = lax.dot_general(
                ones, product, (((1,), (1,)), ((), ())), precision=precise, preferred_element_type=jnp.float32
            )
            dots_sent[half, e] = jnp.concatenate([total, jnp.zeros((8, 128 - slots), jnp.float32)], 1)

    for half in range(2):
        arrive(x_groups[half])
        forward(half)
    back_groups, dots_groups = [], []
    for half in range(2):
        arrive(d_groups[half])
        backward(half)
        back_groups.append(send(lambda e, half=half: back_sent.at[half, e], back_got, back_send, back_recv, half, 7))
        dots(half)
        dots_groups.append(send(lambda e, half=half: dots_sent.at[half, e], dots_got, dots_send, dots_recv, half, 9))

    piece = 256
    steps = units // piece

    def stores(step, slot):
        columns = pl.ds(pl.multiple_of(step * piece, piece), piece)
        return [
            pltpu.make_async_copy(stage.at[0, slot], gate_grad.at[:, columns], stage_sem.at[0, slot]),
            pltpu.make_async_copy(stage.at[1, slot], up_grad.at[:, columns], stage_sem.at[1, slot]),
            pltpu.make_async_copy(stage_down.at[slot], down_grad.at[columns, :], stage_sem.at[2, slot]),
        ]

    @pl.loop(0, steps // 2)
    def _(pair):
        for slot in range(2):
            step = pair * 2 + slot
            columns = pl.ds(pl.multiple_of(step * piece, piece), piece)

            @pl.when(pair > 0)
            def _():
                for store in stores(step, slot):
                    store.wait()

            stage[0, slot] = dot_nn(x_turned[...], one_ref[:, columns]).astype(jnp.bfloat16)
            stage[1, slot] = dot_nn(x_turned[...], two_ref[:, columns]).astype(jnp.bfloat16)
            stage_down[slot] = dot_nn(d_turned[...], hid_ref[:, columns]).T.astype(jnp.bfloat16)
            for store in stores(step, slot):
                store.start()

    for slot in range(2):
        for store in stores(steps - 2 + slot, slot):
            store.wait()
    for group in back_groups + dots_groups:
        arrive(group)
    back_out[...] = back_got[...]
    dots_out[...] = dots_got[...]
    for group in x_groups + d_groups + back_groups + dots_groups:
        for copy in group[1]:
            copy.wait_send()


def expert_phase(x_parts, small, grad, codes_row, gate, up, down):
    rows, width = grad.shape
    units = gate.shape[1]
    slots = rows // NFFN
    both = (2, NFFN, slots, width)
    dots = (2, NFFN, 8, 128)
    vmem, hbm = pl.BlockSpec(memory_space=pltpu.VMEM), pl.BlockSpec(memory_space=pl.ANY)
    sems = pltpu.SemaphoreType.DMA((2, NFFN))
    wide = pltpu.VMEM((rows, width), jnp.float32)
    mids = pltpu.VMEM((2 * rows, units), jnp.bfloat16)
    turned = pltpu.VMEM((width, 2 * rows), jnp.bfloat16)
    moved = pltpu.VMEM(both, jnp.bfloat16)
    return pl.pallas_call(
        expert_phase_kernel,
        in_specs=[vmem] * 5 + [hbm] * 3,
        out_specs=(vmem, vmem, vmem, vmem, hbm, hbm, hbm),
        out_shape=(
            jax.ShapeDtypeStruct(both, jnp.bfloat16),
            jax.ShapeDtypeStruct(dots, jnp.float32),
            *(jax.ShapeDtypeStruct(both[1:], jnp.bfloat16),) * 2,
            jax.ShapeDtypeStruct(gate.shape, jnp.bfloat16),
            jax.ShapeDtypeStruct(up.shape, jnp.bfloat16),
            jax.ShapeDtypeStruct(down.shape, jnp.bfloat16),
        ),
        scratch_shapes=[
            pltpu.VMEM(gate.shape, jnp.bfloat16),
            pltpu.VMEM(up.shape, jnp.bfloat16),
            pltpu.VMEM(down.shape, jnp.bfloat16),
            pltpu.VMEM((2 * rows, width), jnp.bfloat16),
            moved, moved, moved, moved, moved,
            pltpu.VMEM(dots, jnp.float32),
            pltpu.VMEM(dots, jnp.float32),
            wide, wide, mids, mids, mids, turned, turned,
            pltpu.VMEM((2, 2, width, 256), jnp.bfloat16),
            pltpu.VMEM((2, 256, width), jnp.bfloat16),
            *(sems,) * 8,
            pltpu.SemaphoreType.DMA((11,)),
            pltpu.SemaphoreType.DMA((3, 2)),
        ],
        compiler_params=pltpu.CompilerParams(vmem_limit_bytes=63 * MIB, collective_id=2, has_side_effects=True),
        cost_estimate=cost(36 * rows * width * units, 5e7),
    )(*(part.reshape(NFFN, slots, width) for part in x_parts), small, grad, codes_row, gate, up, down)


def split_dot(dot, left, right):
    high = left.astype(jnp.bfloat16)
    low = (left - high.astype(jnp.float32)).astype(jnp.bfloat16)
    return dot(high, right) + dot(low, right)


def put_part(ref, values, begin):
    _, chips, owners, tall, half = ref.shape
    end = begin + values.shape[1]
    for core in range(2):
        low, high = max(begin, core * half), min(end, (core + 1) * half)
        if low < high:
            for z in range(owners):
                for chip in range(chips):
                    row = (z * chips + chip) * tall
                    ref[core, chip, z, :, low - core * half : high - core * half] = values[
                        row : row + tall, low - begin : high - begin
                    ]


def turn_kernel(
    resid_ref, small_ref, grad_ref, prior_ref, codes_ref, returned_ref, dots_ref, table_ref,
    mixer_ref, prior_weight_ref, out_weight_ref, attended_ref, f_ref, gate_ref,
    resid_grad_ref, grads_ref, out_grad_ref, prior_grad_ref, f_got, gate_first,
    back_ref, sums_ref, prior_sums_ref, extra_ref, f_send, f_recv, gate_send, gate_recv, *, owners, reduce,
):
    rows, width = resid_ref.shape
    planes = plane_partners(owners)
    beside, behind, across = plane_chips(lax.axis_index("xy"))
    greet([item[2] for item in planes], [{"xy": beside}, {"xy": behind}] if reduce else [])
    expert = lax.axis_index("expert") * 2 + lax.axis_index("core")
    copies = [pltpu.make_async_copy(f_ref.at[expert], f_got.at[expert], f_send.at[0])]
    copies += [
        remote(f_ref.at[index], f_got.at[expert], f_send.at[step], f_recv.at[step], device)
        for step, index, device in planes
    ]
    if reduce:
        for piece, landing, chip in first_hops(beside, behind, across):
            copies.append(
                remote(
                    gate_ref.at[piece], gate_first.at[landing], gate_send.at[landing], gate_recv.at[landing],
                    {"xy": chip},
                )
            )
    for copy in copies:
        copy.start()
    slots = returned_ref.shape[0]
    sums_ref[...] = jnp.zeros_like(sums_ref)
    prior_sums_ref[...] = jnp.zeros_like(prior_sums_ref)

    @pl.loop(0, rows // SEG)
    def _(step):
        span = pl.ds(pl.multiple_of(step * SEG, SEG), SEG)
        small = small_ref[span, :]
        codes = codes_ref[span, :]
        routes = codes[:, 2:4]
        gates = [small[:, c : c + 1] for c in range(2)]
        mixing = [[small[:, 2 + 2 * m + c : 3 + 2 * m + c] for c in range(2)] for m in range(2)]
        inverse = small[:, 6:7]
        normed = resid_ref[span, :] * inverse
        gain = table_ref[1:2, :]
        hidden = normed * gain
        hidden_b = hidden.astype(jnp.bfloat16)
        grad_b = grad_ref[span, :]
        grad = grad_b.astype(jnp.float32)
        index = lax.broadcasted_iota(jnp.int32, (SEG, slots), 1)
        hits = [codes[:, c : c + 1] == index for c in range(2)]
        dots = dots_ref[...]
        terms = [jnp.sum(jnp.where(hit, dots, 0.0), -1, keepdims=True) for hit in hits]
        chosen = (hits[0] | hits[1]).astype(jnp.bfloat16)
        routed = dot_nn(chosen, returned_ref[...])
        along = jnp.sum(grad * hidden, -1, keepdims=True)
        across = [jnp.sum(grad * table_ref[2 + m : 3 + m, :], -1, keepdims=True) for m in range(2)]
        to_copy = 0.0
        to_mix = [0.0, 0.0]
        for c in range(2):
            route = routes[:, c : c + 1]
            copied = jnp.where(route == NFFN + 1, gates[c], 0.0)
            to_copy = to_copy + copied
            terms[c] = terms[c] + copied * along
            for m in range(2):
                mixed = jnp.where(route == NFFN + 2 + m, gates[c], 0.0)
                to_mix[m] = to_mix[m] + mixed
                terms[c] = terms[c] + mixed * (mixing[m][0] * along + mixing[m][1] * across[m])
        both = terms[0] + terms[1]
        lanes = lax.broadcasted_iota(jnp.int32, (SEG, 128), 1)
        logit_grads = jnp.zeros((SEG, 128), jnp.float32)
        for c in range(2):
            logit_grads = jnp.where(lanes == routes[:, c : c + 1], terms[c] - gates[c] * both, logit_grads)
        scores = logit_grads
        direct = to_copy
        for m in range(2):
            pair = (to_mix[m] * along, to_mix[m] * across[m])
            mean = mixing[m][0] * pair[0] + mixing[m][1] * pair[1]
            for c in range(2):
                scores = jnp.where(lanes == NEXP + 2 * m + c, mixing[m][c] * (pair[c] - mean), scores)
            direct = direct + mixing[m][0] * to_mix[m]
        prior_grad_ref[:, span] = lax.dot_general(
            prior_weight_ref[...], logit_grads[:, :NEXP], (((1,), (1,)), ((), ())),
            precision=precise, preferred_element_type=jnp.float32,
        )
        hidden_grads = split_dot(dot_nn, scores, mixer_ref[...]) + direct * grad + routed
        scaled = hidden_grads * gain
        resid_grads = inverse * (scaled - normed * jnp.mean(scaled * normed, -1, keepdims=True)) + grad
        resid_grad_ref[span, :] = resid_grads
        back_ref[span, :] = resid_grads.astype(jnp.bfloat16)
        weights = jnp.zeros((SEG, 128), jnp.float32)
        for m in range(2):
            weights = jnp.where(lanes == m, mixing[m][1] * to_mix[m], weights)
        sums_ref[0:16, :] += split_dot(dot_nn, scores.T[0:16], hidden_b)
        sums_ref[16:24, :] += split_dot(dot_nn, weights.T[0:8], grad_b)
        sums_ref[24:32, :] += jnp.sum((hidden_grads * normed).reshape(SEG // 8, 8, width), 0)
        prior_sums_ref[...] += jnp.dot(
            prior_ref[:, span],
            jnp.concatenate([logit_grads[:, 96:], logit_grads[:, :96]], 1),
            precision=precise,
            preferred_element_type=jnp.float32,
        )

    sums_ref[24:25, :] = jnp.sum(sums_ref[24:32, :], 0, keepdims=True)
    extra_ref[...] = jnp.concatenate([sums_ref[...], jnp.zeros((96, width), jnp.float32)], 0).T
    kept = NEXP // owners
    for z in range(owners):
        extra_ref[pl.ds(z * (width // owners), kept), :] += prior_sums_ref[z * kept : (z + 1) * kept, :]
    small_part = jnp.concatenate([extra_ref[...], jnp.zeros((width, 128), jnp.float32)], 1).astype(jnp.bfloat16)
    put_part(out_grad_ref, small_part, width)
    back = back_ref[...]
    grads_ref[...] = dot_nt(out_weight_ref[...], back).astype(jnp.bfloat16)
    put_part(out_grad_ref, dot_nn(attended_ref[...], back).astype(jnp.bfloat16), 0)
    for copy in copies:
        copy.wait()


def turn(resid, small, grad, prior, codes, returned, dots, table, mixer, prior_weight, out_weight, attended, f, gate):
    rows, width = resid.shape
    owners = lax.axis_size("expert")
    vmem, hbm = pl.BlockSpec(memory_space=pltpu.VMEM), pl.BlockSpec(memory_space=pl.ANY)
    return pl.pallas_call(
        functools.partial(turn_kernel, owners=owners, reduce=relayed(gate.shape[0])),
        in_specs=[vmem] * 12 + [hbm] * 2,
        out_specs=(vmem, vmem, vmem, vmem, hbm, hbm),
        out_shape=(
            jax.ShapeDtypeStruct((rows, width), jnp.float32),
            jax.ShapeDtypeStruct((width, rows), jnp.bfloat16),
            jax.ShapeDtypeStruct((2, 4, owners, width // owners // 4, (width + 256) // 2), jnp.bfloat16),
            jax.ShapeDtypeStruct(prior.shape, jnp.float32),
            jax.ShapeDtypeStruct(f.shape, f.dtype),
            jax.ShapeDtypeStruct((4, *gate.shape[1:]), gate.dtype),
        ),
        scratch_shapes=[
            pltpu.VMEM((rows, width), jnp.bfloat16),
            pltpu.VMEM((32, width), jnp.float32),
            pltpu.VMEM((prior.shape[0], 128), jnp.float32),
            pltpu.VMEM((width, 128), jnp.float32),
            pltpu.SemaphoreType.DMA((2 * owners,)),
            pltpu.SemaphoreType.DMA((2 * owners,)),
            pltpu.SemaphoreType.DMA((4,)),
            pltpu.SemaphoreType.DMA((4,)),
        ],
        compiler_params=pltpu.CompilerParams(vmem_limit_bytes=63 * MIB, collective_id=4, has_side_effects=True),
        cost_estimate=cost(4 * rows * width * width + 4 * rows * rows * width, 1.5e7),
    )(resid, small, grad, prior, codes, returned, dots, table, mixer, prior_weight, out_weight, attended, f, gate)


def finish_kernel(
    resid_ref, small_ref, codes_ref, fa_ref, fb_ref, table_ref, totals_ref, tokens_grad_ref, *refs, owners, count, reduce
):
    experts, refs = refs[: 3 * count], refs[3 * count :]
    tokens_grad_out, *expert_outs = refs[:4]
    out_ref, *weight_refs, router_ref, prior_ref, constant_ref, vector_ref, gains_ref = refs[4:14]
    held, *work = refs[14:-2]
    load_sem, store_sem = refs[-2:]
    core = lax.axis_index("core")
    place = lax.axis_index("xy") * 2 + core
    load = pltpu.make_async_copy(tokens_grad_ref, held, load_sem.at[0])
    loads = []
    for i in range(3):
        if reduce:
            piece, first, got = experts[3 * i : 3 * i + 3]
            items = (piece.at[place], first.at[core], got.at[4 + core], got.at[6], got.at[7], got.at[5 - core])
        else:
            items = (experts[i],)
        for n, item in enumerate(items):
            target = work[2 * i].at[n] if reduce else work[2 * i + 1]
            loads.append((i, pltpu.make_async_copy(item, target, load_sem.at[1 + 6 * i + n])))
    load.start()
    for _, item in loads:
        item.start()
    stores = [pltpu.make_async_copy(held, tokens_grad_out, store_sem.at[0])]
    stores += [pltpu.make_async_copy(work[2 * i + 1], expert_outs[i], store_sem.at[1 + i]) for i in range(3)]
    rows, width = resid_ref.shape
    half = fa_ref.shape[0]

    @pl.loop(0, rows // SEG)
    def _(step):
        span = pl.ds(pl.multiple_of(step * SEG, SEG), SEG)
        small = small_ref[span, :]
        codes = codes_ref[span, :]
        routes = codes[:, 2:4]
        resid = resid_ref[span, :]
        hidden = resid * small[:, 6:7] * table_ref[1:2, :]
        index = lax.broadcasted_iota(jnp.int32, (SEG, 2 * half), 1)
        total = resid
        direct = 0.0
        for c in range(2):
            gate, route = small[:, c : c + 1], routes[:, c : c + 1]
            chosen = (codes[:, c : c + 1] == index).astype(jnp.bfloat16)
            routed = dot_nn(chosen[:, :half], fa_ref[...]) + dot_nn(chosen[:, half:], fb_ref[...])
            total = total + gate * routed
            direct = direct + jnp.where(route == NFFN + 1, gate, 0.0)
            for m in range(2):
                mixed = jnp.where(route == NFFN + 2 + m, gate, 0.0)
                direct = direct + mixed * small[:, 2 + 2 * m : 3 + 2 * m]
                total = total + mixed * small[:, 3 + 2 * m : 4 + 2 * m] * table_ref[2 + m : 3 + m, :]
        out_ref[span, :] = (total + direct * hidden).astype(jnp.bfloat16)

    load.wait()
    stores[0].start()
    for i in range(3):
        for index, item in loads:
            if index == i:
                item.wait()
        if reduce:
            wide = work[2 * i + 1]
            for n in range(2):
                wide[core if n == 0 else 1 - core] = jnp.sum(work[2 * i][3 * n : 3 * n + 3].astype(jnp.float32), 0)
        stores[1 + i].start()
    span = owners * HEAD_DIM
    chunks = width // span
    offsets, _ = part_columns(width, chunks)
    for i, ref in enumerate(weight_refs[:3]):
        for j in range(chunks):
            begin = offsets[j + 1] + i * span if j < chunks - 1 or i < 2 else offsets[-1]
            ref[:, j * span : (j + 1) * span] = totals_ref[:, begin : begin + span].astype(jnp.float32)
    weight_refs[3][...] = totals_ref[:, :width].astype(jnp.float32)
    extra = totals_ref[:, width : width + 128].astype(jnp.float32)
    prior_ref[...] = extra[: NEXP // owners, 32 : 32 + NEXP]
    turned = extra.T
    router_ref[...] = turned[:NEXP]
    constant_ref[...] = turned[NEXP : NEXP + 4]
    vector_ref[...] = turned[16:18]
    begin = offsets[-1] + span
    gains = totals_ref[:, begin : begin + 128].astype(jnp.float32).T
    member = lax.axis_index("expert")
    share = router_ref.shape[1]
    own_gain = table_ref[0:1, :share]
    for z in range(1, owners):
        own_gain = jnp.where(member == z, table_ref[0:1, z * share : (z + 1) * share], own_gain)
    gains_ref[0:1, :] = gains[0:1] / own_gain
    gains_ref[1:2, :] = turned[24:25]
    for move in stores:
        move.wait()


def finish(resid, small, codes, outs, table, totals, tokens_grad, experts, reduce):
    rows, width = resid.shape
    owners = lax.axis_size("expert")
    share = width // owners
    vmem, hbm = pl.BlockSpec(memory_space=pltpu.VMEM), pl.BlockSpec(memory_space=pl.ANY)
    shape = lambda *dims: jax.ShapeDtypeStruct(dims, jnp.float32)
    count = 3 if reduce else 1
    shapes = [item.shape[1:] for item in experts[count - 1 :: count]]
    work = []
    for dims in shapes:
        work += [pltpu.VMEM((6 if reduce else 1, *dims), jnp.bfloat16), pltpu.VMEM((2, *dims), jnp.float32)]
    return pl.pallas_call(
        functools.partial(finish_kernel, owners=owners, count=count, reduce=reduce),
        in_specs=[vmem] * 7 + [hbm] * (1 + len(experts)),
        out_specs=(hbm,) * 4 + (vmem,) * 10,
        out_shape=(
            shape(rows, width),
            *(shape(2, *dims) for dims in shapes),
            jax.ShapeDtypeStruct((rows, width), jnp.bfloat16),
            *(shape(share, width),) * 4,
            shape(NEXP, share), shape(NEXP // owners, NEXP), shape(4, share), shape(2, share), shape(2, share),
        ),
        scratch_shapes=[
            pltpu.VMEM((rows, width), jnp.float32), *work,
            pltpu.SemaphoreType.DMA((19,)), pltpu.SemaphoreType.DMA((4,)),
        ],
        compiler_params=params(63),
        cost_estimate=cost(8 * rows * rows * width, 8e6),
    )(resid, small, codes, *outs, table, totals, tokens_grad, *experts)


def attend_back_phase_kernel(
    grads_ref, heads_ref, outs_ref, lse_ref, bias_ref, cos_ref, sin_ref, tokens_ref, table_ref,
    query_ref, key_ref, value_ref, resid_grad_ref, out_part_ref, f_ref, gate_ref, up_ref, down_ref, gate_first,
    tokens_grad_ref, f_got, gate_got, up_got, down_got, *rest, reduce,
):
    chunks, owners, _, rows = grads_ref.shape
    width = tokens_ref.shape[1]
    if reduce:
        total_ref, *rest = rest
    else:
        flat_ref, *rest = rest
    (
        d_got, back_sent, back_got, normed_turned, turned_ref, back_sum, column_ref,
        qt_ref, kt_ref, dt_ref, q_ref, k_ref, v_ref, d_ref, delta_ref, dq_ref, dk_ref, dv_ref, triangle,
        d_send, d_recv, back_send, back_recv, weight_send, weight_recv, f_send, f_recv, local_sem, early_sem, *rest,
    ) = rest
    if reduce:
        (
            half_send, half_recv, chip_send, chip_recv, ring_send, ring_recv, all_send, all_recv,
            gate_work, gate_sums, up_sums, down_work, down_sums, work_sem, *rest,
        ) = rest
        count = len(part_columns(width, chunks)[1])
        own_parts, half_got, chip_got, chip_sum, ring_got, ring_sum, all_got = (
            rest[max(0, n * count - 1) : (n + 1) * count - 1] for n in range(7)
        )
        parts = [out_part_ref, *own_parts]
    copies = gate_ref.shape[0]
    member, xy, core = (lax.axis_index(name) for name in ("expert", "xy", "core"))
    place = xy * 2 + core
    ring, others, planes = ring_partners(owners), copy_partners(copies), plane_partners(owners)
    greet([item[2] for item in planes], [item[2] for item in others])

    d_groups = []
    for j in range(chunks):
        local = pltpu.make_async_copy(grads_ref.at[j, member], d_got.at[j, member], local_sem.at[j])
        local.start()
        group = []
        for step, index, device in ring:
            copy = remote(
                grads_ref.at[j, index], d_got.at[j, member], d_send.at[j, step - 1], d_recv.at[j, step - 1], device
            )
            copy.start()
            group.append(copy)
        d_groups.append((local, group))

    inputs = tokens_ref[...].astype(jnp.float32)
    inverse = lax.rsqrt(jnp.mean(inputs * inputs, -1, keepdims=True) + epsilon)
    normed_turned[...] = (inputs * inverse * table_ref[0:1, :]).T.astype(jnp.bfloat16)
    share = width // owners

    offsets, sizes = part_columns(width, chunks)

    def fill(p, values, begin, size):
        if reduce:
            put_part(parts[p], values, begin)
        else:
            begin = offsets[p] + begin
            flat_ref[:, begin : begin + size] = values

    early = pltpu.make_async_copy(resid_grad_ref, tokens_grad_ref, early_sem.at[0])
    early.start()
    last_part = len(sizes) - 1
    fill(last_part, jnp.zeros((width, 128), jnp.bfloat16), sizes[-1] - 128, 128)

    stages = {}

    def over_cores(p):
        copy = remote(parts[p].at[1 - core], half_got[p], half_send.at[p], half_recv.at[p], {"core": 1 - core})
        copy.start()
        stages[p, 0] = [copy]

    def over_chips(p):
        for copy in stages[p, 0]:
            copy.wait_recv()
        half_got[p][...] = (parts[p][core].astype(jnp.float32) + half_got[p][...].astype(jnp.float32)).astype(
            jnp.bfloat16
        )
        stages[p, 1] = []
        for step in (3, 1, 2):
            index = lax.rem(xy + step, 4)
            copy = remote(
                half_got[p].at[index], chip_got[p].at[xy],
                chip_send.at[p, step - 1], chip_recv.at[p, step - 1], {"xy": index},
            )
            copy.start()
            stages[p, 1].append(copy)
        chip_got[p][xy] = half_got[p][xy]

    def over_owners(p):
        for copy in stages[p, 1]:
            copy.wait_recv()
        chip_sum[p][...] = jnp.sum(chip_got[p][...].astype(jnp.float32), 0).astype(jnp.bfloat16)
        stages[p, 2] = []
        for step, index, device in ring:
            copy = remote(
                chip_sum[p].at[index], ring_got[p].at[member],
                ring_send.at[p, step - 1], ring_recv.at[p, step - 1], device,
            )
            copy.start()
            stages[p, 2].append(copy)
        ring_got[p][member] = chip_sum[p][member]

    def to_copies(p):
        for copy in stages[p, 2]:
            copy.wait_recv()
        ring_sum[p][...] = jnp.sum(ring_got[p][...].astype(jnp.float32), 0).astype(jnp.bfloat16)
        stages[p, 3] = []
        for step, _, device in others:
            copy = remote(
                ring_sum[p], all_got[p].at[xy, core], all_send.at[p, step - 1], all_recv.at[p, step - 1], device
            )
            copy.start()
            stages[p, 3].append(copy)
        all_got[p][xy, core] = ring_sum[p][...]

    def advance(*pairs):
        if reduce:
            for stage, p in pairs:
                (over_cores, over_chips, over_owners, to_copies)[stage](p)

    advance((0, 0))

    background = []

    pieces = ((gate_ref, gate_got), (up_ref, up_got), (down_ref, down_got))

    def send_experts():
        for i, (source, target) in enumerate(pieces):
            local = pltpu.make_async_copy(source.at[place], target.at[place], weight_send.at[i, 0])
            local.start()
            background.append(local.wait)
            for step, index, device in others:
                copy = remote(
                    source.at[2 * device["xy"] + device["core"]], target.at[place],
                    weight_send.at[i, step], weight_recv.at[i, step], device,
                )
                copy.start()
                background.append(copy.wait)

    beside, behind, across = plane_chips(xy)
    landed = {}
    sent = []

    def relay(i, source, landing, device):
        copy = remote(
            source, landing_ref(i, landing), weight_send.at[i, landing], weight_recv.at[i, landing], device
        )
        copy.start()
        landed[i, landing] = copy
        sent.append(copy)

    def landing_ref(i, landing):
        return gate_first.at[landing] if i == 0 and landing < 4 else pieces[i][1].at[landing]

    def arrive(i, *landings):
        for landing in landings:
            if (i, landing) in landed:
                landed[i, landing].wait_recv()

    def first_hop(i):
        for piece, landing, chip in first_hops(beside, behind, across):
            relay(i, pieces[i][0].at[piece], landing, {"xy": chip})

    def second_hop(i):
        source, target = pieces[i]
        work, sums = (gate_work, (gate_sums, up_sums)[i]) if i < 2 else (down_work, down_sums)
        arrive(i, 2, 3)
        items = (source.at[behind * 2], landing_ref(i, 2), source.at[beside * 2 + 1], landing_ref(i, 3))
        loads = [pltpu.make_async_copy(ref, work.at[n], work_sem.at[n]) for n, ref in enumerate(items)]
        for item in loads:
            item.start()
        arrive(i, 0, 1)
        other = {"core": 1 - core}
        relay(i, source.at[xy * 2 + 1 - core], 6, other)
        relay(i, (gate_first if i == 0 else target).at[1 - core], 7, other)
        for item in loads:
            item.wait()
        for n, device in enumerate(({"xy": behind, "core": 0}, {"xy": beside, "core": 1})):
            sums[n] = (work[2 * n].astype(jnp.float32) + work[2 * n + 1].astype(jnp.float32)).astype(jnp.bfloat16)
            copy = remote(
                sums.at[n], target.at[4 + core], weight_send.at[i, 4 + n], weight_recv.at[i, 4 + core], device
            )
            copy.start()
            sent.append(copy)
            landed[i, 4 + n] = remote(
                sums.at[n], target.at[4 + n], weight_send.at[i, 4 + n], weight_recv.at[i, 4 + n], device
            )

    if reduce:
        for i in (1, 2):
            first_hop(i)
    else:
        send_experts()

    def head(j):
        local, group = d_groups[j]
        local.wait()
        for copy in group:
            copy.wait_recv()
        attend_back_head(
            bias_ref, cos_ref, sin_ref, heads_ref.at[j], outs_ref.at[j], lse_ref.at[j : j + 1], d_got.at[j],
            back_sent.at[j], qt_ref, kt_ref, dt_ref, q_ref, k_ref, v_ref, d_ref, delta_ref, dq_ref, dk_ref, dv_ref,
            triangle,
        )

    def send_back(j, cuts):
        local = None
        if cuts[0][1] == 0:
            local = pltpu.make_async_copy(back_sent.at[j, member], back_got.at[j, member], local_sem.at[chunks + j])
            local.start()
        groups = []
        for slot, begin, size in cuts:
            span = pl.ds(begin, size)
            group = []
            for step, index, device in ring:
                copy = remote(
                    back_sent.at[j, index, span], back_got.at[j, member, span],
                    back_send.at[slot, step - 1], back_recv.at[slot, step - 1], device,
                )
                copy.start()
                group.append(copy)
            groups.append(group)
        return local, groups

    span_width = owners * HEAD_DIM

    def weights_of(j, group, types=(0, 1, 2)):
        local, copies_in = group
        if 0 in types:
            local.wait()
        for copy in copies_in[1 if 0 not in types else 0]:
            copy.wait_recv()
        total = None
        for i in types:
            for z in range(owners):
                row = i * span_width + z * HEAD_DIM
                turned_ref[row : row + HEAD_DIM, :] = back_got[j, z, i * HEAD_DIM : (i + 1) * HEAD_DIM]
            weight = (query_ref, key_ref, value_ref)[i]
            term = dot_nn(
                weight[:, j * span_width : (j + 1) * span_width], turned_ref[i * span_width : (i + 1) * span_width, :]
            )
            total = term if total is None else total + term
        first = j == 0 and 0 in types
        back_sum[...] = total if first else back_sum[...] + total
        column = jnp.sum(total * normed_turned[...].astype(jnp.float32), -1, keepdims=True)
        column_ref[...] = column if first else column_ref[...] + column
        begin, size = types[0] * span_width, len(types) * span_width
        part = j + 1 if 0 in types else j + 2
        if part == last_part:
            fill(part, jnp.broadcast_to(column_ref[...], (width, 128)).astype(jnp.bfloat16), span_width, 128)
        fill(part, dot_nt(normed_turned[...], turned_ref[begin : begin + size, :]).astype(jnp.bfloat16), 0, size)

    expert = member * 2 + core

    def send_f(distance):
        if distance == 0:
            local = pltpu.make_async_copy(f_ref.at[expert], f_got.at[expert], f_send.at[0])
            local.start()
            background.append(local.wait)
        for step, index, device in planes[3 * distance : 3 * distance + 3]:
            copy = remote(f_ref.at[index], f_got.at[expert], f_send.at[step], f_recv.at[step], device)
            copy.start()
            background.append(copy.wait)

    def expert_step(step, i):
        if reduce:
            step(i)

    part_k, part_v = chunks, chunks + 1
    both = 2 * HEAD_DIM
    head(0)
    groups = [send_back(0, [(0, 0, 3 * HEAD_DIM)])]
    advance((1, 0))
    head(1)
    advance((2, 0))
    groups.append(send_back(1, [(1, 0, 3 * HEAD_DIM)]))
    expert_step(second_hop, 0)
    expert_step(second_hop, 1)
    head(2)
    groups.append(send_back(2, [(2, 0, both), (3, both, HEAD_DIM)]))
    expert_step(second_hop, 2)
    weights_of(0, groups[0])
    advance((0, 1), (3, 0))
    weights_of(1, groups[1])
    advance((1, 1), (0, 2))
    weights_of(2, groups[2], (0, 1))
    advance((0, part_k), (1, 2), (2, 1))
    weights_of(2, groups[2], (2,))
    advance((0, part_v), (1, part_k), (2, 2))
    send_f(0)
    advance((1, part_v), (2, part_k))
    send_f(1)
    normed = inputs * inverse
    first_grads = back_sum[...].T
    advance((2, part_v))
    send_f(2)
    scaled = first_grads * table_ref[0:1, :]
    early.wait()
    tokens_grad_ref[...] += inverse * (scaled - normed * jnp.mean(scaled * normed, -1, keepdims=True))
    advance((3, 1), (3, 2), (3, part_k), (3, part_v))
    if reduce:
        for p in range(len(sizes)):
            for copy in stages[p, 3]:
                copy.wait_recv()
            for stage in range(4):
                for copy in stages[p, stage]:
                    copy.wait_send()
            _, _, tall, half = all_got[p].shape
            for chip in range(4):
                for side in range(2):
                    begin = offsets[p] + side * half
                    total_ref[chip * tall : (chip + 1) * tall, begin : begin + half] = all_got[p][chip, side]
        for i in range(3):
            arrive(i, 4, 5, 6, 7)
        for copy in sent:
            copy.wait_send()
    for local, group in d_groups:
        for copy in group:
            copy.wait_send()
    for local, items in groups:
        for group in items:
            for copy in group:
                copy.wait_send()
    for wait in background:
        wait()


def part_columns(width, chunks):
    sizes = [width + 256] + [width] * (chunks - 1) + [width // 3 * 2, width // 3 + 256]
    return [sum(sizes[:p]) for p in range(len(sizes))], sizes


def attend_back_phase(
    grads, heads, outs, lse, bias, cosine, sine, tokens, table, weights, resid_grads, out_part, f, pieces, gate_first, copies
):
    chunks, owners, _, rows = grads.shape
    width = tokens.shape[1]
    length = owners * rows
    head = (chunks, owners, 3 * HEAD_DIM, rows)
    sizes = part_columns(width, chunks)[1]
    columns, total = sum(sizes), len(sizes)
    share = width // owners
    reduce = relayed(copies)
    vmem, hbm = pl.BlockSpec(memory_space=pltpu.VMEM), pl.BlockSpec(memory_space=pl.ANY)
    gate_shape, down_shape = pieces[0].shape[1:], pieces[2].shape[1:]
    turned = pltpu.VMEM((HEAD_DIM, length), jnp.bfloat16)
    plain = pltpu.VMEM((length, HEAD_DIM), jnp.bfloat16)
    wide = pltpu.VMEM((length, HEAD_DIM), jnp.float32)
    sems = lambda *shape: pltpu.SemaphoreType.DMA(shape)
    scratch = [
        pltpu.VMEM(grads.shape, jnp.bfloat16),
        pltpu.VMEM(head, jnp.bfloat16),
        pltpu.VMEM(head, jnp.bfloat16),
        pltpu.VMEM((width, rows), jnp.bfloat16),
        pltpu.VMEM((3 * owners * HEAD_DIM, rows), jnp.bfloat16),
        pltpu.VMEM((width, rows), jnp.float32),
        pltpu.VMEM((width, 1), jnp.float32),
        turned, turned, turned, plain, plain, plain, plain,
        pltpu.VMEM((1, length), jnp.float32),
        pltpu.VMEM((HEAD_DIM, length), jnp.float32),
        wide, wide,
        pltpu.VMEM((TILE, TILE), jnp.float32),
        *(sems(chunks, owners - 1),) * 2,
        *(sems(chunks + 1, owners - 1),) * 2,
        sems(3, copies), sems(3, copies), sems(2 * owners), sems(2 * owners), sems(2 * chunks), sems(2),
    ]
    if reduce:
        low = lambda *shape: pltpu.VMEM(shape, jnp.bfloat16)
        scratch += [
            sems(total), sems(total), sems(total, 3), sems(total, 3),
            sems(total, owners - 1), sems(total, owners - 1), sems(total, copies - 1), sems(total, copies - 1),
            low(4, *gate_shape), low(2, *gate_shape), low(2, *gate_shape), low(4, *down_shape), low(2, *down_shape),
            sems(4),
        ]
        tall, halves = share // 4, [size // 2 for size in sizes]
        for shape in (
            (2, 4, owners, tall), (4, owners, tall), (4, owners, tall), (owners, tall), (owners, tall), (tall,), (4, 2, tall)
        ):
            scratch += [low(*shape, half) for half in (halves[1:] if len(shape) == 4 and shape[0] == 2 else halves)]
        last_specs, last_shapes = (vmem,), (jax.ShapeDtypeStruct((share, columns), jnp.bfloat16),)
    else:
        last_specs, last_shapes = (vmem,), (jax.ShapeDtypeStruct((width, columns), jnp.bfloat16),)
    tokens_grad, f_got, *gots, totals = pl.pallas_call(
        functools.partial(attend_back_phase_kernel, reduce=reduce),
        in_specs=[vmem] * 12 + [hbm, vmem] + [hbm] * 5,
        out_specs=(vmem, hbm, hbm, hbm, hbm, *last_specs),
        out_shape=(
            jax.ShapeDtypeStruct((rows, width), jnp.float32),
            jax.ShapeDtypeStruct(f.shape, f.dtype),
            *(jax.ShapeDtypeStruct(piece.shape, piece.dtype) for piece in pieces),
            *last_shapes,
        ),
        scratch_shapes=scratch,
        compiler_params=pltpu.CompilerParams(vmem_limit_bytes=63 * MIB, collective_id=3, has_side_effects=True),
        cost_estimate=cost(2e10, 5e7),
    )(grads, heads, outs, lse, bias, cosine, sine, tokens, table, *weights, resid_grads, out_part, f, *pieces, gate_first)
    if not reduce:
        out_part = out_part.transpose(2, 1, 3, 0, 4).reshape(width, sizes[0])
        totals = jnp.concatenate([out_part, totals[:, sizes[0] :]], 1)
        totals = lax.psum_scatter(totals, "expert", scatter_dimension=0, tiled=True)
        totals = lax.psum(totals, ("xy", "core"))
        gots = [jnp.sum(got.reshape(copies // 2, 2, *got.shape[1:]).astype(jnp.float32), 0) for got in gots]
    return (tokens_grad, f_got, totals, gots)


def per_device(
    tokens, prior_logits, routes, parents, cotangent, query_weight, key_weight, value_weight, out_weight,
    attention_gain, expert_gain, router_weight, prior_weight, constant_weight, constant_vector,
    gate_weight, up_weight, down_weight,
):
    owners = lax.axis_size("expert")
    member = lax.axis_index("expert")
    tokens, prior, routes, grad = tokens[0], prior_logits[0].T, routes[0].T, cotangent[0]
    rows, width = tokens.shape
    copies = lax.axis_size("xy") * lax.axis_size("core")
    chunks = width // HEAD_DIM // owners
    zeros = jnp.zeros((4, width), jnp.float32)
    table = jnp.concatenate([attention_gain[None], expert_gain[None], constant_vector, zeros], 0)
    qkv_weights = (query_weight, key_weight, value_weight)
    attended, logs, bias, cosine, sine, codes, codes_row, heads, outs, gate, up, down = attend_phase(
        tokens, table, qkv_weights, parents, routes, (gate_weight, up_weight, down_weight), copies
    )
    attended = attended.reshape(width, rows)
    gate, up, down = (full.reshape(-1, full.shape[-1]) for full in (gate, up, down))
    resid, small, *x_out, mixer = middle(
        tokens, attended, out_weight, table, router_weight.T, constant_weight.T, prior, prior_weight, codes, codes_row
    )
    backs, dots, fa, fb, *grads = expert_phase(x_out, small, grad, codes_row, gate, up, down)
    pieces = [item.reshape(copies, -1, item.shape[-1]) for item in grads]
    dots = dots[:, :, 0, : rows // NFFN].reshape(1, 2 * rows)
    resid_grads, grads_out, out_part, prior_grad, fa, gate_first = turn(
        resid, small, grad, prior, codes, backs.reshape(2 * rows, width), dots, table, mixer, prior_weight,
        out_weight, attended, fa, pieces[0],
    )
    tokens_grad, fb, totals, gots = attend_back_phase(
        grads_out.reshape(chunks, owners, HEAD_DIM, rows), heads, outs, logs, bias, cosine, sine, tokens,
        table, qkv_weights, resid_grads, out_part, fb, pieces, gate_first, copies,
    )
    fs = [f.reshape(rows, width) for f in (fa, fb)]
    reduce = relayed(copies)
    experts = gots
    if reduce:
        experts = [item for i in range(3) for item in (pieces[i], gate_first if i == 0 else gots[i], gots[i])]
    (
        tokens_grad, gate_part, up_part, down_part, result, *qkv_out_grads, router_grad, prior_weight_grad,
        constant_weight_grad, vector_grad, gain_grads,
    ) = finish(resid, small, codes, fs, table, totals, tokens_grad, experts, reduce)
    return (
        result[None],
        tokens_grad[None],
        prior_grad.T[None],
        *qkv_out_grads,
        gain_grads[0],
        gain_grads[1],
        router_grad.T,
        prior_weight_grad,
        constant_weight_grad.T,
        vector_grad,
        gate_part,
        up_part,
        down_part,
    )


def solution(mesh):
    owners, copies = mesh.shape["expert"], mesh.shape["dp"]
    cores = 2
    mesh = Mesh(mesh.devices.reshape(owners, copies // cores, cores), ("expert", "xy", "core"))
    dp = ("xy", "core")
    rows = P(dp, "expert", None)
    shard = P("expert", dp, None)
    in_specs = (rows, rows, rows, P(dp, None), rows) + (P(),) * 10 + (shard,) * 3
    out_specs = (
        (rows,) * 3
        + (P("expert", None),) * 4
        + (P("expert"),) * 2
        + (P("expert", None),) * 3
        + (P(None, "expert"),)
        + (shard,) * 3
    )
    return jax.shard_map(per_device, mesh=mesh, in_specs=in_specs, out_specs=out_specs, check_vma=False)
```

```python
import functools

import jax
import jax.numpy as jnp
from jax import lax
from jax.experimental import pallas as pl
from jax.experimental.pallas import tpu as pltpu
from jax.sharding import Mesh
from jax.sharding import PartitionSpec as P

NFFN = 8
NEXP = 12
SEG = 128
HEAD_DIM = 64
TRUNK = 1024
TILE = 2 * SEG
LOG2E = 1.4426950408889634
masked_score = -1e30
MIB = 2**20
epsilon = 1e-06
precise = lax.Precision.HIGHEST


def dot_nt(left, right):
    return lax.dot_general(left, right, (((1,), (1,)), ((), ())), preferred_element_type=jnp.float32)


def dot_nn(left, right):
    return jnp.dot(left, right, preferred_element_type=jnp.float32)


def tile_parts(tile, start):
    trunk_tiles = TRUNK // TILE
    if tile is not None and tile < trunk_tiles:
        return [(k * TILE, False, k == tile) for k in range(tile + 1)]
    parts = [(k * TILE, False, False) for k in range(trunk_tiles)]
    branch_tiles = 2
    if tile is None:
        parts += [(TRUNK + k * TILE, True, False) for k in range(branch_tiles)]
    else:
        parts += [(TRUNK + k * TILE, True, False) for k in range(tile - trunk_tiles)]
    parts += [(start, True, True)]
    return parts


def causal_bias():
    key_ids = lax.broadcasted_iota(jnp.int32, (TILE, TILE), 0)
    query_ids = lax.broadcasted_iota(jnp.int32, (TILE, TILE), 1)
    return jnp.where(key_ids <= query_ids, 0.0, masked_score).astype(jnp.float32)


def part_scores(scores, part, columns, bias_ref, triangle):
    first, by_lineage, causal = part
    if by_lineage:
        segment = 1 + (first - TRUNK) // SEG
        rows = [bias_ref[pl.ds(segment + i, 1), columns] for i in range(TILE // SEG)]
        scores = jnp.concatenate(
            [scores[i * SEG : (i + 1) * SEG] + rows[i] for i in range(TILE // SEG)], 0
        )
    if causal:
        scores = scores + triangle[...]
    return scores


def for_tiles(length, body):
    trunk_tiles = TRUNK // TILE
    for tile in range(trunk_tiles + 2):
        body(tile, tile * TILE)
    first_leaf = trunk_tiles + 2

    @pl.loop(first_leaf, length // TILE)
    def _(tile):
        body(None, pl.multiple_of(tile * TILE, TILE))


def attend_head(bias_ref, qkv_ref, out_ref, lse_ref, q_ref, k_ref, v_ref, o_ref, s_ref, triangle):
    sources, _, rows = qkv_ref.shape
    length = sources * rows
    factor = HEAD_DIM ** (-0.5) * LOG2E
    triangle[...] = causal_bias()
    extra = lax.broadcasted_iota(jnp.int32, (16, length), 0)
    v_ref[HEAD_DIM:, :] = jnp.where(extra == 0, 1.0, 0.0).astype(jnp.bfloat16)
    for z in range(sources):
        span = pl.ds(z * rows, rows)
        q_ref[:, span] = qkv_ref[z, :HEAD_DIM]
        k_ref[span, :] = qkv_ref[z, HEAD_DIM : 2 * HEAD_DIM].astype(jnp.float32).T.astype(jnp.bfloat16)
        v_ref[:HEAD_DIM, span] = qkv_ref[z, 2 * HEAD_DIM :]

    def body(tile, start):
        columns = pl.ds(start, TILE)
        parts = tile_parts(tile, start)
        query = q_ref[:, columns]
        peak = None
        for i, part in enumerate(parts):
            scores = dot_nn(k_ref[pl.ds(part[0], TILE), :], query)
            scores = part_scores(scores, part, columns, bias_ref, triangle)
            s_ref[i * TILE : (i + 1) * TILE, :] = scores
            top = jnp.max(scores, 0, keepdims=True)
            peak = top if peak is None else jnp.maximum(peak, top)
        shift = peak * factor
        total = None
        for i, part in enumerate(parts):
            weights = jnp.exp2(s_ref[i * TILE : (i + 1) * TILE, :] * factor - shift)
            term = dot_nn(v_ref[:, pl.ds(part[0], TILE)], weights.astype(jnp.bfloat16))
            total = term if total is None else total + term
        norm = total[HEAD_DIM : HEAD_DIM + 1]
        o_ref[:, columns] = (total[:HEAD_DIM] / norm).astype(jnp.bfloat16)
        lse_ref[:, columns] = shift + jnp.log2(norm)

    for_tiles(length, body)
    for z in range(sources):
        out_ref[z] = o_ref[:, pl.ds(z * rows, rows)]


def attend_back_head(
    bias_ref, cos_ref, sin_ref, qkv_ref, out_ref, lse_ref, grad_ref, back_ref,
    qt_ref, kt_ref, dt_ref, q_ref, k_ref, v_ref, d_ref, delta_ref, dq_ref, dk_ref, dv_ref, triangle,
):
    sources, _, rows = qkv_ref.shape
    length = sources * rows
    scaling = HEAD_DIM ** (-0.5)
    factor = scaling * LOG2E
    triangle[...] = causal_bias()

    def turned(values):
        return values.astype(jnp.float32).T.astype(jnp.bfloat16)

    for z in range(sources):
        span = pl.ds(z * rows, rows)
        query, key, value = (qkv_ref[z, i * HEAD_DIM : (i + 1) * HEAD_DIM] for i in range(3))
        grad = grad_ref[z]
        qt_ref[:, span] = query
        kt_ref[:, span] = key
        dt_ref[:, span] = grad
        q_ref[span, :] = turned(query)
        k_ref[span, :] = turned(key)
        v_ref[span, :] = turned(value)
        d_ref[span, :] = turned(grad)
        delta_ref[:, span] = jnp.sum(
            grad.astype(jnp.float32) * out_ref[z].astype(jnp.float32), 0, keepdims=True
        )
    dk_ref[...] = jnp.zeros_like(dk_ref)
    dv_ref[...] = jnp.zeros_like(dv_ref)

    def body(tile, start):
        columns = pl.ds(start, TILE)
        query_t, grad_t = qt_ref[:, columns], dt_ref[:, columns]
        query, grad = q_ref[columns, :], d_ref[columns, :]
        lse, delta = lse_ref[:, columns], delta_ref[:, columns]
        total = None
        for part in tile_parts(tile, start):
            span = pl.ds(part[0], TILE)
            scores = dot_nn(k_ref[span, :], query_t) * factor - lse
            scores = part_scores(scores, part, columns, bias_ref, triangle)
            weights = jnp.exp2(scores)
            weight_grads = dot_nn(v_ref[span, :], grad_t)
            score_grads = (weights * (weight_grads - delta)).astype(jnp.bfloat16)
            dv_ref[span, :] += dot_nn(weights.astype(jnp.bfloat16), grad)
            dk_ref[span, :] += dot_nn(score_grads, query)
            term = dot_nn(kt_ref[:, span], score_grads)
            total = term if total is None else total + term
        dq_ref[:, columns] = total

    for_tiles(length, body)
    half = HEAD_DIM // 2
    for z in range(sources):
        span = pl.ds(z * rows, rows)
        cosine, sine = cos_ref[:, span], sin_ref[:, span]
        for i, values in enumerate((dq_ref[:, span], dk_ref[span, :].T)):
            values = values * scaling
            first, second = values[:half], values[half:]
            back_ref[z, i * HEAD_DIM : (i + 1) * HEAD_DIM] = jnp.concatenate(
                [first * cosine + second * sine, second * cosine - first * sine], 0
            ).astype(jnp.bfloat16)
        back_ref[z, 2 * HEAD_DIM :] = dv_ref[span, :].T.astype(jnp.bfloat16)


def params(limit):
    return pltpu.CompilerParams(vmem_limit_bytes=limit * MIB)


def cost(flops, moved):
    return pl.CostEstimate(flops=int(flops), bytes_accessed=int(moved), transcendentals=0)


def greet(ring, copies):
    barrier = pltpu.get_barrier_semaphore()
    for target in ring + copies:
        pl.semaphore_signal(barrier, inc=1, device_id=target, device_id_type=pl.DeviceIdType.MESH)
    pl.semaphore_wait(barrier, len(ring) + len(copies))


def ring_partners(owners):
    member = lax.axis_index("expert")
    result = []
    for step in sorted(range(1, owners), key=lambda k: -min(k, owners - k)):
        index = lax.rem(member + step, owners)
        result.append((step, index, {"expert": index}))
    return result


def copy_partners(total):
    place = lax.axis_index("xy") * 2 + lax.axis_index("core")
    result = []
    for step in sorted(range(1, total), key=lambda k: -(k % 8 in (6, 2, 4))):
        index = lax.rem(place + step, total)
        result.append((step, lax.rem(index, 2), {"xy": index // 2, "core": lax.rem(index, 2)}))
    return result


def plane_chips(xy):
    return xy + 1 - 2 * lax.rem(xy, 2), lax.rem(xy + 2, 4), 3 - xy


def first_hops(beside, behind, across):
    return (
        (across * 2, 2, beside), (across * 2 + 1, 3, behind), (beside * 2, 0, beside), (behind * 2 + 1, 1, behind),
    )


def relayed(copies):
    return copies == 8


def remote(source, target, send, receive, device):
    return pltpu.make_async_remote_copy(
        src_ref=source, dst_ref=target, send_sem=send, recv_sem=receive,
        device_id=device, device_id_type=pl.DeviceIdType.MESH,
    )


def reach_of(parents):
    shape = (128, 128)
    one, two = lax.broadcasted_iota(jnp.int32, shape, 0), lax.broadcasted_iota(jnp.int32, shape, 1)
    count = parents.shape[1]
    none = lambda size: jnp.full((1, size), -1, jnp.int32)
    parent_row = jnp.concatenate([none(1), parents, none(127 - count)], 1)
    reach = jnp.where((one == two) | (one == parent_row), 1.0, 0.0).astype(jnp.bfloat16)
    for _ in range(3):
        reach = jnp.minimum(dot_nn(reach, reach), 1.0).astype(jnp.bfloat16)
    return reach


def place_tables(reach, first, size):
    ids = lax.broadcasted_iota(jnp.int32, (1, size), 1) + first
    later = ids - TRUNK
    segment = jnp.where(later < 0, 0, 1 + lax.shift_right_arithmetic(later, 7))
    inside = jnp.where(later < 0, later, (later & (SEG - 1)) - SEG)
    own = jnp.where(segment == lax.broadcasted_iota(jnp.int32, (128, size), 0), 1.0, 0.0).astype(jnp.bfloat16)
    seen = dot_nn(reach[:16], own)
    index = lax.broadcasted_iota(jnp.int32, (16, 1), 0)
    lengths = jnp.where(index == 0, float(TRUNK), float(SEG))
    places = jnp.sum(seen * lengths, 0, keepdims=True) + inside.astype(jnp.float32)
    turn = lax.broadcasted_iota(jnp.int32, (HEAD_DIM // 2, 1), 0).astype(jnp.float32)
    angles = jnp.exp(turn * (-2.0 / HEAD_DIM * 9.210340371976184)) * places
    return seen, jnp.cos(angles), jnp.sin(angles)


def slot_codes(routes_ref, codes_ref, codes_row_ref):
    rows = routes_ref.shape[1]
    half_slots = rows // NFFN
    turned = jnp.concatenate([routes_ref[...].astype(jnp.float32), jnp.zeros((126, rows), jnp.float32)], 0).T
    routes = turned.astype(jnp.int32)
    lanes = lax.broadcasted_iota(jnp.int32, (rows, 128), 1)
    matches = [
        jnp.where((lanes == routes[:, c : c + 1]) & (lanes < NFFN), 1.0, 0.0).astype(jnp.float32) for c in range(2)
    ]
    square = (rows, rows)
    earlier = lax.broadcasted_iota(jnp.int32, square, 0) > lax.broadcasted_iota(jnp.int32, square, 1)
    before = dot_nn(
        jnp.where(earlier, 1.0, 0.0).astype(jnp.bfloat16), (matches[0] + matches[1]).astype(jnp.bfloat16)
    )
    codes = jnp.zeros((rows, 128), jnp.float32)
    for c in range(2):
        rank = jnp.sum(matches[c] * before, -1, keepdims=True)
        route = routes[:, c : c + 1].astype(jnp.float32)
        late = jnp.where(rank >= half_slots, float((NFFN - 1) * half_slots), 0.0)
        code = jnp.where(route < NFFN, route * half_slots + rank + late, float(4 * rows))
        codes = jnp.where(lanes == c, code, jnp.where(lanes == 2 + c, route, codes))
    codes_ref[...] = codes.astype(jnp.int32)
    codes_row_ref[...] = codes.T[:8].astype(jnp.int32)


def attend_phase_kernel(
    tokens_ref, table_ref, query_ref, key_ref, value_ref, parents_ref, routes_ref, gate_ref, up_ref, down_ref,
    attended_ref, lse_ref, bias_ref, cos_ref, sin_ref, codes_ref, codes_row_ref, heads_ref, outs_ref,
    gate_full, up_full, down_full,
    normed_ref, qkv_sent, qkv_got, out_sent, out_got, q_ref, k_ref, v_ref, o_ref, s_ref, triangle,
    qkv_send, qkv_recv, out_send, out_recv, weight_send, weight_recv, local_sem,
):
    chunks, owners, _, rows = qkv_sent.shape
    member = lax.axis_index("expert")
    copies = gate_full.shape[0]
    ring, others = ring_partners(owners), copy_partners(copies)
    greet([item[2] for item in ring], [item[2] for item in others])
    weights = ((gate_ref, gate_full), (up_ref, up_full), (down_ref, down_full))
    place = lax.axis_index("xy") * 2 + lax.axis_index("core")
    core = lax.axis_index("core")
    started = []

    relays = relayed(copies)
    xy = lax.axis_index("xy")
    beside, behind, across = plane_chips(xy)
    arrivals = {}

    def send_weight(i):
        shard, full = weights[i]
        local = pltpu.make_async_copy(shard.at[core], full.at[place], weight_send.at[i, 0])
        local.start()
        started.append(local.wait)
        if relays:
            targets = [(2, beside, 0), (4, behind, 0), (2, beside, 1), (4, behind, 1)]
            targets = [(1, 1 - core, {"core": 1 - core})] + [
                (base + core, other, {"xy": chip, "core": other}) for base, chip, other in targets
            ]
            for n, (slot, other, device) in enumerate(targets):
                copy = remote(
                    shard.at[other], full.at[place], weight_send.at[i, 1 + n], weight_recv.at[i, slot], device
                )
                copy.start()
                started.append(copy.wait_send)
            for slot in range(1, 8):
                arrivals[i, slot] = remote(
                    shard.at[core], full.at[place], weight_send.at[i, 0], weight_recv.at[i, slot], {"core": 1 - core}
                )
        else:
            for step, other_core, device in others:
                copy = remote(
                    shard.at[other_core], full.at[place], weight_send.at[i, step], weight_recv.at[i, step], device
                )
                copy.start()
                started.append(copy.wait)

    def relay_weight(i):
        full = weights[i][1]
        for slot, piece, chip, landing in ((4, behind * 2, beside, 6), (3, beside * 2 + 1, behind, 7)):
            arrivals.pop((i, slot)).wait_recv()
            copy = remote(
                full.at[piece], full.at[piece], weight_send.at[i, landing], weight_recv.at[i, landing], {"xy": chip}
            )
            copy.start()
            started.append(copy.wait_send)

    for i in range(3):
        send_weight(i)

    inputs = tokens_ref[...].astype(jnp.float32)
    inverse = lax.rsqrt(jnp.mean(inputs * inputs, -1, keepdims=True) + epsilon)
    normed_ref[...] = (inputs * inverse * table_ref[0:1, :]).astype(jnp.bfloat16)
    half = HEAD_DIM // 2
    span_width = owners * HEAD_DIM
    qkv_copies = []
    for j in range(chunks):
        group = []
        for i in (2, 0, 1):
            weight = (query_ref, key_ref, value_ref)[i]
            if j == 0 and i == 0:
                reach = reach_of(parents_ref[...])
                _, cosine, sine = place_tables(reach, member * rows, rows)
            turned = dot_nn(normed_ref[...], weight[:, j * span_width : (j + 1) * span_width]).T
            base = i * HEAD_DIM
            for z in range(owners):
                first = turned[z * HEAD_DIM : z * HEAD_DIM + half]
                second = turned[z * HEAD_DIM + half : (z + 1) * HEAD_DIM]
                if i < 2:
                    first, second = first * cosine - second * sine, second * cosine + first * sine
                qkv_sent[j, z, base : base + half] = first.astype(jnp.bfloat16)
                qkv_sent[j, z, base + half : base + HEAD_DIM] = second.astype(jnp.bfloat16)
            if (j, i) == (0, 2):
                slot, span = chunks, pl.ds(base, HEAD_DIM)
            elif i == 1:
                slot, span = j, pl.ds(0, (3 if j else 2) * HEAD_DIM)
            else:
                continue
            for step, index, device in ring:
                copy = remote(
                    qkv_sent.at[j, index, span], qkv_got.at[j, member, span],
                    qkv_send.at[slot, step - 1], qkv_recv.at[slot, step - 1], device,
                )
                copy.start()
                group.append(copy)
        local = pltpu.make_async_copy(qkv_sent.at[j, member], qkv_got.at[j, member], local_sem.at[j])
        local.start()
        qkv_copies.append((local, group))
    seen, whole_cosine, whole_sine = place_tables(reach, 0, owners * rows)
    bias_ref[...] = jnp.where(seen > 0.5, 0.0, masked_score)
    cos_ref[...] = whole_cosine
    sin_ref[...] = whole_sine
    slot_codes(routes_ref, codes_ref, codes_row_ref)

    out_copies = []
    kept = []
    for j in range(chunks):
        local, group = qkv_copies[j]
        local.wait()
        for copy in group:
            copy.wait_recv()
        keep = pltpu.make_async_copy(qkv_got.at[j], heads_ref.at[j], local_sem.at[chunks + j])
        keep.start()
        kept.append(keep)
        attend_head(
            bias_ref, qkv_got.at[j], out_sent.at[j], lse_ref.at[j : j + 1], q_ref, k_ref, v_ref, o_ref, s_ref, triangle
        )
        local = pltpu.make_async_copy(out_sent.at[j, member], out_got.at[j, member], local_sem.at[2 * chunks + j])
        local.start()
        keep = pltpu.make_async_copy(out_sent.at[j], outs_ref.at[j], local_sem.at[3 * chunks + j])
        keep.start()
        kept += [local, keep]
        for step, index, device in ring:
            copy = remote(
                out_sent.at[j, index], out_got.at[j, member],
                out_send.at[j, step - 1], out_recv.at[j, step - 1], device,
            )
            copy.start()
            out_copies.append(copy)
        if relays and j == 1:
            for i in range(3):
                relay_weight(i)
    for copy in out_copies:
        copy.wait_recv()
    for copy in kept:
        copy.wait()
    attended_ref[...] = out_got[...]
    for local, group in qkv_copies:
        for copy in group:
            copy.wait_send()
    for copy in out_copies:
        copy.wait_send()
    for copy in arrivals.values():
        copy.wait_recv()
    for wait in started:
        wait()


def attend_phase(tokens, table, weights, parents, routes, shards, copies):
    rows, width = tokens.shape
    owners = lax.axis_size("expert")
    length = rows * owners
    chunks = width // HEAD_DIM // owners
    head = (chunks, owners, 3 * HEAD_DIM, rows)
    out = (chunks, owners, HEAD_DIM, rows)
    vmem, hbm = pl.BlockSpec(memory_space=pltpu.VMEM), pl.BlockSpec(memory_space=pl.ANY)
    fulls = [jax.ShapeDtypeStruct((copies, *shard.shape[1:]), shard.dtype) for shard in shards]
    part_total = TRUNK // TILE + 3
    sems = lambda *shape: pltpu.SemaphoreType.DMA(shape)
    return pl.pallas_call(
        attend_phase_kernel,
        in_specs=[vmem] * 7 + [hbm] * 3,
        out_specs=(vmem,) * 7 + (hbm,) * 5,
        out_shape=(
            jax.ShapeDtypeStruct(out, jnp.bfloat16),
            jax.ShapeDtypeStruct((8, length), jnp.float32),
            jax.ShapeDtypeStruct((16, length), jnp.float32),
            *(jax.ShapeDtypeStruct((HEAD_DIM // 2, length), jnp.float32),) * 2,
            jax.ShapeDtypeStruct((rows, 128), jnp.int32),
            jax.ShapeDtypeStruct((8, rows), jnp.int32),
            jax.ShapeDtypeStruct(head, jnp.bfloat16),
            jax.ShapeDtypeStruct(out, jnp.bfloat16),
            *fulls,
        ),
        scratch_shapes=[
            pltpu.VMEM((rows, width), jnp.bfloat16),
            pltpu.VMEM(head, jnp.bfloat16),
            pltpu.VMEM(head, jnp.bfloat16),
            pltpu.VMEM(out, jnp.bfloat16),
            pltpu.VMEM(out, jnp.bfloat16),
            pltpu.VMEM((HEAD_DIM, length), jnp.bfloat16),
            pltpu.VMEM((length, HEAD_DIM), jnp.bfloat16),
            pltpu.VMEM((HEAD_DIM + 16, length), jnp.bfloat16),
            pltpu.VMEM((HEAD_DIM, length), jnp.bfloat16),
            pltpu.VMEM((part_total * TILE, TILE), jnp.float32),
            pltpu.VMEM((TILE, TILE), jnp.float32),
            sems(chunks + 1, owners - 1), sems(chunks + 1, owners - 1), sems(chunks, owners - 1), sems(chunks, owners - 1),
            sems(3, copies), sems(3, copies), sems(4 * chunks),
        ],
        compiler_params=pltpu.CompilerParams(vmem_limit_bytes=63 * MIB, collective_id=1, has_side_effects=True),
        cost_estimate=cost(1e10, 5e7),
    )(tokens, table, *weights, parents, routes, *shards)


def lane_pick(values, lanes, index):
    return jnp.sum(jnp.where(lanes == index, values, 0.0), -1, keepdims=True)


def middle_kernel(
    tokens_ref, attended_ref, out_weight_ref, table_ref, router_ref, constant_ref, prior_ref, prior_weight_ref,
    codes_ref, codes_row_ref, resid_ref, small_ref, first_ref, second_ref, mixer_ref, hidden_ref,
):
    rows, width = tokens_ref.shape
    mixer = [ref[...].astype(jnp.float32) for ref in (router_ref, constant_ref)]
    mixer_ref[...] = jnp.concatenate([*mixer, jnp.zeros((128 - NEXP - 4, width), jnp.float32)], 0).astype(jnp.bfloat16)
    missing = jnp.zeros((16 - NEXP, SEG), jnp.float32)

    @pl.loop(0, rows // SEG)
    def _(step):
        span = pl.ds(pl.multiple_of(step * SEG, SEG), SEG)
        attended = attended_ref[:, span].astype(jnp.float32).T.astype(jnp.bfloat16)
        resid = tokens_ref[span, :].astype(jnp.float32) + dot_nn(attended, out_weight_ref[...])
        inverse = lax.rsqrt(jnp.mean(resid * resid, -1, keepdims=True) + epsilon)
        hidden = (resid * inverse * table_ref[1:2, :]).astype(jnp.bfloat16)
        resid_ref[span, :] = resid
        hidden_ref[span, :] = hidden
        logits = dot_nt(hidden, mixer_ref[...])
        prior = jnp.concatenate([prior_ref[:, span], missing], 0).T[:, :NEXP]
        carried = jnp.dot(prior, prior_weight_ref[...], precision=precise, preferred_element_type=jnp.float32)
        logits = logits + jnp.concatenate([carried, jnp.zeros((SEG, 128 - NEXP), jnp.float32)], 1)
        lanes = lax.broadcasted_iota(jnp.int32, logits.shape, 1)
        routes = codes_ref[span, 2:4]
        columns = []
        pairs = [[lane_pick(logits, lanes, routes[:, c : c + 1]) for c in range(2)]]
        pairs += [[logits[:, NEXP + 2 * m + c : NEXP + 2 * m + c + 1] for c in range(2)] for m in range(2)]
        for one, two in pairs:
            peak = jnp.maximum(one, two)
            one, two = jnp.exp(one - peak), jnp.exp(two - peak)
            columns += [one / (one + two), two / (one + two)]
        columns.append(inverse)
        small = jnp.zeros_like(logits)
        for i, column in enumerate(columns):
            small = jnp.where(lanes == i, column, small)
        small_ref[span, :] = small

    slots = first_ref.shape[0]
    for half, ref in enumerate((first_ref, second_ref)):
        index = lax.broadcasted_iota(jnp.int32, (slots, rows), 0) + half * slots
        chosen = (codes_row_ref[0:1, :] == index) | (codes_row_ref[1:2, :] == index)
        ref[...] = dot_nn(chosen.astype(jnp.bfloat16), hidden_ref[...]).astype(jnp.bfloat16)


def middle(tokens, attended, out_weight, table, router, constant, prior, prior_weight, codes, codes_row):
    rows, width = tokens.shape
    slots = rows
    return pl.pallas_call(
        middle_kernel,
        out_shape=(
            jax.ShapeDtypeStruct((rows, width), jnp.float32),
            jax.ShapeDtypeStruct((rows, 128), jnp.float32),
            jax.ShapeDtypeStruct((slots, width), jnp.bfloat16),
            jax.ShapeDtypeStruct((slots, width), jnp.bfloat16),
            jax.ShapeDtypeStruct((128, width), jnp.bfloat16),
        ),
        scratch_shapes=[pltpu.VMEM((rows, width), jnp.bfloat16)],
        compiler_params=params(63),
        cost_estimate=cost(4 * rows * width * width + 4 * rows * rows * width, 1e7),
    )(tokens, attended, out_weight, table, router, constant, prior, prior_weight, codes, codes_row)


def plane_partners(owners):
    total = 2 * owners
    place = lax.axis_index("expert") * 2 + lax.axis_index("core")
    result = []
    for step in sorted(range(1, total), key=lambda k: -min(k, total - k)):
        index = lax.rem(place + step, total)
        result.append((step, index, {"expert": index // 2, "core": lax.rem(index, 2)}))
    return result


def expert_phase_kernel(
    xa_ref, xb_ref, small_ref, grad_ref, codes_ref, gate_hbm, up_hbm, down_hbm,
    back_out, dots_out, fa_out, fb_out, gate_grad, up_grad, down_grad,
    gate_ref, up_ref, down_ref, scaled_ref, d_sent, x_got, d_got, back_sent, back_got, dots_sent, dots_got,
    f_sum, back_sum, hid_ref, one_ref, two_ref, x_turned, d_turned, stage, stage_down,
    x_send, x_recv, d_send, d_recv, back_send, back_recv, dots_send, dots_recv, local_sem, stage_sem,
):
    experts, slots, width = x_got.shape[1:]
    rows = experts * slots
    units = gate_ref.shape[1]
    owners = experts // 2
    place = lax.axis_index("expert") * 2 + lax.axis_index("core")
    partners = plane_partners(owners)
    greet([item[2] for item in partners], [])
    loads = [
        pltpu.make_async_copy(source, target, local_sem.at[i])
        for i, (source, target) in enumerate(((gate_hbm, gate_ref), (up_hbm, up_ref), (down_hbm, down_ref)))
    ]
    for load in loads:
        load.start()

    def send(source, target, sends, receives, half, locals_at):
        copies = []
        local = pltpu.make_async_copy(source(place), target.at[half, place], local_sem.at[locals_at + half])
        local.start()
        for step, index, device in partners:
            copy = remote(source(index), target.at[half, place], sends.at[half, step], receives.at[half, step], device)
            copy.start()
            copies.append(copy)
        return local, copies

    def arrive(group):
        group[0].wait()
        for copy in group[1]:
            copy.wait_recv()

    x_refs = (xa_ref, xb_ref)
    x_groups = [send(lambda e, ref=ref: ref.at[e], x_got, x_send, x_recv, h, 3) for h, ref in enumerate(x_refs)]
    for c in range(2):
        scaled_ref[c * rows : (c + 1) * rows, :] = (
            small_ref[:, c : c + 1] * grad_ref[...].astype(jnp.float32)
        ).astype(jnp.bfloat16)
    d_groups = []
    for half in range(2):
        index = lax.broadcasted_iota(jnp.int32, (rows, rows), 0) + half * rows
        chosen = jnp.concatenate([(codes_ref[c : c + 1, :] == index).astype(jnp.bfloat16) for c in range(2)], 1)
        d_sent[half] = dot_nn(chosen, scaled_ref[...]).astype(jnp.bfloat16).reshape(experts, slots, width)
        d_groups.append(send(lambda e, half=half: d_sent.at[half, e], d_got, d_send, d_recv, half, 5))
    for load in loads:
        load.wait()

    part = 512
    tile = rows // 2

    def forward(half):
        x = x_got[half].reshape(rows, width)
        f_sum[...] = jnp.zeros_like(f_sum)
        x_turned[:, half * rows : (half + 1) * rows] = x.astype(jnp.float32).T.astype(jnp.bfloat16)

        @pl.loop(0, units // part)
        def _(step):
            columns = pl.ds(pl.multiple_of(step * part, part), part)
            for r in range(2):
                near = slice(r * tile, (r + 1) * tile)
                far = pl.ds(half * rows + r * tile, tile)
                gate_pre = dot_nn(x[near], gate_ref[:, columns])
                up_pre = dot_nn(x[near], up_ref[:, columns])
                sigmoid = 1.0 / (1.0 + jnp.exp(-gate_pre))
                active = gate_pre * sigmoid
                hid = (active * up_pre).astype(jnp.bfloat16)
                hid_ref[far, columns] = hid
                one_ref[far, columns] = (up_pre * (sigmoid + active * (1.0 - sigmoid))).astype(jnp.bfloat16)
                two_ref[far, columns] = active.astype(jnp.bfloat16)
                f_sum[near, :] += dot_nn(hid, down_ref[columns, :])

        (fa_out, fb_out)[half][...] = f_sum[...].astype(jnp.bfloat16).reshape(experts, slots, width)

    def backward(half):
        d = d_got[half].reshape(rows, width)
        back_sum[...] = jnp.zeros_like(back_sum)
        d_turned[:, half * rows : (half + 1) * rows] = d.astype(jnp.float32).T.astype(jnp.bfloat16)

        @pl.loop(0, units // part)
        def _(step):
            columns = pl.ds(pl.multiple_of(step * part, part), part)
            for r in range(2):
                near = slice(r * tile, (r + 1) * tile)
                far = pl.ds(half * rows + r * tile, tile)
                mid = dot_nt(d[near], down_ref[columns, :])
                dg = (mid * one_ref[far, columns].astype(jnp.float32)).astype(jnp.bfloat16)
                du = (mid * two_ref[far, columns].astype(jnp.float32)).astype(jnp.bfloat16)
                one_ref[far, columns] = dg
                two_ref[far, columns] = du
                back_sum[near, :] += dot_nt(dg, gate_ref[:, columns]) + dot_nt(du, up_ref[:, columns])

        back_sent[half] = back_sum[...].astype(jnp.bfloat16).reshape(experts, slots, width)

    def dots(half):
        ones = jnp.ones((8, width), jnp.float32)
        for e in range(experts):
            product = (fa_out, fb_out)[half][e].astype(jnp.float32) * d_got[half, e].astype(jnp.float32)
            total = lax.dot_general(
                ones, product, (((1,), (1,)), ((), ())), precision=precise, preferred_element_type=jnp.float32
            )
            dots_sent[half, e] = jnp.concatenate([total, jnp.zeros((8, 128 - slots), jnp.float32)], 1)

    for half in range(2):
        arrive(x_groups[half])
        forward(half)
    back_groups, dots_groups = [], []
    for half in range(2):
        arrive(d_groups[half])
        backward(half)
        back_groups.append(send(lambda e, half=half: back_sent.at[half, e], back_got, back_send, back_recv, half, 7))
        dots(half)
        dots_groups.append(send(lambda e, half=half: dots_sent.at[half, e], dots_got, dots_send, dots_recv, half, 9))

    piece = 256
    steps = units // piece

    def stores(step, slot):
        columns = pl.ds(pl.multiple_of(step * piece, piece), piece)
        return [
            pltpu.make_async_copy(stage.at[0, slot], gate_grad.at[:, columns], stage_sem.at[0, slot]),
            pltpu.make_async_copy(stage.at[1, slot], up_grad.at[:, columns], stage_sem.at[1, slot]),
            pltpu.make_async_copy(stage_down.at[slot], down_grad.at[columns, :], stage_sem.at[2, slot]),
        ]

    @pl.loop(0, steps // 2)
    def _(pair):
        for slot in range(2):
            step = pair * 2 + slot
            columns = pl.ds(pl.multiple_of(step * piece, piece), piece)

            @pl.when(pair > 0)
            def _():
                for store in stores(step, slot):
                    store.wait()

            stage[0, slot] = dot_nn(x_turned[...], one_ref[:, columns]).astype(jnp.bfloat16)
            stage[1, slot] = dot_nn(x_turned[...], two_ref[:, columns]).astype(jnp.bfloat16)
            stage_down[slot] = dot_nn(d_turned[...], hid_ref[:, columns]).T.astype(jnp.bfloat16)
            for store in stores(step, slot):
                store.start()

    for slot in range(2):
        for store in stores(steps - 2 + slot, slot):
            store.wait()
    for group in back_groups + dots_groups:
        arrive(group)
    back_out[...] = back_got[...]
    dots_out[...] = dots_got[...]
    for group in x_groups + d_groups + back_groups + dots_groups:
        for copy in group[1]:
            copy.wait_send()


def expert_phase(x_parts, small, grad, codes_row, gate, up, down):
    rows, width = grad.shape
    units = gate.shape[1]
    slots = rows // NFFN
    both = (2, NFFN, slots, width)
    dots = (2, NFFN, 8, 128)
    vmem, hbm = pl.BlockSpec(memory_space=pltpu.VMEM), pl.BlockSpec(memory_space=pl.ANY)
    sems = pltpu.SemaphoreType.DMA((2, NFFN))
    wide = pltpu.VMEM((rows, width), jnp.float32)
    mids = pltpu.VMEM((2 * rows, units), jnp.bfloat16)
    turned = pltpu.VMEM((width, 2 * rows), jnp.bfloat16)
    moved = pltpu.VMEM(both, jnp.bfloat16)
    return pl.pallas_call(
        expert_phase_kernel,
        in_specs=[vmem] * 5 + [hbm] * 3,
        out_specs=(vmem, vmem, vmem, vmem, hbm, hbm, hbm),
        out_shape=(
            jax.ShapeDtypeStruct(both, jnp.bfloat16),
            jax.ShapeDtypeStruct(dots, jnp.float32),
            *(jax.ShapeDtypeStruct(both[1:], jnp.bfloat16),) * 2,
            jax.ShapeDtypeStruct(gate.shape, jnp.bfloat16),
            jax.ShapeDtypeStruct(up.shape, jnp.bfloat16),
            jax.ShapeDtypeStruct(down.shape, jnp.bfloat16),
        ),
        scratch_shapes=[
            pltpu.VMEM(gate.shape, jnp.bfloat16),
            pltpu.VMEM(up.shape, jnp.bfloat16),
            pltpu.VMEM(down.shape, jnp.bfloat16),
            pltpu.VMEM((2 * rows, width), jnp.bfloat16),
            moved, moved, moved, moved, moved,
            pltpu.VMEM(dots, jnp.float32),
            pltpu.VMEM(dots, jnp.float32),
            wide, wide, mids, mids, mids, turned, turned,
            pltpu.VMEM((2, 2, width, 256), jnp.bfloat16),
            pltpu.VMEM((2, 256, width), jnp.bfloat16),
            *(sems,) * 8,
            pltpu.SemaphoreType.DMA((11,)),
            pltpu.SemaphoreType.DMA((3, 2)),
        ],
        compiler_params=pltpu.CompilerParams(vmem_limit_bytes=63 * MIB, collective_id=2, has_side_effects=True),
        cost_estimate=cost(36 * rows * width * units, 5e7),
    )(*(part.reshape(NFFN, slots, width) for part in x_parts), small, grad, codes_row, gate, up, down)


def split_dot(dot, left, right):
    high = left.astype(jnp.bfloat16)
    low = (left - high.astype(jnp.float32)).astype(jnp.bfloat16)
    return dot(high, right) + dot(low, right)


def put_part(ref, values, begin):
    _, chips, owners, tall, half = ref.shape
    end = begin + values.shape[1]
    for core in range(2):
        low, high = max(begin, core * half), min(end, (core + 1) * half)
        if low < high:
            for z in range(owners):
                for chip in range(chips):
                    row = (z * chips + chip) * tall
                    ref[core, chip, z, :, low - core * half : high - core * half] = values[
                        row : row + tall, low - begin : high - begin
                    ]


def turn_kernel(
    resid_ref, small_ref, grad_ref, prior_ref, codes_ref, returned_ref, dots_ref, table_ref,
    mixer_ref, prior_weight_ref, out_weight_ref, attended_ref, f_ref, gate_ref,
    resid_grad_ref, grads_ref, out_grad_ref, prior_grad_ref, f_got, gate_first,
    back_ref, sums_ref, prior_sums_ref, extra_ref, f_send, f_recv, gate_send, gate_recv, *, owners, reduce,
):
    rows, width = resid_ref.shape
    planes = plane_partners(owners)
    beside, behind, across = plane_chips(lax.axis_index("xy"))
    greet([item[2] for item in planes], [{"xy": beside}, {"xy": behind}] if reduce else [])
    expert = lax.axis_index("expert") * 2 + lax.axis_index("core")
    copies = [pltpu.make_async_copy(f_ref.at[expert], f_got.at[expert], f_send.at[0])]
    copies += [
        remote(f_ref.at[index], f_got.at[expert], f_send.at[step], f_recv.at[step], device)
        for step, index, device in planes
    ]
    if reduce:
        for piece, landing, chip in first_hops(beside, behind, across):
            copies.append(
                remote(
                    gate_ref.at[piece], gate_first.at[landing], gate_send.at[landing], gate_recv.at[landing],
                    {"xy": chip},
                )
            )
    for copy in copies:
        copy.start()
    slots = returned_ref.shape[0]
    sums_ref[...] = jnp.zeros_like(sums_ref)
    prior_sums_ref[...] = jnp.zeros_like(prior_sums_ref)

    @pl.loop(0, rows // SEG)
    def _(step):
        span = pl.ds(pl.multiple_of(step * SEG, SEG), SEG)
        small = small_ref[span, :]
        codes = codes_ref[span, :]
        routes = codes[:, 2:4]
        gates = [small[:, c : c + 1] for c in range(2)]
        mixing = [[small[:, 2 + 2 * m + c : 3 + 2 * m + c] for c in range(2)] for m in range(2)]
        inverse = small[:, 6:7]
        normed = resid_ref[span, :] * inverse
        gain = table_ref[1:2, :]
        hidden = normed * gain
        hidden_b = hidden.astype(jnp.bfloat16)
        grad_b = grad_ref[span, :]
        grad = grad_b.astype(jnp.float32)
        index = lax.broadcasted_iota(jnp.int32, (SEG, slots), 1)
        hits = [codes[:, c : c + 1] == index for c in range(2)]
        dots = dots_ref[...]
        terms = [jnp.sum(jnp.where(hit, dots, 0.0), -1, keepdims=True) for hit in hits]
        chosen = (hits[0] | hits[1]).astype(jnp.bfloat16)
        routed = dot_nn(chosen, returned_ref[...])
        along = jnp.sum(grad * hidden, -1, keepdims=True)
        across = [jnp.sum(grad * table_ref[2 + m : 3 + m, :], -1, keepdims=True) for m in range(2)]
        to_copy = 0.0
        to_mix = [0.0, 0.0]
        for c in range(2):
            route = routes[:, c : c + 1]
            copied = jnp.where(route == NFFN + 1, gates[c], 0.0)
            to_copy = to_copy + copied
            terms[c] = terms[c] + copied * along
            for m in range(2):
                mixed = jnp.where(route == NFFN + 2 + m, gates[c], 0.0)
                to_mix[m] = to_mix[m] + mixed
                terms[c] = terms[c] + mixed * (mixing[m][0] * along + mixing[m][1] * across[m])
        both = terms[0] + terms[1]
        lanes = lax.broadcasted_iota(jnp.int32, (SEG, 128), 1)
        logit_grads = jnp.zeros((SEG, 128), jnp.float32)
        for c in range(2):
            logit_grads = jnp.where(lanes == routes[:, c : c + 1], terms[c] - gates[c] * both, logit_grads)
        scores = logit_grads
        direct = to_copy
        for m in range(2):
            pair = (to_mix[m] * along, to_mix[m] * across[m])
            mean = mixing[m][0] * pair[0] + mixing[m][1] * pair[1]
            for c in range(2):
                scores = jnp.where(lanes == NEXP + 2 * m + c, mixing[m][c] * (pair[c] - mean), scores)
            direct = direct + mixing[m][0] * to_mix[m]
        prior_grad_ref[:, span] = lax.dot_general(
            prior_weight_ref[...], logit_grads[:, :NEXP], (((1,), (1,)), ((), ())),
            precision=precise, preferred_element_type=jnp.float32,
        )
        hidden_grads = split_dot(dot_nn, scores, mixer_ref[...]) + direct * grad + routed
        scaled = hidden_grads * gain
        resid_grads = inverse * (scaled - normed * jnp.mean(scaled * normed, -1, keepdims=True)) + grad
        resid_grad_ref[span, :] = resid_grads
        back_ref[span, :] = resid_grads.astype(jnp.bfloat16)
        weights = jnp.zeros((SEG, 128), jnp.float32)
        for m in range(2):
            weights = jnp.where(lanes == m, mixing[m][1] * to_mix[m], weights)
        sums_ref[0:16, :] += split_dot(dot_nn, scores.T[0:16], hidden_b)
        sums_ref[16:24, :] += split_dot(dot_nn, weights.T[0:8], grad_b)
        sums_ref[24:32, :] += jnp.sum((hidden_grads * normed).reshape(SEG // 8, 8, width), 0)
        prior_sums_ref[...] += jnp.dot(
            prior_ref[:, span],
            jnp.concatenate([logit_grads[:, 96:], logit_grads[:, :96]], 1),
            precision=precise,
            preferred_element_type=jnp.float32,
        )

    sums_ref[24:25, :] = jnp.sum(sums_ref[24:32, :], 0, keepdims=True)
    extra_ref[...] = jnp.concatenate([sums_ref[...], jnp.zeros((96, width), jnp.float32)], 0).T
    kept = NEXP // owners
    for z in range(owners):
        extra_ref[pl.ds(z * (width // owners), kept), :] += prior_sums_ref[z * kept : (z + 1) * kept, :]
    small_part = jnp.concatenate([extra_ref[...], jnp.zeros((width, 128), jnp.float32)], 1).astype(jnp.bfloat16)
    put_part(out_grad_ref, small_part, width)
    back = back_ref[...]
    grads_ref[...] = dot_nt(out_weight_ref[...], back).astype(jnp.bfloat16)
    put_part(out_grad_ref, dot_nn(attended_ref[...], back).astype(jnp.bfloat16), 0)
    for copy in copies:
        copy.wait()


def turn(resid, small, grad, prior, codes, returned, dots, table, mixer, prior_weight, out_weight, attended, f, gate):
    rows, width = resid.shape
    owners = lax.axis_size("expert")
    vmem, hbm = pl.BlockSpec(memory_space=pltpu.VMEM), pl.BlockSpec(memory_space=pl.ANY)
    return pl.pallas_call(
        functools.partial(turn_kernel, owners=owners, reduce=relayed(gate.shape[0])),
        in_specs=[vmem] * 12 + [hbm] * 2,
        out_specs=(vmem, vmem, vmem, vmem, hbm, hbm),
        out_shape=(
            jax.ShapeDtypeStruct((rows, width), jnp.float32),
            jax.ShapeDtypeStruct((width, rows), jnp.bfloat16),
            jax.ShapeDtypeStruct((2, 4, owners, width // owners // 4, (width + 256) // 2), jnp.bfloat16),
            jax.ShapeDtypeStruct(prior.shape, jnp.float32),
            jax.ShapeDtypeStruct(f.shape, f.dtype),
            jax.ShapeDtypeStruct((4, *gate.shape[1:]), gate.dtype),
        ),
        scratch_shapes=[
            pltpu.VMEM((rows, width), jnp.bfloat16),
            pltpu.VMEM((32, width), jnp.float32),
            pltpu.VMEM((prior.shape[0], 128), jnp.float32),
            pltpu.VMEM((width, 128), jnp.float32),
            pltpu.SemaphoreType.DMA((2 * owners,)),
            pltpu.SemaphoreType.DMA((2 * owners,)),
            pltpu.SemaphoreType.DMA((4,)),
            pltpu.SemaphoreType.DMA((4,)),
        ],
        compiler_params=pltpu.CompilerParams(vmem_limit_bytes=63 * MIB, collective_id=4, has_side_effects=True),
        cost_estimate=cost(4 * rows * width * width + 4 * rows * rows * width, 1.5e7),
    )(resid, small, grad, prior, codes, returned, dots, table, mixer, prior_weight, out_weight, attended, f, gate)


def finish_kernel(
    resid_ref, small_ref, codes_ref, fa_ref, fb_ref, table_ref, totals_ref, tokens_grad_ref, *refs, owners, count, reduce
):
    experts, refs = refs[: 3 * count], refs[3 * count :]
    tokens_grad_out, *expert_outs = refs[:4]
    out_ref, *weight_refs, router_ref, prior_ref, constant_ref, vector_ref, gains_ref = refs[4:14]
    held, *work = refs[14:-2]
    load_sem, store_sem = refs[-2:]
    core = lax.axis_index("core")
    place = lax.axis_index("xy") * 2 + core
    load = pltpu.make_async_copy(tokens_grad_ref, held, load_sem.at[0])
    loads = []
    for i in range(3):
        if reduce:
            piece, first, got = experts[3 * i : 3 * i + 3]
            items = (piece.at[place], first.at[core], got.at[4 + core], got.at[6], got.at[7], got.at[5 - core])
        else:
            items = (experts[i],)
        for n, item in enumerate(items):
            target = work[2 * i].at[n] if reduce else work[2 * i + 1]
            loads.append((i, pltpu.make_async_copy(item, target, load_sem.at[1 + 6 * i + n])))
    load.start()
    for _, item in loads:
        item.start()
    stores = [pltpu.make_async_copy(held, tokens_grad_out, store_sem.at[0])]
    stores += [pltpu.make_async_copy(work[2 * i + 1], expert_outs[i], store_sem.at[1 + i]) for i in range(3)]
    rows, width = resid_ref.shape
    half = fa_ref.shape[0]

    @pl.loop(0, rows // SEG)
    def _(step):
        span = pl.ds(pl.multiple_of(step * SEG, SEG), SEG)
        small = small_ref[span, :]
        codes = codes_ref[span, :]
        routes = codes[:, 2:4]
        resid = resid_ref[span, :]
        hidden = resid * small[:, 6:7] * table_ref[1:2, :]
        index = lax.broadcasted_iota(jnp.int32, (SEG, 2 * half), 1)
        total = resid
        direct = 0.0
        for c in range(2):
            gate, route = small[:, c : c + 1], routes[:, c : c + 1]
            chosen = (codes[:, c : c + 1] == index).astype(jnp.bfloat16)
            routed = dot_nn(chosen[:, :half], fa_ref[...]) + dot_nn(chosen[:, half:], fb_ref[...])
            total = total + gate * routed
            direct = direct + jnp.where(route == NFFN + 1, gate, 0.0)
            for m in range(2):
                mixed = jnp.where(route == NFFN + 2 + m, gate, 0.0)
                direct = direct + mixed * small[:, 2 + 2 * m : 3 + 2 * m]
                total = total + mixed * small[:, 3 + 2 * m : 4 + 2 * m] * table_ref[2 + m : 3 + m, :]
        out_ref[span, :] = (total + direct * hidden).astype(jnp.bfloat16)

    load.wait()
    stores[0].start()
    for i in range(3):
        for index, item in loads:
            if index == i:
                item.wait()
        if reduce:
            wide = work[2 * i + 1]
            for n in range(2):
                wide[core if n == 0 else 1 - core] = jnp.sum(work[2 * i][3 * n : 3 * n + 3].astype(jnp.float32), 0)
        stores[1 + i].start()
    span = owners * HEAD_DIM
    chunks = width // span
    offsets, _ = part_columns(width, chunks)
    for i, ref in enumerate(weight_refs[:3]):
        for j in range(chunks):
            begin = offsets[j + 1] + i * span if j < chunks - 1 or i < 2 else offsets[-1]
            ref[:, j * span : (j + 1) * span] = totals_ref[:, begin : begin + span].astype(jnp.float32)
    weight_refs[3][...] = totals_ref[:, :width].astype(jnp.float32)
    extra = totals_ref[:, width : width + 128].astype(jnp.float32)
    prior_ref[...] = extra[: NEXP // owners, 32 : 32 + NEXP]
    turned = extra.T
    router_ref[...] = turned[:NEXP]
    constant_ref[...] = turned[NEXP : NEXP + 4]
    vector_ref[...] = turned[16:18]
    begin = offsets[-1] + span
    gains = totals_ref[:, begin : begin + 128].astype(jnp.float32).T
    member = lax.axis_index("expert")
    share = router_ref.shape[1]
    own_gain = table_ref[0:1, :share]
    for z in range(1, owners):
        own_gain = jnp.where(member == z, table_ref[0:1, z * share : (z + 1) * share], own_gain)
    gains_ref[0:1, :] = gains[0:1] / own_gain
    gains_ref[1:2, :] = turned[24:25]
    for move in stores:
        move.wait()


def finish(resid, small, codes, outs, table, totals, tokens_grad, experts, reduce):
    rows, width = resid.shape
    owners = lax.axis_size("expert")
    share = width // owners
    vmem, hbm = pl.BlockSpec(memory_space=pltpu.VMEM), pl.BlockSpec(memory_space=pl.ANY)
    shape = lambda *dims: jax.ShapeDtypeStruct(dims, jnp.float32)
    count = 3 if reduce else 1
    shapes = [item.shape[1:] for item in experts[count - 1 :: count]]
    work = []
    for dims in shapes:
        work += [pltpu.VMEM((6 if reduce else 1, *dims), jnp.bfloat16), pltpu.VMEM((2, *dims), jnp.float32)]
    return pl.pallas_call(
        functools.partial(finish_kernel, owners=owners, count=count, reduce=reduce),
        in_specs=[vmem] * 7 + [hbm] * (1 + len(experts)),
        out_specs=(hbm,) * 4 + (vmem,) * 10,
        out_shape=(
            shape(rows, width),
            *(shape(2, *dims) for dims in shapes),
            jax.ShapeDtypeStruct((rows, width), jnp.bfloat16),
            *(shape(share, width),) * 4,
            shape(NEXP, share), shape(NEXP // owners, NEXP), shape(4, share), shape(2, share), shape(2, share),
        ),
        scratch_shapes=[
            pltpu.VMEM((rows, width), jnp.float32), *work,
            pltpu.SemaphoreType.DMA((19,)), pltpu.SemaphoreType.DMA((4,)),
        ],
        compiler_params=params(63),
        cost_estimate=cost(8 * rows * rows * width, 8e6),
    )(resid, small, codes, *outs, table, totals, tokens_grad, *experts)


def attend_back_phase_kernel(
    grads_ref, heads_ref, outs_ref, lse_ref, bias_ref, cos_ref, sin_ref, tokens_ref, table_ref,
    query_ref, key_ref, value_ref, resid_grad_ref, out_part_ref, f_ref, gate_ref, up_ref, down_ref, gate_first,
    tokens_grad_ref, f_got, gate_got, up_got, down_got, *rest, reduce,
):
    chunks, owners, _, rows = grads_ref.shape
    width = tokens_ref.shape[1]
    if reduce:
        total_ref, *rest = rest
    else:
        flat_ref, *rest = rest
    (
        d_got, back_sent, back_got, normed_turned, turned_ref, back_sum, column_ref,
        qt_ref, kt_ref, dt_ref, q_ref, k_ref, v_ref, d_ref, delta_ref, dq_ref, dk_ref, dv_ref, triangle,
        d_send, d_recv, back_send, back_recv, weight_send, weight_recv, f_send, f_recv, local_sem, early_sem, *rest,
    ) = rest
    if reduce:
        (
            half_send, half_recv, chip_send, chip_recv, ring_send, ring_recv, all_send, all_recv,
            gate_work, gate_sums, up_sums, down_work, down_sums, work_sem, *rest,
        ) = rest
        count = len(part_columns(width, chunks)[1])
        own_parts, half_got, chip_got, chip_sum, ring_got, ring_sum, all_got = (
            rest[max(0, n * count - 1) : (n + 1) * count - 1] for n in range(7)
        )
        parts = [out_part_ref, *own_parts]
    copies = gate_ref.shape[0]
    member, xy, core = (lax.axis_index(name) for name in ("expert", "xy", "core"))
    place = xy * 2 + core
    ring, others, planes = ring_partners(owners), copy_partners(copies), plane_partners(owners)
    greet([item[2] for item in planes], [item[2] for item in others])

    d_groups = []
    for j in range(chunks):
        local = pltpu.make_async_copy(grads_ref.at[j, member], d_got.at[j, member], local_sem.at[j])
        local.start()
        group = []
        for step, index, device in ring:
            copy = remote(
                grads_ref.at[j, index], d_got.at[j, member], d_send.at[j, step - 1], d_recv.at[j, step - 1], device
            )
            copy.start()
            group.append(copy)
        d_groups.append((local, group))

    inputs = tokens_ref[...].astype(jnp.float32)
    inverse = lax.rsqrt(jnp.mean(inputs * inputs, -1, keepdims=True) + epsilon)
    normed_turned[...] = (inputs * inverse * table_ref[0:1, :]).T.astype(jnp.bfloat16)
    share = width // owners

    offsets, sizes = part_columns(width, chunks)

    def fill(p, values, begin, size):
        if reduce:
            put_part(parts[p], values, begin)
        else:
            begin = offsets[p] + begin
            flat_ref[:, begin : begin + size] = values

    early = pltpu.make_async_copy(resid_grad_ref, tokens_grad_ref, early_sem.at[0])
    early.start()
    last_part = len(sizes) - 1
    fill(last_part, jnp.zeros((width, 128), jnp.bfloat16), sizes[-1] - 128, 128)

    stages = {}

    def over_cores(p):
        copy = remote(parts[p].at[1 - core], half_got[p], half_send.at[p], half_recv.at[p], {"core": 1 - core})
        copy.start()
        stages[p, 0] = [copy]

    def over_chips(p):
        for copy in stages[p, 0]:
            copy.wait_recv()
        half_got[p][...] = (parts[p][core].astype(jnp.float32) + half_got[p][...].astype(jnp.float32)).astype(
            jnp.bfloat16
        )
        stages[p, 1] = []
        for step in (3, 1, 2):
            index = lax.rem(xy + step, 4)
            copy = remote(
                half_got[p].at[index], chip_got[p].at[xy],
                chip_send.at[p, step - 1], chip_recv.at[p, step - 1], {"xy": index},
            )
            copy.start()
            stages[p, 1].append(copy)
        chip_got[p][xy] = half_got[p][xy]

    def over_owners(p):
        for copy in stages[p, 1]:
            copy.wait_recv()
        chip_sum[p][...] = jnp.sum(chip_got[p][...].astype(jnp.float32), 0).astype(jnp.bfloat16)
        stages[p, 2] = []
        for step, index, device in ring:
            copy = remote(
                chip_sum[p].at[index], ring_got[p].at[member],
                ring_send.at[p, step - 1], ring_recv.at[p, step - 1], device,
            )
            copy.start()
            stages[p, 2].append(copy)
        ring_got[p][member] = chip_sum[p][member]

    def to_copies(p):
        for copy in stages[p, 2]:
            copy.wait_recv()
        ring_sum[p][...] = jnp.sum(ring_got[p][...].astype(jnp.float32), 0).astype(jnp.bfloat16)
        stages[p, 3] = []
        for step, _, device in others:
            copy = remote(
                ring_sum[p], all_got[p].at[xy, core], all_send.at[p, step - 1], all_recv.at[p, step - 1], device
            )
            copy.start()
            stages[p, 3].append(copy)
        all_got[p][xy, core] = ring_sum[p][...]

    def advance(*pairs):
        if reduce:
            for stage, p in pairs:
                (over_cores, over_chips, over_owners, to_copies)[stage](p)

    advance((0, 0))

    background = []

    pieces = ((gate_ref, gate_got), (up_ref, up_got), (down_ref, down_got))

    def send_experts():
        for i, (source, target) in enumerate(pieces):
            local = pltpu.make_async_copy(source.at[place], target.at[place], weight_send.at[i, 0])
            local.start()
            background.append(local.wait)
            for step, index, device in others:
                copy = remote(
                    source.at[2 * device["xy"] + device["core"]], target.at[place],
                    weight_send.at[i, step], weight_recv.at[i, step], device,
                )
                copy.start()
                background.append(copy.wait)

    beside, behind, across = plane_chips(xy)
    landed = {}
    sent = []

    def relay(i, source, landing, device):
        copy = remote(
            source, landing_ref(i, landing), weight_send.at[i, landing], weight_recv.at[i, landing], device
        )
        copy.start()
        landed[i, landing] = copy
        sent.append(copy)

    def landing_ref(i, landing):
        return gate_first.at[landing] if i == 0 and landing < 4 else pieces[i][1].at[landing]

    def arrive(i, *landings):
        for landing in landings:
            if (i, landing) in landed:
                landed[i, landing].wait_recv()

    def first_hop(i):
        for piece, landing, chip in first_hops(beside, behind, across):
            relay(i, pieces[i][0].at[piece], landing, {"xy": chip})

    def second_hop(i):
        source, target = pieces[i]
        work, sums = (gate_work, (gate_sums, up_sums)[i]) if i < 2 else (down_work, down_sums)
        arrive(i, 2, 3)
        items = (source.at[behind * 2], landing_ref(i, 2), source.at[beside * 2 + 1], landing_ref(i, 3))
        loads = [pltpu.make_async_copy(ref, work.at[n], work_sem.at[n]) for n, ref in enumerate(items)]
        for item in loads:
            item.start()
        arrive(i, 0, 1)
        other = {"core": 1 - core}
        relay(i, source.at[xy * 2 + 1 - core], 6, other)
        relay(i, (gate_first if i == 0 else target).at[1 - core], 7, other)
        for item in loads:
            item.wait()
        for n, device in enumerate(({"xy": behind, "core": 0}, {"xy": beside, "core": 1})):
            sums[n] = (work[2 * n].astype(jnp.float32) + work[2 * n + 1].astype(jnp.float32)).astype(jnp.bfloat16)
            copy = remote(
                sums.at[n], target.at[4 + core], weight_send.at[i, 4 + n], weight_recv.at[i, 4 + core], device
            )
            copy.start()
            sent.append(copy)
            landed[i, 4 + n] = remote(
                sums.at[n], target.at[4 + n], weight_send.at[i, 4 + n], weight_recv.at[i, 4 + n], device
            )

    if reduce:
        for i in (1, 2):
            first_hop(i)
    else:
        send_experts()

    def head(j):
        local, group = d_groups[j]
        local.wait()
        for copy in group:
            copy.wait_recv()
        attend_back_head(
            bias_ref, cos_ref, sin_ref, heads_ref.at[j], outs_ref.at[j], lse_ref.at[j : j + 1], d_got.at[j],
            back_sent.at[j], qt_ref, kt_ref, dt_ref, q_ref, k_ref, v_ref, d_ref, delta_ref, dq_ref, dk_ref, dv_ref,
            triangle,
        )

    def send_back(j, cuts):
        local = None
        if cuts[0][1] == 0:
            local = pltpu.make_async_copy(back_sent.at[j, member], back_got.at[j, member], local_sem.at[chunks + j])
            local.start()
        groups = []
        for slot, begin, size in cuts:
            span = pl.ds(begin, size)
            group = []
            for step, index, device in ring:
                copy = remote(
                    back_sent.at[j, index, span], back_got.at[j, member, span],
                    back_send.at[slot, step - 1], back_recv.at[slot, step - 1], device,
                )
                copy.start()
                group.append(copy)
            groups.append(group)
        return local, groups

    span_width = owners * HEAD_DIM

    def weights_of(j, group, types=(0, 1, 2)):
        local, copies_in = group
        if 0 in types:
            local.wait()
        for copy in copies_in[1 if 0 not in types else 0]:
            copy.wait_recv()
        total = None
        for i in types:
            for z in range(owners):
                row = i * span_width + z * HEAD_DIM
                turned_ref[row : row + HEAD_DIM, :] = back_got[j, z, i * HEAD_DIM : (i + 1) * HEAD_DIM]
            weight = (query_ref, key_ref, value_ref)[i]
            term = dot_nn(
                weight[:, j * span_width : (j + 1) * span_width], turned_ref[i * span_width : (i + 1) * span_width, :]
            )
            total = term if total is None else total + term
        first = j == 0 and 0 in types
        back_sum[...] = total if first else back_sum[...] + total
        column = jnp.sum(total * normed_turned[...].astype(jnp.float32), -1, keepdims=True)
        column_ref[...] = column if first else column_ref[...] + column
        begin, size = types[0] * span_width, len(types) * span_width
        part = j + 1 if 0 in types else j + 2
        if part == last_part:
            fill(part, jnp.broadcast_to(column_ref[...], (width, 128)).astype(jnp.bfloat16), span_width, 128)
        fill(part, dot_nt(normed_turned[...], turned_ref[begin : begin + size, :]).astype(jnp.bfloat16), 0, size)

    expert = member * 2 + core

    def send_f(distance):
        if distance == 0:
            local = pltpu.make_async_copy(f_ref.at[expert], f_got.at[expert], f_send.at[0])
            local.start()
            background.append(local.wait)
        for step, index, device in planes[3 * distance : 3 * distance + 3]:
            copy = remote(f_ref.at[index], f_got.at[expert], f_send.at[step], f_recv.at[step], device)
            copy.start()
            background.append(copy.wait)

    def expert_step(step, i):
        if reduce:
            step(i)

    part_k, part_v = chunks, chunks + 1
    both = 2 * HEAD_DIM
    head(0)
    groups = [send_back(0, [(0, 0, 3 * HEAD_DIM)])]
    advance((1, 0))
    head(1)
    advance((2, 0))
    groups.append(send_back(1, [(1, 0, 3 * HEAD_DIM)]))
    expert_step(second_hop, 0)
    expert_step(second_hop, 1)
    head(2)
    groups.append(send_back(2, [(2, 0, both), (3, both, HEAD_DIM)]))
    expert_step(second_hop, 2)
    weights_of(0, groups[0])
    advance((0, 1), (3, 0))
    weights_of(1, groups[1])
    advance((1, 1), (0, 2))
    weights_of(2, groups[2], (0, 1))
    advance((0, part_k), (1, 2), (2, 1))
    weights_of(2, groups[2], (2,))
    advance((0, part_v), (1, part_k), (2, 2))
    send_f(0)
    advance((1, part_v), (2, part_k))
    send_f(1)
    normed = inputs * inverse
    first_grads = back_sum[...].T
    advance((2, part_v))
    send_f(2)
    scaled = first_grads * table_ref[0:1, :]
    early.wait()
    tokens_grad_ref[...] += inverse * (scaled - normed * jnp.mean(scaled * normed, -1, keepdims=True))
    advance((3, 1), (3, 2), (3, part_k), (3, part_v))
    if reduce:
        for p in range(len(sizes)):
            for copy in stages[p, 3]:
                copy.wait_recv()
            for stage in range(4):
                for copy in stages[p, stage]:
                    copy.wait_send()
            _, _, tall, half = all_got[p].shape
            for chip in range(4):
                for side in range(2):
                    begin = offsets[p] + side * half
                    total_ref[chip * tall : (chip + 1) * tall, begin : begin + half] = all_got[p][chip, side]
        for i in range(3):
            arrive(i, 4, 5, 6, 7)
        for copy in sent:
            copy.wait_send()
    for local, group in d_groups:
        for copy in group:
            copy.wait_send()
    for local, items in groups:
        for group in items:
            for copy in group:
                copy.wait_send()
    for wait in background:
        wait()


def part_columns(width, chunks):
    sizes = [width + 256] + [width] * (chunks - 1) + [width // 3 * 2, width // 3 + 256]
    return [sum(sizes[:p]) for p in range(len(sizes))], sizes


def attend_back_phase(
    grads, heads, outs, lse, bias, cosine, sine, tokens, table, weights, resid_grads, out_part, f, pieces, gate_first, copies
):
    chunks, owners, _, rows = grads.shape
    width = tokens.shape[1]
    length = owners * rows
    head = (chunks, owners, 3 * HEAD_DIM, rows)
    sizes = part_columns(width, chunks)[1]
    columns, total = sum(sizes), len(sizes)
    share = width // owners
    reduce = relayed(copies)
    vmem, hbm = pl.BlockSpec(memory_space=pltpu.VMEM), pl.BlockSpec(memory_space=pl.ANY)
    gate_shape, down_shape = pieces[0].shape[1:], pieces[2].shape[1:]
    turned = pltpu.VMEM((HEAD_DIM, length), jnp.bfloat16)
    plain = pltpu.VMEM((length, HEAD_DIM), jnp.bfloat16)
    wide = pltpu.VMEM((length, HEAD_DIM), jnp.float32)
    sems = lambda *shape: pltpu.SemaphoreType.DMA(shape)
    scratch = [
        pltpu.VMEM(grads.shape, jnp.bfloat16),
        pltpu.VMEM(head, jnp.bfloat16),
        pltpu.VMEM(head, jnp.bfloat16),
        pltpu.VMEM((width, rows), jnp.bfloat16),
        pltpu.VMEM((3 * owners * HEAD_DIM, rows), jnp.bfloat16),
        pltpu.VMEM((width, rows), jnp.float32),
        pltpu.VMEM((width, 1), jnp.float32),
        turned, turned, turned, plain, plain, plain, plain,
        pltpu.VMEM((1, length), jnp.float32),
        pltpu.VMEM((HEAD_DIM, length), jnp.float32),
        wide, wide,
        pltpu.VMEM((TILE, TILE), jnp.float32),
        *(sems(chunks, owners - 1),) * 2,
        *(sems(chunks + 1, owners - 1),) * 2,
        sems(3, copies), sems(3, copies), sems(2 * owners), sems(2 * owners), sems(2 * chunks), sems(2),
    ]
    if reduce:
        low = lambda *shape: pltpu.VMEM(shape, jnp.bfloat16)
        scratch += [
            sems(total), sems(total), sems(total, 3), sems(total, 3),
            sems(total, owners - 1), sems(total, owners - 1), sems(total, copies - 1), sems(total, copies - 1),
            low(4, *gate_shape), low(2, *gate_shape), low(2, *gate_shape), low(4, *down_shape), low(2, *down_shape),
            sems(4),
        ]
        tall, halves = share // 4, [size // 2 for size in sizes]
        for shape in (
            (2, 4, owners, tall), (4, owners, tall), (4, owners, tall), (owners, tall), (owners, tall), (tall,), (4, 2, tall)
        ):
            scratch += [low(*shape, half) for half in (halves[1:] if len(shape) == 4 and shape[0] == 2 else halves)]
        last_specs, last_shapes = (vmem,), (jax.ShapeDtypeStruct((share, columns), jnp.bfloat16),)
    else:
        last_specs, last_shapes = (vmem,), (jax.ShapeDtypeStruct((width, columns), jnp.bfloat16),)
    tokens_grad, f_got, *gots, totals = pl.pallas_call(
        functools.partial(attend_back_phase_kernel, reduce=reduce),
        in_specs=[vmem] * 12 + [hbm, vmem] + [hbm] * 5,
        out_specs=(vmem, hbm, hbm, hbm, hbm, *last_specs),
        out_shape=(
            jax.ShapeDtypeStruct((rows, width), jnp.float32),
            jax.ShapeDtypeStruct(f.shape, f.dtype),
            *(jax.ShapeDtypeStruct(piece.shape, piece.dtype) for piece in pieces),
            *last_shapes,
        ),
        scratch_shapes=scratch,
        compiler_params=pltpu.CompilerParams(vmem_limit_bytes=63 * MIB, collective_id=3, has_side_effects=True),
        cost_estimate=cost(2e10, 5e7),
    )(grads, heads, outs, lse, bias, cosine, sine, tokens, table, *weights, resid_grads, out_part, f, *pieces, gate_first)
    if not reduce:
        out_part = out_part.transpose(2, 1, 3, 0, 4).reshape(width, sizes[0])
        totals = jnp.concatenate([out_part, totals[:, sizes[0] :]], 1)
        totals = lax.psum_scatter(totals, "expert", scatter_dimension=0, tiled=True)
        totals = lax.psum(totals, ("xy", "core"))
        gots = [jnp.sum(got.reshape(copies // 2, 2, *got.shape[1:]).astype(jnp.float32), 0) for got in gots]
    return (tokens_grad, f_got, totals, gots)


def per_device(
    tokens, prior_logits, routes, parents, cotangent, query_weight, key_weight, value_weight, out_weight,
    attention_gain, expert_gain, router_weight, prior_weight, constant_weight, constant_vector,
    gate_weight, up_weight, down_weight,
):
    owners = lax.axis_size("expert")
    member = lax.axis_index("expert")
    tokens, prior, routes, grad = tokens[0], prior_logits[0].T, routes[0].T, cotangent[0]
    rows, width = tokens.shape
    copies = lax.axis_size("xy") * lax.axis_size("core")
    chunks = width // HEAD_DIM // owners
    zeros = jnp.zeros((4, width), jnp.float32)
    table = jnp.concatenate([attention_gain[None], expert_gain[None], constant_vector, zeros], 0)
    qkv_weights = (query_weight, key_weight, value_weight)
    attended, logs, bias, cosine, sine, codes, codes_row, heads, outs, gate, up, down = attend_phase(
        tokens, table, qkv_weights, parents, routes, (gate_weight, up_weight, down_weight), copies
    )
    attended = attended.reshape(width, rows)
    gate, up, down = (full.reshape(-1, full.shape[-1]) for full in (gate, up, down))
    resid, small, *x_out, mixer = middle(
        tokens, attended, out_weight, table, router_weight.T, constant_weight.T, prior, prior_weight, codes, codes_row
    )
    backs, dots, fa, fb, *grads = expert_phase(x_out, small, grad, codes_row, gate, up, down)
    pieces = [item.reshape(copies, -1, item.shape[-1]) for item in grads]
    dots = dots[:, :, 0, : rows // NFFN].reshape(1, 2 * rows)
    resid_grads, grads_out, out_part, prior_grad, fa, gate_first = turn(
        resid, small, grad, prior, codes, backs.reshape(2 * rows, width), dots, table, mixer, prior_weight,
        out_weight, attended, fa, pieces[0],
    )
    tokens_grad, fb, totals, gots = attend_back_phase(
        grads_out.reshape(chunks, owners, HEAD_DIM, rows), heads, outs, logs, bias, cosine, sine, tokens,
        table, qkv_weights, resid_grads, out_part, fb, pieces, gate_first, copies,
    )
    fs = [f.reshape(rows, width) for f in (fa, fb)]
    reduce = relayed(copies)
    experts = gots
    if reduce:
        experts = [item for i in range(3) for item in (pieces[i], gate_first if i == 0 else gots[i], gots[i])]
    (
        tokens_grad, gate_part, up_part, down_part, result, *qkv_out_grads, router_grad, prior_weight_grad,
        constant_weight_grad, vector_grad, gain_grads,
    ) = finish(resid, small, codes, fs, table, totals, tokens_grad, experts, reduce)
    return (
        result[None],
        tokens_grad[None],
        prior_grad.T[None],
        *qkv_out_grads,
        gain_grads[0],
        gain_grads[1],
        router_grad.T,
        prior_weight_grad,
        constant_weight_grad.T,
        vector_grad,
        gate_part,
        up_part,
        down_part,
    )


def solution(mesh):
    owners, copies = mesh.shape["expert"], mesh.shape["dp"]
    cores = 2
    mesh = Mesh(mesh.devices.reshape(owners, copies // cores, cores), ("expert", "xy", "core"))
    dp = ("xy", "core")
    rows = P(dp, "expert", None)
    shard = P("expert", dp, None)
    in_specs = (rows, rows, rows, P(dp, None), rows) + (P(),) * 10 + (shard,) * 3
    out_specs = (
        (rows,) * 3
        + (P("expert", None),) * 4
        + (P("expert"),) * 2
        + (P("expert", None),) * 3
        + (P(None, "expert"),)
        + (shard,) * 3
    )
    return jax.shard_map(per_device, mesh=mesh, in_specs=in_specs, out_specs=out_specs, check_vma=False)
```
